256 devices in a mesh: grp: 8 (over z_lo, core), dev: 32 (over y, z_hi, x).
Axes of the slice: x: 4, y: 4, z: 8 (z_hi: 2, z_lo: 4; z = z_hi * 4 + z_lo), core: 2. Of those that a mesh axis runs over, the one named last changes fastest.
Arguments:
- patches: bfloat16 [8192, 4, 768], P(('grp', 'dev')), may hold values from -6 to 6
- tile_region: int32 [8, 1024], P('grp', 'dev'), may hold values from 0 to 31, as said below
- region_slide: int32 [8, 32], P('grp', 'dev'), may hold values from 0 to 3, never falling along the last dimension, each value on 1 to 16 neighbouring positions
- bin_label: int32 [8, 4], P('grp'), may hold values from 0 to 3
- censored: int32 [8, 4], P('grp'), may hold values 0 or 1
- patch_w: bfloat16 [768, 384], replicated, may hold values from -0.21875 to 0.21875
- tile_qkv: bfloat16 [384, 1152], replicated, may hold values from -0.3125 to 0.3125
- tile_out: bfloat16 [384, 384], replicated, may hold values from -0.3125 to 0.3125
- tile_up: bfloat16 [384, 1536], replicated, may hold values from -0.3125 to 0.3125
- tile_down: bfloat16 [1536, 384], replicated, may hold values from -0.15625 to 0.15625
- region_qkv: bfloat16 [384, 1152], replicated, may hold values from -0.3125 to 0.3125
- region_out: bfloat16 [384, 384], replicated, may hold values from -0.3125 to 0.3125
- region_up: bfloat16 [384, 1536], replicated, may hold values from -0.3125 to 0.3125
- region_down: bfloat16 [1536, 384], replicated, may hold values from -0.15625 to 0.15625
- slide_in: bfloat16 [384, 192], replicated, may hold values from -0.3125 to 0.3125
- slide_qkv: bfloat16 [192, 576], replicated, may hold values from -0.4375 to 0.4375
- slide_out: bfloat16 [192, 192], replicated, may hold values from -0.4375 to 0.4375
- slide_up: bfloat16 [192, 192], replicated, may hold values from -0.4375 to 0.4375
- slide_down: bfloat16 [192, 192], replicated, may hold values from -0.4375 to 0.4375
- slide_head: bfloat16 [192, 4], replicated, may hold values from -0.4375 to 0.4375
Outputs:
- slide_losses: float32 [8, 4], P('grp')
- tile_grads: float32 [2064384], P(('grp', 'dev'))
- region_grads: float32 [1769472], P(('grp', 'dev'))
- slide_grads: float32 [295680], P(('grp', 'dev'))
The draws below stay inside these ranges and needn't reach their ends.
Inputs may be any that keep to these rules, and one draw needn't show every extreme that they name: `tile_region`: every region of a group holds between 1 and 64 of the group's tiles, and in every group some region holds exactly 64.
All inputs are finite; a program needn't handle non-finite values. No bound on the sum of `censored` on one device may be relied on, other than what follows from the above.
Results may differ from the reference program's by a relative error of at most 0.03.
Values may be sent and summed in bfloat16 or wider, within the bound.
No kernel may reach another device: no remote copies, remote signals or barrier semaphores. Data moves between devices by JAX's collectives and lax.ppermute only.
A program may use at most 128 MiB of HBM per device.

```python
import math
import jax
import jax.numpy as jnp
import numpy as np
from jax import lax

D = 384
HEADS = 6
FF = 1536
PIX = 768
PATCHES = 4
SLOTS = 64
REG_DEV = 1
D_SL = 192
H_SL = 3
FF_SL = 192
NBINS = 4
SL_GRP = 4
TILE_DEV = 32
GROUPS = 8
TILE_GRP = 1024
REG_GRP = 32
DEVICES = 256


def draw_tile_region(key, part):
    key = jax.random.fold_in(key, 11)

    def one_group(group_key):
        key_first, key_second, key_order, key_tiles = jax.random.split(group_key, 4)
        quads = REG_GRP // 4
        first = jax.random.randint(key_first, (quads,), 1, SLOTS + 1)
        first = first.at[0].set(SLOTS)
        second = jax.random.randint(key_second, (quads,), 1, SLOTS - 1)
        counts = jnp.stack([first, SLOTS + 1 - first, second, SLOTS - 1 - second], axis=1).reshape(-1)
        counts = jax.random.permutation(key_order, counts)
        ends = jnp.cumsum(counts)
        places = jnp.arange(TILE_GRP, dtype=jnp.int32)
        region = jnp.sum((places[:, None] >= ends[None, :]).astype(jnp.int32), axis=1).astype(jnp.int32)
        return jax.random.permutation(key_tiles, region)
    group_keys = jax.random.split(key, GROUPS)
    return jax.vmap(one_group)(group_keys)


def place_ends(array, key, smallest, top_value):
    dims = array.shape
    index_at = [jax.random.randint(jax.random.fold_in(key, axis), (), 0, dims[axis]) for axis in range(len(dims))]
    array = array.at[tuple(index_at)].set(smallest)
    longest = dims.index(max(dims))
    index_at[longest] = (index_at[longest] + 1) % dims[longest]
    return array.at[tuple(index_at)].set(top_value)


def level_of(key, dims, cuts, smallest, top_value):
    level = 1.0
    for dim, parts in cuts:
        heights = jax.random.uniform(jax.random.fold_in(jax.random.fold_in(key, 6), dim), (parts,), jnp.float32, smallest / len(cuts), top_value / len(cuts))
        level = level * jnp.repeat(jnp.exp(heights), dims[dim] // parts).reshape((-1,) + (1,) * (len(dims) - 1 - dim))
    return level


def split_up(number_of, total, bound, slope):
    loads = [(1 << 20) // math.isqrt(grade ** slope) + 1 for grade in range(2, number_of + 1)]
    rest, holding = total - bound - (number_of - 1), [1] * (number_of - 1)
    while rest > 0:
        candidates = [i for i in range(number_of - 1) if holding[i] < bound]
        whole, left = sum([loads[i] for i in candidates]), rest
        for i in candidates:
            more = min(bound - holding[i], max(1, left * loads[i] // whole), rest)
            holding[i] = holding[i] + more
            rest = rest - more
    return np.array([bound] + holding)


def ragged_sizes(key, number_of, total, most, lean):
    if number_of == 2:
        one = jax.random.randint(key, (), max(1, total - most), min(most, total - 1) + 1)
        return jnp.stack([one, total - one])
    lengths = jnp.asarray(split_up(number_of, total, most, lean), jnp.int32)
    couples = (number_of - 1) // 2
    donor, sink = lengths[1:1 + 2 * couples:2], lengths[2:2 + 2 * couples:2]
    room = jnp.minimum(donor - 1, most - sink)
    shifted = jax.random.randint(jax.random.fold_in(key, 1), (couples,), 0, 1 << 20) % (room + 1)
    lengths = lengths.at[1:1 + 2 * couples:2].set(donor - shifted).at[2:2 + 2 * couples:2].set(sink + shifted)
    return lengths[jax.random.permutation(jax.random.fold_in(key, 2), number_of)]


def scatter_about(stream_key, extent, spread, bound, cuts=(), kind=jnp.bfloat16):
    factor_of = level_of(stream_key, extent, cuts, -0.22, 0.18) if cuts else 1.0
    entries = jax.random.normal(stream_key, extent, jnp.float32) * spread * factor_of
    return jnp.minimum(jnp.maximum(entries, -bound), bound).astype(kind)


def setup_inputs(seed: int = 0) -> dict:
    seeds = jax.random.split(jax.random.key(seed), 21)
    patches = scatter_about(seeds[0], (TILE_GRP * GROUPS, PATCHES, PIX), 1.0, 6.0, ((0, 256),))
    tile_region = draw_tile_region(jax.random.fold_in(seeds[20], 71), 0)
    region_slide = jax.vmap(lambda own: jnp.searchsorted(jnp.cumsum(ragged_sizes(own, SL_GRP, REG_GRP, REG_GRP // 2, 1)), jnp.arange(REG_GRP), side="right"))(jax.random.split(seeds[2], GROUPS)).reshape((GROUPS, REG_GRP)).astype(jnp.int32)
    bin_label = place_ends(jax.random.randint(seeds[3], (GROUPS, SL_GRP), 0, NBINS), jax.random.fold_in(seeds[3], 1), 0, NBINS - 1).astype(jnp.int32)
    censored = place_ends((jax.random.randint(seeds[4], (GROUPS, SL_GRP), 0, 3) < 1).astype(jnp.int32), jax.random.fold_in(seeds[4], 1), 0, 1)
    patch_w = scatter_about(seeds[5], (PIX, D), PIX ** -0.5, 0.21875)
    tile_qkv = scatter_about(seeds[6], (D, 3 * D), D ** -0.5, 0.3125)
    tile_out = scatter_about(seeds[7], (D, D), D ** -0.5, 0.3125)
    tile_up = scatter_about(seeds[8], (D, FF), D ** -0.5, 0.3125)
    tile_down = scatter_about(seeds[9], (FF, D), FF ** -0.5, 0.15625)
    region_qkv = scatter_about(seeds[10], (D, 3 * D), D ** -0.5, 0.3125)
    region_out = scatter_about(seeds[11], (D, D), D ** -0.5, 0.3125)
    region_up = scatter_about(seeds[12], (D, FF), D ** -0.5, 0.3125)
    region_down = scatter_about(seeds[13], (FF, D), FF ** -0.5, 0.15625)
    slide_in = scatter_about(seeds[14], (D, D_SL), D ** -0.5, 0.3125)
    slide_qkv = scatter_about(seeds[15], (D_SL, 3 * D_SL), D_SL ** -0.5, 0.4375)
    slide_out = scatter_about(seeds[16], (D_SL, D_SL), D_SL ** -0.5, 0.4375)
    slide_up = scatter_about(seeds[17], (D_SL, FF_SL), D_SL ** -0.5, 0.4375)
    slide_down = scatter_about(seeds[18], (FF_SL, D_SL), FF_SL ** -0.5, 0.4375)
    slide_head = scatter_about(seeds[19], (D_SL, NBINS), D_SL ** -0.5, 0.4375)
    return dict(patches=patches, tile_region=tile_region, region_slide=region_slide, bin_label=bin_label, censored=censored, patch_w=patch_w, tile_qkv=tile_qkv, tile_out=tile_out, tile_up=tile_up, tile_down=tile_down, region_qkv=region_qkv, region_out=region_out, region_up=region_up, region_down=region_down, slide_in=slide_in, slide_qkv=slide_qkv, slide_out=slide_out, slide_up=slide_up, slide_down=slide_down, slide_head=slide_head)


def layer_norm(values):
    average = lax.optimization_barrier(jnp.mean(values, axis=-1, keepdims=True))
    centred = values - average
    variance = lax.optimization_barrier(jnp.mean(centred * centred, axis=-1, keepdims=True))
    return centred * lax.rsqrt(variance + 1e-06)

def encoder(stream, allowed, w_qkv, w_out, w_up, w_down, head_count):
    batches, length, feature = stream.shape
    head_size = feature // head_count
    normed = layer_norm(stream).astype(jnp.bfloat16)
    packed = jnp.einsum('bsd,de->bse', normed.astype(jnp.float32), w_qkv.astype(jnp.float32)).astype(jnp.bfloat16)
    packed = packed.reshape(batches, length, 3, head_count, head_size)
    scores = jnp.einsum('bqhe,bkhe->bhqk', packed[:, :, 0].astype(jnp.float32), packed[:, :, 1].astype(jnp.float32)) / math.sqrt(head_size)
    scores = jnp.where(allowed[:, None], scores, -1e+30)
    attend = jax.nn.softmax(scores, axis=-1).astype(jnp.bfloat16)
    mixture = jnp.einsum('bhqk,bkhe->bqhe', attend.astype(jnp.float32), packed[:, :, 2].astype(jnp.float32)).astype(jnp.bfloat16)
    mixture = mixture.reshape(batches, length, feature)
    stream = stream + jnp.einsum('bsd,de->bse', mixture.astype(jnp.float32), w_out.astype(jnp.float32))
    normed = layer_norm(stream).astype(jnp.bfloat16)
    hidden = jax.nn.gelu(jnp.einsum('bsd,de->bse', normed.astype(jnp.float32), w_up.astype(jnp.float32))).astype(jnp.bfloat16)
    return stream + jnp.einsum('bsd,de->bse', hidden.astype(jnp.float32), w_down.astype(jnp.float32))

def tile_embed(patch_block, patch_w, w_qkv, w_out, w_up, w_down):
    tile_count, length, pixels = patch_block.shape
    tokens = jnp.einsum('npc,cd->npd', patch_block.astype(jnp.float32), patch_w.astype(jnp.float32))
    allowed = jnp.ones((tile_count, 1, length), bool)
    tokens = encoder(tokens, allowed, w_qkv, w_out, w_up, w_down, HEADS)
    return lax.optimization_barrier(jnp.mean(layer_norm(tokens), axis=1)).astype(jnp.bfloat16)

def region_embed(tokens, usable, w_qkv, w_out, w_up, w_down):
    stream = encoder(tokens.astype(jnp.float32), usable[:, None, :], w_qkv, w_out, w_up, w_down, HEADS)
    normed = layer_norm(stream)
    weight = usable.astype(jnp.float32)
    pooled = lax.optimization_barrier(jnp.sum(normed * weight[:, :, None], axis=1)) / lax.optimization_barrier(jnp.sum(weight, axis=1))[:, None]
    return pooled.astype(jnp.bfloat16)

def slide_loss(embedding, slides, labels, censor_row, slide_in, w_qkv, w_out, w_up, w_down, w_head):
    rows = jnp.dot(embedding, slide_in, preferred_element_type=jnp.float32)[None]
    allowed = (slides[:, None] == slides[None, :])[None]
    rows = encoder(rows, allowed, w_qkv, w_out, w_up, w_down, H_SL)
    normed = layer_norm(rows)[0]
    member = (slides[None, :] == jnp.arange(SL_GRP, dtype=jnp.int32)[:, None]).astype(jnp.float32)
    pooled = jnp.dot(member, normed, precision=lax.Precision.HIGHEST) / lax.optimization_barrier(jnp.sum(member, axis=1))[:, None]
    logits = jnp.dot(pooled.astype(jnp.bfloat16), w_head, preferred_element_type=jnp.float32)
    log_hazard = jax.nn.log_sigmoid(logits)
    log_stay = jax.nn.log_sigmoid(-logits)
    log_surv = jnp.cumsum(log_stay, axis=-1)
    log_before = log_surv - log_stay
    choose = (labels[:, None] == jnp.arange(NBINS, dtype=jnp.int32)[None, :]).astype(jnp.float32)
    observed = lax.optimization_barrier(jnp.sum(choose * (log_before + log_hazard), axis=1))
    survived = lax.optimization_barrier(jnp.sum(choose * log_surv, axis=1))
    weight = censor_row.astype(jnp.float32)
    return -(1.0 - weight) * observed - weight * survived

def slot_table(assign, regions):
    tile_count = assign.shape[0]
    onehot = (assign[:, None] == jnp.arange(regions, dtype=jnp.int32)[None, :]).astype(jnp.int32)
    before = jnp.cumsum(onehot, axis=0) - onehot
    position = lax.optimization_barrier(jnp.sum(before * onehot, axis=1))
    counts = lax.optimization_barrier(jnp.sum(onehot, axis=0))
    lookup = jnp.full((regions, SLOTS), tile_count, jnp.int32)
    lookup = lookup.at[assign, position].set(jnp.arange(tile_count, dtype=jnp.int32))
    return (lookup, counts)

def flatten(gradients):
    return jnp.concatenate([gradient.astype(jnp.float32).reshape(-1) for gradient in gradients])

def accumulate(step, inputs, params):
    start = tuple((jnp.zeros(param.shape, jnp.float32) for param in params))

    def advance(carry, item):
        extra, gradients = step(item)
        return (tuple((total + gradient.astype(jnp.float32) for total, gradient in zip(carry, gradients))), extra)
    return lax.scan(advance, start, inputs)

def reference(patches, tile_region, region_slide, bin_label, censored, patch_w, tile_qkv, tile_out, tile_up, tile_down, region_qkv, region_out, region_up, region_down, slide_in, slide_qkv, slide_out, slide_up, slide_down, slide_head):
    tile_params = (patch_w, tile_qkv, tile_out, tile_up, tile_down)
    region_params = (region_qkv, region_out, region_up, region_down)
    slide_params = (slide_in, slide_qkv, slide_out, slide_up, slide_down, slide_head)
    scaling = 1.0 / (SL_GRP * GROUPS)
    blocks = patches.reshape(DEVICES, TILE_DEV, PATCHES, PIX)
    embeds = lax.map(lambda patch_block: tile_embed(patch_block, *tile_params), blocks)
    embeds = embeds.reshape(GROUPS, TILE_GRP, D)
    tables, counts = jax.vmap(lambda assign: slot_table(assign, REG_GRP))(tile_region)
    usable = jnp.arange(SLOTS, dtype=jnp.int32)[None, None, :] < counts[:, :, None]
    padded = jnp.concatenate([embeds, jnp.zeros((GROUPS, 1, D), jnp.bfloat16)], axis=1)
    gathered = jax.vmap(lambda embedding, lookup: embedding[lookup])(padded, tables)
    region_tokens = gathered.reshape(DEVICES, REG_DEV, SLOTS, D)
    region_usable = usable.reshape(DEVICES, REG_DEV, SLOTS)
    region_embs = lax.map(lambda inputs: region_embed(inputs[0], inputs[1], *region_params), (region_tokens, region_usable))
    region_embs = region_embs.reshape(GROUPS, REG_GRP, D)

    def slide_step(inputs):
        embedding, slides, labels, censor_row = inputs
        losses, pullback = jax.vjp(lambda emb_rows, *params: slide_loss(emb_rows, slides, labels, censor_row, *params), embedding, *slide_params)
        cotangents = pullback(jnp.full(losses.shape, scaling, jnp.float32))
        return ((losses, cotangents[0]), cotangents[1:])
    slide_sums, slide_extra = accumulate(slide_step, (region_embs, region_slide, bin_label, censored), slide_params)
    losses, emb_cot = slide_extra

    def region_step(inputs):
        tokens, usable_rows, cotangent = inputs
        unused, pullback = jax.vjp(lambda token_rows, *params: region_embed(token_rows, usable_rows, *params), tokens, *region_params)
        cotangents = pullback(cotangent)
        return (cotangents[0], cotangents[1:])
    region_sums, token_cot = accumulate(region_step, (region_tokens, region_usable, emb_cot.reshape(DEVICES, REG_DEV, D)), region_params)
    token_cot = token_cot.reshape(GROUPS, REG_GRP * SLOTS, D).astype(jnp.bfloat16).astype(jnp.float32)

    def scatter_back(cotangent, lookup):
        return jnp.zeros((TILE_GRP + 1, D), jnp.float32).at[lookup.reshape(-1)].add(cotangent)[:TILE_GRP]
    tile_cot = jax.vmap(scatter_back)(token_cot, tables).astype(jnp.bfloat16).reshape(DEVICES, TILE_DEV, D)

    def tile_step(inputs):
        patch_block, cotangent = inputs
        unused, pullback = jax.vjp(lambda *params: tile_embed(patch_block, *params), *tile_params)
        return (jnp.zeros((), jnp.float32), pullback(cotangent))
    tile_sums, unused_extra = accumulate(tile_step, (blocks, tile_cot), tile_params)
    return (losses, flatten(tile_sums), flatten(region_sums), flatten(slide_sums))
```

```python
import functools
import math

import jax
import jax.numpy as jnp
from jax import lax
from jax.experimental import pallas as pl
from jax.experimental.pallas import tpu as pltpu
from jax.sharding import PartitionSpec as P

D = 384
HEADS = 6
FF = 1536
PATCHES = 4
SLOTS = 64
D_SL = 192
H_SL = 3
NBINS = 4
SL_GRP = 4
HEAD = 64
F32 = jnp.float32
BF16 = jnp.bfloat16
LANES = 128
GELU_C = math.sqrt(2.0 / math.pi)


def mm(a, b):
    return jnp.dot(a, b, preferred_element_type=F32)


def mm_nt(a, b):
    return lax.dot_general(a, b, (((1,), (1,)), ((), ())), preferred_element_type=F32)


def mm_tn(a, b):
    return lax.dot_general(a, b, (((0,), (0,)), ((), ())), preferred_element_type=F32)


def norm_parts(x):
    average = jnp.mean(x, axis=-1, keepdims=True)
    centred = x - average
    variance = jnp.mean(centred * centred, axis=-1, keepdims=True)
    rstd = lax.rsqrt(variance + 1e-06)
    return centred * rstd, rstd


def norm_back(grad, normed, rstd):
    first = jnp.mean(grad, axis=-1, keepdims=True)
    second = jnp.mean(grad * normed, axis=-1, keepdims=True)
    return rstd * (grad - first - normed * second)


def gelu_parts(x):
    t = jnp.tanh(GELU_C * (x + 0.044715 * (x * x * x)))
    value = 0.5 * x * (1.0 + t)
    slope = 0.5 * (1.0 + t) + 0.5 * x * (1.0 - t * t) * (GELU_C * (1.0 + 3.0 * 0.044715 * (x * x)))
    return value, slope


def encode(x, allowed, w_qkv, w_out, w_up, w_down, heads, res):
    packed_ref, attend_ref, mixture_ref, mid_ref, up_ref, out_ref = res
    width = x.shape[1]
    normed, _ = norm_parts(x)
    packed_ref[...] = mm(normed.astype(BF16), w_qkv[...]).astype(BF16)
    send(packed_ref)
    for h in range(heads):
        q = packed_ref[:, h * HEAD : (h + 1) * HEAD]
        k = packed_ref[:, width + h * HEAD : width + (h + 1) * HEAD]
        v = packed_ref[:, 2 * width + h * HEAD : 2 * width + (h + 1) * HEAD]
        scores = jnp.where(allowed, mm_nt(q, k) * 0.125, -1e30)
        scores = jnp.exp(scores - jnp.max(scores, axis=-1, keepdims=True))
        weights = scores / jnp.sum(scores, axis=-1, keepdims=True)
        attend_ref[h] = weights
        mixture_ref[:, h * HEAD : (h + 1) * HEAD] = mm(weights.astype(BF16), v).astype(BF16)
    send(attend_ref)
    send(mixture_ref)
    x1 = x + mm(mixture_ref[...], w_out[...])
    mid_ref[...] = x1
    send(mid_ref)
    normed, _ = norm_parts(x1)
    up = mm(normed.astype(BF16), w_up[...])
    up_ref[...] = up
    send(up_ref)
    hidden, _ = gelu_parts(up)
    out = x1 + mm(hidden.astype(BF16), w_down[...])
    out_ref[...] = out
    send(out_ref)
    return out


def encode_back(grad, x, w_qkv, w_out, w_up, w_down, heads, res, packed_grad, put):
    packed_ref, attend_ref, mixture_ref, mid_ref, up_ref, _ = res
    width = x.shape[1]
    grad_b = grad.astype(BF16)
    hidden, slope = gelu_parts(up_ref[...])
    up_grad = (mm_nt(grad_b, w_down[...]).astype(BF16).astype(F32) * slope).astype(BF16)
    put(3, hidden.astype(BF16), grad_b)
    normed, rstd = norm_parts(mid_ref[...])
    put(2, normed.astype(BF16), up_grad)
    normed_grad = mm_nt(up_grad, w_up[...]).astype(BF16).astype(F32)
    mid_grad = grad + norm_back(normed_grad, normed, rstd)
    mid_b = mid_grad.astype(BF16)
    put(1, mixture_ref[...], mid_b)
    mix_grad = mm_nt(mid_b, w_out[...]).astype(BF16)
    for h in range(heads):
        q = packed_ref[:, h * HEAD : (h + 1) * HEAD]
        k = packed_ref[:, width + h * HEAD : width + (h + 1) * HEAD]
        v = packed_ref[:, 2 * width + h * HEAD : 2 * width + (h + 1) * HEAD]
        head_grad = mix_grad[:, h * HEAD : (h + 1) * HEAD]
        weights = attend_ref[h]
        weights_grad = mm_nt(head_grad, v).astype(BF16).astype(F32)
        v_grad = mm_tn(weights.astype(BF16), head_grad)
        inner = jnp.sum(weights_grad * weights, axis=-1, keepdims=True)
        scores_grad = (weights * (weights_grad - inner) * 0.125).astype(BF16)
        packed_grad[:, h * HEAD : (h + 1) * HEAD] = mm(scores_grad, k).astype(BF16)
        packed_grad[:, width + h * HEAD : width + (h + 1) * HEAD] = mm_tn(scores_grad, q).astype(BF16)
        packed_grad[:, 2 * width + h * HEAD : 2 * width + (h + 1) * HEAD] = v_grad.astype(BF16)
    normed, rstd = norm_parts(x)
    put(0, normed.astype(BF16), packed_grad[...])
    normed_grad = mm_nt(packed_grad[...], w_qkv[...]).astype(BF16).astype(F32)
    return mid_grad + norm_back(normed_grad, normed, rstd)


def put_rows(flat, base, a, b):
    rows, columns = a.shape[1], b.shape[1]
    chunks = columns // 128
    left = a.T
    for c in range(0, chunks, 3):
        part = mm(left, b[:, c * 128 : (c + 3) * 128]).astype(BF16).astype(F32)
        for j in range(3):
            flat[pl.ds(base + c + j, rows, stride=chunks), :] = part[:, j * 128 : (j + 1) * 128]


def same_tile():
    row = lax.broadcasted_iota(jnp.int32, (128, 128), 0)
    column = lax.broadcasted_iota(jnp.int32, (128, 128), 1)
    return lax.rem(row, 32) == lax.rem(column, 32)


class Late:
    def __init__(self, source, buffer, sem):
        self.copy = pltpu.make_async_copy(source, buffer, sem)
        self.buffer, self.here = buffer, False
        self.copy.start()

    def ref(self):
        if not self.here:
            self.copy.wait()
            self.here = True
        return self.buffer

    def __getitem__(self, index):
        return self.ref()[index]


class Early:
    def __init__(self, target, buffer, sem):
        self.copy = pltpu.make_async_copy(buffer, target, sem)
        self.buffer = buffer

    def __getitem__(self, index):
        return self.buffer[index]

    def __setitem__(self, index, value):
        self.buffer[index] = value

    def finish(self):
        self.copy.wait()


def send(ref):
    if isinstance(ref, Early):
        ref.copy.start()


def broadcast_out(block, out, sems):
    copies = [pltpu.make_async_copy(block, out.at[i], sems.at[i]) for i in range(32)]
    for copy in copies:
        copy.start()
    for copy in copies:
        copy.wait()


def tile_forward(where, ids, slide, *refs):
    ins, outs, bufs, obufs, block, sems, osems, bsems = cut(refs, 6, 8, 6, 7, 1, 1, 1, 1)
    late = [Late(r, b, sems[0].at[i]) for i, (r, b) in enumerate(zip(ins, bufs))]
    res = [Early(r, b, osems[0].at[i]) for i, (r, b) in enumerate(zip(outs[1:], obufs))]
    patches, patch_w, w_qkv, w_out, w_up, w_down = late
    x = mm(patches[...], patch_w[...])
    res[0][...] = x
    send(res[0])
    out = encode(x, same_tile(), w_qkv, w_out, w_up, w_down, HEADS, res[1:])
    normed, _ = norm_parts(out)
    total = (normed[0:32] + normed[32:64]) + (normed[64:96] + normed[96:128])
    total = (total * 0.25).astype(BF16)
    message = block[0]
    for c in range(3):
        message[c * 32 : (c + 1) * 32, :] = total[:, c * LANES : (c + 1) * LANES]
    row = lax.broadcasted_iota(jnp.int32, (16, LANES), 0)
    lane = lax.broadcasted_iota(jnp.int32, (16, LANES), 1)
    mine = (lane >= 32 * lax.rem(where[0], 4)) & (lane < 32 * lax.rem(where[0], 4) + 32)
    tail = jnp.where((row == 0) & mine, ids[...].astype(F32), 0.0) + jnp.where(row == 1, slide[...].astype(F32), 0.0)
    message[96:112, :] = tail.astype(BF16)
    broadcast_out(message, outs[0], bsems[0])
    for r in res:
        r.finish()


def cut(refs, *sizes):
    parts, at = [], 0
    for size in sizes:
        parts.append(refs[at : at + size])
        at += size
    assert at == len(refs)
    return parts


def tails_of(tails):
    tails = tails.astype(F32)
    row = lax.broadcasted_iota(jnp.int32, tails.shape, 1)
    ids = jnp.sum(jnp.where(row == 0, tails, 0.0), axis=1)
    slides = jnp.sum(jnp.where(row == 1, tails, 0.0), axis=1)
    to = lax.broadcasted_iota(jnp.int32, (8, 32), 0)
    source = lax.broadcasted_iota(jnp.int32, (8, 32), 1)
    near = (source >= 4 * to) & (source < 4 * to + 4)
    ids = mm(jnp.where(near, 1.0, 0.0).astype(BF16), ids.astype(BF16))
    return ids, slides[:, 0:1]


def slots_of(ids, region):
    member = jnp.where(ids == region.astype(F32), 1.0, 0.0)
    row = lax.broadcasted_iota(jnp.int32, (128, 128), 0)
    column = lax.broadcasted_iota(jnp.int32, (128, 128), 1)
    within = mm(member.astype(BF16), jnp.where(row < column, 1.0, 0.0).astype(BF16))
    sums = jnp.sum(member, axis=1, keepdims=True)
    row8 = lax.broadcasted_iota(jnp.int32, (8, 8), 0)
    column8 = lax.broadcasted_iota(jnp.int32, (8, 8), 1)
    earlier = jnp.where(column8 < row8, 1.0, 0.0).astype(BF16)
    ahead = mm(earlier, jnp.broadcast_to(sums, (8, 128)).astype(BF16))
    count = jnp.sum(sums, axis=0, keepdims=True)
    return member, (within + ahead).astype(jnp.int32), count


def choice(member, slot, b):
    k = lax.broadcasted_iota(jnp.int32, (SLOTS, 128), 0)
    return jnp.where((slot[b : b + 1] == k) & (member[b : b + 1] > 0.0), 1.0, 0.0).astype(BF16)


def region_forward(where, *refs):
    ins, outs, bufs, obufs, block, sems, osems, bsems = cut(refs, 5, 8, 5, 7, 1, 1, 1, 1)
    late = [Late(r, b, sems[0].at[i]) for i, (r, b) in enumerate(zip(ins, bufs))]
    res = [Early(r, b, osems[0].at[i]) for i, (r, b) in enumerate(zip(outs[1:], obufs))]
    rows, w_qkv, w_out, w_up, w_down = late
    ids, _ = tails_of(rows[:, 96:112, :])
    member, slot, count = slots_of(ids, where[0])
    parts = [jnp.zeros((SLOTS, LANES), F32)] * 3
    for b in range(8):
        pick = choice(member, slot, b)
        for c in range(3):
            block_rows = rows[4 * b : 4 * b + 4, 32 * c : 32 * c + 32, :].reshape(128, LANES)
            parts[c] = parts[c] + mm(pick, block_rows)
    for c in range(3):
        res[0][:, c * LANES : (c + 1) * LANES] = parts[c]
    send(res[0])
    key = lax.broadcasted_iota(jnp.int32, (SLOTS, SLOTS), 1).astype(F32)
    out = encode(res[0][...], key < count, w_qkv, w_out, w_up, w_down, HEADS, res[1:])
    normed, _ = norm_parts(out)
    usable = lax.broadcasted_iota(jnp.int32, (SLOTS, 1), 0).astype(F32) < count
    total = jnp.sum(jnp.where(usable, normed, 0.0), axis=0, keepdims=True)
    embed = (total / count).astype(BF16).astype(F32)
    message = block[0]
    message[...] = jnp.zeros((8, LANES), F32)
    for c in range(3):
        message[c : c + 1, :] = embed[:, c * LANES : (c + 1) * LANES]
    broadcast_out(message, outs[0], bsems[0])
    for r in res:
        r.finish()


def slide_step(embeds, slide_row, slide_col, label, censor, slide_in, w_qkv, w_out, w_up, w_down, head, losses, grads, res, packed_grad, scaling):
    emb = embeds[...]
    x = mm(emb, slide_in[...])
    out = encode(x, slide_col == slide_row, w_qkv, w_out, w_up, w_down, H_SL, res)
    normed, rstd = norm_parts(out)
    sums, sizes, masks = [], [], []
    for s in range(SL_GRP):
        mask = jnp.where(slide_col == float(s), 1.0, 0.0)
        size = jnp.sum(mask, axis=0, keepdims=True)
        masks.append(mask)
        sizes.append(size)
        sums.append(jnp.sum(mask * normed, axis=0, keepdims=True) / size)
    pooled = jnp.concatenate(sums, axis=0).astype(BF16)
    logits = mm(pooled, head[...])
    soft = jnp.log1p(jnp.exp(-jnp.abs(logits)))
    log_hazard = -(jnp.maximum(-logits, 0.0) + soft)
    log_stay = -(jnp.maximum(logits, 0.0) + soft)
    bin_at = lax.broadcasted_iota(jnp.int32, (SL_GRP, NBINS), 1)
    at = (bin_at == label[...]).astype(F32)
    before = (bin_at < label[...]).astype(F32)
    held = censor[...].astype(F32)
    past = jnp.sum(before * log_stay, axis=1, keepdims=True)
    seen = past + jnp.sum(at * log_hazard, axis=1, keepdims=True)
    lived = past + jnp.sum(at * log_stay, axis=1, keepdims=True)
    losses[...] = -(1.0 - held) * seen - held * lived
    chance = 1.0 / (1.0 + jnp.exp(-logits))
    logit_grad = (scaling * (before * chance + at * (chance - (1.0 - held)))).astype(BF16)
    grads[5][...] = mm_tn(pooled, logit_grad).astype(BF16)
    pooled_grad = mm_nt(logit_grad, head[...]).astype(BF16).astype(F32)
    grad = jnp.zeros_like(normed)
    for s in range(SL_GRP):
        grad = grad + masks[s] * (pooled_grad[s : s + 1] / sizes[s])
    grad = norm_back(grad, normed, rstd)

    def put(i, a, b):
        grads[i + 1][...] = mm_tn(a, b).astype(BF16)

    grad = encode_back(grad, x, w_qkv, w_out, w_up, w_down, H_SL, res, packed_grad, put).astype(BF16)
    grads[0][...] = mm_tn(emb, grad).astype(BF16)
    return mm_nt(grad, slide_in[...]).astype(BF16)


def region_backward(scaling, where, label, censor, *refs):
    ins, outs, bufs, obufs, extra, sems, osems = cut(refs, 19, 15, 19, 15, 9, 1, 1)
    order = list(range(8)) + [18, 13, 17, 16, 14, 15, 9, 8, 10, 11, 12]
    late = dict()
    for i in list(dict.fromkeys(order)):
        late[i] = Late(ins[i], bufs[i], sems[0].at[i])
    early = [Early(r, b, osems[0].at[i]) for i, (r, b) in enumerate(zip(outs, obufs))]
    message, tails = late[0], late[1]
    slide_weights = [late[i] for i in range(2, 8)]
    w_qkv, w_out, w_up, w_down = [late[i] for i in range(8, 12)]
    x_ref, res = late[12], [late[i] for i in range(13, 19)]
    losses, spread, pairs, slide_grads = early[0], early[1], early[2:9], early[9:15]
    packed_grad, slide_packed_grad, embeds = extra[:3]
    ids, slide_col = tails_of(tails[...])
    rows32 = lax.broadcasted_iota(jnp.int32, (32, 32), 0)
    columns32 = lax.broadcasted_iota(jnp.int32, (32, 32), 1)
    slide_row = jnp.sum(jnp.where(rows32 == columns32, slide_col, 0.0), axis=0, keepdims=True)
    arrived = message[...]
    at = lax.broadcasted_iota(jnp.int32, arrived.shape, 1)
    for c in range(3):
        part = jnp.sum(jnp.where(at == c, arrived, 0.0), axis=1)
        embeds[:, c * LANES : (c + 1) * LANES] = part.astype(BF16)
    cots = slide_step(
        embeds, slide_row, slide_col, label, censor, *slide_weights, losses, slide_grads, extra[3:9], slide_packed_grad, scaling
    ).astype(F32)
    for g in [losses] + slide_grads:
        send(g)
    mine = lax.broadcasted_iota(jnp.int32, (32, 1), 0) == where[0]
    own = jnp.sum(jnp.where(mine, cots, 0.0), axis=0, keepdims=True)
    member, slot, count = slots_of(ids, where[0])
    usable = lax.broadcasted_iota(jnp.int32, (SLOTS, 1), 0).astype(F32) < count
    grad = jnp.where(usable, own / count, 0.0)
    normed, rstd = norm_parts(res[5][...])
    grad = norm_back(grad, normed, rstd)

    def put(i, a, b):
        at = {3: 0, 2: 2, 1: 4, 0: 5}[i]
        if i != 1:
            pairs[at][...] = a
            send(pairs[at])
            at += 1
        pairs[at][...] = b
        send(pairs[at])

    grad = encode_back(grad, x_ref[...], w_qkv, w_out, w_up, w_down, HEADS, res, packed_grad, put).astype(BF16)
    for b in range(8):
        spread[b * 128 : (b + 1) * 128, :] = mm_tn(choice(member, slot, b), grad).astype(BF16)
    send(spread)
    for e in early:
        e.finish()


def two_halves(flat, rows, core, halves, stage, sems, extra=None):
    run = 32 * rows
    copies = []
    for side in range(2):
        which = core if side == 0 else 1 - core
        for z in range(4):
            start = pl.multiple_of((2 * z + which) * run, 32)
            stage[side, z * run : (z + 1) * run, :] = flat[pl.ds(start, run), :].astype(BF16)
            part = pl.ds(z * run, run)
            copies.append(pltpu.make_async_copy(stage.at[side, part, :], halves[side].at[part, :], sems.at[side, z]))
            copies[-1].start()
        if extra is not None:
            stage[side, 4 * run : 4 * run + 80, :] = extra.ref()[which]
            part = pl.ds(4 * run, 80)
            copies.append(pltpu.make_async_copy(stage.at[side, part, :], halves[side].at[part, :], sems.at[side, 4]))
            copies[-1].start()
    for copy in copies:
        copy.wait()


def region_weights(core, *refs):
    ins, halves, bufs, flat, stage, sems, osems = cut(refs, 8, 2, 8, 1, 1, 1, 1)
    late = [Late(r, b, sems[0].at[i]) for i, (r, b) in enumerate(zip(ins, bufs))]
    hidden, grad, second, up_grad, mixture, mid_grad, first, packed_grad = late
    put_rows(flat[0], 9216, hidden[...], grad[...])
    put_rows(flat[0], 4608, second[...], up_grad[...])
    put_rows(flat[0], 3456, mixture[...], mid_grad[...])
    put_rows(flat[0], 0, first[...], packed_grad[...])
    two_halves(flat[0], 54, core[0], halves, stage[0], osems[0])


def tile_backward(core, ids, *refs):
    ins, halves, bufs, packed_grad, flat, stage, sems, osems = cut(refs, 14, 2, 14, 1, 1, 1, 1, 1)
    late = [Late(ins[i], bufs[i], sems[0].at[i]) for i in (0, 13, 6, 12, 11, 5, 10, 4, 9, 8, 3, 7, 1, 2)]
    late = dict(zip((0, 13, 6, 12, 11, 5, 10, 4, 9, 8, 3, 7, 1, 2), late))
    arrived, patches, slide_rows = late[0], late[1], late[2]
    w_qkv, w_out, w_up, w_down = [late[i] for i in range(3, 7)]
    x_ref, res = late[7], [late[i] for i in range(8, 14)]
    rows32 = lax.broadcasted_iota(jnp.int32, (32, 32), 0)
    columns32 = lax.broadcasted_iota(jnp.int32, (32, 32), 1)
    assign = jnp.sum(jnp.where(rows32 == columns32, ids[...].astype(F32), 0.0), axis=1, keepdims=True)
    cot = jnp.zeros((32, D), F32)
    for r in range(32):
        cot = cot + jnp.where(assign == float(r), arrived[r].astype(F32), 0.0)
    cot = cot * 0.25
    grad = jnp.concatenate([cot] * PATCHES, axis=0)
    normed, rstd = norm_parts(res[5][...])
    grad = norm_back(grad, normed, rstd)
    bases = (2304, 5760, 6912, 11520)

    def put(i, a, b):
        put_rows(flat[0], bases[i], a, b)

    grad = encode_back(grad, x_ref[...], w_qkv, w_out, w_up, w_down, HEADS, res, packed_grad[0], put)
    put_rows(flat[0], 0, patches[...], grad.astype(BF16))
    two_halves(flat[0], 63, core[0], halves, stage[0], osems[0], slide_rows)


def fold(rows, pad, tail, *refs):
    mine, got = refs[:2]
    refs = refs[2:]
    if tail:
        out, extra = refs[:2]
        refs = refs[2:]
    else:
        out = refs[0]
        refs = refs[1:]
    a, b, total, stage, chunks, sems, osems = refs[:7]
    run = 32 * rows
    arriving = []
    for z in range(4 + tail):
        part = pl.ds(z * run, run if z < 4 else 80)
        for side, (source, buffer) in enumerate(((mine, a), (got, b))):
            arriving.append(pltpu.make_async_copy(source.at[part, :], buffer.at[part, :], sems.at[side, z]))
            arriving[-1].start()
    for z in range(4):
        arriving[2 * z].wait()
        arriving[2 * z + 1].wait()
        part = pl.ds(z * run, run)
        total[part, :] = a[part, :].astype(F32) + b[part, :].astype(F32)
    leaving = []
    if tail:
        arriving[8].wait()
        arriving[9].wait()
        part = pl.ds(4 * run, 80)
        refs[7][...] = (a[part, :].astype(F32) + b[part, :].astype(F32)).astype(BF16)
        leaving.append(pltpu.make_async_copy(refs[7], extra, osems.at[16]))
        leaving[-1].start()
    if pad:
        stage[8 * rows :, :] = jnp.zeros((pad, LANES), F32)
    for y in range(4):
        for x in range(4):
            for z in range(4):
                for h in range(2):
                    source = (z * 32 + y * 8 + h * 4 + x) * rows
                    target = (z * 2 + h) * rows
                    stage[target : target + rows, :] = total[source : source + rows, :]
            chunks[y * 4 + x] = stage[...].astype(BF16)
            leaving.append(pltpu.make_async_copy(chunks.at[y * 4 + x], out.at[y * 4 + x], osems.at[y * 4 + x]))
            leaving[-1].start()
    for copy in leaving:
        copy.wait()


def merge(tile_in, region_in, slide_in, out, tile_buf, region_buf, slide_buf, total, region_total, slide_total, stage, chunks, sems, osems):
    tile_late = Late(tile_in, tile_buf, sems.at[0])
    region_late = Late(region_in, region_buf, sems.at[1])
    slide_late = Late(slide_in, slide_buf, sems.at[2])
    slide_total[...] = slide_late[...].astype(F32)

    def added(late, target, rows):
        for start in range(0, rows, 48 if rows % 48 == 0 else 64):
            size = 48 if rows % 48 == 0 else 64
            value = late[0, start : start + size, :].astype(F32)
            for i in range(1, 16):
                value = value + late[i, start : start + size, :].astype(F32)
            target[start : start + size, :] = value

    added(region_late, region_total, 432)
    added(tile_late, total, 512)
    leaving = []
    for i in range(8):
        stage[0:63, :] = total[i * 63 : (i + 1) * 63, :]
        stage[63:64, :] = jnp.zeros((1, LANES), F32)
        stage[64:118, :] = region_total[i * 54 : (i + 1) * 54, :]
        stage[118:128, :] = slide_total[i * 10 : (i + 1) * 10, :]
        chunks[i] = stage[...].astype(BF16)
        leaving.append(pltpu.make_async_copy(chunks.at[i], out.at[i], osems.at[i]))
        leaving[-1].start()
    for copy in leaving:
        copy.wait()


def call(kernel, outs, scratch, inputs, scalars=0, whole=0):
    specs = [pl.BlockSpec(memory_space=pltpu.SMEM)] * scalars
    specs += [pl.BlockSpec(memory_space=pltpu.VMEM)] * whole
    specs += [pl.BlockSpec(memory_space=pl.ANY)] * (len(inputs) - scalars - whole)
    return pl.pallas_call(
        kernel,
        out_shape=[jax.ShapeDtypeStruct(shape, kind) for shape, kind in outs],
        in_specs=specs,
        out_specs=[pl.BlockSpec(memory_space=pl.ANY)] * len(outs),
        scratch_shapes=[pltpu.VMEM(*item) if isinstance(item, tuple) else item for item in scratch],
        compiler_params=pltpu.CompilerParams(vmem_limit_bytes=60 * 1024 * 1024),
    )(*inputs)


def like(arrays):
    return [(a.shape, a.dtype) for a in arrays]


def semaphores(*shape):
    return pltpu.SemaphoreType.DMA(shape)


def residuals(tokens, width, hidden, heads):
    return [
        ((tokens, 3 * width), BF16),
        ((heads, tokens, tokens), F32),
        ((tokens, width), BF16),
        ((tokens, width), F32),
        ((tokens, hidden), F32),
        ((tokens, width), F32),
    ]


def index_of(z, core, y, z_hi, x):
    return (z * 2 + core) * 32 + y * 8 + z_hi * 4 + x


PLANES = [[index_of(z, c, y, h, x) for y in range(4) for x in range(4)] for z in range(4) for c in range(2) for h in range(2)]
COLUMNS = [[index_of(z, c, y, h, x) for z in range(4) for h in range(2)] for c in range(2) for y in range(4) for x in range(4)]
OTHER_CORE = [(g, g + 1 - 2 * (g % 2)) for g in range(8)]
ALL = ("grp", "dev")


def exchange(array, groups):
    return lax.all_to_all(array, ALL, 0, 0, axis_index_groups=groups)


def folded(mine, other, rows, pad, tail):
    got = lax.ppermute(other, "grp", OTHER_CORE)
    height = 128 * rows + 80 * tail
    chunk = 8 * rows + pad
    return call(
        functools.partial(fold, rows, pad, tail),
        [((16, chunk, LANES), BF16)] + [((80, LANES), BF16)] * tail,
        [((height, LANES), BF16)] * 2
        + [((128 * rows, LANES), F32), ((chunk, LANES), F32), ((16, chunk, LANES), BF16)]
        + [semaphores(2, 5), semaphores(17)]
        + [((80, LANES), BF16)] * tail,
        (mine, got),
    )


def body(
    patches,
    tile_region,
    region_slide,
    bin_label,
    censored,
    patch_w,
    tile_qkv,
    tile_out,
    tile_up,
    tile_down,
    region_qkv,
    region_out,
    region_up,
    region_down,
    slide_in,
    slide_qkv,
    slide_out,
    slide_up,
    slide_down,
    slide_head,
):
    member_index = lax.axis_index("dev").astype(jnp.int32)
    where = member_index.reshape(1)
    core = lax.rem(lax.axis_index("grp").astype(jnp.int32), 2).reshape(1)
    scaling = 1.0 / (bin_label.shape[1] * lax.axis_size("grp"))
    tokens = patches.transpose(1, 0, 2).reshape(128, 768)
    ids = jnp.tile(tile_region, (1, 4))
    tile_res = [((128, D), F32)] + residuals(128, D, FF, HEADS)
    ins = (tokens, patch_w, tile_qkv, tile_out, tile_up, tile_down)
    message, *tile_kept = call(
        tile_forward,
        [((32, 112, LANES), BF16)] + tile_res,
        like(ins) + tile_res + [((112, LANES), BF16), semaphores(6), semaphores(7), semaphores(32)],
        (where, ids, region_slide) + ins,
        scalars=1,
        whole=2,
    )
    rows = lax.all_to_all(message, "dev", 0, 0)
    region_res = [((SLOTS, D), F32)] + residuals(SLOTS, D, FF, HEADS)
    ins = (rows, region_qkv, region_out, region_up, region_down)
    message, *region_kept = call(
        region_forward,
        [((32, 8, LANES), F32)] + region_res,
        like(ins) + region_res + [((8, LANES), F32), semaphores(5), semaphores(7), semaphores(32)],
        (where,) + ins,
        scalars=1,
    )
    all_regions = lax.all_to_all(message, "dev", 0, 0)
    slide_weights = (slide_in, slide_qkv, slide_out, slide_up, slide_down, slide_head)
    pairs = [
        ((SLOTS, FF), BF16),
        ((SLOTS, D), BF16),
        ((SLOTS, D), BF16),
        ((SLOTS, FF), BF16),
        ((SLOTS, D), BF16),
        ((SLOTS, D), BF16),
        ((SLOTS, 3 * D), BF16),
    ]
    outs = [((SL_GRP, 1), F32), ((1024, D), BF16)] + pairs + like(slide_weights)
    ins = (all_regions, rows[:, 96:112, :]) + slide_weights + (region_qkv, region_out, region_up, region_down) + tuple(region_kept)
    losses, spread, *rest = call(
        functools.partial(region_backward, scaling),
        outs,
        like(ins)
        + outs
        + [((SLOTS, 3 * D), BF16), ((32, 3 * D_SL), BF16), ((32, D), BF16)]
        + residuals(32, D_SL, D_SL, H_SL)
        + [semaphores(19), semaphores(15)],
        (where, bin_label.reshape(SL_GRP, 1), censored.reshape(SL_GRP, 1)) + ins,
        scalars=1,
        whole=2,
    )
    arrived = lax.all_to_all(spread.reshape(32, 32, D), "dev", 0, 0)
    hidden, down_grad, second, up_grad, mid_grad, first, packed_grad = rest[:7]
    ins = (hidden, down_grad, second, up_grad, region_kept[3], mid_grad, first, packed_grad)
    mine, other = call(
        region_weights,
        [((6912, LANES), BF16)] * 2,
        like(ins) + [((13824, LANES), F32), ((2, 6912, LANES), BF16), semaphores(8), semaphores(2, 5)],
        (core,) + ins,
        scalars=1,
    )
    (region_chunks,) = folded(mine, other, 54, 0, 0)
    region_parts = exchange(region_chunks, PLANES)
    slide_flat = jnp.concatenate([g.astype(F32).reshape(-1) for g in rest[7:]]).reshape(4, 2, 4, 2, 4, 1155)
    y, x = member_index // 8, lax.rem(member_index, 4)
    zero = jnp.zeros((), jnp.int32)
    slide_rows = lax.dynamic_slice(slide_flat, (zero, zero, y, zero, x, zero), (4, 2, 1, 2, 1, 1155))
    slide_rows = slide_rows.reshape(4, 2, 2, 1155).transpose(1, 0, 2, 3)
    slide_rows = jnp.pad(slide_rows, ((0, 0), (0, 0), (0, 0), (0, 125))).astype(BF16).reshape(2, 80, LANES)
    ins = (arrived, tokens, slide_rows, tile_qkv, tile_out, tile_up, tile_down) + tuple(tile_kept)
    mine, other = call(
        tile_backward,
        [((8144, LANES), BF16)] * 2,
        like(ins)
        + [((128, 3 * D), BF16), ((16128, LANES), F32), ((2, 8144, LANES), BF16), semaphores(14), semaphores(2, 5)],
        (core, tile_region) + ins,
        scalars=1,
        whole=1,
    )
    tile_chunks, slide_sums = folded(mine, other, 63, 8, 1)
    tile_parts = exchange(tile_chunks, PLANES)
    ins = (tile_parts, region_parts, slide_sums)
    (last,) = call(
        merge,
        [((8, 128, LANES), BF16)],
        like(ins)
        + [((512, LANES), F32), ((432, LANES), F32), ((80, LANES), F32), ((128, LANES), F32), ((8, 128, LANES), BF16)]
        + [semaphores(3), semaphores(8)],
        ins,
    )
    total = jnp.sum(exchange(last, COLUMNS).astype(F32), axis=0)
    tile_result = total[0:63].reshape(8064)
    region_result = total[64:118].reshape(6912)
    slide_result = total[118:128].reshape(1280)[:1155] * 0.5
    return (losses.reshape(1, SL_GRP), tile_result, region_result, slide_result)


def solution(mesh):
    placed = (P(ALL, None, None), P("grp", "dev"), P("grp", "dev"), P("grp", None), P("grp", None)) + (P(),) * 15
    return jax.shard_map(
        body,
        mesh=mesh,
        in_specs=placed,
        out_specs=(P("grp", None), P(ALL), P(ALL), P(ALL)),
        check_vma=False,
    )
```

```python
import functools
import math

import jax
import jax.numpy as jnp
from jax import lax
from jax.experimental import pallas as pl
from jax.experimental.pallas import tpu as pltpu
from jax.sharding import PartitionSpec as P

D = 384
HEADS = 6
FF = 1536
PATCHES = 4
SLOTS = 64
D_SL = 192
H_SL = 3
NBINS = 4
SL_GRP = 4
HEAD = 64
F32 = jnp.float32
BF16 = jnp.bfloat16
LANES = 128
US = 550_000_000
GELU_C = math.sqrt(2.0 / math.pi)


def mm(a, b):
    return jnp.dot(a, b, preferred_element_type=F32)


def mm_nt(a, b):
    return lax.dot_general(a, b, (((1,), (1,)), ((), ())), preferred_element_type=F32)


def mm_tn(a, b):
    return lax.dot_general(a, b, (((0,), (0,)), ((), ())), preferred_element_type=F32)


def norm_parts(x):
    average = jnp.mean(x, axis=-1, keepdims=True)
    centred = x - average
    variance = jnp.mean(centred * centred, axis=-1, keepdims=True)
    rstd = lax.rsqrt(variance + 1e-06)
    return centred * rstd, rstd


def norm_back(grad, normed, rstd):
    first = jnp.mean(grad, axis=-1, keepdims=True)
    second = jnp.mean(grad * normed, axis=-1, keepdims=True)
    return rstd * (grad - first - normed * second)


def gelu_parts(x):
    t = jnp.tanh(GELU_C * (x + 0.044715 * (x * x * x)))
    value = 0.5 * x * (1.0 + t)
    slope = 0.5 * (1.0 + t) + 0.5 * x * (1.0 - t * t) * (GELU_C * (1.0 + 3.0 * 0.044715 * (x * x)))
    return value, slope


def encode(x, allowed, w_qkv, w_out, w_up, w_down, heads, res):
    packed_ref, attend_ref, mixture_ref, mid_ref, up_ref, out_ref = res
    width = x.shape[1]
    normed, _ = norm_parts(x)
    packed_ref[...] = mm(normed.astype(BF16), w_qkv[...]).astype(BF16)
    send(packed_ref)
    for h in range(heads):
        q = packed_ref[:, h * HEAD : (h + 1) * HEAD]
        k = packed_ref[:, width + h * HEAD : width + (h + 1) * HEAD]
        v = packed_ref[:, 2 * width + h * HEAD : 2 * width + (h + 1) * HEAD]
        scores = jnp.where(allowed, mm_nt(q, k) * 0.125, -1e30)
        scores = jnp.exp(scores - jnp.max(scores, axis=-1, keepdims=True))
        weights = scores / jnp.sum(scores, axis=-1, keepdims=True)
        attend_ref[h] = weights
        mixture_ref[:, h * HEAD : (h + 1) * HEAD] = mm(weights.astype(BF16), v).astype(BF16)
    send(attend_ref)
    send(mixture_ref)
    x1 = x + mm(mixture_ref[...], w_out[...])
    mid_ref[...] = x1
    send(mid_ref)
    normed, _ = norm_parts(x1)
    up = mm(normed.astype(BF16), w_up[...])
    up_ref[...] = up
    send(up_ref)
    hidden, _ = gelu_parts(up)
    out = x1 + mm(hidden.astype(BF16), w_down[...])
    out_ref[...] = out
    send(out_ref)
    return out


def encode_back(grad, x, w_qkv, w_out, w_up, w_down, heads, res, packed_grad, put):
    packed_ref, attend_ref, mixture_ref, mid_ref, up_ref, _ = res
    width = x.shape[1]
    grad_b = grad.astype(BF16)
    hidden, slope = gelu_parts(up_ref[...])
    up_grad = (mm_nt(grad_b, w_down[...]).astype(BF16).astype(F32) * slope).astype(BF16)
    put(3, hidden.astype(BF16), grad_b)
    normed, rstd = norm_parts(mid_ref[...])
    put(2, normed.astype(BF16), up_grad)
    normed_grad = mm_nt(up_grad, w_up[...]).astype(BF16).astype(F32)
    mid_grad = grad + norm_back(normed_grad, normed, rstd)
    mid_b = mid_grad.astype(BF16)
    put(1, mixture_ref[...], mid_b)
    mix_grad = mm_nt(mid_b, w_out[...]).astype(BF16)
    for h in range(heads):
        q = packed_ref[:, h * HEAD : (h + 1) * HEAD]
        k = packed_ref[:, width + h * HEAD : width + (h + 1) * HEAD]
        v = packed_ref[:, 2 * width + h * HEAD : 2 * width + (h + 1) * HEAD]
        head_grad = mix_grad[:, h * HEAD : (h + 1) * HEAD]
        weights = attend_ref[h]
        weights_grad = mm_nt(head_grad, v).astype(BF16).astype(F32)
        v_grad = mm_tn(weights.astype(BF16), head_grad)
        inner = jnp.sum(weights_grad * weights, axis=-1, keepdims=True)
        scores_grad = (weights * (weights_grad - inner) * 0.125).astype(BF16)
        packed_grad[:, h * HEAD : (h + 1) * HEAD] = mm(scores_grad, k).astype(BF16)
        packed_grad[:, width + h * HEAD : width + (h + 1) * HEAD] = mm_tn(scores_grad, q).astype(BF16)
        packed_grad[:, 2 * width + h * HEAD : 2 * width + (h + 1) * HEAD] = v_grad.astype(BF16)
    normed, rstd = norm_parts(x)
    put(0, normed.astype(BF16), packed_grad[...])
    normed_grad = mm_nt(packed_grad[...], w_qkv[...]).astype(BF16).astype(F32)
    return mid_grad + norm_back(normed_grad, normed, rstd)


def put_rows(flat, base, a, b):
    rows, columns = a.shape[1], b.shape[1]
    chunks = columns // 128
    left = a.T
    for c in range(0, chunks, 3):
        part = mm(left, b[:, c * 128 : (c + 3) * 128]).astype(BF16).astype(F32)
        for j in range(3):
            flat[pl.ds(base + c + j, rows, stride=chunks), :] = part[:, j * 128 : (j + 1) * 128]


def same_tile():
    row = lax.broadcasted_iota(jnp.int32, (128, 128), 0)
    column = lax.broadcasted_iota(jnp.int32, (128, 128), 1)
    return lax.rem(row, 32) == lax.rem(column, 32)


class Late:
    def __init__(self, source, buffer, sem):
        self.copy = pltpu.make_async_copy(source, buffer, sem)
        self.buffer, self.here = buffer, False
        self.copy.start()

    def ref(self):
        if not self.here:
            self.copy.wait()
            self.here = True
        return self.buffer

    def __getitem__(self, index):
        return self.ref()[index]


class Early:
    def __init__(self, target, buffer, sem):
        self.copy = pltpu.make_async_copy(buffer, target, sem)
        self.buffer = buffer

    def __getitem__(self, index):
        return self.buffer[index]

    def __setitem__(self, index, value):
        self.buffer[index] = value

    def finish(self):
        self.copy.wait()


def send(ref):
    if isinstance(ref, Early):
        ref.copy.start()


def leave(pairs, sems):
    copies = [pltpu.make_async_copy(a, b, sems.at[i]) for i, (a, b) in enumerate(pairs)]
    for copy in copies:
        copy.start()
    for copy in copies:
        copy.wait()


def broadcast_out(block, out, sems):
    copies = [pltpu.make_async_copy(block, out.at[i], sems.at[i]) for i in range(32)]
    for copy in copies:
        copy.start()
    for copy in copies:
        copy.wait()


def tile_forward(where, ids, slide, *refs):
    ins, outs, bufs, obufs, block, sems, osems, bsems = cut(refs, 6, 8, 6, 7, 1, 1, 1, 1)
    late = [Late(r, b, sems[0].at[i]) for i, (r, b) in enumerate(zip(ins, bufs))]
    res = [Early(r, b, osems[0].at[i]) for i, (r, b) in enumerate(zip(outs[1:], obufs))]
    patches, patch_w, w_qkv, w_out, w_up, w_down = late
    x = mm(patches[...], patch_w[...])
    res[0][...] = x
    send(res[0])
    out = encode(x, same_tile(), w_qkv, w_out, w_up, w_down, HEADS, res[1:])
    normed, _ = norm_parts(out)
    total = (normed[0:32] + normed[32:64]) + (normed[64:96] + normed[96:128])
    total = (total * 0.25).astype(BF16)
    message = block[0]
    for c in range(3):
        message[c * 32 : (c + 1) * 32, :] = total[:, c * LANES : (c + 1) * LANES]
    row = lax.broadcasted_iota(jnp.int32, (16, LANES), 0)
    lane = lax.broadcasted_iota(jnp.int32, (16, LANES), 1)
    mine = (lane >= 32 * lax.rem(where[0], 4)) & (lane < 32 * lax.rem(where[0], 4) + 32)
    four = jnp.concatenate([ids[...].astype(F32)] * 4, axis=1)
    tail = jnp.where((row == 0) & mine, four, 0.0) + jnp.where(row == 1, slide[...].astype(F32), 0.0)
    message[96:112, :] = tail.astype(BF16)
    leave([(message, outs[0])], bsems[0])
    for r in res:
        r.finish()


def cut(refs, *sizes):
    parts, at = [], 0
    for size in sizes:
        parts.append(refs[at : at + size])
        at += size
    assert at == len(refs)
    return parts


def tails_of(tails):
    tails = tails.astype(F32)
    row = lax.broadcasted_iota(jnp.int32, tails.shape, 1)
    ids = jnp.sum(jnp.where(row == 0, tails, 0.0), axis=1)
    slides = jnp.sum(jnp.where(row == 1, tails, 0.0), axis=1)
    to = lax.broadcasted_iota(jnp.int32, (8, 32), 0)
    source = lax.broadcasted_iota(jnp.int32, (8, 32), 1)
    near = (source >= 4 * to) & (source < 4 * to + 4)
    ids = mm(jnp.where(near, 1.0, 0.0).astype(BF16), ids.astype(BF16))
    return ids, slides[:, 0:1]


def slots_of(ids, region):
    member = jnp.where(ids == region.astype(F32), 1.0, 0.0)
    row = lax.broadcasted_iota(jnp.int32, (128, 128), 0)
    column = lax.broadcasted_iota(jnp.int32, (128, 128), 1)
    within = mm(member.astype(BF16), jnp.where(row < column, 1.0, 0.0).astype(BF16))
    sums = jnp.sum(member, axis=1, keepdims=True)
    row8 = lax.broadcasted_iota(jnp.int32, (8, 8), 0)
    column8 = lax.broadcasted_iota(jnp.int32, (8, 8), 1)
    earlier = jnp.where(column8 < row8, 1.0, 0.0).astype(BF16)
    ahead = mm(earlier, jnp.broadcast_to(sums, (8, 128)).astype(BF16))
    count = jnp.sum(sums, axis=0, keepdims=True)
    return member, (within + ahead).astype(jnp.int32), count


def choice(member, slot, b):
    k = lax.broadcasted_iota(jnp.int32, (SLOTS, 128), 0)
    return jnp.where((slot[b : b + 1] == k) & (member[b : b + 1] > 0.0), 1.0, 0.0).astype(BF16)


def region_forward(where, *refs):
    ins, outs, bufs, rows, obufs, block, sems, osems, bsems, rsems = cut(refs, 5, 9, 4, 1, 7, 1, 1, 1, 1, 1)
    rows = rows[0]
    h = lax.rem(where[0] // 4, 2)
    arriving = []
    for i in range(16):
        base = i // 4 * 8 + i % 4
        for side, z in enumerate((h, 1 - h)):
            source = ins[0].at[i, 112 * side : 112 * side + 112, :]
            arriving.append(pltpu.make_async_copy(source, rows.at[base + 4 * z], rsems[0].at[2 * i + side]))
            arriving[-1].start()
    w_qkv, w_out, w_up, w_down = [Late(r, b, sems[0].at[i]) for i, (r, b) in enumerate(zip(ins[1:], bufs))]
    res = [Early(r, b, osems[0].at[i]) for i, (r, b) in enumerate(zip(outs[2:], obufs))]
    for copy in arriving:
        copy.wait()
    tails = pltpu.make_async_copy(rows.at[:, 96:112, :], outs[1], bsems[0].at[32])
    tails.start()
    ids, _ = tails_of(rows[:, 96:112, :])
    member, slot, count = slots_of(ids, where[0])
    parts = [jnp.zeros((SLOTS, LANES), F32)] * 3
    for b in range(8):
        pick = choice(member, slot, b)
        for c in range(3):
            block_rows = rows[4 * b : 4 * b + 4, 32 * c : 32 * c + 32, :].reshape(128, LANES)
            parts[c] = parts[c] + mm(pick, block_rows)
    for c in range(3):
        res[0][:, c * LANES : (c + 1) * LANES] = parts[c]
    send(res[0])
    key = lax.broadcasted_iota(jnp.int32, (SLOTS, SLOTS), 1).astype(F32)
    out = encode(res[0][...], key < count, w_qkv, w_out, w_up, w_down, HEADS, res[1:])
    normed, _ = norm_parts(out)
    usable = lax.broadcasted_iota(jnp.int32, (SLOTS, 1), 0).astype(F32) < count
    total = jnp.sum(jnp.where(usable, normed, 0.0), axis=0, keepdims=True)
    embed = (total / count).astype(BF16).astype(F32)
    message = block[0]
    message[...] = jnp.zeros((8, LANES), F32)
    for c in range(3):
        message[c : c + 1, :] = embed[:, c * LANES : (c + 1) * LANES]
    broadcast_out(message, outs[0], bsems[0])
    tails.wait()
    for r in res:
        r.finish()


def slide_step(embeds, slide_row, slide_col, label, censor, slide_in, w_qkv, w_out, w_up, w_down, head, losses, grads, res, packed_grad, scaling):
    emb = embeds[...]
    x = mm(emb, slide_in[...])
    out = encode(x, slide_col == slide_row, w_qkv, w_out, w_up, w_down, H_SL, res)
    normed, rstd = norm_parts(out)
    sums, sizes, masks = [], [], []
    for s in range(SL_GRP):
        mask = jnp.where(slide_col == float(s), 1.0, 0.0)
        size = jnp.sum(mask, axis=0, keepdims=True)
        masks.append(mask)
        sizes.append(size)
        sums.append(jnp.sum(mask * normed, axis=0, keepdims=True) / size)
    pooled = jnp.concatenate(sums, axis=0).astype(BF16)
    logits = mm(pooled, head[...])
    soft = jnp.log1p(jnp.exp(-jnp.abs(logits)))
    log_hazard = -(jnp.maximum(-logits, 0.0) + soft)
    log_stay = -(jnp.maximum(logits, 0.0) + soft)
    bin_at = lax.broadcasted_iota(jnp.int32, (SL_GRP, NBINS), 1)
    at = (bin_at == label[...]).astype(F32)
    before = (bin_at < label[...]).astype(F32)
    held = censor[...].astype(F32)
    past = jnp.sum(before * log_stay, axis=1, keepdims=True)
    seen = past + jnp.sum(at * log_hazard, axis=1, keepdims=True)
    lived = past + jnp.sum(at * log_stay, axis=1, keepdims=True)
    losses[...] = -(1.0 - held) * seen - held * lived
    chance = 1.0 / (1.0 + jnp.exp(-logits))
    logit_grad = (scaling * (before * chance + at * (chance - (1.0 - held)))).astype(BF16)
    grads[5][...] = mm_tn(pooled, logit_grad).astype(BF16)
    pooled_grad = mm_nt(logit_grad, head[...]).astype(BF16).astype(F32)
    grad = jnp.zeros_like(normed)
    for s in range(SL_GRP):
        grad = grad + masks[s] * (pooled_grad[s : s + 1] / sizes[s])
    grad = norm_back(grad, normed, rstd)

    def put(i, a, b):
        grads[i + 1][...] = mm_tn(a, b).astype(BF16)

    grad = encode_back(grad, x, w_qkv, w_out, w_up, w_down, H_SL, res, packed_grad, put).astype(BF16)
    grads[0][...] = mm_tn(emb, grad).astype(BF16)
    return mm_nt(grad, slide_in[...]).astype(BF16)


def region_backward(scaling, where, label, censor, *refs):
    ins, outs, bufs, obufs, extra, sems, osems = cut(refs, 19, 15, 19, 15, 9, 1, 1)
    order = list(range(8)) + [18, 13, 17, 16, 14, 15, 9, 8, 10, 11, 12]
    late = dict()
    for i in list(dict.fromkeys(order)):
        late[i] = Late(ins[i], bufs[i], sems[0].at[i])
    early = [Early(r, b, osems[0].at[i]) for i, (r, b) in enumerate(zip(outs, obufs))]
    message, tails = late[0], late[1]
    slide_weights = [late[i] for i in range(2, 8)]
    w_qkv, w_out, w_up, w_down = [late[i] for i in range(8, 12)]
    x_ref, res = late[12], [late[i] for i in range(13, 19)]
    losses, spread, pairs, slide_grads = early[0], early[1], early[2:9], early[9:15]
    packed_grad, slide_packed_grad, embeds = extra[:3]
    ids, slide_col = tails_of(tails[...])
    rows32 = lax.broadcasted_iota(jnp.int32, (32, 32), 0)
    columns32 = lax.broadcasted_iota(jnp.int32, (32, 32), 1)
    slide_row = jnp.sum(jnp.where(rows32 == columns32, slide_col, 0.0), axis=0, keepdims=True)
    arrived = message[...]
    at = lax.broadcasted_iota(jnp.int32, arrived.shape, 1)
    for c in range(3):
        part = jnp.sum(jnp.where(at == c, arrived, 0.0), axis=1)
        embeds[:, c * LANES : (c + 1) * LANES] = part.astype(BF16)
    cots = slide_step(
        embeds, slide_row, slide_col, label, censor, *slide_weights, losses, slide_grads, extra[3:9], slide_packed_grad, scaling
    ).astype(F32)
    for g in [losses] + slide_grads:
        send(g)
    mine = lax.broadcasted_iota(jnp.int32, (32, 1), 0) == where[0]
    own = jnp.sum(jnp.where(mine, cots, 0.0), axis=0, keepdims=True)
    member, slot, count = slots_of(ids, where[0])
    usable = lax.broadcasted_iota(jnp.int32, (SLOTS, 1), 0).astype(F32) < count
    grad = jnp.where(usable, own / count, 0.0)
    normed, rstd = norm_parts(res[5][...])
    grad = norm_back(grad, normed, rstd)

    def put(i, a, b):
        at = {3: 0, 2: 2, 1: 4, 0: 5}[i]
        if i != 1:
            pairs[at][...] = a
            send(pairs[at])
            at += 1
        pairs[at][...] = b
        send(pairs[at])

    grad = encode_back(grad, x_ref[...], w_qkv, w_out, w_up, w_down, HEADS, res, packed_grad, put).astype(BF16)
    for b in range(8):
        spread[b * 128 : (b + 1) * 128, :] = mm_tn(choice(member, slot, b), grad).astype(BF16)
    send(spread)
    for e in early:
        e.finish()


def two_halves(flat, rows, core, halves, stage, sems, extra=None):
    run = 32 * rows
    copies = []
    for side in range(2):
        which = core if side == 0 else 1 - core
        for z in range(4):
            start = pl.multiple_of((2 * z + which) * run, 32)
            stage[side, z * run : (z + 1) * run, :] = flat[pl.ds(start, run), :].astype(BF16)
            part = pl.ds(z * run, run)
            copies.append(pltpu.make_async_copy(stage.at[side, part, :], halves[side].at[part, :], sems.at[side, z]))
            copies[-1].start()
        if extra is not None:
            stage[side, 4 * run : 4 * run + 80, :] = extra.ref()[which]
            part = pl.ds(4 * run, 80)
            copies.append(pltpu.make_async_copy(stage.at[side, part, :], halves[side].at[part, :], sems.at[side, 4]))
            copies[-1].start()
    for copy in copies:
        copy.wait()


def region_weights(core, *refs):
    ins, halves, bufs, flat, stage, sems, osems = cut(refs, 8, 2, 8, 1, 1, 1, 1)
    late = [Late(r, b, sems[0].at[i]) for i, (r, b) in enumerate(zip(ins, bufs))]
    hidden, grad, second, up_grad, mixture, mid_grad, first, packed_grad = late
    put_rows(flat[0], 9216, hidden[...], grad[...])
    put_rows(flat[0], 4608, second[...], up_grad[...])
    put_rows(flat[0], 3456, mixture[...], mid_grad[...])
    put_rows(flat[0], 0, first[...], packed_grad[...])
    two_halves(flat[0], 54, core[0], halves, stage[0], osems[0])


def tile_backward(core, ids, *refs):
    ins, _, halves, bufs, packed_grad, flat, stage, sems, osems = cut(refs, 14, 1, 2, 14, 1, 1, 1, 1, 1)
    late = [Late(ins[i], bufs[i], sems[0].at[i]) for i in (0, 13, 6, 12, 11, 5, 10, 4, 9, 8, 3, 7, 1, 2)]
    late = dict(zip((0, 13, 6, 12, 11, 5, 10, 4, 9, 8, 3, 7, 1, 2), late))
    arrived, patches, slide_rows = late[0], late[1], late[2]
    w_qkv, w_out, w_up, w_down = [late[i] for i in range(3, 7)]
    x_ref, res = late[7], [late[i] for i in range(8, 14)]
    rows32 = lax.broadcasted_iota(jnp.int32, (32, 32), 0)
    columns32 = lax.broadcasted_iota(jnp.int32, (32, 32), 1)
    assign = jnp.sum(jnp.where(rows32 == columns32, ids[...].astype(F32), 0.0), axis=1, keepdims=True)
    cot = jnp.zeros((32, D), F32)
    for r in range(32):
        cot = cot + jnp.where(assign == float(r), arrived[r].astype(F32), 0.0)
    cot = cot * 0.25
    grad = jnp.concatenate([cot] * PATCHES, axis=0)
    normed, rstd = norm_parts(res[5][...])
    grad = norm_back(grad, normed, rstd)
    bases = (2304, 5760, 6912, 11520)

    def put(i, a, b):
        put_rows(flat[0], bases[i], a, b)

    grad = encode_back(grad, x_ref[...], w_qkv, w_out, w_up, w_down, HEADS, res, packed_grad[0], put)
    put_rows(flat[0], 0, patches[...], grad.astype(BF16))
    two_halves(flat[0], 63, core[0], halves, stage[0], osems[0], slide_rows)


def fold(rows, pad, tail, *refs):
    mine, got = refs[:2]
    refs = refs[2:]
    if tail:
        out, extra = refs[:2]
        refs = refs[2:]
    else:
        out = refs[0]
        refs = refs[1:]
    a, b, total, stage, chunks, sems, osems = refs[:7]
    run = 32 * rows
    arriving = []
    for z in range(4 + tail):
        part = pl.ds(z * run, run if z < 4 else 80)
        for side, (source, buffer) in enumerate(((mine, a), (got, b))):
            arriving.append(pltpu.make_async_copy(source.at[part, :], buffer.at[part, :], sems.at[side, z]))
            arriving[-1].start()
    for z in range(4):
        arriving[2 * z].wait()
        arriving[2 * z + 1].wait()
        part = pl.ds(z * run, run)
        total[part, :] = a[part, :].astype(F32) + b[part, :].astype(F32)
    leaving = []
    if tail:
        arriving[8].wait()
        arriving[9].wait()
        part = pl.ds(4 * run, 80)
        refs[7][...] = (a[part, :].astype(F32) + b[part, :].astype(F32)).astype(BF16)
        leaving.append(pltpu.make_async_copy(refs[7], extra, osems.at[16]))
        leaving[-1].start()
    if pad:
        stage[8 * rows :, :] = jnp.zeros((pad, LANES), F32)
    for y in range(4):
        for x in range(4):
            for z in range(4):
                for h in range(2):
                    source = (z * 32 + y * 8 + h * 4 + x) * rows
                    target = (z * 2 + h) * rows
                    stage[target : target + rows, :] = total[source : source + rows, :]
            chunks[y * 4 + x] = stage[...].astype(BF16)
            leaving.append(pltpu.make_async_copy(chunks.at[y * 4 + x], out.at[y * 4 + x], osems.at[y * 4 + x]))
            leaving[-1].start()
    for copy in leaving:
        copy.wait()


def merge(tile_in, region_in, slide_in, out, tile_buf, region_buf, slide_buf, total, region_total, slide_total, stage, chunks, sems, osems):
    tile_late = Late(tile_in, tile_buf, sems.at[0])
    region_late = Late(region_in, region_buf, sems.at[1])
    slide_late = Late(slide_in, slide_buf, sems.at[2])
    slide_total[...] = slide_late[...].astype(F32)

    def added(late, target, rows):
        for start in range(0, rows, 48 if rows % 48 == 0 else 64):
            size = 48 if rows % 48 == 0 else 64
            value = late[0, start : start + size, :].astype(F32)
            for i in range(1, 16):
                value = value + late[i, start : start + size, :].astype(F32)
            target[start : start + size, :] = value

    added(region_late, region_total, 432)
    added(tile_late, total, 512)
    leaving = []
    for i in range(8):
        stage[0:63, :] = total[i * 63 : (i + 1) * 63, :]
        stage[63:64, :] = jnp.zeros((1, LANES), F32)
        stage[64:118, :] = region_total[i * 54 : (i + 1) * 54, :]
        stage[118:128, :] = slide_total[i * 10 : (i + 1) * 10, :]
        chunks[i] = stage[...].astype(BF16)
        leaving.append(pltpu.make_async_copy(chunks.at[i], out.at[i], osems.at[i]))
        leaving[-1].start()
    for copy in leaving:
        copy.wait()


def call(kernel, macs, outs, scratch, inputs, scalars=0, whole=0):
    specs = [pl.BlockSpec(memory_space=pltpu.SMEM)] * scalars
    specs += [pl.BlockSpec(memory_space=pltpu.VMEM)] * whole
    specs += [pl.BlockSpec(memory_space=pl.ANY)] * (len(inputs) - scalars - whole)
    moved = sum(math.prod(a.shape) * a.dtype.itemsize for a in inputs) + sum(math.prod(a) * jnp.dtype(k).itemsize for a, k in outs)
    cost = pl.CostEstimate(flops=2 * macs, bytes_accessed=moved, transcendentals=0)
    return pl.pallas_call(
        kernel,
        out_shape=[jax.ShapeDtypeStruct(shape, kind) for shape, kind in outs],
        in_specs=specs,
        out_specs=[pl.BlockSpec(memory_space=pl.ANY)] * len(outs),
        scratch_shapes=[pltpu.VMEM(*item) if isinstance(item, tuple) else item for item in scratch],
        compiler_params=pltpu.CompilerParams(vmem_limit_bytes=60 * 1024 * 1024),
        cost_estimate=cost,
    )(*inputs)


def like(arrays):
    return [(a.shape, a.dtype) for a in arrays]


def semaphores(*shape):
    return pltpu.SemaphoreType.DMA(shape)


def residuals(tokens, width, hidden, heads):
    return [
        ((tokens, 3 * width), BF16),
        ((heads, tokens, tokens), F32),
        ((tokens, width), BF16),
        ((tokens, width), F32),
        ((tokens, hidden), F32),
        ((tokens, width), F32),
    ]


def index_of(z, core, y, z_hi, x):
    return (z * 2 + core) * 32 + y * 8 + z_hi * 4 + x


PLANES = [[index_of(z, c, y, h, x) for y in range(4) for x in range(4)] for z in range(4) for c in range(2) for h in range(2)]
COLUMNS = [[index_of(z, c, y, h, x) for z in range(4) for h in range(2)] for c in range(2) for y in range(4) for x in range(4)]
OTHER_CORE = [(g, g + 1 - 2 * (g % 2)) for g in range(8)]
OTHER_PLANE = [(d, d + 4 - 8 * (d // 4 % 2)) for d in range(32)]
ALL = ("grp", "dev")


def exchange(array, groups):
    return lax.all_to_all(array, ALL, 0, 0, axis_index_groups=groups)


def folded(mine, other, rows, pad, tail):
    got = lax.ppermute(other, "grp", OTHER_CORE)
    height = 128 * rows + 80 * tail
    chunk = 8 * rows + pad
    return call(
        functools.partial(fold, rows, pad, tail),
        4 * US,
        [((16, chunk, LANES), BF16)] + [((80, LANES), BF16)] * tail,
        [((height, LANES), BF16)] * 2
        + [((128 * rows, LANES), F32), ((chunk, LANES), F32), ((16, chunk, LANES), BF16)]
        + [semaphores(2, 5), semaphores(17)]
        + [((80, LANES), BF16)] * tail,
        (mine, got),
    )


def body(
    patches,
    tile_region,
    region_slide,
    bin_label,
    censored,
    patch_w,
    tile_qkv,
    tile_out,
    tile_up,
    tile_down,
    region_qkv,
    region_out,
    region_up,
    region_down,
    slide_in,
    slide_qkv,
    slide_out,
    slide_up,
    slide_down,
    slide_head,
):
    member_index = lax.axis_index("dev").astype(jnp.int32)
    where = member_index.reshape(1)
    core = lax.rem(lax.axis_index("grp").astype(jnp.int32), 2).reshape(1)
    scaling = 1.0 / (bin_label.shape[1] * lax.axis_size("grp"))
    tokens = patches.transpose(1, 0, 2).reshape(128, 768)
    tile_res = [((128, D), F32)] + residuals(128, D, FF, HEADS)
    ins = (tokens, patch_w, tile_qkv, tile_out, tile_up, tile_down)
    message, *tile_kept = call(
        tile_forward,
        7 * US,
        [((112, LANES), BF16)] + tile_res,
        like(ins) + tile_res + [((112, LANES), BF16), semaphores(6), semaphores(7), semaphores(1)],
        (where, tile_region, region_slide) + ins,
        scalars=1,
        whole=2,
    )
    both = jnp.concatenate([message, lax.ppermute(message, "dev", OTHER_PLANE)], axis=0)
    rows = exchange(jnp.broadcast_to(both[None], (16, 224, LANES)), PLANES)
    region_res = [((SLOTS, D), F32)] + residuals(SLOTS, D, FF, HEADS)
    ins = (region_qkv, region_out, region_up, region_down)
    message, tails, *region_kept = call(
        region_forward,
        6 * US,
        [((32, 8, LANES), F32), ((32, 16, LANES), BF16)] + region_res,
        like(ins)
        + [((32, 112, LANES), BF16)]
        + region_res
        + [((8, LANES), F32), semaphores(4), semaphores(7), semaphores(33), semaphores(32)],
        (where, rows) + ins,
        scalars=1,
    )
    all_regions = lax.all_to_all(message, "dev", 0, 0)
    slide_weights = (slide_in, slide_qkv, slide_out, slide_up, slide_down, slide_head)
    pairs = [
        ((SLOTS, FF), BF16),
        ((SLOTS, D), BF16),
        ((SLOTS, D), BF16),
        ((SLOTS, FF), BF16),
        ((SLOTS, D), BF16),
        ((SLOTS, D), BF16),
        ((SLOTS, 3 * D), BF16),
    ]
    outs = [((SL_GRP, 1), F32), ((1024, D), BF16)] + pairs + like(slide_weights)
    ins = (all_regions, tails) + slide_weights + (region_qkv, region_out, region_up, region_down) + tuple(region_kept)
    losses, spread, *rest = call(
        functools.partial(region_backward, scaling),
        12 * US,
        outs,
        like(ins)
        + outs
        + [((SLOTS, 3 * D), BF16), ((32, 3 * D_SL), BF16), ((32, D), BF16)]
        + residuals(32, D_SL, D_SL, H_SL)
        + [semaphores(19), semaphores(15)],
        (where, bin_label.reshape(SL_GRP, 1), censored.reshape(SL_GRP, 1)) + ins,
        scalars=1,
        whole=2,
    )
    arrived = lax.all_to_all(spread.reshape(32, 32, D), "dev", 0, 0)
    hidden, down_grad, second, up_grad, mid_grad, first, packed_grad = rest[:7]
    ins = (hidden, down_grad, second, up_grad, region_kept[3], mid_grad, first, packed_grad)
    mine, other = call(
        region_weights,
        5 * US,
        [((6912, LANES), BF16)] * 2,
        like(ins) + [((13824, LANES), F32), ((2, 6912, LANES), BF16), semaphores(8), semaphores(2, 5)],
        (core,) + ins,
        scalars=1,
    )
    (region_chunks,) = folded(mine, other, 54, 0, 0)
    region_parts = exchange(region_chunks, PLANES)
    slide_flat = jnp.concatenate([g.astype(F32).reshape(-1) for g in rest[7:]]).reshape(4, 2, 4, 2, 4, 1155)
    y, x = member_index // 8, lax.rem(member_index, 4)
    zero = jnp.zeros((), jnp.int32)
    slide_rows = lax.dynamic_slice(slide_flat, (zero, zero, y, zero, x, zero), (4, 2, 1, 2, 1, 1155))
    slide_rows = slide_rows.reshape(4, 2, 2, 1155).transpose(1, 0, 2, 3)
    slide_rows = jnp.pad(slide_rows, ((0, 0), (0, 0), (0, 0), (0, 125))).astype(BF16).reshape(2, 80, LANES)
    ins = (arrived, tokens, slide_rows, tile_qkv, tile_out, tile_up, tile_down) + tuple(tile_kept)
    mine, other = call(
        tile_backward,
        13 * US,
        [((8144, LANES), BF16)] * 2,
        like(ins)
        + [((128, 3 * D), BF16), ((16128, LANES), F32), ((2, 8144, LANES), BF16), semaphores(14), semaphores(2, 5)],
        (core, tile_region) + ins + (region_chunks,),
        scalars=1,
        whole=1,
    )
    tile_chunks, slide_sums = folded(mine, other, 63, 8, 1)
    tile_parts = exchange(tile_chunks, PLANES)
    ins = (tile_parts, region_parts, slide_sums)
    (last,) = call(
        merge,
        3 * US,
        [((8, 128, LANES), BF16)],
        like(ins)
        + [((512, LANES), F32), ((432, LANES), F32), ((80, LANES), F32), ((128, LANES), F32), ((8, 128, LANES), BF16)]
        + [semaphores(3), semaphores(8)],
        ins,
    )
    total = jnp.sum(exchange(last, COLUMNS).astype(F32), axis=0)
    tile_result = total[0:63].reshape(8064)
    region_result = total[64:118].reshape(6912)
    slide_result = total[118:128].reshape(1280)[:1155] * 0.5
    return (losses.reshape(1, SL_GRP), tile_result, region_result, slide_result)


def solution(mesh):
    placed = (P(ALL, None, None), P("grp", "dev"), P("grp", "dev"), P("grp", None), P("grp", None)) + (P(),) * 15
    return jax.shard_map(
        body,
        mesh=mesh,
        in_specs=placed,
        out_specs=(P("grp", None), P(ALL), P(ALL), P(ALL)),
        check_vma=False,
    )
```

```python
import functools
import math

import jax
import jax.numpy as jnp
from jax import lax
from jax.experimental import pallas as pl
from jax.experimental.pallas import tpu as pltpu
from jax.sharding import PartitionSpec as P

D = 384
HEADS = 6
FF = 1536
PATCHES = 4
SLOTS = 64
D_SL = 192
H_SL = 3
NBINS = 4
SL_GRP = 4
HEAD = 64
F32 = jnp.float32
BF16 = jnp.bfloat16
LANES = 128
US = 550_000_000
GELU_C = math.sqrt(2.0 / math.pi)


def mm(a, b):
    return jnp.dot(a, b, preferred_element_type=F32)


def mm_nt(a, b):
    return lax.dot_general(a, b, (((1,), (1,)), ((), ())), preferred_element_type=F32)


def mm_tn(a, b):
    return lax.dot_general(a, b, (((0,), (0,)), ((), ())), preferred_element_type=F32)


def norm_parts(x):
    average = jnp.mean(x, axis=-1, keepdims=True)
    centred = x - average
    variance = jnp.mean(centred * centred, axis=-1, keepdims=True)
    rstd = lax.rsqrt(variance + 1e-06)
    return centred * rstd, rstd


def norm_back(grad, normed, rstd):
    first = jnp.mean(grad, axis=-1, keepdims=True)
    second = jnp.mean(grad * normed, axis=-1, keepdims=True)
    return rstd * (grad - first - normed * second)


def gelu_parts(x):
    t = jnp.tanh(GELU_C * (x + 0.044715 * (x * x * x)))
    value = 0.5 * x * (1.0 + t)
    slope = 0.5 * (1.0 + t) + 0.5 * x * (1.0 - t * t) * (GELU_C * (1.0 + 3.0 * 0.044715 * (x * x)))
    return value, slope


def encode(x, allowed, w_qkv, w_out, w_up, w_down, heads, res):
    packed_ref, attend_ref, mixture_ref, mid_ref, up_ref, out_ref = res
    width = x.shape[1]
    normed, _ = norm_parts(x)
    packed_ref[...] = mm(normed.astype(BF16), w_qkv[...]).astype(BF16)
    send(packed_ref)
    for h in range(heads):
        q = packed_ref[:, h * HEAD : (h + 1) * HEAD]
        k = packed_ref[:, width + h * HEAD : width + (h + 1) * HEAD]
        v = packed_ref[:, 2 * width + h * HEAD : 2 * width + (h + 1) * HEAD]
        scores = jnp.where(allowed, mm_nt(q, k) * 0.125, -1e30)
        scores = jnp.exp(scores - jnp.max(scores, axis=-1, keepdims=True))
        weights = scores / jnp.sum(scores, axis=-1, keepdims=True)
        attend_ref[h] = weights
        mixture_ref[:, h * HEAD : (h + 1) * HEAD] = mm(weights.astype(BF16), v).astype(BF16)
    send(attend_ref)
    send(mixture_ref)
    x1 = x + mm(mixture_ref[...], w_out[...])
    mid_ref[...] = x1
    send(mid_ref)
    normed, _ = norm_parts(x1)
    up = mm(normed.astype(BF16), w_up[...])
    up_ref[...] = up
    send(up_ref)
    hidden, _ = gelu_parts(up)
    out = x1 + mm(hidden.astype(BF16), w_down[...])
    out_ref[...] = out
    send(out_ref)
    return out


def encode_back(grad, x, w_qkv, w_out, w_up, w_down, heads, res, packed_grad, put):
    packed_ref, attend_ref, mixture_ref, mid_ref, up_ref, _ = res
    width = x.shape[1]
    grad_b = grad.astype(BF16)
    hidden, slope = gelu_parts(up_ref[...])
    up_grad = (mm_nt(grad_b, w_down[...]).astype(BF16).astype(F32) * slope).astype(BF16)
    put(3, hidden.astype(BF16), grad_b)
    normed, rstd = norm_parts(mid_ref[...])
    put(2, normed.astype(BF16), up_grad)
    normed_grad = mm_nt(up_grad, w_up[...]).astype(BF16).astype(F32)
    mid_grad = grad + norm_back(normed_grad, normed, rstd)
    mid_b = mid_grad.astype(BF16)
    put(1, mixture_ref[...], mid_b)
    mix_grad = mm_nt(mid_b, w_out[...]).astype(BF16)
    for h in range(heads):
        q = packed_ref[:, h * HEAD : (h + 1) * HEAD]
        k = packed_ref[:, width + h * HEAD : width + (h + 1) * HEAD]
        v = packed_ref[:, 2 * width + h * HEAD : 2 * width + (h + 1) * HEAD]
        head_grad = mix_grad[:, h * HEAD : (h + 1) * HEAD]
        weights = attend_ref[h]
        weights_grad = mm_nt(head_grad, v).astype(BF16).astype(F32)
        v_grad = mm_tn(weights.astype(BF16), head_grad)
        inner = jnp.sum(weights_grad * weights, axis=-1, keepdims=True)
        scores_grad = (weights * (weights_grad - inner) * 0.125).astype(BF16)
        packed_grad[:, h * HEAD : (h + 1) * HEAD] = mm(scores_grad, k).astype(BF16)
        packed_grad[:, width + h * HEAD : width + (h + 1) * HEAD] = mm_tn(scores_grad, q).astype(BF16)
        packed_grad[:, 2 * width + h * HEAD : 2 * width + (h + 1) * HEAD] = v_grad.astype(BF16)
    normed, rstd = norm_parts(x)
    put(0, normed.astype(BF16), packed_grad[...])
    normed_grad = mm_nt(packed_grad[...], w_qkv[...]).astype(BF16).astype(F32)
    return mid_grad + norm_back(normed_grad, normed, rstd)


def put_rows(flat, base, a, b):
    rows, columns = a.shape[1], b.shape[1]
    chunks = columns // 128
    left = a.T
    for c in range(0, chunks, 3):
        part = mm(left, b[:, c * 128 : (c + 3) * 128]).astype(BF16).astype(F32)
        for j in range(3):
            flat[pl.ds(base + c + j, rows, stride=chunks), :] = part[:, j * 128 : (j + 1) * 128]


def same_tile():
    row = lax.broadcasted_iota(jnp.int32, (128, 128), 0)
    column = lax.broadcasted_iota(jnp.int32, (128, 128), 1)
    return lax.rem(row, 32) == lax.rem(column, 32)


class Late:
    def __init__(self, source, buffer, sem):
        self.copy = pltpu.make_async_copy(source, buffer, sem)
        self.buffer, self.here = buffer, False
        self.copy.start()

    def ref(self):
        if not self.here:
            self.copy.wait()
            self.here = True
        return self.buffer

    def __getitem__(self, index):
        return self.ref()[index]


class Early:
    def __init__(self, target, buffer, sem):
        self.copy = pltpu.make_async_copy(buffer, target, sem)
        self.buffer = buffer

    def __getitem__(self, index):
        return self.buffer[index]

    def __setitem__(self, index, value):
        self.buffer[index] = value

    def finish(self):
        self.copy.wait()


def send(ref):
    if isinstance(ref, Early):
        ref.copy.start()


def leave(pairs, sems):
    copies = [pltpu.make_async_copy(a, b, sems.at[i]) for i, (a, b) in enumerate(pairs)]
    for copy in copies:
        copy.start()
    for copy in copies:
        copy.wait()


def broadcast_out(block, out, sems):
    copies = [pltpu.make_async_copy(block, out.at[i], sems.at[i]) for i in range(32)]
    for copy in copies:
        copy.start()
    for copy in copies:
        copy.wait()


def tile_forward(where, ids, slide, *refs):
    ins, outs, bufs, obufs, block, sems, osems, bsems = cut(refs, 6, 8, 6, 7, 1, 1, 1, 1)
    late = [Late(r, b, sems[0].at[i]) for i, (r, b) in enumerate(zip(ins, bufs))]
    res = [Early(r, b, osems[0].at[i]) for i, (r, b) in enumerate(zip(outs[1:], obufs))]
    patches, patch_w, w_qkv, w_out, w_up, w_down = late
    x = mm(patches[...], patch_w[...])
    res[0][...] = x
    send(res[0])
    out = encode(x, same_tile(), w_qkv, w_out, w_up, w_down, HEADS, res[1:])
    normed, _ = norm_parts(out)
    total = (normed[0:32] + normed[32:64]) + (normed[64:96] + normed[96:128])
    total = (total * 0.25).astype(BF16)
    message = block[0]
    for c in range(3):
        message[c * 32 : (c + 1) * 32, :] = total[:, c * LANES : (c + 1) * LANES]
    row = lax.broadcasted_iota(jnp.int32, (16, LANES), 0)
    lane = lax.broadcasted_iota(jnp.int32, (16, LANES), 1)
    mine = (lane >= 32 * lax.rem(where[0], 4)) & (lane < 32 * lax.rem(where[0], 4) + 32)
    four = jnp.concatenate([ids[...].astype(F32)] * 4, axis=1)
    tail = jnp.where((row == 0) & mine, four, 0.0) + jnp.where(row == 1, slide[...].astype(F32), 0.0)
    message[96:112, :] = tail.astype(BF16)
    leave([(message, outs[0])], bsems[0])
    for r in res:
        r.finish()


def cut(refs, *sizes):
    parts, at = [], 0
    for size in sizes:
        parts.append(refs[at : at + size])
        at += size
    assert at == len(refs)
    return parts


def tails_of(tails):
    tails = tails.astype(F32)
    row = lax.broadcasted_iota(jnp.int32, tails.shape, 1)
    ids = jnp.sum(jnp.where(row == 0, tails, 0.0), axis=1)
    slides = jnp.sum(jnp.where(row == 1, tails, 0.0), axis=1)
    to = lax.broadcasted_iota(jnp.int32, (8, 32), 0)
    source = lax.broadcasted_iota(jnp.int32, (8, 32), 1)
    near = (source >= 4 * to) & (source < 4 * to + 4)
    ids = mm(jnp.where(near, 1.0, 0.0).astype(BF16), ids.astype(BF16))
    return ids, slides[:, 0:1]


def slots_of(ids, region):
    member = jnp.where(ids == region.astype(F32), 1.0, 0.0)
    row = lax.broadcasted_iota(jnp.int32, (128, 128), 0)
    column = lax.broadcasted_iota(jnp.int32, (128, 128), 1)
    within = mm(member.astype(BF16), jnp.where(row < column, 1.0, 0.0).astype(BF16))
    sums = jnp.sum(member, axis=1, keepdims=True)
    row8 = lax.broadcasted_iota(jnp.int32, (8, 8), 0)
    column8 = lax.broadcasted_iota(jnp.int32, (8, 8), 1)
    earlier = jnp.where(column8 < row8, 1.0, 0.0).astype(BF16)
    ahead = mm(earlier, jnp.broadcast_to(sums, (8, 128)).astype(BF16))
    count = jnp.sum(sums, axis=0, keepdims=True)
    return member, (within + ahead).astype(jnp.int32), count


def choice(member, slot, b):
    k = lax.broadcasted_iota(jnp.int32, (SLOTS, 128), 0)
    return jnp.where((slot[b : b + 1] == k) & (member[b : b + 1] > 0.0), 1.0, 0.0).astype(BF16)


def region_forward(where, *refs):
    ins, outs, bufs, rows, obufs, block, sems, osems, bsems, rsems = cut(refs, 5, 9, 4, 1, 7, 1, 1, 1, 1, 1)
    rows = rows[0]
    h = lax.rem(where[0] // 4, 2)
    arriving = []
    for i in range(16):
        base = i // 4 * 8 + i % 4
        for side, z in enumerate((h, 1 - h)):
            source = ins[0].at[i, 112 * side : 112 * side + 112, :]
            arriving.append(pltpu.make_async_copy(source, rows.at[base + 4 * z], rsems[0].at[2 * i + side]))
            arriving[-1].start()
    w_qkv, w_out, w_up, w_down = [Late(r, b, sems[0].at[i]) for i, (r, b) in enumerate(zip(ins[1:], bufs))]
    res = [Early(r, b, osems[0].at[i]) for i, (r, b) in enumerate(zip(outs[2:], obufs))]
    for copy in arriving:
        copy.wait()
    tails = pltpu.make_async_copy(rows.at[:, 96:112, :], outs[1], bsems[0].at[32])
    tails.start()
    ids, _ = tails_of(rows[:, 96:112, :])
    member, slot, count = slots_of(ids, where[0])
    parts = [jnp.zeros((SLOTS, LANES), F32)] * 3
    for b in range(8):
        pick = choice(member, slot, b)
        for c in range(3):
            block_rows = rows[4 * b : 4 * b + 4, 32 * c : 32 * c + 32, :].reshape(128, LANES)
            parts[c] = parts[c] + mm(pick, block_rows)
    for c in range(3):
        res[0][:, c * LANES : (c + 1) * LANES] = parts[c]
    send(res[0])
    key = lax.broadcasted_iota(jnp.int32, (SLOTS, SLOTS), 1).astype(F32)
    out = encode(res[0][...], key < count, w_qkv, w_out, w_up, w_down, HEADS, res[1:])
    normed, _ = norm_parts(out)
    usable = lax.broadcasted_iota(jnp.int32, (SLOTS, 1), 0).astype(F32) < count
    total = jnp.sum(jnp.where(usable, normed, 0.0), axis=0, keepdims=True)
    embed = (total / count).astype(BF16).astype(F32)
    message = block[0]
    message[...] = jnp.zeros((8, LANES), F32)
    for c in range(3):
        message[c : c + 1, :] = embed[:, c * LANES : (c + 1) * LANES]
    broadcast_out(message, outs[0], bsems[0])
    tails.wait()
    for r in res:
        r.finish()


def slide_step(embeds, slide_row, slide_col, label, censor, slide_in, w_qkv, w_out, w_up, w_down, head, losses, grads, res, packed_grad, scaling):
    emb = embeds[...]
    x = mm(emb, slide_in[...])
    out = encode(x, slide_col == slide_row, w_qkv, w_out, w_up, w_down, H_SL, res)
    normed, rstd = norm_parts(out)
    sums, sizes, masks = [], [], []
    for s in range(SL_GRP):
        mask = jnp.where(slide_col == float(s), 1.0, 0.0)
        size = jnp.sum(mask, axis=0, keepdims=True)
        masks.append(mask)
        sizes.append(size)
        sums.append(jnp.sum(mask * normed, axis=0, keepdims=True) / size)
    pooled = jnp.concatenate(sums, axis=0).astype(BF16)
    logits = mm(pooled, head[...])
    soft = jnp.log1p(jnp.exp(-jnp.abs(logits)))
    log_hazard = -(jnp.maximum(-logits, 0.0) + soft)
    log_stay = -(jnp.maximum(logits, 0.0) + soft)
    bin_at = lax.broadcasted_iota(jnp.int32, (SL_GRP, NBINS), 1)
    at = (bin_at == label[...]).astype(F32)
    before = (bin_at < label[...]).astype(F32)
    held = censor[...].astype(F32)
    past = jnp.sum(before * log_stay, axis=1, keepdims=True)
    seen = past + jnp.sum(at * log_hazard, axis=1, keepdims=True)
    lived = past + jnp.sum(at * log_stay, axis=1, keepdims=True)
    losses[...] = -(1.0 - held) * seen - held * lived
    chance = 1.0 / (1.0 + jnp.exp(-logits))
    logit_grad = (scaling * (before * chance + at * (chance - (1.0 - held)))).astype(BF16)
    grads[5][...] = mm_tn(pooled, logit_grad).astype(BF16)
    pooled_grad = mm_nt(logit_grad, head[...]).astype(BF16).astype(F32)
    grad = jnp.zeros_like(normed)
    for s in range(SL_GRP):
        grad = grad + masks[s] * (pooled_grad[s : s + 1] / sizes[s])
    grad = norm_back(grad, normed, rstd)

    def put(i, a, b):
        grads[i + 1][...] = mm_tn(a, b).astype(BF16)

    grad = encode_back(grad, x, w_qkv, w_out, w_up, w_down, H_SL, res, packed_grad, put).astype(BF16)
    grads[0][...] = mm_tn(emb, grad).astype(BF16)
    return mm_nt(grad, slide_in[...]).astype(BF16)


def region_backward(scaling, where, label, censor, *refs):
    ins, outs, bufs, obufs, extra, sems, osems = cut(refs, 19, 15, 19, 15, 9, 1, 1)
    order = list(range(8)) + [18, 13, 17, 16, 14, 15, 9, 8, 10, 11, 12]
    late = dict()
    for i in list(dict.fromkeys(order)):
        late[i] = Late(ins[i], bufs[i], sems[0].at[i])
    early = [Early(r, b, osems[0].at[i]) for i, (r, b) in enumerate(zip(outs, obufs))]
    message, tails = late[0], late[1]
    slide_weights = [late[i] for i in range(2, 8)]
    w_qkv, w_out, w_up, w_down = [late[i] for i in range(8, 12)]
    x_ref, res = late[12], [late[i] for i in range(13, 19)]
    losses, spread, pairs, slide_grads = early[0], early[1], early[2:9], early[9:15]
    packed_grad, slide_packed_grad, embeds = extra[:3]
    ids, slide_col = tails_of(tails[...])
    rows32 = lax.broadcasted_iota(jnp.int32, (32, 32), 0)
    columns32 = lax.broadcasted_iota(jnp.int32, (32, 32), 1)
    slide_row = jnp.sum(jnp.where(rows32 == columns32, slide_col, 0.0), axis=0, keepdims=True)
    arrived = message[...]
    at = lax.broadcasted_iota(jnp.int32, arrived.shape, 1)
    for c in range(3):
        part = jnp.sum(jnp.where(at == c, arrived, 0.0), axis=1)
        embeds[:, c * LANES : (c + 1) * LANES] = part.astype(BF16)
    cots = slide_step(
        embeds, slide_row, slide_col, label, censor, *slide_weights, losses, slide_grads, extra[3:9], slide_packed_grad, scaling
    ).astype(F32)
    for g in [losses] + slide_grads:
        send(g)
    mine = lax.broadcasted_iota(jnp.int32, (32, 1), 0) == where[0]
    own = jnp.sum(jnp.where(mine, cots, 0.0), axis=0, keepdims=True)
    member, slot, count = slots_of(ids, where[0])
    usable = lax.broadcasted_iota(jnp.int32, (SLOTS, 1), 0).astype(F32) < count
    grad = jnp.where(usable, own / count, 0.0)
    normed, rstd = norm_parts(res[5][...])
    grad = norm_back(grad, normed, rstd)

    def put(i, a, b):
        at = {3: 0, 2: 2, 1: 4, 0: 5}[i]
        if i != 1:
            pairs[at][...] = a
            send(pairs[at])
            at += 1
        pairs[at][...] = b
        send(pairs[at])

    grad = encode_back(grad, x_ref[...], w_qkv, w_out, w_up, w_down, HEADS, res, packed_grad, put).astype(BF16)
    for b in range(8):
        spread[b * 128 : (b + 1) * 128, :] = mm_tn(choice(member, slot, b), grad).astype(BF16)
    send(spread)
    for e in early:
        e.finish()


def two_halves(flat, rows, core, halves, stage, sems, extra=None):
    run = 32 * rows
    copies = []
    for side in range(2):
        which = core if side == 0 else 1 - core
        for z in range(4):
            start = pl.multiple_of((2 * z + which) * run, 32)
            stage[side, z * run : (z + 1) * run, :] = flat[pl.ds(start, run), :].astype(BF16)
            part = pl.ds(z * run, run)
            copies.append(pltpu.make_async_copy(stage.at[side, part, :], halves[side].at[part, :], sems.at[side, z]))
            copies[-1].start()
        if extra is not None:
            stage[side, 4 * run : 4 * run + 80, :] = extra.ref()[which]
            part = pl.ds(4 * run, 80)
            copies.append(pltpu.make_async_copy(stage.at[side, part, :], halves[side].at[part, :], sems.at[side, 4]))
            copies[-1].start()
    for copy in copies:
        copy.wait()


def region_weights(core, *refs):
    ins, halves, bufs, flat, stage, sems, osems = cut(refs, 8, 2, 8, 1, 1, 1, 1)
    late = [Late(r, b, sems[0].at[i]) for i, (r, b) in enumerate(zip(ins, bufs))]
    hidden, grad, second, up_grad, mixture, mid_grad, first, packed_grad = late
    put_rows(flat[0], 9216, hidden[...], grad[...])
    put_rows(flat[0], 4608, second[...], up_grad[...])
    put_rows(flat[0], 3456, mixture[...], mid_grad[...])
    put_rows(flat[0], 0, first[...], packed_grad[...])
    two_halves(flat[0], 54, core[0], halves, stage[0], osems[0])


def tile_backward(core, ids, *refs):
    ins, _, halves, bufs, packed_grad, flat, stage, sems, osems = cut(refs, 14, 1, 2, 14, 1, 1, 1, 1, 1)
    late = [Late(ins[i], bufs[i], sems[0].at[i]) for i in (0, 13, 6, 12, 11, 5, 10, 4, 9, 8, 3, 7, 1, 2)]
    late = dict(zip((0, 13, 6, 12, 11, 5, 10, 4, 9, 8, 3, 7, 1, 2), late))
    arrived, patches, slide_rows = late[0], late[1], late[2]
    w_qkv, w_out, w_up, w_down = [late[i] for i in range(3, 7)]
    x_ref, res = late[7], [late[i] for i in range(8, 14)]
    rows32 = lax.broadcasted_iota(jnp.int32, (32, 32), 0)
    columns32 = lax.broadcasted_iota(jnp.int32, (32, 32), 1)
    assign = jnp.sum(jnp.where(rows32 == columns32, ids[...].astype(F32), 0.0), axis=1, keepdims=True)
    cot = jnp.zeros((32, D), F32)
    for r in range(32):
        cot = cot + jnp.where(assign == float(r), arrived[r].astype(F32), 0.0)
    cot = cot * 0.25
    grad = jnp.concatenate([cot] * PATCHES, axis=0)
    normed, rstd = norm_parts(res[5][...])
    grad = norm_back(grad, normed, rstd)
    bases = (2304, 5760, 6912, 11520)

    def put(i, a, b):
        put_rows(flat[0], bases[i], a, b)

    grad = encode_back(grad, x_ref[...], w_qkv, w_out, w_up, w_down, HEADS, res, packed_grad[0], put)
    put_rows(flat[0], 0, patches[...], grad.astype(BF16))
    two_halves(flat[0], 63, core[0], halves, stage[0], osems[0], slide_rows)


def fold(rows, pad, tail, *refs):
    mine, got = refs[:2]
    refs = refs[2:]
    if tail:
        out, extra = refs[:2]
        refs = refs[2:]
    else:
        out = refs[0]
        refs = refs[1:]
    a, b, total, stage, chunks, sems, osems = refs[:7]
    run = 32 * rows
    arriving = []
    for z in range(4 + tail):
        part = pl.ds(z * run, run if z < 4 else 80)
        for side, (source, buffer) in enumerate(((mine, a), (got, b))):
            arriving.append(pltpu.make_async_copy(source.at[part, :], buffer.at[part, :], sems.at[side, z]))
            arriving[-1].start()
    for z in range(4):
        arriving[2 * z].wait()
        arriving[2 * z + 1].wait()
        part = pl.ds(z * run, run)
        total[part, :] = a[part, :].astype(F32) + b[part, :].astype(F32)
    leaving = []
    if tail:
        arriving[8].wait()
        arriving[9].wait()
        part = pl.ds(4 * run, 80)
        refs[7][...] = (a[part, :].astype(F32) + b[part, :].astype(F32)).astype(BF16)
        leaving.append(pltpu.make_async_copy(refs[7], extra, osems.at[16]))
        leaving[-1].start()
    if pad:
        stage[8 * rows :, :] = jnp.zeros((pad, LANES), F32)
    for y in range(4):
        for x in range(4):
            for z in range(4):
                for h in range(2):
                    source = (z * 32 + y * 8 + h * 4 + x) * rows
                    target = (z * 2 + h) * rows
                    stage[target : target + rows, :] = total[source : source + rows, :]
            to = y * 4 + x if tail else x * 4 + y
            chunks[to] = stage[...].astype(BF16)
            leaving.append(pltpu.make_async_copy(chunks.at[to], out.at[to], osems.at[to]))
            leaving[-1].start()
    for copy in leaving:
        copy.wait()


def merge(tile_in, region_in, slide_in, out, tile_buf, region_buf, slide_buf, total, region_total, slide_total, stage, chunks, sems, osems):
    tile_late = Late(tile_in, tile_buf, sems.at[0])
    region_late = Late(region_in, region_buf, sems.at[1])
    slide_late = Late(slide_in, slide_buf, sems.at[2])
    slide_total[...] = slide_late[...].astype(F32)

    def added(late, target, rows):
        size = 64
        for start in range(0, rows, size):
            value = late[0, start : start + size, :].astype(F32)
            for i in range(1, 16):
                value = value + late[i, start : start + size, :].astype(F32)
            target[start : start + size, :] = value

    added(tile_late, total, 512)
    region_total[...] = region_late[...].astype(F32)
    leaving = []
    for i in range(8):
        stage[0:63, :] = total[i * 63 : (i + 1) * 63, :]
        stage[63:64, :] = jnp.zeros((1, LANES), F32)
        stage[64:118, :] = region_total[i * 54 : (i + 1) * 54, :]
        stage[118:128, :] = slide_total[i * 10 : (i + 1) * 10, :]
        chunks[i] = stage[...].astype(BF16)
        leaving.append(pltpu.make_async_copy(chunks.at[i], out.at[i], osems.at[i]))
        leaving[-1].start()
    for copy in leaving:
        copy.wait()


def call(kernel, macs, outs, scratch, inputs, scalars=0, whole=0):
    specs = [pl.BlockSpec(memory_space=pltpu.SMEM)] * scalars
    specs += [pl.BlockSpec(memory_space=pltpu.VMEM)] * whole
    specs += [pl.BlockSpec(memory_space=pl.ANY)] * (len(inputs) - scalars - whole)
    moved = sum(math.prod(a.shape) * a.dtype.itemsize for a in inputs) + sum(math.prod(a) * jnp.dtype(k).itemsize for a, k in outs)
    cost = pl.CostEstimate(flops=2 * macs, bytes_accessed=moved, transcendentals=0)
    return pl.pallas_call(
        kernel,
        out_shape=[jax.ShapeDtypeStruct(shape, kind) for shape, kind in outs],
        in_specs=specs,
        out_specs=[pl.BlockSpec(memory_space=pl.ANY)] * len(outs),
        scratch_shapes=[pltpu.VMEM(*item) if isinstance(item, tuple) else item for item in scratch],
        compiler_params=pltpu.CompilerParams(vmem_limit_bytes=60 * 1024 * 1024),
        cost_estimate=cost,
    )(*inputs)


def like(arrays):
    return [(a.shape, a.dtype) for a in arrays]


def semaphores(*shape):
    return pltpu.SemaphoreType.DMA(shape)


def residuals(tokens, width, hidden, heads):
    return [
        ((tokens, 3 * width), BF16),
        ((heads, tokens, tokens), F32),
        ((tokens, width), BF16),
        ((tokens, width), F32),
        ((tokens, hidden), F32),
        ((tokens, width), F32),
    ]


def index_of(z, core, y, z_hi, x):
    return (z * 2 + core) * 32 + y * 8 + z_hi * 4 + x


PLANES = [[index_of(z, c, y, h, x) for y in range(4) for x in range(4)] for z in range(4) for c in range(2) for h in range(2)]
ROWS = [[index_of(z, c, y, h, x) for x in range(4)] for z in range(4) for c in range(2) for h in range(2) for y in range(4)]
FILES = [[index_of(z, c, y, h, x) for y in range(4)] for z in range(4) for c in range(2) for h in range(2) for x in range(4)]
COLUMNS = [[index_of(z, c, y, h, x) for z in range(4) for h in range(2)] for c in range(2) for y in range(4) for x in range(4)]
OTHER_CORE = [(g, g + 1 - 2 * (g % 2)) for g in range(8)]
OTHER_PLANE = [(d, d + 4 - 8 * (d // 4 % 2)) for d in range(32)]
ALL = ("grp", "dev")


def scattered(array, groups):
    return lax.psum_scatter(array, ALL, scatter_dimension=0, tiled=False, axis_index_groups=groups)


def exchange(array, groups):
    return lax.all_to_all(array, ALL, 0, 0, axis_index_groups=groups)


def folded(mine, other, rows, pad, tail):
    got = lax.ppermute(other, "grp", OTHER_CORE)
    height = 128 * rows + 80 * tail
    chunk = 8 * rows + pad
    return call(
        functools.partial(fold, rows, pad, tail),
        4 * US,
        [((16, chunk, LANES), BF16)] + [((80, LANES), BF16)] * tail,
        [((height, LANES), BF16)] * 2
        + [((128 * rows, LANES), F32), ((chunk, LANES), F32), ((16, chunk, LANES), BF16)]
        + [semaphores(2, 5), semaphores(17)]
        + [((80, LANES), BF16)] * tail,
        (mine, got),
    )


def body(
    patches,
    tile_region,
    region_slide,
    bin_label,
    censored,
    patch_w,
    tile_qkv,
    tile_out,
    tile_up,
    tile_down,
    region_qkv,
    region_out,
    region_up,
    region_down,
    slide_in,
    slide_qkv,
    slide_out,
    slide_up,
    slide_down,
    slide_head,
):
    member_index = lax.axis_index("dev").astype(jnp.int32)
    where = member_index.reshape(1)
    core = lax.rem(lax.axis_index("grp").astype(jnp.int32), 2).reshape(1)
    scaling = 1.0 / (bin_label.shape[1] * lax.axis_size("grp"))
    tokens = patches.transpose(1, 0, 2).reshape(128, 768)
    tile_res = [((128, D), F32)] + residuals(128, D, FF, HEADS)
    ins = (tokens, patch_w, tile_qkv, tile_out, tile_up, tile_down)
    message, *tile_kept = call(
        tile_forward,
        7 * US,
        [((112, LANES), BF16)] + tile_res,
        like(ins) + tile_res + [((112, LANES), BF16), semaphores(6), semaphores(7), semaphores(1)],
        (where, tile_region, region_slide) + ins,
        scalars=1,
        whole=2,
    )
    both = jnp.concatenate([message, lax.ppermute(message, "dev", OTHER_PLANE)], axis=0)
    rows = exchange(jnp.broadcast_to(both[None], (16, 224, LANES)), PLANES)
    region_res = [((SLOTS, D), F32)] + residuals(SLOTS, D, FF, HEADS)
    ins = (region_qkv, region_out, region_up, region_down)
    message, tails, *region_kept = call(
        region_forward,
        6 * US,
        [((32, 8, LANES), F32), ((32, 16, LANES), BF16)] + region_res,
        like(ins)
        + [((32, 112, LANES), BF16)]
        + region_res
        + [((8, LANES), F32), semaphores(4), semaphores(7), semaphores(33), semaphores(32)],
        (where, rows) + ins,
        scalars=1,
    )
    all_regions = lax.all_to_all(message, "dev", 0, 0)
    slide_weights = (slide_in, slide_qkv, slide_out, slide_up, slide_down, slide_head)
    pairs = [
        ((SLOTS, FF), BF16),
        ((SLOTS, D), BF16),
        ((SLOTS, D), BF16),
        ((SLOTS, FF), BF16),
        ((SLOTS, D), BF16),
        ((SLOTS, D), BF16),
        ((SLOTS, 3 * D), BF16),
    ]
    outs = [((SL_GRP, 1), F32), ((1024, D), BF16)] + pairs + like(slide_weights)
    ins = (all_regions, tails) + slide_weights + (region_qkv, region_out, region_up, region_down) + tuple(region_kept)
    losses, spread, *rest = call(
        functools.partial(region_backward, scaling),
        12 * US,
        outs,
        like(ins)
        + outs
        + [((SLOTS, 3 * D), BF16), ((32, 3 * D_SL), BF16), ((32, D), BF16)]
        + residuals(32, D_SL, D_SL, H_SL)
        + [semaphores(19), semaphores(15)],
        (where, bin_label.reshape(SL_GRP, 1), censored.reshape(SL_GRP, 1)) + ins,
        scalars=1,
        whole=2,
    )
    arrived = lax.all_to_all(spread.reshape(32, 32, D), "dev", 0, 0)
    hidden, down_grad, second, up_grad, mid_grad, first, packed_grad = rest[:7]
    ins = (hidden, down_grad, second, up_grad, region_kept[3], mid_grad, first, packed_grad)
    mine, other = call(
        region_weights,
        5 * US,
        [((6912, LANES), BF16)] * 2,
        like(ins) + [((13824, LANES), F32), ((2, 6912, LANES), BF16), semaphores(8), semaphores(2, 5)],
        (core,) + ins,
        scalars=1,
    )
    (region_chunks,) = folded(mine, other, 54, 0, 0)
    region_parts = scattered(region_chunks.reshape(4, 1728, LANES), ROWS)
    region_parts = scattered(region_parts.reshape(4, 432, LANES), FILES)
    slide_flat = jnp.concatenate([g.astype(F32).reshape(-1) for g in rest[7:]]).reshape(4, 2, 4, 2, 4, 1155)
    y, x = member_index // 8, lax.rem(member_index, 4)
    zero = jnp.zeros((), jnp.int32)
    slide_rows = lax.dynamic_slice(slide_flat, (zero, zero, y, zero, x, zero), (4, 2, 1, 2, 1, 1155))
    slide_rows = slide_rows.reshape(4, 2, 2, 1155).transpose(1, 0, 2, 3)
    slide_rows = jnp.pad(slide_rows, ((0, 0), (0, 0), (0, 0), (0, 125))).astype(BF16).reshape(2, 80, LANES)
    ins = (arrived, tokens, slide_rows, tile_qkv, tile_out, tile_up, tile_down) + tuple(tile_kept)
    mine, other = call(
        tile_backward,
        13 * US,
        [((8144, LANES), BF16)] * 2,
        like(ins)
        + [((128, 3 * D), BF16), ((16128, LANES), F32), ((2, 8144, LANES), BF16), semaphores(14), semaphores(2, 5)],
        (core, tile_region) + ins + (region_chunks,),
        scalars=1,
        whole=1,
    )
    tile_chunks, slide_sums = folded(mine, other, 63, 8, 1)
    tile_parts = exchange(tile_chunks, PLANES)
    ins = (tile_parts, region_parts, slide_sums)
    (last,) = call(
        merge,
        3 * US,
        [((8, 128, LANES), BF16)],
        like(ins)
        + [((512, LANES), F32), ((432, LANES), F32), ((80, LANES), F32), ((128, LANES), F32), ((8, 128, LANES), BF16)]
        + [semaphores(3), semaphores(8)],
        ins,
    )
    total = jnp.sum(exchange(last, COLUMNS).astype(F32), axis=0)
    tile_result = total[0:63].reshape(8064)
    region_result = total[64:118].reshape(6912)
    slide_result = total[118:128].reshape(1280)[:1155] * 0.5
    return (losses.reshape(1, SL_GRP), tile_result, region_result, slide_result)


def solution(mesh):
    placed = (P(ALL, None, None), P("grp", "dev"), P("grp", "dev"), P("grp", None), P("grp", None)) + (P(),) * 15
    return jax.shard_map(
        body,
        mesh=mesh,
        in_specs=placed,
        out_specs=(P("grp", None), P(ALL), P(ALL), P(ALL)),
        check_vma=False,
    )
```

```python
import functools
import math

import jax
import jax.numpy as jnp
from jax import lax
from jax.experimental import pallas as pl
from jax.experimental.pallas import tpu as pltpu
from jax.sharding import PartitionSpec as P

D = 384
HEADS = 6
FF = 1536
PATCHES = 4
SLOTS = 64
D_SL = 192
H_SL = 3
NBINS = 4
SL_GRP = 4
HEAD = 64
F32 = jnp.float32
BF16 = jnp.bfloat16
LANES = 128
US = 550_000_000
GELU_C = math.sqrt(2.0 / math.pi)


def mm(a, b):
    return jnp.dot(a, b, preferred_element_type=F32)


def mm_nt(a, b):
    return lax.dot_general(a, b, (((1,), (1,)), ((), ())), preferred_element_type=F32)


def mm_tn(a, b):
    return lax.dot_general(a, b, (((0,), (0,)), ((), ())), preferred_element_type=F32)


def norm_parts(x):
    average = jnp.mean(x, axis=-1, keepdims=True)
    centred = x - average
    variance = jnp.mean(centred * centred, axis=-1, keepdims=True)
    rstd = lax.rsqrt(variance + 1e-06)
    return centred * rstd, rstd


def norm_back(grad, normed, rstd):
    first = jnp.mean(grad, axis=-1, keepdims=True)
    second = jnp.mean(grad * normed, axis=-1, keepdims=True)
    return rstd * (grad - first - normed * second)


def gelu_parts(x):
    t = jnp.tanh(GELU_C * (x + 0.044715 * (x * x * x)))
    value = 0.5 * x * (1.0 + t)
    slope = 0.5 * (1.0 + t) + 0.5 * x * (1.0 - t * t) * (GELU_C * (1.0 + 3.0 * 0.044715 * (x * x)))
    return value, slope


def encode(x, allowed, w_qkv, w_out, w_up, w_down, heads, res):
    packed_ref, attend_ref, mixture_ref, mid_ref, up_ref, out_ref = res
    width = x.shape[1]
    normed, _ = norm_parts(x)
    packed_ref[...] = mm(normed.astype(BF16), w_qkv[...]).astype(BF16)
    send(packed_ref)
    for h in range(heads):
        q = packed_ref[:, h * HEAD : (h + 1) * HEAD]
        k = packed_ref[:, width + h * HEAD : width + (h + 1) * HEAD]
        v = packed_ref[:, 2 * width + h * HEAD : 2 * width + (h + 1) * HEAD]
        scores = jnp.where(allowed, mm_nt(q, k) * 0.125, -1e30)
        scores = jnp.exp(scores - jnp.max(scores, axis=-1, keepdims=True))
        weights = scores / jnp.sum(scores, axis=-1, keepdims=True)
        attend_ref[h] = weights
        mixture_ref[:, h * HEAD : (h + 1) * HEAD] = mm(weights.astype(BF16), v).astype(BF16)
    send(attend_ref)
    send(mixture_ref)
    x1 = x + mm(mixture_ref[...], w_out[...])
    mid_ref[...] = x1
    send(mid_ref)
    normed, _ = norm_parts(x1)
    up = mm(normed.astype(BF16), w_up[...])
    up_ref[...] = up
    send(up_ref)
    hidden, _ = gelu_parts(up)
    out = x1 + mm(hidden.astype(BF16), w_down[...])
    out_ref[...] = out
    send(out_ref)
    return out


def encode_back(grad, x, w_qkv, w_out, w_up, w_down, heads, res, packed_grad, put):
    packed_ref, attend_ref, mixture_ref, mid_ref, up_ref, _ = res
    width = x.shape[1]
    grad_b = grad.astype(BF16)
    hidden, slope = gelu_parts(up_ref[...])
    up_grad = (mm_nt(grad_b, w_down[...]).astype(BF16).astype(F32) * slope).astype(BF16)
    put(3, hidden.astype(BF16), grad_b)
    normed, rstd = norm_parts(mid_ref[...])
    put(2, normed.astype(BF16), up_grad)
    normed_grad = mm_nt(up_grad, w_up[...]).astype(BF16).astype(F32)
    mid_grad = grad + norm_back(normed_grad, normed, rstd)
    mid_b = mid_grad.astype(BF16)
    put(1, mixture_ref[...], mid_b)
    mix_grad = mm_nt(mid_b, w_out[...]).astype(BF16)
    for h in range(heads):
        q = packed_ref[:, h * HEAD : (h + 1) * HEAD]
        k = packed_ref[:, width + h * HEAD : width + (h + 1) * HEAD]
        v = packed_ref[:, 2 * width + h * HEAD : 2 * width + (h + 1) * HEAD]
        head_grad = mix_grad[:, h * HEAD : (h + 1) * HEAD]
        weights = attend_ref[h]
        weights_grad = mm_nt(head_grad, v).astype(BF16).astype(F32)
        v_grad = mm_tn(weights.astype(BF16), head_grad)
        inner = jnp.sum(weights_grad * weights, axis=-1, keepdims=True)
        scores_grad = (weights * (weights_grad - inner) * 0.125).astype(BF16)
        packed_grad[:, h * HEAD : (h + 1) * HEAD] = mm(scores_grad, k).astype(BF16)
        packed_grad[:, width + h * HEAD : width + (h + 1) * HEAD] = mm_tn(scores_grad, q).astype(BF16)
        packed_grad[:, 2 * width + h * HEAD : 2 * width + (h + 1) * HEAD] = v_grad.astype(BF16)
    normed, rstd = norm_parts(x)
    put(0, normed.astype(BF16), packed_grad[...])
    normed_grad = mm_nt(packed_grad[...], w_qkv[...]).astype(BF16).astype(F32)
    return mid_grad + norm_back(normed_grad, normed, rstd)


def put_rows(flat, base, a, b):
    rows, columns = a.shape[1], b.shape[1]
    chunks = columns // 128
    left = a.T
    for c in range(0, chunks, 3):
        part = mm(left, b[:, c * 128 : (c + 3) * 128]).astype(BF16).astype(F32)
        for j in range(3):
            flat[pl.ds(base + c + j, rows, stride=chunks), :] = part[:, j * 128 : (j + 1) * 128]


def same_tile():
    row = lax.broadcasted_iota(jnp.int32, (128, 128), 0)
    column = lax.broadcasted_iota(jnp.int32, (128, 128), 1)
    return lax.rem(row, 32) == lax.rem(column, 32)


class Late:
    def __init__(self, source, buffer, sem):
        self.copy = pltpu.make_async_copy(source, buffer, sem)
        self.buffer, self.here = buffer, False
        self.copy.start()

    def ref(self):
        if not self.here:
            self.copy.wait()
            self.here = True
        return self.buffer

    def __getitem__(self, index):
        return self.ref()[index]


class Early:
    def __init__(self, target, buffer, sem):
        self.copy = pltpu.make_async_copy(buffer, target, sem)
        self.buffer = buffer

    def __getitem__(self, index):
        return self.buffer[index]

    def __setitem__(self, index, value):
        self.buffer[index] = value

    def finish(self):
        self.copy.wait()


def send(ref):
    if isinstance(ref, Early):
        ref.copy.start()


def leave(pairs, sems):
    copies = [pltpu.make_async_copy(a, b, sems.at[i]) for i, (a, b) in enumerate(pairs)]
    for copy in copies:
        copy.start()
    for copy in copies:
        copy.wait()


def broadcast_out(block, out, sems):
    copies = [pltpu.make_async_copy(block, out.at[i], sems.at[i]) for i in range(32)]
    for copy in copies:
        copy.start()
    for copy in copies:
        copy.wait()


def tile_forward(where, ids, slide, *refs):
    ins, outs, bufs, obufs, block, sems, osems, bsems = cut(refs, 6, 8, 6, 7, 1, 1, 1, 1)
    late = [Late(r, b, sems[0].at[i]) for i, (r, b) in enumerate(zip(ins, bufs))]
    res = [Early(r, b, osems[0].at[i]) for i, (r, b) in enumerate(zip(outs[1:], obufs))]
    patches, patch_w, w_qkv, w_out, w_up, w_down = late
    x = mm(patches[...], patch_w[...])
    res[0][...] = x
    send(res[0])
    out = encode(x, same_tile(), w_qkv, w_out, w_up, w_down, HEADS, res[1:])
    normed, _ = norm_parts(out)
    total = (normed[0:32] + normed[32:64]) + (normed[64:96] + normed[96:128])
    total = (total * 0.25).astype(BF16)
    message = block[0]
    for c in range(3):
        message[c * 32 : (c + 1) * 32, :] = total[:, c * LANES : (c + 1) * LANES]
    row = lax.broadcasted_iota(jnp.int32, (16, LANES), 0)
    lane = lax.broadcasted_iota(jnp.int32, (16, LANES), 1)
    mine = (lane >= 32 * lax.rem(where[0], 4)) & (lane < 32 * lax.rem(where[0], 4) + 32)
    four = jnp.concatenate([ids[...].astype(F32)] * 4, axis=1)
    tail = jnp.where((row == 0) & mine, four, 0.0) + jnp.where(row == 1, slide[...].astype(F32), 0.0)
    message[96:112, :] = tail.astype(BF16)
    leave([(message, outs[0])], bsems[0])
    for r in res:
        r.finish()


def cut(refs, *sizes):
    parts, at = [], 0
    for size in sizes:
        parts.append(refs[at : at + size])
        at += size
    assert at == len(refs)
    return parts


def tails_of(tails):
    tails = tails.astype(F32)
    row = lax.broadcasted_iota(jnp.int32, tails.shape, 1)
    ids = jnp.sum(jnp.where(row == 0, tails, 0.0), axis=1)
    slides = jnp.sum(jnp.where(row == 1, tails, 0.0), axis=1)
    to = lax.broadcasted_iota(jnp.int32, (8, 32), 0)
    source = lax.broadcasted_iota(jnp.int32, (8, 32), 1)
    near = (source >= 4 * to) & (source < 4 * to + 4)
    ids = mm(jnp.where(near, 1.0, 0.0).astype(BF16), ids.astype(BF16))
    return ids, slides[:, 0:1]


def slots_of(ids, region):
    member = jnp.where(ids == region.astype(F32), 1.0, 0.0)
    row = lax.broadcasted_iota(jnp.int32, (128, 128), 0)
    column = lax.broadcasted_iota(jnp.int32, (128, 128), 1)
    within = mm(member.astype(BF16), jnp.where(row < column, 1.0, 0.0).astype(BF16))
    sums = jnp.sum(member, axis=1, keepdims=True)
    row8 = lax.broadcasted_iota(jnp.int32, (8, 8), 0)
    column8 = lax.broadcasted_iota(jnp.int32, (8, 8), 1)
    earlier = jnp.where(column8 < row8, 1.0, 0.0).astype(BF16)
    ahead = mm(earlier, jnp.broadcast_to(sums, (8, 128)).astype(BF16))
    count = jnp.sum(sums, axis=0, keepdims=True)
    return member, (within + ahead).astype(jnp.int32), count


def choice(member, slot, b):
    k = lax.broadcasted_iota(jnp.int32, (SLOTS, 128), 0)
    return jnp.where((slot[b : b + 1] == k) & (member[b : b + 1] > 0.0), 1.0, 0.0).astype(BF16)


def region_forward(where, *refs):
    ins, outs, bufs, rows, obufs, block, sems, osems, bsems, rsems = cut(refs, 5, 9, 4, 1, 7, 1, 1, 1, 1, 1)
    rows = rows[0]
    h = lax.rem(where[0] // 4, 2)
    arriving = []
    for i in range(16):
        base = i // 4 * 8 + i % 4
        for side, z in enumerate((h, 1 - h)):
            source = ins[0].at[i, 112 * side : 112 * side + 112, :]
            arriving.append(pltpu.make_async_copy(source, rows.at[base + 4 * z], rsems[0].at[2 * i + side]))
            arriving[-1].start()
    w_qkv, w_out, w_up, w_down = [Late(r, b, sems[0].at[i]) for i, (r, b) in enumerate(zip(ins[1:], bufs))]
    res = [Early(r, b, osems[0].at[i]) for i, (r, b) in enumerate(zip(outs[2:], obufs))]
    for copy in arriving:
        copy.wait()
    tails = pltpu.make_async_copy(rows.at[:, 96:112, :], outs[1], bsems[0].at[32])
    tails.start()
    ids, _ = tails_of(rows[:, 96:112, :])
    member, slot, count = slots_of(ids, where[0])
    parts = [jnp.zeros((SLOTS, LANES), F32)] * 3
    for b in range(8):
        pick = choice(member, slot, b)
        for c in range(3):
            block_rows = rows[4 * b : 4 * b + 4, 32 * c : 32 * c + 32, :].reshape(128, LANES)
            parts[c] = parts[c] + mm(pick, block_rows)
    for c in range(3):
        res[0][:, c * LANES : (c + 1) * LANES] = parts[c]
    send(res[0])
    key = lax.broadcasted_iota(jnp.int32, (SLOTS, SLOTS), 1).astype(F32)
    out = encode(res[0][...], key < count, w_qkv, w_out, w_up, w_down, HEADS, res[1:])
    normed, _ = norm_parts(out)
    usable = lax.broadcasted_iota(jnp.int32, (SLOTS, 1), 0).astype(F32) < count
    total = jnp.sum(jnp.where(usable, normed, 0.0), axis=0, keepdims=True)
    embed = (total / count).astype(BF16).astype(F32)
    message = block[0]
    message[...] = jnp.zeros((8, LANES), F32)
    for c in range(3):
        message[c : c + 1, :] = embed[:, c * LANES : (c + 1) * LANES]
    broadcast_out(message, outs[0], bsems[0])
    tails.wait()
    for r in res:
        r.finish()


def slide_step(embeds, slide_row, slide_col, label, censor, slide_in, w_qkv, w_out, w_up, w_down, head, losses, grads, res, packed_grad, scaling):
    emb = embeds[...]
    x = mm(emb, slide_in[...])
    out = encode(x, slide_col == slide_row, w_qkv, w_out, w_up, w_down, H_SL, res)
    normed, rstd = norm_parts(out)
    sums, sizes, masks = [], [], []
    for s in range(SL_GRP):
        mask = jnp.where(slide_col == float(s), 1.0, 0.0)
        size = jnp.sum(mask, axis=0, keepdims=True)
        masks.append(mask)
        sizes.append(size)
        sums.append(jnp.sum(mask * normed, axis=0, keepdims=True) / size)
    pooled = jnp.concatenate(sums, axis=0).astype(BF16)
    logits = mm(pooled, head[...])
    soft = jnp.log1p(jnp.exp(-jnp.abs(logits)))
    log_hazard = -(jnp.maximum(-logits, 0.0) + soft)
    log_stay = -(jnp.maximum(logits, 0.0) + soft)
    bin_at = lax.broadcasted_iota(jnp.int32, (SL_GRP, NBINS), 1)
    at = (bin_at == label[...]).astype(F32)
    before = (bin_at < label[...]).astype(F32)
    held = censor[...].astype(F32)
    past = jnp.sum(before * log_stay, axis=1, keepdims=True)
    seen = past + jnp.sum(at * log_hazard, axis=1, keepdims=True)
    lived = past + jnp.sum(at * log_stay, axis=1, keepdims=True)
    losses[...] = -(1.0 - held) * seen - held * lived
    chance = 1.0 / (1.0 + jnp.exp(-logits))
    logit_grad = (scaling * (before * chance + at * (chance - (1.0 - held)))).astype(BF16)
    grads[5][...] = mm_tn(pooled, logit_grad).astype(BF16)
    pooled_grad = mm_nt(logit_grad, head[...]).astype(BF16).astype(F32)
    grad = jnp.zeros_like(normed)
    for s in range(SL_GRP):
        grad = grad + masks[s] * (pooled_grad[s : s + 1] / sizes[s])
    grad = norm_back(grad, normed, rstd)

    def put(i, a, b):
        grads[i + 1][...] = mm_tn(a, b).astype(BF16)

    grad = encode_back(grad, x, w_qkv, w_out, w_up, w_down, H_SL, res, packed_grad, put).astype(BF16)
    grads[0][...] = mm_tn(emb, grad).astype(BF16)
    return mm_nt(grad, slide_in[...]).astype(BF16)


def region_backward(scaling, where, label, censor, *refs):
    ins, outs, bufs, obufs, extra, sems, osems = cut(refs, 19, 15, 19, 15, 9, 1, 1)
    order = list(range(8)) + [18, 13, 17, 16, 14, 15, 9, 8, 10, 11, 12]
    late = dict()
    for i in list(dict.fromkeys(order)):
        late[i] = Late(ins[i], bufs[i], sems[0].at[i])
    early = [Early(r, b, osems[0].at[i]) for i, (r, b) in enumerate(zip(outs, obufs))]
    message, tails = late[0], late[1]
    slide_weights = [late[i] for i in range(2, 8)]
    w_qkv, w_out, w_up, w_down = [late[i] for i in range(8, 12)]
    x_ref, res = late[12], [late[i] for i in range(13, 19)]
    losses, spread, pairs, slide_grads = early[0], early[1], early[2:9], early[9:15]
    packed_grad, slide_packed_grad, embeds = extra[:3]
    ids, slide_col = tails_of(tails[...])
    rows32 = lax.broadcasted_iota(jnp.int32, (32, 32), 0)
    columns32 = lax.broadcasted_iota(jnp.int32, (32, 32), 1)
    slide_row = jnp.sum(jnp.where(rows32 == columns32, slide_col, 0.0), axis=0, keepdims=True)
    arrived = message[...]
    at = lax.broadcasted_iota(jnp.int32, arrived.shape, 1)
    for c in range(3):
        part = jnp.sum(jnp.where(at == c, arrived, 0.0), axis=1)
        embeds[:, c * LANES : (c + 1) * LANES] = part.astype(BF16)
    cots = slide_step(
        embeds, slide_row, slide_col, label, censor, *slide_weights, losses, slide_grads, extra[3:9], slide_packed_grad, scaling
    ).astype(F32)
    for g in [losses] + slide_grads:
        send(g)
    mine = lax.broadcasted_iota(jnp.int32, (32, 1), 0) == where[0]
    own = jnp.sum(jnp.where(mine, cots, 0.0), axis=0, keepdims=True)
    member, slot, count = slots_of(ids, where[0])
    usable = lax.broadcasted_iota(jnp.int32, (SLOTS, 1), 0).astype(F32) < count
    grad = jnp.where(usable, own / count, 0.0)
    normed, rstd = norm_parts(res[5][...])
    grad = norm_back(grad, normed, rstd)

    def put(i, a, b):
        at = {3: 0, 2: 2, 1: 4, 0: 5}[i]
        if i != 1:
            pairs[at][...] = a
            send(pairs[at])
            at += 1
        pairs[at][...] = b
        send(pairs[at])

    grad = encode_back(grad, x_ref[...], w_qkv, w_out, w_up, w_down, HEADS, res, packed_grad, put).astype(BF16)
    for b in range(8):
        spread[b * 128 : (b + 1) * 128, :] = mm_tn(choice(member, slot, b), grad).astype(BF16)
    send(spread)
    for e in early:
        e.finish()


def two_halves(flat, rows, core, halves, stage, sems, extra=None):
    run = 32 * rows
    copies = []
    for side in range(2):
        which = core if side == 0 else 1 - core
        for z in range(4):
            start = pl.multiple_of((2 * z + which) * run, 32)
            stage[side, z * run : (z + 1) * run, :] = flat[pl.ds(start, run), :].astype(BF16)
            part = pl.ds(z * run, run)
            copies.append(pltpu.make_async_copy(stage.at[side, part, :], halves[side].at[part, :], sems.at[side, z]))
            copies[-1].start()
        if extra is not None:
            stage[side, 4 * run : 4 * run + 80, :] = extra.ref()[which]
            part = pl.ds(4 * run, 80)
            copies.append(pltpu.make_async_copy(stage.at[side, part, :], halves[side].at[part, :], sems.at[side, 4]))
            copies[-1].start()
    for copy in copies:
        copy.wait()


def region_weights(core, *refs):
    ins, halves, bufs, flat, stage, sems, osems = cut(refs, 8, 2, 8, 1, 1, 1, 1)
    late = [Late(r, b, sems[0].at[i]) for i, (r, b) in enumerate(zip(ins, bufs))]
    hidden, grad, second, up_grad, mixture, mid_grad, first, packed_grad = late
    put_rows(flat[0], 9216, hidden[...], grad[...])
    put_rows(flat[0], 4608, second[...], up_grad[...])
    put_rows(flat[0], 3456, mixture[...], mid_grad[...])
    put_rows(flat[0], 0, first[...], packed_grad[...])
    two_halves(flat[0], 54, core[0], halves, stage[0], osems[0])


def tile_backward(core, ids, *refs):
    ins, _, halves, bufs, packed_grad, flat, stage, sems, osems = cut(refs, 14, 1, 2, 14, 1, 1, 1, 1, 1)
    late = [Late(ins[i], bufs[i], sems[0].at[i]) for i in (0, 13, 6, 12, 11, 5, 10, 4, 9, 8, 3, 7, 1, 2)]
    late = dict(zip((0, 13, 6, 12, 11, 5, 10, 4, 9, 8, 3, 7, 1, 2), late))
    arrived, patches, slide_rows = late[0], late[1], late[2]
    w_qkv, w_out, w_up, w_down = [late[i] for i in range(3, 7)]
    x_ref, res = late[7], [late[i] for i in range(8, 14)]
    rows32 = lax.broadcasted_iota(jnp.int32, (32, 32), 0)
    columns32 = lax.broadcasted_iota(jnp.int32, (32, 32), 1)
    assign = jnp.sum(jnp.where(rows32 == columns32, ids[...].astype(F32), 0.0), axis=1, keepdims=True)
    cot = jnp.zeros((32, D), F32)
    for r in range(32):
        cot = cot + jnp.where(assign == float(r), arrived[r].astype(F32), 0.0)
    cot = cot * 0.25
    grad = jnp.concatenate([cot] * PATCHES, axis=0)
    normed, rstd = norm_parts(res[5][...])
    grad = norm_back(grad, normed, rstd)
    bases = (2304, 5760, 6912, 11520)

    def put(i, a, b):
        put_rows(flat[0], bases[i], a, b)

    grad = encode_back(grad, x_ref[...], w_qkv, w_out, w_up, w_down, HEADS, res, packed_grad[0], put)
    put_rows(flat[0], 0, patches[...], grad.astype(BF16))
    two_halves(flat[0], 63, core[0], halves, stage[0], osems[0], slide_rows)


def fold(rows, pad, tail, *refs):
    mine, got = refs[:2]
    refs = refs[2:]
    if tail:
        out, extra = refs[:2]
        refs = refs[2:]
    else:
        out = refs[0]
        refs = refs[1:]
    a, b, total, stage, chunks, sems, osems = refs[:7]
    run = 32 * rows
    arriving = []
    for z in range(4 + tail):
        part = pl.ds(z * run, run if z < 4 else 80)
        for side, (source, buffer) in enumerate(((mine, a), (got, b))):
            arriving.append(pltpu.make_async_copy(source.at[part, :], buffer.at[part, :], sems.at[side, z]))
            arriving[-1].start()
    for z in range(4):
        arriving[2 * z].wait()
        arriving[2 * z + 1].wait()
        part = pl.ds(z * run, run)
        total[part, :] = a[part, :].astype(F32) + b[part, :].astype(F32)
    leaving = []
    if tail:
        arriving[8].wait()
        arriving[9].wait()
        part = pl.ds(4 * run, 80)
        refs[7][...] = (a[part, :].astype(F32) + b[part, :].astype(F32)).astype(BF16)
        leaving.append(pltpu.make_async_copy(refs[7], extra, osems.at[16]))
        leaving[-1].start()
    if pad:
        stage[8 * rows :, :] = jnp.zeros((pad, LANES), F32)
    for y in range(4):
        for x in range(4):
            for z in range(4):
                for h in range(2):
                    source = (z * 32 + y * 8 + h * 4 + x) * rows
                    target = (z * 2 + h) * rows
                    stage[target : target + rows, :] = total[source : source + rows, :]
            chunks[y * 4 + x] = stage[...].astype(BF16)
            leaving.append(pltpu.make_async_copy(chunks.at[y * 4 + x], out.at[y * 4 + x], osems.at[y * 4 + x]))
            leaving[-1].start()
    for copy in leaving:
        copy.wait()


def gate(source, unread, target):
    pass


def plane_sum(parts, out, buffer, total, sems):
    copies = [pltpu.make_async_copy(parts.at[:, i * 144 : (i + 1) * 144, :], buffer.at[:, i * 144 : (i + 1) * 144, :], sems.at[i]) for i in range(3)]
    for copy in copies:
        copy.start()
    for i in range(3):
        copies[i].wait()
        for start in range(i * 144, (i + 1) * 144, 48):
            value = buffer[0, start : start + 48, :].astype(F32)
            for j in range(1, 16):
                value = value + buffer[j, start : start + 48, :].astype(F32)
            total[start : start + 48, :] = value
    leave([(total, out)], sems)


def merge(tile_in, region_in, slide_in, out, tile_buf, region_buf, slide_buf, total, slide_total, stage, chunks, sems, osems):
    tile_late = Late(tile_in, tile_buf, sems.at[0])
    region_late = Late(region_in, region_buf, sems.at[1])
    slide_late = Late(slide_in, slide_buf, sems.at[2])
    slide_total[...] = slide_late[...].astype(F32)

    for start in range(0, 512, 64):
        value = tile_late[0, start : start + 64, :].astype(F32)
        for i in range(1, 16):
            value = value + tile_late[i, start : start + 64, :].astype(F32)
        total[start : start + 64, :] = value
    region_total = region_late.ref()
    leaving = []
    for i in range(8):
        stage[0:63, :] = total[i * 63 : (i + 1) * 63, :]
        stage[63:64, :] = jnp.zeros((1, LANES), F32)
        stage[64:118, :] = region_total[i * 54 : (i + 1) * 54, :]
        stage[118:128, :] = slide_total[i * 10 : (i + 1) * 10, :]
        chunks[i] = stage[...].astype(BF16)
        leaving.append(pltpu.make_async_copy(chunks.at[i], out.at[i], osems.at[i]))
        leaving[-1].start()
    for copy in leaving:
        copy.wait()


def call(kernel, macs, outs, scratch, inputs, scalars=0, whole=0):
    specs = [pl.BlockSpec(memory_space=pltpu.SMEM)] * scalars
    specs += [pl.BlockSpec(memory_space=pltpu.VMEM)] * whole
    specs += [pl.BlockSpec(memory_space=pl.ANY)] * (len(inputs) - scalars - whole)
    moved = sum(math.prod(a.shape) * a.dtype.itemsize for a in inputs) + sum(math.prod(a) * jnp.dtype(k).itemsize for a, k in outs)
    cost = pl.CostEstimate(flops=2 * macs, bytes_accessed=moved, transcendentals=0)
    return pl.pallas_call(
        kernel,
        out_shape=[jax.ShapeDtypeStruct(shape, kind) for shape, kind in outs],
        in_specs=specs,
        out_specs=[pl.BlockSpec(memory_space=pl.ANY)] * len(outs),
        scratch_shapes=[pltpu.VMEM(*item) if isinstance(item, tuple) else item for item in scratch],
        compiler_params=pltpu.CompilerParams(vmem_limit_bytes=60 * 1024 * 1024),
        cost_estimate=cost,
    )(*inputs)


def like(arrays):
    return [(a.shape, a.dtype) for a in arrays]


def semaphores(*shape):
    return pltpu.SemaphoreType.DMA(shape)


def residuals(tokens, width, hidden, heads):
    return [
        ((tokens, 3 * width), BF16),
        ((heads, tokens, tokens), F32),
        ((tokens, width), BF16),
        ((tokens, width), F32),
        ((tokens, hidden), F32),
        ((tokens, width), F32),
    ]


def index_of(z, core, y, z_hi, x):
    return (z * 2 + core) * 32 + y * 8 + z_hi * 4 + x


PLANES = [[index_of(z, c, y, h, x) for y in range(4) for x in range(4)] for z in range(4) for c in range(2) for h in range(2)]
COLUMNS = [[index_of(z, c, y, h, x) for z in range(4) for h in range(2)] for c in range(2) for y in range(4) for x in range(4)]
OTHER_CORE = [(g, g + 1 - 2 * (g % 2)) for g in range(8)]
OTHER_PLANE = [(d, d + 4 - 8 * (d // 4 % 2)) for d in range(32)]
ALL = ("grp", "dev")


def exchange(array, groups):
    return lax.all_to_all(array, ALL, 0, 0, axis_index_groups=groups)


def folded(mine, other, rows, pad, tail):
    got = lax.ppermute(other, "grp", OTHER_CORE)
    height = 128 * rows + 80 * tail
    chunk = 8 * rows + pad
    return call(
        functools.partial(fold, rows, pad, tail),
        4 * US,
        [((16, chunk, LANES), BF16)] + [((80, LANES), BF16)] * tail,
        [((height, LANES), BF16)] * 2
        + [((128 * rows, LANES), F32), ((chunk, LANES), F32), ((16, chunk, LANES), BF16)]
        + [semaphores(2, 5), semaphores(17)]
        + [((80, LANES), BF16)] * tail,
        (mine, got),
    )


def body(
    patches,
    tile_region,
    region_slide,
    bin_label,
    censored,
    patch_w,
    tile_qkv,
    tile_out,
    tile_up,
    tile_down,
    region_qkv,
    region_out,
    region_up,
    region_down,
    slide_in,
    slide_qkv,
    slide_out,
    slide_up,
    slide_down,
    slide_head,
):
    member_index = lax.axis_index("dev").astype(jnp.int32)
    where = member_index.reshape(1)
    core = lax.rem(lax.axis_index("grp").astype(jnp.int32), 2).reshape(1)
    scaling = 1.0 / (bin_label.shape[1] * lax.axis_size("grp"))
    tokens = patches.transpose(1, 0, 2).reshape(128, 768)
    tile_res = [((128, D), F32)] + residuals(128, D, FF, HEADS)
    ins = (tokens, patch_w, tile_qkv, tile_out, tile_up, tile_down)
    message, *tile_kept = call(
        tile_forward,
        7 * US,
        [((112, LANES), BF16)] + tile_res,
        like(ins) + tile_res + [((112, LANES), BF16), semaphores(6), semaphores(7), semaphores(1)],
        (where, tile_region, region_slide) + ins,
        scalars=1,
        whole=2,
    )
    both = jnp.concatenate([message, lax.ppermute(message, "dev", OTHER_PLANE)], axis=0)
    rows = exchange(jnp.broadcast_to(both[None], (16, 224, LANES)), PLANES)
    region_res = [((SLOTS, D), F32)] + residuals(SLOTS, D, FF, HEADS)
    ins = (region_qkv, region_out, region_up, region_down)
    message, tails, *region_kept = call(
        region_forward,
        6 * US,
        [((32, 8, LANES), F32), ((32, 16, LANES), BF16)] + region_res,
        like(ins)
        + [((32, 112, LANES), BF16)]
        + region_res
        + [((8, LANES), F32), semaphores(4), semaphores(7), semaphores(33), semaphores(32)],
        (where, rows) + ins,
        scalars=1,
    )
    all_regions = lax.all_to_all(message, "dev", 0, 0)
    slide_weights = (slide_in, slide_qkv, slide_out, slide_up, slide_down, slide_head)
    pairs = [
        ((SLOTS, FF), BF16),
        ((SLOTS, D), BF16),
        ((SLOTS, D), BF16),
        ((SLOTS, FF), BF16),
        ((SLOTS, D), BF16),
        ((SLOTS, D), BF16),
        ((SLOTS, 3 * D), BF16),
    ]
    outs = [((SL_GRP, 1), F32), ((1024, D), BF16)] + pairs + like(slide_weights)
    ins = (all_regions, tails) + slide_weights + (region_qkv, region_out, region_up, region_down) + tuple(region_kept)
    losses, spread, *rest = call(
        functools.partial(region_backward, scaling),
        12 * US,
        outs,
        like(ins)
        + outs
        + [((SLOTS, 3 * D), BF16), ((32, 3 * D_SL), BF16), ((32, D), BF16)]
        + residuals(32, D_SL, D_SL, H_SL)
        + [semaphores(19), semaphores(15)],
        (where, bin_label.reshape(SL_GRP, 1), censored.reshape(SL_GRP, 1)) + ins,
        scalars=1,
        whole=2,
    )
    arrived = lax.all_to_all(spread.reshape(32, 32, D), "dev", 0, 0)
    hidden, down_grad, second, up_grad, mid_grad, first, packed_grad = rest[:7]
    ins = (hidden, down_grad, second, up_grad, region_kept[3], mid_grad, first, packed_grad)
    mine, other = call(
        region_weights,
        5 * US,
        [((6912, LANES), BF16)] * 2,
        like(ins) + [((13824, LANES), F32), ((2, 6912, LANES), BF16), semaphores(8), semaphores(2, 5)],
        (core,) + ins,
        scalars=1,
    )
    (region_chunks,) = folded(mine, other, 54, 0, 0)
    region_parts = exchange(region_chunks, PLANES)
    (region_sums,) = call(
        plane_sum,
        2 * US,
        [((432, LANES), F32)],
        like((region_parts,)) + [((432, LANES), F32), semaphores(3)],
        (region_parts,),
    )
    slide_flat = jnp.concatenate([g.astype(F32).reshape(-1) for g in rest[7:]]).reshape(4, 2, 4, 2, 4, 1155)
    y, x = member_index // 8, lax.rem(member_index, 4)
    zero = jnp.zeros((), jnp.int32)
    slide_rows = lax.dynamic_slice(slide_flat, (zero, zero, y, zero, x, zero), (4, 2, 1, 2, 1, 1155))
    slide_rows = slide_rows.reshape(4, 2, 2, 1155).transpose(1, 0, 2, 3)
    slide_rows = jnp.pad(slide_rows, ((0, 0), (0, 0), (0, 0), (0, 125))).astype(BF16).reshape(2, 80, LANES)
    ins = (arrived, tokens, slide_rows, tile_qkv, tile_out, tile_up, tile_down) + tuple(tile_kept)
    mine, other = call(
        tile_backward,
        13 * US,
        [((8144, LANES), BF16)] * 2,
        like(ins)
        + [((128, 3 * D), BF16), ((16128, LANES), F32), ((2, 8144, LANES), BF16), semaphores(14), semaphores(2, 5)],
        (core, tile_region) + ins + (region_chunks,),
        scalars=1,
        whole=1,
    )
    other = pl.pallas_call(
        gate,
        out_shape=jax.ShapeDtypeStruct(other.shape, other.dtype),
        in_specs=[pl.BlockSpec(memory_space=pl.ANY)] * 2,
        out_specs=pl.BlockSpec(memory_space=pl.ANY),
        input_output_aliases={0: 0},
    )(other, region_parts)
    tile_chunks, slide_sums = folded(mine, other, 63, 8, 1)
    tile_parts = exchange(tile_chunks, PLANES)
    ins = (tile_parts, region_sums, slide_sums)
    (last,) = call(
        merge,
        3 * US,
        [((8, 128, LANES), BF16)],
        like(ins)
        + [((512, LANES), F32), ((80, LANES), F32), ((128, LANES), F32), ((8, 128, LANES), BF16)]
        + [semaphores(3), semaphores(8)],
        ins,
    )
    total = jnp.sum(exchange(last, COLUMNS).astype(F32), axis=0)
    tile_result = total[0:63].reshape(8064)
    region_result = total[64:118].reshape(6912)
    slide_result = total[118:128].reshape(1280)[:1155] * 0.5
    return (losses.reshape(1, SL_GRP), tile_result, region_result, slide_result)


def solution(mesh):
    placed = (P(ALL, None, None), P("grp", "dev"), P("grp", "dev"), P("grp", None), P("grp", None)) + (P(),) * 15
    return jax.shard_map(
        body,
        mesh=mesh,
        in_specs=placed,
        out_specs=(P("grp", None), P(ALL), P(ALL), P(ALL)),
        check_vma=False,
    )
```

```python
import functools
import math

import jax
import jax.numpy as jnp
from jax import lax
from jax.experimental import pallas as pl
from jax.experimental.pallas import tpu as pltpu
from jax.sharding import PartitionSpec as P

D = 384
HEADS = 6
FF = 1536
PATCHES = 4
SLOTS = 64
D_SL = 192
H_SL = 3
NBINS = 4
SL_GRP = 4
HEAD = 64
F32 = jnp.float32
BF16 = jnp.bfloat16
LANES = 128
US = 550_000_000
GELU_C = math.sqrt(2.0 / math.pi)


def mm(a, b):
    return jnp.dot(a, b, preferred_element_type=F32)


def mm_nt(a, b):
    return lax.dot_general(a, b, (((1,), (1,)), ((), ())), preferred_element_type=F32)


def mm_tn(a, b):
    return lax.dot_general(a, b, (((0,), (0,)), ((), ())), preferred_element_type=F32)


def norm_parts(x):
    average = jnp.mean(x, axis=-1, keepdims=True)
    centred = x - average
    variance = jnp.mean(centred * centred, axis=-1, keepdims=True)
    rstd = lax.rsqrt(variance + 1e-06)
    return centred * rstd, rstd


def norm_back(grad, normed, rstd):
    first = jnp.mean(grad, axis=-1, keepdims=True)
    second = jnp.mean(grad * normed, axis=-1, keepdims=True)
    return rstd * (grad - first - normed * second)


def gelu_parts(x):
    t = jnp.tanh(GELU_C * (x + 0.044715 * (x * x * x)))
    value = 0.5 * x * (1.0 + t)
    slope = 0.5 * (1.0 + t) + 0.5 * x * (1.0 - t * t) * (GELU_C * (1.0 + 3.0 * 0.044715 * (x * x)))
    return value, slope


def encode(x, allowed, w_qkv, w_out, w_up, w_down, heads, res):
    packed_ref, attend_ref, mixture_ref, mid_ref, up_ref, out_ref = res
    width = x.shape[1]
    normed, _ = norm_parts(x)
    packed_ref[...] = mm(normed.astype(BF16), w_qkv[...]).astype(BF16)
    send(packed_ref)
    for h in range(heads):
        q = packed_ref[:, h * HEAD : (h + 1) * HEAD]
        k = packed_ref[:, width + h * HEAD : width + (h + 1) * HEAD]
        v = packed_ref[:, 2 * width + h * HEAD : 2 * width + (h + 1) * HEAD]
        scores = jnp.where(allowed, mm_nt(q, k) * 0.125, -1e30)
        scores = jnp.exp(scores - jnp.max(scores, axis=-1, keepdims=True))
        weights = scores / jnp.sum(scores, axis=-1, keepdims=True)
        attend_ref[h] = weights
        mixture_ref[:, h * HEAD : (h + 1) * HEAD] = mm(weights.astype(BF16), v).astype(BF16)
    send(attend_ref)
    send(mixture_ref)
    x1 = x + mm(mixture_ref[...], w_out[...])
    mid_ref[...] = x1
    send(mid_ref)
    normed, _ = norm_parts(x1)
    up = mm(normed.astype(BF16), w_up[...])
    up_ref[...] = up
    send(up_ref)
    hidden, _ = gelu_parts(up)
    out = x1 + mm(hidden.astype(BF16), w_down[...])
    out_ref[...] = out
    send(out_ref)
    return out


def encode_back(grad, x, w_qkv, w_out, w_up, w_down, heads, res, packed_grad, put):
    packed_ref, attend_ref, mixture_ref, mid_ref, up_ref, _ = res
    width = x.shape[1]
    grad_b = grad.astype(BF16)
    hidden, slope = gelu_parts(up_ref[...])
    up_grad = (mm_nt(grad_b, w_down[...]).astype(BF16).astype(F32) * slope).astype(BF16)
    put(3, hidden.astype(BF16), grad_b)
    normed, rstd = norm_parts(mid_ref[...])
    put(2, normed.astype(BF16), up_grad)
    normed_grad = mm_nt(up_grad, w_up[...]).astype(BF16).astype(F32)
    mid_grad = grad + norm_back(normed_grad, normed, rstd)
    mid_b = mid_grad.astype(BF16)
    put(1, mixture_ref[...], mid_b)
    mix_grad = mm_nt(mid_b, w_out[...]).astype(BF16)
    for h in range(heads):
        q = packed_ref[:, h * HEAD : (h + 1) * HEAD]
        k = packed_ref[:, width + h * HEAD : width + (h + 1) * HEAD]
        v = packed_ref[:, 2 * width + h * HEAD : 2 * width + (h + 1) * HEAD]
        head_grad = mix_grad[:, h * HEAD : (h + 1) * HEAD]
        weights = attend_ref[h]
        weights_grad = mm_nt(head_grad, v).astype(BF16).astype(F32)
        v_grad = mm_tn(weights.astype(BF16), head_grad)
        inner = jnp.sum(weights_grad * weights, axis=-1, keepdims=True)
        scores_grad = (weights * (weights_grad - inner) * 0.125).astype(BF16)
        packed_grad[:, h * HEAD : (h + 1) * HEAD] = mm(scores_grad, k).astype(BF16)
        packed_grad[:, width + h * HEAD : width + (h + 1) * HEAD] = mm_tn(scores_grad, q).astype(BF16)
        packed_grad[:, 2 * width + h * HEAD : 2 * width + (h + 1) * HEAD] = v_grad.astype(BF16)
    normed, rstd = norm_parts(x)
    put(0, normed.astype(BF16), packed_grad[...])
    normed_grad = mm_nt(packed_grad[...], w_qkv[...]).astype(BF16).astype(F32)
    return mid_grad + norm_back(normed_grad, normed, rstd)


def put_rows(flat, base, a, b):
    rows, columns = a.shape[1], b.shape[1]
    chunks = columns // 128
    left = a.T
    for c in range(0, chunks, 3):
        part = mm(left, b[:, c * 128 : (c + 3) * 128]).astype(BF16).astype(F32)
        for j in range(3):
            flat[pl.ds(base + c + j, rows, stride=chunks), :] = part[:, j * 128 : (j + 1) * 128]


def same_tile():
    row = lax.broadcasted_iota(jnp.int32, (128, 128), 0)
    column = lax.broadcasted_iota(jnp.int32, (128, 128), 1)
    return lax.rem(row, 32) == lax.rem(column, 32)


class Late:
    def __init__(self, source, buffer, sem):
        self.copy = pltpu.make_async_copy(source, buffer, sem)
        self.buffer, self.here = buffer, False
        self.copy.start()

    def ref(self):
        if not self.here:
            self.copy.wait()
            self.here = True
        return self.buffer

    def __getitem__(self, index):
        return self.ref()[index]


class Early:
    def __init__(self, target, buffer, sem, part=None):
        self.copy = pltpu.make_async_copy(buffer if part is None else buffer.at[part], target, sem)
        self.buffer = buffer

    def __getitem__(self, index):
        return self.buffer[index]

    def __setitem__(self, index, value):
        self.buffer[index] = value

    def finish(self):
        self.copy.wait()


def send(ref):
    if isinstance(ref, Early):
        ref.copy.start()


def leave(pairs, sems):
    copies = [pltpu.make_async_copy(a, b, sems.at[i]) for i, (a, b) in enumerate(pairs)]
    for copy in copies:
        copy.start()
    for copy in copies:
        copy.wait()


def broadcast_out(block, out, sems):
    copies = [pltpu.make_async_copy(block, out.at[i], sems.at[i]) for i in range(16)]
    for copy in copies:
        copy.start()
    for copy in copies:
        copy.wait()


def tile_forward(where, ids, slide, *refs):
    ins, outs, bufs, obufs, block, sems, osems, bsems = cut(refs, 6, 8, 6, 7, 1, 1, 1, 1)
    late = [Late(r, b, sems[0].at[i]) for i, (r, b) in enumerate(zip(ins, bufs))]
    res = [Early(r, b, osems[0].at[i]) for i, (r, b) in enumerate(zip(outs[1:], obufs))]
    patches, patch_w, w_qkv, w_out, w_up, w_down = late
    x = mm(patches[...], patch_w[...])
    res[0][...] = x
    send(res[0])
    out = encode(x, same_tile(), w_qkv, w_out, w_up, w_down, HEADS, res[1:])
    normed, _ = norm_parts(out)
    total = (normed[0:32] + normed[32:64]) + (normed[64:96] + normed[96:128])
    total = (total * 0.25).astype(BF16)
    message = block[0]
    for c in range(3):
        message[c * 32 : (c + 1) * 32, :] = total[:, c * LANES : (c + 1) * LANES]
    row = lax.broadcasted_iota(jnp.int32, (16, LANES), 0)
    lane = lax.broadcasted_iota(jnp.int32, (16, LANES), 1)
    mine = (lane >= 32 * lax.rem(where[0], 4)) & (lane < 32 * lax.rem(where[0], 4) + 32)
    four = jnp.concatenate([ids[...].astype(F32)] * 4, axis=1)
    tail = jnp.where((row == 0) & mine, four, 0.0) + jnp.where(row == 1, slide[...].astype(F32), 0.0)
    message[96:112, :] = tail.astype(BF16)
    leave([(message, outs[0])], bsems[0])
    for r in res:
        r.finish()


def cut(refs, *sizes):
    parts, at = [], 0
    for size in sizes:
        parts.append(refs[at : at + size])
        at += size
    assert at == len(refs)
    return parts


def tails_of(tails):
    tails = tails.astype(F32)
    row = lax.broadcasted_iota(jnp.int32, tails.shape, 1)
    ids = jnp.sum(jnp.where(row == 0, tails, 0.0), axis=1)
    slides = jnp.sum(jnp.where(row == 1, tails, 0.0), axis=1)
    to = lax.broadcasted_iota(jnp.int32, (8, 32), 0)
    source = lax.broadcasted_iota(jnp.int32, (8, 32), 1)
    near = (source >= 4 * to) & (source < 4 * to + 4)
    ids = mm(jnp.where(near, 1.0, 0.0).astype(BF16), ids.astype(BF16))
    return ids, slides[:, 0:1]


def slots_of(ids, region):
    member = jnp.where(ids == region.astype(F32), 1.0, 0.0)
    row = lax.broadcasted_iota(jnp.int32, (128, 128), 0)
    column = lax.broadcasted_iota(jnp.int32, (128, 128), 1)
    within = mm(member.astype(BF16), jnp.where(row < column, 1.0, 0.0).astype(BF16))
    sums = jnp.sum(member, axis=1, keepdims=True)
    row8 = lax.broadcasted_iota(jnp.int32, (8, 8), 0)
    column8 = lax.broadcasted_iota(jnp.int32, (8, 8), 1)
    earlier = jnp.where(column8 < row8, 1.0, 0.0).astype(BF16)
    ahead = mm(earlier, jnp.broadcast_to(sums, (8, 128)).astype(BF16))
    count = jnp.sum(sums, axis=0, keepdims=True)
    return member, (within + ahead).astype(jnp.int32), count


def both_slots(ids, device):
    first = device - 4 * lax.rem(device // 4, 2)
    return first, [slots_of(ids, first + 4 * b) for b in range(2)]


def choice(slots, i):
    k = lax.broadcasted_iota(jnp.int32, (SLOTS, 128), 0)
    parts = [jnp.where((slot[i : i + 1] == k) & (member[i : i + 1] > 0.0), 1.0, 0.0) for member, slot, _ in slots]
    return jnp.concatenate(parts, axis=0).astype(BF16)


def usable_of(slots):
    k = lax.broadcasted_iota(jnp.int32, (SLOTS, 1), 0).astype(F32)
    return [k < count for _, _, count in slots]


def region_forward(where, *refs):
    ins, outs, bufs, rows, obufs, block, sems, osems, bsems, rsems = cut(refs, 5, 9, 4, 1, 7, 1, 1, 1, 1, 1)
    rows = rows[0]
    h = lax.rem(where[0] // 4, 2)
    arriving = []
    for i in range(16):
        base = i // 4 * 8 + i % 4
        for side, z in enumerate((h, 1 - h)):
            source = ins[0].at[i, 112 * side : 112 * side + 112, :]
            arriving.append(pltpu.make_async_copy(source, rows.at[base + 4 * z], rsems[0].at[2 * i + side]))
            arriving[-1].start()
    w_qkv, w_out, w_up, w_down = [Late(r, b, sems[0].at[i]) for i, (r, b) in enumerate(zip(ins[1:], bufs))]
    res = [Early(r, b, osems[0].at[i]) for i, (r, b) in enumerate(zip(outs[2:], obufs))]
    for copy in arriving:
        copy.wait()
    tails = pltpu.make_async_copy(rows.at[:, 96:112, :], outs[1], bsems[0].at[32])
    tails.start()
    ids, _ = tails_of(rows[:, 96:112, :])
    _, slots = both_slots(ids, where[0])
    parts = [jnp.zeros((2 * SLOTS, LANES), F32)] * 3
    for b in range(8):
        pick = choice(slots, b)
        for c in range(3):
            block_rows = rows[4 * b : 4 * b + 4, 32 * c : 32 * c + 32, :].reshape(128, LANES)
            parts[c] = parts[c] + mm(pick, block_rows)
    for c in range(3):
        res[0][:, c * LANES : (c + 1) * LANES] = parts[c]
    send(res[0])
    row = lax.broadcasted_iota(jnp.int32, (2 * SLOTS, 2 * SLOTS), 0)
    key = lax.broadcasted_iota(jnp.int32, (2 * SLOTS, 2 * SLOTS), 1)
    at = key.astype(F32)
    allowed = ((row < SLOTS) & (at < slots[0][2])) | ((row >= SLOTS) & (key >= SLOTS) & (at < slots[1][2] + SLOTS))
    out = encode(res[0][...], allowed, w_qkv, w_out, w_up, w_down, HEADS, res[1:])
    normed, _ = norm_parts(out)
    message = block[0]
    message[...] = jnp.zeros((8, LANES), F32)
    for b, usable in enumerate(usable_of(slots)):
        total = jnp.sum(jnp.where(usable, normed[b * SLOTS : (b + 1) * SLOTS], 0.0), axis=0, keepdims=True)
        embed = (total / slots[b][2]).astype(BF16).astype(F32)
        for c in range(3):
            message[3 * b + c : 3 * b + c + 1, :] = embed[:, c * LANES : (c + 1) * LANES]
    broadcast_out(message, outs[0], bsems[0])
    tails.wait()
    for r in res:
        r.finish()


def slide_step(embeds, slide_row, slide_col, label, censor, slide_in, w_qkv, w_out, w_up, w_down, head, losses, grads, res, packed_grad, scaling):
    emb = embeds[...]
    x = mm(emb, slide_in[...])
    out = encode(x, slide_col == slide_row, w_qkv, w_out, w_up, w_down, H_SL, res)
    normed, rstd = norm_parts(out)
    sums, sizes, masks = [], [], []
    for s in range(SL_GRP):
        mask = jnp.where(slide_col == float(s), 1.0, 0.0)
        size = jnp.sum(mask, axis=0, keepdims=True)
        masks.append(mask)
        sizes.append(size)
        sums.append(jnp.sum(mask * normed, axis=0, keepdims=True) / size)
    pooled = jnp.concatenate(sums, axis=0).astype(BF16)
    logits = mm(pooled, head[...])
    soft = jnp.log1p(jnp.exp(-jnp.abs(logits)))
    log_hazard = -(jnp.maximum(-logits, 0.0) + soft)
    log_stay = -(jnp.maximum(logits, 0.0) + soft)
    bin_at = lax.broadcasted_iota(jnp.int32, (SL_GRP, NBINS), 1)
    at = (bin_at == label[...]).astype(F32)
    before = (bin_at < label[...]).astype(F32)
    held = censor[...].astype(F32)
    past = jnp.sum(before * log_stay, axis=1, keepdims=True)
    seen = past + jnp.sum(at * log_hazard, axis=1, keepdims=True)
    lived = past + jnp.sum(at * log_stay, axis=1, keepdims=True)
    losses[...] = -(1.0 - held) * seen - held * lived
    chance = 1.0 / (1.0 + jnp.exp(-logits))
    logit_grad = (scaling * (before * chance + at * (chance - (1.0 - held)))).astype(BF16)
    grads[5][...] = mm_tn(pooled, logit_grad).astype(BF16)
    pooled_grad = mm_nt(logit_grad, head[...]).astype(BF16).astype(F32)
    grad = jnp.zeros_like(normed)
    for s in range(SL_GRP):
        grad = grad + masks[s] * (pooled_grad[s : s + 1] / sizes[s])
    grad = norm_back(grad, normed, rstd)

    def put(i, a, b):
        grads[i + 1][...] = mm_tn(a, b).astype(BF16)

    grad = encode_back(grad, x, w_qkv, w_out, w_up, w_down, H_SL, res, packed_grad, put).astype(BF16)
    grads[0][...] = mm_tn(emb, grad).astype(BF16)
    return mm_nt(grad, slide_in[...]).astype(BF16)


def region_backward(scaling, where, label, censor, *refs):
    ins, outs, bufs, obufs, extra, sems, osems = cut(refs, 19, 16, 19, 16, 10, 1, 1)
    h = lax.rem(where[0] // 4, 2)
    order = list(range(8)) + [18, 13, 17, 16, 14, 15, 9, 8, 10, 11, 12]
    late = dict()
    for i in list(dict.fromkeys(order)):
        late[i] = Late(ins[i], bufs[i], sems[0].at[i])
    early = []
    for i, (r, b) in enumerate(zip(outs, obufs)):
        part = pl.ds(pl.multiple_of(h * SLOTS, SLOTS), SLOTS) if 2 <= i < 10 else None
        if i != 1:
            early.append(Early(r, b, osems[0].at[i], part))
        else:
            early.append(b)
    message, tails = late[0], late[1]
    slide_weights = [late[i] for i in range(2, 8)]
    w_qkv, w_out, w_up, w_down = [late[i] for i in range(8, 12)]
    x_ref, res = late[12], [late[i] for i in range(13, 19)]
    losses, spread, pairs, slide_grads = early[0], early[1], early[2:10], early[10:16]
    packed_grad, slide_packed_grad, embeds, placed = extra[:4]
    ids, slide_col = tails_of(tails[...])
    rows32 = lax.broadcasted_iota(jnp.int32, (32, 32), 0)
    columns32 = lax.broadcasted_iota(jnp.int32, (32, 32), 1)
    slide_row = jnp.sum(jnp.where(rows32 == columns32, slide_col, 0.0), axis=0, keepdims=True)
    arrived = message[...]
    at = lax.broadcasted_iota(jnp.int32, arrived.shape, 1)
    for b in range(2):
        for c in range(3):
            part = jnp.sum(jnp.where(at == 3 * b + c, arrived, 0.0), axis=1)
            for y in range(4):
                placed[8 * y + 4 * b : 8 * y + 4 * b + 4, c * LANES : (c + 1) * LANES] = part[4 * y : 4 * y + 4]
    embeds[...] = placed[...].astype(BF16)
    cots = slide_step(
        embeds, slide_row, slide_col, label, censor, *slide_weights, losses, slide_grads, extra[4:10], slide_packed_grad, scaling
    ).astype(F32)
    for g in [losses] + slide_grads:
        send(g)
    first, slots = both_slots(ids, where[0])
    grads = []
    for b, usable in enumerate(usable_of(slots)):
        mine = lax.broadcasted_iota(jnp.int32, (32, 1), 0) == first + 4 * b
        own = jnp.sum(jnp.where(mine, cots, 0.0), axis=0, keepdims=True)
        grads.append(jnp.where(usable, own / slots[b][2], 0.0))
    grad = jnp.concatenate(grads, axis=0)
    normed, rstd = norm_parts(res[5][...])
    grad = norm_back(grad, normed, rstd)

    def put(i, a, b):
        for at, value in ((6 - 2 * i, a), (7 - 2 * i, b)):
            pairs[at][...] = value
            send(pairs[at])

    grad = encode_back(grad, x_ref[...], w_qkv, w_out, w_up, w_down, HEADS, res, packed_grad, put).astype(BF16)
    for b in range(8):
        spread[b] = mm_tn(choice(slots, b), grad).astype(BF16)
    leave([(spread.at[2 * y + h], outs[1].at[y]) for y in range(4)], sems[0])
    for e in early:
        if e is not spread:
            e.finish()


def two_halves(flat, rows, core, halves, stage, sems, extra=None):
    run = 32 * rows
    copies = []
    for side in range(2):
        which = core if side == 0 else 1 - core
        for z in range(4):
            start = pl.multiple_of((2 * z + which) * run, 32)
            stage[side, z * run : (z + 1) * run, :] = flat[pl.ds(start, run), :].astype(BF16)
            part = pl.ds(z * run, run)
            copies.append(pltpu.make_async_copy(stage.at[side, part, :], halves[side].at[part, :], sems.at[side, z]))
            copies[-1].start()
        if extra is not None:
            stage[side, 4 * run : 4 * run + 80, :] = extra.ref()[which]
            part = pl.ds(4 * run, 80)
            copies.append(pltpu.make_async_copy(stage.at[side, part, :], halves[side].at[part, :], sems.at[side, 4]))
            copies[-1].start()
    for copy in copies:
        copy.wait()


def region_weights(core, *refs):
    ins, halves, bufs, flat, stage, sems, osems = cut(refs, 8, 2, 8, 1, 1, 1, 1)
    late = [Late(r, b, sems[0].at[i]) for i, (r, b) in enumerate(zip(ins, bufs))]
    hidden, grad, second, up_grad, mixture, mid_grad, first, packed_grad = late
    put_rows(flat[0], 9216, hidden[...], grad[...])
    put_rows(flat[0], 4608, second[...], up_grad[...])
    put_rows(flat[0], 3456, mixture[...], mid_grad[...])
    put_rows(flat[0], 0, first[...], packed_grad[...])
    two_halves(flat[0], 54, core[0], halves, stage[0], osems[0])


def tile_backward(core, ids, *refs):
    ins, _, halves, bufs, packed_grad, flat, stage, sems, osems = cut(refs, 14, 1, 2, 14, 1, 1, 1, 1, 1)
    late = [Late(ins[i], bufs[i], sems[0].at[i]) for i in (0, 13, 6, 12, 11, 5, 10, 4, 9, 8, 3, 7, 1, 2)]
    late = dict(zip((0, 13, 6, 12, 11, 5, 10, 4, 9, 8, 3, 7, 1, 2), late))
    arrived, patches, slide_rows = late[0], late[1], late[2]
    w_qkv, w_out, w_up, w_down = [late[i] for i in range(3, 7)]
    x_ref, res = late[7], [late[i] for i in range(8, 14)]
    rows32 = lax.broadcasted_iota(jnp.int32, (32, 32), 0)
    columns32 = lax.broadcasted_iota(jnp.int32, (32, 32), 1)
    assign = jnp.sum(jnp.where(rows32 == columns32, ids[...].astype(F32), 0.0), axis=1, keepdims=True)
    cot = jnp.zeros((32, D), F32)
    for i in range(16):
        region = float(i // 4 * 8 + i % 4)
        cot = cot + jnp.where((assign == region) | (assign == region + 4.0), arrived[i].astype(F32), 0.0)
    cot = cot * 0.25
    grad = jnp.concatenate([cot] * PATCHES, axis=0)
    normed, rstd = norm_parts(res[5][...])
    grad = norm_back(grad, normed, rstd)
    bases = (2304, 5760, 6912, 11520)

    def put(i, a, b):
        put_rows(flat[0], bases[i], a, b)

    grad = encode_back(grad, x_ref[...], w_qkv, w_out, w_up, w_down, HEADS, res, packed_grad[0], put)
    put_rows(flat[0], 0, patches[...], grad.astype(BF16))
    two_halves(flat[0], 63, core[0], halves, stage[0], osems[0], slide_rows)


def fold(rows, pad, tail, *refs):
    mine, got = refs[:2]
    refs = refs[2 + tail :]
    if tail:
        out, extra = refs[:2]
        refs = refs[2:]
    else:
        out = refs[0]
        refs = refs[1:]
    a, b, total, stage, chunks, sems, osems = refs[:7]
    run = 32 * rows
    arriving = []
    for z in range(4 + tail):
        part = pl.ds(z * run, run if z < 4 else 80)
        for side, (source, buffer) in enumerate(((mine, a), (got, b))):
            arriving.append(pltpu.make_async_copy(source.at[part, :], buffer.at[part, :], sems.at[side, z]))
            arriving[-1].start()
    for z in range(4):
        arriving[2 * z].wait()
        arriving[2 * z + 1].wait()
        part = pl.ds(z * run, run)
        total[part, :] = a[part, :].astype(F32) + b[part, :].astype(F32)
    leaving = []
    if tail:
        arriving[8].wait()
        arriving[9].wait()
        part = pl.ds(4 * run, 80)
        refs[7][...] = (a[part, :].astype(F32) + b[part, :].astype(F32)).astype(BF16)
        leaving.append(pltpu.make_async_copy(refs[7], extra, osems.at[16]))
        leaving[-1].start()
    if pad:
        stage[8 * rows :, :] = jnp.zeros((pad, LANES), F32)
    for y in range(4):
        for x in range(4):
            for z in range(4):
                for h in range(2):
                    source = (z * 32 + y * 8 + h * 4 + x) * rows
                    target = (z * 2 + h) * rows
                    stage[target : target + rows, :] = total[source : source + rows, :]
            chunks[y * 4 + x] = stage[...].astype(BF16)
            leaving.append(pltpu.make_async_copy(chunks.at[y * 4 + x], out.at[y * 4 + x], osems.at[y * 4 + x]))
            leaving[-1].start()
    for copy in leaving:
        copy.wait()


def plane_sum(parts, out, buffer, total, sems):
    copies = [pltpu.make_async_copy(parts.at[:, i * 144 : (i + 1) * 144, :], buffer.at[:, i * 144 : (i + 1) * 144, :], sems.at[i]) for i in range(3)]
    for copy in copies:
        copy.start()
    for i in range(3):
        copies[i].wait()
        for start in range(i * 144, (i + 1) * 144, 48):
            value = buffer[0, start : start + 48, :].astype(F32)
            for j in range(1, 16):
                value = value + buffer[j, start : start + 48, :].astype(F32)
            total[start : start + 48, :] = value
    leave([(total, out)], sems)


def merge(tile_in, region_in, slide_in, out, tile_buf, region_buf, slide_buf, total, slide_total, stage, chunks, sems, osems):
    tile_late = Late(tile_in, tile_buf, sems.at[0])
    region_late = Late(region_in, region_buf, sems.at[1])
    slide_late = Late(slide_in, slide_buf, sems.at[2])
    slide_total[...] = slide_late[...].astype(F32)

    for start in range(0, 512, 64):
        value = tile_late[0, start : start + 64, :].astype(F32)
        for i in range(1, 16):
            value = value + tile_late[i, start : start + 64, :].astype(F32)
        total[start : start + 64, :] = value
    region_total = region_late.ref()
    leaving = []
    for i in range(8):
        stage[0:63, :] = total[i * 63 : (i + 1) * 63, :]
        stage[63:64, :] = jnp.zeros((1, LANES), F32)
        stage[64:118, :] = region_total[i * 54 : (i + 1) * 54, :]
        stage[118:128, :] = slide_total[i * 10 : (i + 1) * 10, :]
        chunks[i] = stage[...].astype(BF16)
        leaving.append(pltpu.make_async_copy(chunks.at[i], out.at[i], osems.at[i]))
        leaving[-1].start()
    for copy in leaving:
        copy.wait()


def call(kernel, macs, outs, scratch, inputs, scalars=0, whole=0):
    specs = [pl.BlockSpec(memory_space=pltpu.SMEM)] * scalars
    specs += [pl.BlockSpec(memory_space=pltpu.VMEM)] * whole
    specs += [pl.BlockSpec(memory_space=pl.ANY)] * (len(inputs) - scalars - whole)
    moved = sum(math.prod(a.shape) * a.dtype.itemsize for a in inputs) + sum(math.prod(a) * jnp.dtype(k).itemsize for a, k in outs)
    cost = pl.CostEstimate(flops=2 * macs, bytes_accessed=moved, transcendentals=0)
    return pl.pallas_call(
        kernel,
        out_shape=[jax.ShapeDtypeStruct(shape, kind) for shape, kind in outs],
        in_specs=specs,
        out_specs=[pl.BlockSpec(memory_space=pl.ANY)] * len(outs),
        scratch_shapes=[pltpu.VMEM(*item) if isinstance(item, tuple) else item for item in scratch],
        compiler_params=pltpu.CompilerParams(vmem_limit_bytes=60 * 1024 * 1024),
        cost_estimate=cost,
    )(*inputs)


def like(arrays):
    return [(a.shape, a.dtype) for a in arrays]


def semaphores(*shape):
    return pltpu.SemaphoreType.DMA(shape)


def residuals(tokens, width, hidden, heads):
    return [
        ((tokens, 3 * width), BF16),
        ((heads, tokens, tokens), F32),
        ((tokens, width), BF16),
        ((tokens, width), F32),
        ((tokens, hidden), F32),
        ((tokens, width), F32),
    ]


def index_of(z, core, y, z_hi, x):
    return (z * 2 + core) * 32 + y * 8 + z_hi * 4 + x


PLANES = [[index_of(z, c, y, h, x) for y in range(4) for x in range(4)] for z in range(4) for c in range(2) for h in range(2)]
COLUMNS = [[index_of(z, c, y, h, x) for z in range(4) for h in range(2)] for c in range(2) for y in range(4) for x in range(4)]
OTHER_CORE = [(g, g + 1 - 2 * (g % 2)) for g in range(8)]
OTHER_PLANE = [(d, d + 4 - 8 * (d // 4 % 2)) for d in range(32)]
ALL = ("grp", "dev")


def exchange(array, groups):
    return lax.all_to_all(array, ALL, 0, 0, axis_index_groups=groups)


def folded(mine, other, rows, pad, tail, after=()):
    got = lax.ppermute(other, "grp", OTHER_CORE)
    height = 128 * rows + 80 * tail
    chunk = 8 * rows + pad
    return call(
        functools.partial(fold, rows, pad, tail),
        4 * US,
        [((16, chunk, LANES), BF16)] + [((80, LANES), BF16)] * tail,
        [((height, LANES), BF16)] * 2
        + [((128 * rows, LANES), F32), ((chunk, LANES), F32), ((16, chunk, LANES), BF16)]
        + [semaphores(2, 5), semaphores(17)]
        + [((80, LANES), BF16)] * tail,
        (mine, got) + after,
    )


def body(
    patches,
    tile_region,
    region_slide,
    bin_label,
    censored,
    patch_w,
    tile_qkv,
    tile_out,
    tile_up,
    tile_down,
    region_qkv,
    region_out,
    region_up,
    region_down,
    slide_in,
    slide_qkv,
    slide_out,
    slide_up,
    slide_down,
    slide_head,
):
    member_index = lax.axis_index("dev").astype(jnp.int32)
    where = member_index.reshape(1)
    core = lax.rem(lax.axis_index("grp").astype(jnp.int32), 2).reshape(1)
    scaling = 1.0 / (bin_label.shape[1] * lax.axis_size("grp"))
    tokens = patches.transpose(1, 0, 2).reshape(128, 768)
    tile_res = [((128, D), F32)] + residuals(128, D, FF, HEADS)
    ins = (tokens, patch_w, tile_qkv, tile_out, tile_up, tile_down)
    message, *tile_kept = call(
        tile_forward,
        7 * US,
        [((112, LANES), BF16)] + tile_res,
        like(ins) + tile_res + [((112, LANES), BF16), semaphores(6), semaphores(7), semaphores(1)],
        (where, tile_region, region_slide) + ins,
        scalars=1,
        whole=2,
    )
    both = jnp.concatenate([message, lax.ppermute(message, "dev", OTHER_PLANE)], axis=0)
    rows = exchange(jnp.broadcast_to(both[None], (16, 224, LANES)), PLANES)
    region_res = [((2 * SLOTS, D), F32)] + residuals(2 * SLOTS, D, FF, HEADS)
    ins = (region_qkv, region_out, region_up, region_down)
    message, tails, *region_kept = call(
        region_forward,
        6 * US,
        [((16, 8, LANES), F32), ((32, 16, LANES), BF16)] + region_res,
        like(ins)
        + [((32, 112, LANES), BF16)]
        + region_res
        + [((8, LANES), F32), semaphores(4), semaphores(7), semaphores(33), semaphores(32)],
        (where, rows) + ins,
        scalars=1,
    )
    all_regions = exchange(message, PLANES)
    slide_weights = (slide_in, slide_qkv, slide_out, slide_up, slide_down, slide_head)
    widths = (FF, D, D, FF, D, D, D, 3 * D)
    pairs = [((SLOTS, n), BF16) for n in widths]
    losses_out = [((SL_GRP, 1), F32)]
    outs = losses_out + [((4, 128, D), BF16)] + pairs + like(slide_weights)
    buffers = losses_out + [((8, 128, D), BF16)] + [((2 * SLOTS, n), BF16) for n in widths] + like(slide_weights)
    ins = (all_regions, tails) + slide_weights + (region_qkv, region_out, region_up, region_down) + tuple(region_kept)
    losses, spread, *rest = call(
        functools.partial(region_backward, scaling),
        12 * US,
        outs,
        like(ins)
        + buffers
        + [((2 * SLOTS, 3 * D), BF16), ((32, 3 * D_SL), BF16), ((32, D), BF16), ((32, D), F32)]
        + residuals(32, D_SL, D_SL, H_SL)
        + [semaphores(19), semaphores(16)],
        (where, bin_label.reshape(SL_GRP, 1), censored.reshape(SL_GRP, 1)) + ins,
        scalars=1,
        whole=2,
    )
    arrived = exchange(spread.reshape(16, 32, D), PLANES)
    ins = tuple(rest[:8])
    mine, other = call(
        region_weights,
        5 * US,
        [((6912, LANES), BF16)] * 2,
        like(ins) + [((13824, LANES), F32), ((2, 6912, LANES), BF16), semaphores(8), semaphores(2, 5)],
        (core,) + ins,
        scalars=1,
    )
    (region_chunks,) = folded(mine, other, 54, 0, 0)
    region_parts = exchange(region_chunks, PLANES)
    (region_sums,) = call(
        plane_sum,
        20 * US,
        [((432, LANES), F32)],
        like((region_parts,)) + [((432, LANES), F32), semaphores(3)],
        (region_parts,),
    )
    slide_flat = jnp.concatenate([g.astype(F32).reshape(-1) for g in rest[8:]]).reshape(4, 2, 4, 2, 4, 1155)
    y, x = member_index // 8, lax.rem(member_index, 4)
    zero = jnp.zeros((), jnp.int32)
    slide_rows = lax.dynamic_slice(slide_flat, (zero, zero, y, zero, x, zero), (4, 2, 1, 2, 1, 1155))
    slide_rows = slide_rows.reshape(4, 2, 2, 1155).transpose(1, 0, 2, 3)
    slide_rows = jnp.pad(slide_rows, ((0, 0), (0, 0), (0, 0), (0, 125))).astype(BF16).reshape(2, 80, LANES)
    ins = (arrived, tokens, slide_rows, tile_qkv, tile_out, tile_up, tile_down) + tuple(tile_kept)
    mine, other = call(
        tile_backward,
        13 * US,
        [((8144, LANES), BF16)] * 2,
        like(ins)
        + [((128, 3 * D), BF16), ((16128, LANES), F32), ((2, 8144, LANES), BF16), semaphores(14), semaphores(2, 5)],
        (core, tile_region) + ins + (region_chunks,),
        scalars=1,
        whole=1,
    )
    tile_chunks, slide_sums = folded(mine, other, 63, 8, 1, (region_sums,))
    tile_parts = exchange(tile_chunks, PLANES)
    ins = (tile_parts, region_sums, slide_sums)
    (last,) = call(
        merge,
        3 * US,
        [((8, 128, LANES), BF16)],
        like(ins)
        + [((512, LANES), F32), ((80, LANES), F32), ((128, LANES), F32), ((8, 128, LANES), BF16)]
        + [semaphores(3), semaphores(8)],
        ins,
    )
    total = jnp.sum(exchange(last, COLUMNS).astype(F32), axis=0)
    tile_result = total[0:63].reshape(8064)
    region_result = total[64:118].reshape(6912)
    slide_result = total[118:128].reshape(1280)[:1155] * 0.5
    return (losses.reshape(1, SL_GRP), tile_result, region_result, slide_result)


def solution(mesh):
    placed = (P(ALL, None, None), P("grp", "dev"), P("grp", "dev"), P("grp", None), P("grp", None)) + (P(),) * 15
    return jax.shard_map(
        body,
        mesh=mesh,
        in_specs=placed,
        out_specs=(P("grp", None), P(ALL), P(ALL), P(ALL)),
        check_vma=False,
    )
```

```python
import functools
import math

import jax
import jax.numpy as jnp
from jax import lax
from jax.experimental import pallas as pl
from jax.experimental.pallas import tpu as pltpu
from jax.sharding import PartitionSpec as P

D = 384
HEADS = 6
FF = 1536
PATCHES = 4
SLOTS = 64
D_SL = 192
H_SL = 3
NBINS = 4
SL_GRP = 4
HEAD = 64
F32 = jnp.float32
BF16 = jnp.bfloat16
LANES = 128
US = 550_000_000
GELU_C = math.sqrt(2.0 / math.pi)


def mm(a, b):
    return jnp.dot(a, b, preferred_element_type=F32)


def mm_nt(a, b):
    return lax.dot_general(a, b, (((1,), (1,)), ((), ())), preferred_element_type=F32)


def mm_tn(a, b):
    return lax.dot_general(a, b, (((0,), (0,)), ((), ())), preferred_element_type=F32)


def norm_parts(x):
    average = jnp.mean(x, axis=-1, keepdims=True)
    centred = x - average
    variance = jnp.mean(centred * centred, axis=-1, keepdims=True)
    rstd = lax.rsqrt(variance + 1e-06)
    return centred * rstd, rstd


def norm_back(grad, normed, rstd):
    first = jnp.mean(grad, axis=-1, keepdims=True)
    second = jnp.mean(grad * normed, axis=-1, keepdims=True)
    return rstd * (grad - first - normed * second)


def gelu_parts(x):
    t = jnp.tanh(GELU_C * (x + 0.044715 * (x * x * x)))
    value = 0.5 * x * (1.0 + t)
    slope = 0.5 * (1.0 + t) + 0.5 * x * (1.0 - t * t) * (GELU_C * (1.0 + 3.0 * 0.044715 * (x * x)))
    return value, slope


def encode(x, allowed, w_qkv, w_out, w_up, w_down, heads, res):
    packed_ref, attend_ref, mixture_ref, mid_ref, up_ref, out_ref = res
    width = x.shape[1]
    normed, _ = norm_parts(x)
    packed_ref[...] = mm(normed.astype(BF16), w_qkv[...]).astype(BF16)
    send(packed_ref)
    for h in range(heads):
        q = packed_ref[:, h * HEAD : (h + 1) * HEAD]
        k = packed_ref[:, width + h * HEAD : width + (h + 1) * HEAD]
        v = packed_ref[:, 2 * width + h * HEAD : 2 * width + (h + 1) * HEAD]
        scores = jnp.where(allowed, mm_nt(q, k) * 0.125, -1e30)
        scores = jnp.exp(scores - jnp.max(scores, axis=-1, keepdims=True))
        weights = scores / jnp.sum(scores, axis=-1, keepdims=True)
        attend_ref[h] = weights
        mixture_ref[:, h * HEAD : (h + 1) * HEAD] = mm(weights.astype(BF16), v).astype(BF16)
    send(attend_ref)
    send(mixture_ref)
    x1 = x + mm(mixture_ref[...], w_out[...])
    mid_ref[...] = x1
    send(mid_ref)
    normed, _ = norm_parts(x1)
    up = mm(normed.astype(BF16), w_up[...])
    up_ref[...] = up
    send(up_ref)
    hidden, _ = gelu_parts(up)
    out = x1 + mm(hidden.astype(BF16), w_down[...])
    out_ref[...] = out
    send(out_ref)
    return out


def encode_back(grad, x, w_qkv, w_out, w_up, w_down, heads, res, packed_grad, put):
    packed_ref, attend_ref, mixture_ref, mid_ref, up_ref, _ = res
    width = x.shape[1]
    grad_b = grad.astype(BF16)
    hidden, slope = gelu_parts(up_ref[...])
    up_grad = (mm_nt(grad_b, w_down[...]).astype(BF16).astype(F32) * slope).astype(BF16)
    put(3, hidden.astype(BF16), grad_b)
    normed, rstd = norm_parts(mid_ref[...])
    put(2, normed.astype(BF16), up_grad)
    normed_grad = mm_nt(up_grad, w_up[...]).astype(BF16).astype(F32)
    mid_grad = grad + norm_back(normed_grad, normed, rstd)
    mid_b = mid_grad.astype(BF16)
    put(1, mixture_ref[...], mid_b)
    mix_grad = mm_nt(mid_b, w_out[...]).astype(BF16)
    for h in range(heads):
        q = packed_ref[:, h * HEAD : (h + 1) * HEAD]
        k = packed_ref[:, width + h * HEAD : width + (h + 1) * HEAD]
        v = packed_ref[:, 2 * width + h * HEAD : 2 * width + (h + 1) * HEAD]
        head_grad = mix_grad[:, h * HEAD : (h + 1) * HEAD]
        weights = attend_ref[h]
        weights_grad = mm_nt(head_grad, v).astype(BF16).astype(F32)
        v_grad = mm_tn(weights.astype(BF16), head_grad)
        inner = jnp.sum(weights_grad * weights, axis=-1, keepdims=True)
        scores_grad = (weights * (weights_grad - inner) * 0.125).astype(BF16)
        packed_grad[:, h * HEAD : (h + 1) * HEAD] = mm(scores_grad, k).astype(BF16)
        packed_grad[:, width + h * HEAD : width + (h + 1) * HEAD] = mm_tn(scores_grad, q).astype(BF16)
        packed_grad[:, 2 * width + h * HEAD : 2 * width + (h + 1) * HEAD] = v_grad.astype(BF16)
    normed, rstd = norm_parts(x)
    put(0, normed.astype(BF16), packed_grad[...])
    normed_grad = mm_nt(packed_grad[...], w_qkv[...]).astype(BF16).astype(F32)
    return mid_grad + norm_back(normed_grad, normed, rstd)


def put_rows(flat, base, a, b):
    rows, columns = a.shape[1], b.shape[1]
    chunks = columns // 128
    left = a.T
    for c in range(0, chunks, 3):
        part = mm(left, b[:, c * 128 : (c + 3) * 128]).astype(BF16).astype(F32)
        for j in range(3):
            flat[pl.ds(base + c + j, rows, stride=chunks), :] = part[:, j * 128 : (j + 1) * 128]


def same_tile():
    row = lax.broadcasted_iota(jnp.int32, (128, 128), 0)
    column = lax.broadcasted_iota(jnp.int32, (128, 128), 1)
    return lax.rem(row, 32) == lax.rem(column, 32)


class Late:
    def __init__(self, source, buffer, sem):
        self.copy = pltpu.make_async_copy(source, buffer, sem)
        self.buffer, self.here = buffer, False
        self.copy.start()

    def ref(self):
        if not self.here:
            self.copy.wait()
            self.here = True
        return self.buffer

    def __getitem__(self, index):
        return self.ref()[index]


class Early:
    def __init__(self, target, buffer, sem):
        self.copy = pltpu.make_async_copy(buffer, target, sem)
        self.buffer = buffer

    def __getitem__(self, index):
        return self.buffer[index]

    def __setitem__(self, index, value):
        self.buffer[index] = value

    def finish(self):
        self.copy.wait()


def send(ref):
    if isinstance(ref, Early):
        ref.copy.start()


def leave(pairs, sems):
    copies = [pltpu.make_async_copy(a, b, sems.at[i]) for i, (a, b) in enumerate(pairs)]
    for copy in copies:
        copy.start()
    for copy in copies:
        copy.wait()


def broadcast_out(block, out, sems):
    copies = [pltpu.make_async_copy(block, out.at[i], sems.at[i]) for i in range(16)]
    for copy in copies:
        copy.start()
    for copy in copies:
        copy.wait()


def tile_forward(where, ids, slide, *refs):
    ins, outs, bufs, obufs, block, sems, osems, bsems = cut(refs, 6, 8, 6, 7, 1, 1, 1, 1)
    late = [Late(r, b, sems[0].at[i]) for i, (r, b) in enumerate(zip(ins, bufs))]
    res = [Early(r, b, osems[0].at[i]) for i, (r, b) in enumerate(zip(outs[1:], obufs))]
    patches, patch_w, w_qkv, w_out, w_up, w_down = late
    x = mm(patches[...], patch_w[...])
    res[0][...] = x
    send(res[0])
    out = encode(x, same_tile(), w_qkv, w_out, w_up, w_down, HEADS, res[1:])
    normed, _ = norm_parts(out)
    total = (normed[0:32] + normed[32:64]) + (normed[64:96] + normed[96:128])
    total = (total * 0.25).astype(BF16)
    message = block[0]
    for c in range(3):
        message[c * 32 : (c + 1) * 32, :] = total[:, c * LANES : (c + 1) * LANES]
    row = lax.broadcasted_iota(jnp.int32, (16, LANES), 0)
    lane = lax.broadcasted_iota(jnp.int32, (16, LANES), 1)
    mine = (lane >= 32 * lax.rem(where[0], 4)) & (lane < 32 * lax.rem(where[0], 4) + 32)
    four = jnp.concatenate([ids[...].astype(F32)] * 4, axis=1)
    tail = jnp.where((row == 0) & mine, four, 0.0) + jnp.where(row == 1, slide[...].astype(F32), 0.0)
    message[96:112, :] = tail.astype(BF16)
    leave([(message, outs[0])], bsems[0])
    for r in res:
        r.finish()


def cut(refs, *sizes):
    parts, at = [], 0
    for size in sizes:
        parts.append(refs[at : at + size])
        at += size
    assert at == len(refs)
    return parts


def tails_of(tails):
    tails = tails.astype(F32)
    row = lax.broadcasted_iota(jnp.int32, tails.shape, 1)
    ids = jnp.sum(jnp.where(row == 0, tails, 0.0), axis=1)
    slides = jnp.sum(jnp.where(row == 1, tails, 0.0), axis=1)
    to = lax.broadcasted_iota(jnp.int32, (8, 32), 0)
    source = lax.broadcasted_iota(jnp.int32, (8, 32), 1)
    near = (source >= 4 * to) & (source < 4 * to + 4)
    ids = mm(jnp.where(near, 1.0, 0.0).astype(BF16), ids.astype(BF16))
    return ids, slides[:, 0:1]


def slots_of(ids, region):
    member = jnp.where(ids == region.astype(F32), 1.0, 0.0)
    row = lax.broadcasted_iota(jnp.int32, (128, 128), 0)
    column = lax.broadcasted_iota(jnp.int32, (128, 128), 1)
    within = mm(member.astype(BF16), jnp.where(row < column, 1.0, 0.0).astype(BF16))
    sums = jnp.sum(member, axis=1, keepdims=True)
    row8 = lax.broadcasted_iota(jnp.int32, (8, 8), 0)
    column8 = lax.broadcasted_iota(jnp.int32, (8, 8), 1)
    earlier = jnp.where(column8 < row8, 1.0, 0.0).astype(BF16)
    ahead = mm(earlier, jnp.broadcast_to(sums, (8, 128)).astype(BF16))
    count = jnp.sum(sums, axis=0, keepdims=True)
    return member, (within + ahead).astype(jnp.int32), count


def both_slots(ids, device):
    first = device - 4 * lax.rem(device // 4, 2)
    return first, [slots_of(ids, first + 4 * b) for b in range(2)]


def choice(slots, i):
    k = lax.broadcasted_iota(jnp.int32, (SLOTS, 128), 0)
    parts = [jnp.where((slot[i : i + 1] == k) & (member[i : i + 1] > 0.0), 1.0, 0.0) for member, slot, _ in slots]
    return jnp.concatenate(parts, axis=0).astype(BF16)


def usable_of(slots):
    k = lax.broadcasted_iota(jnp.int32, (SLOTS, 1), 0).astype(F32)
    return [k < count for _, _, count in slots]


def region_forward(where, *refs):
    ins, outs, bufs, rows, obufs, block, sems, osems, bsems, rsems = cut(refs, 5, 9, 4, 1, 7, 1, 1, 1, 1, 1)
    rows = rows[0]
    h = lax.rem(where[0] // 4, 2)
    arriving = []
    for i in range(16):
        base = i // 4 * 8 + i % 4
        for side, z in enumerate((h, 1 - h)):
            source = ins[0].at[i, 112 * side : 112 * side + 112, :]
            arriving.append(pltpu.make_async_copy(source, rows.at[base + 4 * z], rsems[0].at[2 * i + side]))
            arriving[-1].start()
    w_qkv, w_out, w_up, w_down = [Late(r, b, sems[0].at[i]) for i, (r, b) in enumerate(zip(ins[1:], bufs))]
    res = [Early(r, b, osems[0].at[i]) for i, (r, b) in enumerate(zip(outs[2:], obufs))]
    for copy in arriving:
        copy.wait()
    tails = pltpu.make_async_copy(rows.at[:, 96:112, :], outs[1], bsems[0].at[32])
    tails.start()
    ids, _ = tails_of(rows[:, 96:112, :])
    _, slots = both_slots(ids, where[0])
    parts = [jnp.zeros((2 * SLOTS, LANES), F32)] * 3
    for b in range(8):
        pick = choice(slots, b)
        for c in range(3):
            block_rows = rows[4 * b : 4 * b + 4, 32 * c : 32 * c + 32, :].reshape(128, LANES)
            parts[c] = parts[c] + mm(pick, block_rows)
    for c in range(3):
        res[0][:, c * LANES : (c + 1) * LANES] = parts[c]
    send(res[0])
    row = lax.broadcasted_iota(jnp.int32, (2 * SLOTS, 2 * SLOTS), 0)
    key = lax.broadcasted_iota(jnp.int32, (2 * SLOTS, 2 * SLOTS), 1)
    at = key.astype(F32)
    allowed = ((row < SLOTS) & (at < slots[0][2])) | ((row >= SLOTS) & (key >= SLOTS) & (at < slots[1][2] + SLOTS))
    out = encode(res[0][...], allowed, w_qkv, w_out, w_up, w_down, HEADS, res[1:])
    normed, _ = norm_parts(out)
    message = block[0]
    message[...] = jnp.zeros((8, LANES), F32)
    for b, usable in enumerate(usable_of(slots)):
        total = jnp.sum(jnp.where(usable, normed[b * SLOTS : (b + 1) * SLOTS], 0.0), axis=0, keepdims=True)
        embed = (total / slots[b][2]).astype(BF16).astype(F32)
        for c in range(3):
            message[3 * b + c : 3 * b + c + 1, :] = embed[:, c * LANES : (c + 1) * LANES]
    broadcast_out(message, outs[0], bsems[0])
    tails.wait()
    for r in res:
        r.finish()


def slide_step(embeds, slide_row, slide_col, label, censor, slide_in, w_qkv, w_out, w_up, w_down, head, losses, grads, res, packed_grad, scaling):
    emb = embeds[...]
    x = mm(emb, slide_in[...])
    out = encode(x, slide_col == slide_row, w_qkv, w_out, w_up, w_down, H_SL, res)
    normed, rstd = norm_parts(out)
    sums, sizes, masks = [], [], []
    for s in range(SL_GRP):
        mask = jnp.where(slide_col == float(s), 1.0, 0.0)
        size = jnp.sum(mask, axis=0, keepdims=True)
        masks.append(mask)
        sizes.append(size)
        sums.append(jnp.sum(mask * normed, axis=0, keepdims=True) / size)
    pooled = jnp.concatenate(sums, axis=0).astype(BF16)
    logits = mm(pooled, head[...])
    soft = jnp.log1p(jnp.exp(-jnp.abs(logits)))
    log_hazard = -(jnp.maximum(-logits, 0.0) + soft)
    log_stay = -(jnp.maximum(logits, 0.0) + soft)
    bin_at = lax.broadcasted_iota(jnp.int32, (SL_GRP, NBINS), 1)
    at = (bin_at == label[...]).astype(F32)
    before = (bin_at < label[...]).astype(F32)
    held = censor[...].astype(F32)
    past = jnp.sum(before * log_stay, axis=1, keepdims=True)
    seen = past + jnp.sum(at * log_hazard, axis=1, keepdims=True)
    lived = past + jnp.sum(at * log_stay, axis=1, keepdims=True)
    losses[...] = -(1.0 - held) * seen - held * lived
    chance = 1.0 / (1.0 + jnp.exp(-logits))
    logit_grad = (scaling * (before * chance + at * (chance - (1.0 - held)))).astype(BF16)
    grads[5][...] = mm_tn(pooled, logit_grad).astype(BF16)
    pooled_grad = mm_nt(logit_grad, head[...]).astype(BF16).astype(F32)
    grad = jnp.zeros_like(normed)
    for s in range(SL_GRP):
        grad = grad + masks[s] * (pooled_grad[s : s + 1] / sizes[s])
    grad = norm_back(grad, normed, rstd)

    def put(i, a, b):
        grads[i + 1][...] = mm_tn(a, b).astype(BF16)

    grad = encode_back(grad, x, w_qkv, w_out, w_up, w_down, H_SL, res, packed_grad, put).astype(BF16)
    grads[0][...] = mm_tn(emb, grad).astype(BF16)
    return mm_nt(grad, slide_in[...]).astype(BF16)


def region_backward(scaling, where, label, censor, *refs):
    ins, outs, bufs, obufs, extra, sems, osems = cut(refs, 19, 16, 19, 16, 10, 1, 1)
    h = lax.rem(where[0] // 4, 2)
    order = list(range(8)) + [18, 13, 17, 16, 14, 15, 9, 8, 10, 11, 12]
    late = dict()
    for i in list(dict.fromkeys(order)):
        late[i] = Late(ins[i], bufs[i], sems[0].at[i])
    early = []
    for i, (r, b) in enumerate(zip(outs, obufs)):
        early.append(Early(r, b, osems[0].at[i]) if i != 1 else b)
    message, tails = late[0], late[1]
    slide_weights = [late[i] for i in range(2, 8)]
    w_qkv, w_out, w_up, w_down = [late[i] for i in range(8, 12)]
    x_ref, res = late[12], [late[i] for i in range(13, 19)]
    losses, spread, pairs, slide_grads = early[0], early[1], early[2:10], early[10:16]
    packed_grad, slide_packed_grad, embeds, placed = extra[:4]
    ids, slide_col = tails_of(tails[...])
    rows32 = lax.broadcasted_iota(jnp.int32, (32, 32), 0)
    columns32 = lax.broadcasted_iota(jnp.int32, (32, 32), 1)
    slide_row = jnp.sum(jnp.where(rows32 == columns32, slide_col, 0.0), axis=0, keepdims=True)
    arrived = message[...]
    at = lax.broadcasted_iota(jnp.int32, arrived.shape, 1)
    for b in range(2):
        for c in range(3):
            part = jnp.sum(jnp.where(at == 3 * b + c, arrived, 0.0), axis=1)
            for y in range(4):
                placed[8 * y + 4 * b : 8 * y + 4 * b + 4, c * LANES : (c + 1) * LANES] = part[4 * y : 4 * y + 4]
    embeds[...] = placed[...].astype(BF16)
    cots = slide_step(
        embeds, slide_row, slide_col, label, censor, *slide_weights, losses, slide_grads, extra[4:10], slide_packed_grad, scaling
    ).astype(F32)
    for g in [losses] + slide_grads:
        send(g)
    first, slots = both_slots(ids, where[0])
    grads = []
    for b, usable in enumerate(usable_of(slots)):
        mine = lax.broadcasted_iota(jnp.int32, (32, 1), 0) == first + 4 * b
        own = jnp.sum(jnp.where(mine, cots, 0.0), axis=0, keepdims=True)
        grads.append(jnp.where(usable, own / slots[b][2], 0.0))
    grad = jnp.concatenate(grads, axis=0)
    normed, rstd = norm_parts(res[5][...])
    grad = norm_back(grad, normed, rstd)

    def put(i, a, b):
        for at, value in ((6 - 2 * i, a), (7 - 2 * i, b)):
            pairs[at][...] = value
            send(pairs[at])

    grad = encode_back(grad, x_ref[...], w_qkv, w_out, w_up, w_down, HEADS, res, packed_grad, put).astype(BF16)
    for b in range(8):
        spread[b] = mm_tn(choice(slots, b), grad).astype(BF16)
    leave([(spread.at[2 * y + h], outs[1].at[y]) for y in range(4)], sems[0])
    for e in early:
        if e is not spread:
            e.finish()


def two_halves(flat, runs, core, halves, stage, sems):
    run = 32 * 63
    copies = []
    for side in range(2):
        which = core if side == 0 else 1 - core
        for z in runs:
            start = pl.multiple_of((2 * z + which) * run, 32)
            stage[side, z * run : (z + 1) * run, :] = flat[pl.ds(start, run), :].astype(BF16)
            part = pl.ds(z * run, run)
            copies.append(pltpu.make_async_copy(stage.at[side, part, :], halves[side].at[part, :], sems.at[side, z]))
            copies[-1].start()
    return copies


def region_weights(core, where, *refs):
    ins, halves, bufs, flat, run_buf, stage, sems, osems = cut(refs, 8, 2, 8, 1, 1, 1, 1, 1)
    late = [Late(r, b, sems[0].at[i]) for i, (r, b) in enumerate(zip(ins, bufs))]
    hidden, grad, second, up_grad, mixture, mid_grad, first, packed_grad = late
    put_rows(flat[0], 9216, hidden[...], grad[...])
    put_rows(flat[0], 4608, second[...], up_grad[...])
    put_rows(flat[0], 3456, mixture[...], mid_grad[...])
    put_rows(flat[0], 0, first[...], packed_grad[...])
    h = lax.rem(where[0] // 4, 2)
    copies = []
    for side in range(2):
        which = core[0] if side == 0 else 1 - core[0]
        for z in range(4):
            for y in range(4):
                start = pl.multiple_of((2 * z + which) * 1728 + y * 432 + h * 216, 8)
                run_buf[0][y * 216 : (y + 1) * 216, :] = flat[0][pl.ds(start, 216), :]
            part = pl.ds(z * 864, 864)
            stage[0][side, z * 864 : (z + 1) * 864, :] = run_buf[0][...].astype(BF16)
            copies.append(pltpu.make_async_copy(stage[0].at[side, part, :], halves[side].at[part, :], osems[0].at[side, z]))
            copies[-1].start()
    for copy in copies:
        copy.wait()


def tile_backward(core, ids, *refs):
    ins, _, halves, bufs, packed_grad, flat, stage, sems, osems = cut(refs, 14, 1, 2, 14, 1, 1, 1, 1, 1)
    late = [Late(ins[i], bufs[i], sems[0].at[i]) for i in (0, 13, 6, 12, 11, 5, 10, 4, 9, 8, 3, 7, 1, 2)]
    late = dict(zip((0, 13, 6, 12, 11, 5, 10, 4, 9, 8, 3, 7, 1, 2), late))
    arrived, patches, slide_rows = late[0], late[1], late[2]
    w_qkv, w_out, w_up, w_down = [late[i] for i in range(3, 7)]
    x_ref, res = late[7], [late[i] for i in range(8, 14)]
    rows32 = lax.broadcasted_iota(jnp.int32, (32, 32), 0)
    columns32 = lax.broadcasted_iota(jnp.int32, (32, 32), 1)
    assign = jnp.sum(jnp.where(rows32 == columns32, ids[...].astype(F32), 0.0), axis=1, keepdims=True)
    cot = jnp.zeros((32, D), F32)
    for i in range(16):
        region = float(i // 4 * 8 + i % 4)
        cot = cot + jnp.where((assign == region) | (assign == region + 4.0), arrived[i].astype(F32), 0.0)
    cot = cot * 0.25
    grad = jnp.concatenate([cot] * PATCHES, axis=0)
    normed, rstd = norm_parts(res[5][...])
    grad = norm_back(grad, normed, rstd)
    bases = (2304, 5760, 6912, 11520)

    leaving = []

    def put(i, a, b):
        put_rows(flat[0], bases[i], a, b)
        if i == 2:
            leaving.extend(two_halves(flat[0], (2, 3), core[0], halves, stage[0], osems[0]))

    grad = encode_back(grad, x_ref[...], w_qkv, w_out, w_up, w_down, HEADS, res, packed_grad[0], put)
    for side in range(2):
        which = core[0] if side == 0 else 1 - core[0]
        stage[0][side, 8064:8144, :] = slide_rows.ref()[which]
        part = pl.ds(8064, 80)
        leaving.append(pltpu.make_async_copy(stage[0].at[side, part, :], halves[side].at[part, :], osems[0].at[side, 4]))
        leaving[-1].start()
    put_rows(flat[0], 0, patches[...], grad.astype(BF16))
    leaving.extend(two_halves(flat[0], (0, 1), core[0], halves, stage[0], osems[0]))
    for copy in leaving:
        copy.wait()


def fold(rows, pad, tail, *refs):
    mine, got = refs[:2]
    refs = refs[2 + tail :]
    if tail:
        out, extra = refs[:2]
        refs = refs[2:]
    else:
        out = refs[0]
        refs = refs[1:]
    a, b, total, stage, chunks, sems, osems = refs[:7]
    planes = 2 if tail else 1
    run = 16 * planes * rows
    arriving = []
    for z in range(4 + tail):
        part = pl.ds(z * run, run if z < 4 else 80)
        for side, (source, buffer) in enumerate(((mine, a), (got, b))):
            arriving.append(pltpu.make_async_copy(source.at[part, :], buffer.at[part, :], sems.at[side, z]))
            arriving[-1].start()
    for z in range(4):
        arriving[2 * z].wait()
        arriving[2 * z + 1].wait()
        part = pl.ds(z * run, run)
        total[part, :] = a[part, :].astype(F32) + b[part, :].astype(F32)
    leaving = []
    if tail:
        arriving[8].wait()
        arriving[9].wait()
        part = pl.ds(4 * run, 80)
        refs[7][...] = (a[part, :].astype(F32) + b[part, :].astype(F32)).astype(BF16)
        leaving.append(pltpu.make_async_copy(refs[7], extra, osems.at[16]))
        leaving[-1].start()
    if pad:
        stage[4 * planes * rows :, :] = jnp.zeros((pad, LANES), F32)
    for y in range(4):
        for x in range(4):
            for z in range(4):
                for h in range(planes):
                    source = (z * 16 * planes + y * 4 * planes + h * 4 + x) * rows
                    target = (z * planes + h) * rows
                    stage[target : target + rows, :] = total[source : source + rows, :]
            chunks[y * 4 + x] = stage[...].astype(BF16)
            leaving.append(pltpu.make_async_copy(chunks.at[y * 4 + x], out.at[y * 4 + x], osems.at[y * 4 + x]))
            leaving[-1].start()
    for copy in leaving:
        copy.wait()


def plane_sum(parts, out, buffer, total, sems):
    copies = []
    for i in range(2):
        part = pl.ds(i * 112, 112)
        copies.append(pltpu.make_async_copy(parts.at[:, part, :], buffer.at[:, part, :], sems.at[i]))
        copies[-1].start()
    for i in range(2):
        copies[i].wait()
        rows = slice(i * 112, (i + 1) * 112)
        value = buffer[0, rows, :].astype(F32)
        for j in range(1, 16):
            value = value + buffer[j, rows, :].astype(F32)
        total[rows, :] = value
    leave([(total, out)], sems)


def merge(where, tile_in, region_in, slide_in, out, tile_buf, region_buf, slide_buf, total, slide_total, stage, chunks, sems, osems):
    tile_late = Late(tile_in, tile_buf, sems.at[0])
    region_late = Late(region_in, region_buf, sems.at[1])
    slide_late = Late(slide_in, slide_buf, sems.at[2])
    slide_total[...] = slide_late[...].astype(F32)

    for start in range(0, 512, 64):
        value = tile_late[0, start : start + 64, :].astype(F32)
        for i in range(1, 16):
            value = value + tile_late[i, start : start + 64, :].astype(F32)
        total[start : start + 64, :] = value
    region_total = region_late.ref()
    h = lax.rem(where[0] // 4, 2)
    leaving = []
    for i in range(8):
        stage[0:63, :] = total[i * 63 : (i + 1) * 63, :]
        stage[63:64, :] = jnp.zeros((1, LANES), F32)
        rows = region_total[i // 2 * 54 : (i // 2 + 1) * 54, :]
        stage[64:118, :] = jnp.where(h == i % 2, rows, 0.0)
        stage[118:128, :] = slide_total[i * 10 : (i + 1) * 10, :]
        chunks[i] = stage[...].astype(BF16)
        leaving.append(pltpu.make_async_copy(chunks.at[i], out.at[i], osems.at[i]))
        leaving[-1].start()
    for copy in leaving:
        copy.wait()


def call(kernel, macs, outs, scratch, inputs, scalars=0, whole=0):
    specs = [pl.BlockSpec(memory_space=pltpu.SMEM)] * scalars
    specs += [pl.BlockSpec(memory_space=pltpu.VMEM)] * whole
    specs += [pl.BlockSpec(memory_space=pl.ANY)] * (len(inputs) - scalars - whole)
    moved = sum(math.prod(a.shape) * a.dtype.itemsize for a in inputs) + sum(math.prod(a) * jnp.dtype(k).itemsize for a, k in outs)
    cost = pl.CostEstimate(flops=2 * macs, bytes_accessed=moved, transcendentals=0)
    return pl.pallas_call(
        kernel,
        out_shape=[jax.ShapeDtypeStruct(shape, kind) for shape, kind in outs],
        in_specs=specs,
        out_specs=[pl.BlockSpec(memory_space=pl.ANY)] * len(outs),
        scratch_shapes=[pltpu.VMEM(*item) if isinstance(item, tuple) else item for item in scratch],
        compiler_params=pltpu.CompilerParams(vmem_limit_bytes=60 * 1024 * 1024),
        cost_estimate=cost,
    )(*inputs)


def like(arrays):
    return [(a.shape, a.dtype) for a in arrays]


def semaphores(*shape):
    return pltpu.SemaphoreType.DMA(shape)


def residuals(tokens, width, hidden, heads):
    return [
        ((tokens, 3 * width), BF16),
        ((heads, tokens, tokens), F32),
        ((tokens, width), BF16),
        ((tokens, width), F32),
        ((tokens, hidden), F32),
        ((tokens, width), F32),
    ]


def index_of(z, core, y, z_hi, x):
    return (z * 2 + core) * 32 + y * 8 + z_hi * 4 + x


PLANES = [[index_of(z, c, y, h, x) for y in range(4) for x in range(4)] for z in range(4) for c in range(2) for h in range(2)]
COLUMNS = [[index_of(z, c, y, h, x) for z in range(4) for h in range(2)] for c in range(2) for y in range(4) for x in range(4)]
OTHER_CORE = [(g, g + 1 - 2 * (g % 2)) for g in range(8)]
OTHER_PLANE = [(d, d + 4 - 8 * (d // 4 % 2)) for d in range(32)]
ALL = ("grp", "dev")


def exchange(array, groups):
    return lax.all_to_all(array, ALL, 0, 0, axis_index_groups=groups)


def folded(mine, other, rows, pad, tail, after=()):
    got = lax.ppermute(other, "grp", OTHER_CORE)
    planes = 1 + tail
    height = 64 * planes * rows + 80 * tail
    chunk = 4 * planes * rows + pad
    return call(
        functools.partial(fold, rows, pad, tail),
        4 * US,
        [((16, chunk, LANES), BF16)] + [((80, LANES), BF16)] * tail,
        [((height, LANES), BF16)] * 2
        + [((64 * planes * rows, LANES), F32), ((chunk, LANES), F32), ((16, chunk, LANES), BF16)]
        + [semaphores(2, 5), semaphores(17)]
        + [((80, LANES), BF16)] * tail,
        (mine, got) + after,
    )


def body(
    patches,
    tile_region,
    region_slide,
    bin_label,
    censored,
    patch_w,
    tile_qkv,
    tile_out,
    tile_up,
    tile_down,
    region_qkv,
    region_out,
    region_up,
    region_down,
    slide_in,
    slide_qkv,
    slide_out,
    slide_up,
    slide_down,
    slide_head,
):
    member_index = lax.axis_index("dev").astype(jnp.int32)
    where = member_index.reshape(1)
    core = lax.rem(lax.axis_index("grp").astype(jnp.int32), 2).reshape(1)
    scaling = 1.0 / (bin_label.shape[1] * lax.axis_size("grp"))
    tokens = patches.transpose(1, 0, 2).reshape(128, 768)
    tile_res = [((128, D), F32)] + residuals(128, D, FF, HEADS)
    ins = (tokens, patch_w, tile_qkv, tile_out, tile_up, tile_down)
    message, *tile_kept = call(
        tile_forward,
        7 * US,
        [((112, LANES), BF16)] + tile_res,
        like(ins) + tile_res + [((112, LANES), BF16), semaphores(6), semaphores(7), semaphores(1)],
        (where, tile_region, region_slide) + ins,
        scalars=1,
        whole=2,
    )
    both = jnp.concatenate([message, lax.ppermute(message, "dev", OTHER_PLANE)], axis=0)
    rows = exchange(jnp.broadcast_to(both[None], (16, 224, LANES)), PLANES)
    region_res = [((2 * SLOTS, D), F32)] + residuals(2 * SLOTS, D, FF, HEADS)
    ins = (region_qkv, region_out, region_up, region_down)
    message, tails, *region_kept = call(
        region_forward,
        6 * US,
        [((16, 8, LANES), F32), ((32, 16, LANES), BF16)] + region_res,
        like(ins)
        + [((32, 112, LANES), BF16)]
        + region_res
        + [((8, LANES), F32), semaphores(4), semaphores(7), semaphores(33), semaphores(32)],
        (where, rows) + ins,
        scalars=1,
    )
    all_regions = exchange(message, PLANES)
    slide_weights = (slide_in, slide_qkv, slide_out, slide_up, slide_down, slide_head)
    widths = (FF, D, D, FF, D, D, D, 3 * D)
    pairs = [((2 * SLOTS, n), BF16) for n in widths]
    losses_out = [((SL_GRP, 1), F32)]
    outs = losses_out + [((4, 128, D), BF16)] + pairs + like(slide_weights)
    buffers = losses_out + [((8, 128, D), BF16)] + pairs + like(slide_weights)
    ins = (all_regions, tails) + slide_weights + (region_qkv, region_out, region_up, region_down) + tuple(region_kept)
    losses, spread, *rest = call(
        functools.partial(region_backward, scaling),
        12 * US,
        outs,
        like(ins)
        + buffers
        + [((2 * SLOTS, 3 * D), BF16), ((32, 3 * D_SL), BF16), ((32, D), BF16), ((32, D), F32)]
        + residuals(32, D_SL, D_SL, H_SL)
        + [semaphores(19), semaphores(16)],
        (where, bin_label.reshape(SL_GRP, 1), censored.reshape(SL_GRP, 1)) + ins,
        scalars=1,
        whole=2,
    )
    arrived = exchange(spread.reshape(16, 32, D), PLANES)
    ins = tuple(rest[:8])
    mine, other = call(
        region_weights,
        5 * US,
        [((3456, LANES), BF16)] * 2,
        like(ins)
        + [((13824, LANES), F32), ((864, LANES), F32), ((2, 3456, LANES), BF16), semaphores(8), semaphores(2, 4)],
        (core, where) + ins,
        scalars=2,
    )
    (region_chunks,) = folded(mine, other, 54, 8, 0)
    region_parts = exchange(region_chunks, PLANES)
    (region_sums,) = call(
        plane_sum,
        20 * US,
        [((224, LANES), F32)],
        like((region_parts,)) + [((224, LANES), F32), semaphores(2)],
        (region_parts,),
    )
    slide_flat = jnp.concatenate([g.astype(F32).reshape(-1) for g in rest[8:]]).reshape(4, 2, 4, 2, 4, 1155)
    y, x = member_index // 8, lax.rem(member_index, 4)
    zero = jnp.zeros((), jnp.int32)
    slide_rows = lax.dynamic_slice(slide_flat, (zero, zero, y, zero, x, zero), (4, 2, 1, 2, 1, 1155))
    slide_rows = slide_rows.reshape(4, 2, 2, 1155).transpose(1, 0, 2, 3)
    slide_rows = jnp.pad(slide_rows, ((0, 0), (0, 0), (0, 0), (0, 125))).astype(BF16).reshape(2, 80, LANES)
    ins = (arrived, tokens, slide_rows, tile_qkv, tile_out, tile_up, tile_down) + tuple(tile_kept)
    mine, other = call(
        tile_backward,
        13 * US,
        [((8144, LANES), BF16)] * 2,
        like(ins)
        + [((128, 3 * D), BF16), ((16128, LANES), F32), ((2, 8144, LANES), BF16), semaphores(14), semaphores(2, 5)],
        (core, tile_region) + ins + (region_chunks,),
        scalars=1,
        whole=1,
    )
    tile_chunks, slide_sums = folded(mine, other, 63, 8, 1, (region_sums,))
    tile_parts = exchange(tile_chunks, PLANES)
    ins = (tile_parts, region_sums, slide_sums)
    (last,) = call(
        merge,
        3 * US,
        [((8, 128, LANES), BF16)],
        like(ins)
        + [((512, LANES), F32), ((80, LANES), F32), ((128, LANES), F32), ((8, 128, LANES), BF16)]
        + [semaphores(3), semaphores(8)],
        (where,) + ins,
        scalars=1,
    )
    total = jnp.sum(exchange(last, COLUMNS).astype(F32), axis=0)
    tile_result = total[0:63].reshape(8064)
    region_result = total[64:118].reshape(6912)
    slide_result = total[118:128].reshape(1280)[:1155] * 0.5
    return (losses.reshape(1, SL_GRP), tile_result, region_result, slide_result)


def solution(mesh):
    placed = (P(ALL, None, None), P("grp", "dev"), P("grp", "dev"), P("grp", None), P("grp", None)) + (P(),) * 15
    return jax.shard_map(
        body,
        mesh=mesh,
        in_specs=placed,
        out_specs=(P("grp", None), P(ALL), P(ALL), P(ALL)),
        check_vma=False,
    )
```

```python
import functools
import math

import jax
import jax.numpy as jnp
from jax import lax
from jax.experimental import pallas as pl
from jax.experimental.pallas import tpu as pltpu
from jax.sharding import PartitionSpec as P

D = 384
HEADS = 6
FF = 1536
PATCHES = 4
SLOTS = 64
D_SL = 192
H_SL = 3
NBINS = 4
SL_GRP = 4
HEAD = 64
F32 = jnp.float32
BF16 = jnp.bfloat16
LANES = 128
US = 550_000_000
GELU_C = math.sqrt(2.0 / math.pi)


def mm(a, b):
    return jnp.dot(a, b, preferred_element_type=F32)


def mm_nt(a, b):
    return lax.dot_general(a, b, (((1,), (1,)), ((), ())), preferred_element_type=F32)


def mm_tn(a, b):
    return lax.dot_general(a, b, (((0,), (0,)), ((), ())), preferred_element_type=F32)


def norm_parts(x):
    average = jnp.mean(x, axis=-1, keepdims=True)
    centred = x - average
    variance = jnp.mean(centred * centred, axis=-1, keepdims=True)
    rstd = lax.rsqrt(variance + 1e-06)
    return centred * rstd, rstd


def norm_back(grad, normed, rstd):
    first = jnp.mean(grad, axis=-1, keepdims=True)
    second = jnp.mean(grad * normed, axis=-1, keepdims=True)
    return rstd * (grad - first - normed * second)


def gelu_parts(x):
    t = jnp.tanh(GELU_C * (x + 0.044715 * (x * x * x)))
    value = 0.5 * x * (1.0 + t)
    slope = 0.5 * (1.0 + t) + 0.5 * x * (1.0 - t * t) * (GELU_C * (1.0 + 3.0 * 0.044715 * (x * x)))
    return value, slope


def encode(x, allowed, w_qkv, w_out, w_up, w_down, heads, res):
    packed_ref, attend_ref, mixture_ref, mid_ref, up_ref, out_ref = res
    width = x.shape[1]
    normed, _ = norm_parts(x)
    packed_ref[...] = mm(normed.astype(BF16), w_qkv[...]).astype(BF16)
    send(packed_ref)
    for h in range(heads):
        q = packed_ref[:, h * HEAD : (h + 1) * HEAD]
        k = packed_ref[:, width + h * HEAD : width + (h + 1) * HEAD]
        v = packed_ref[:, 2 * width + h * HEAD : 2 * width + (h + 1) * HEAD]
        scores = jnp.where(allowed, mm_nt(q, k) * 0.125, -1e30)
        scores = jnp.exp(scores - jnp.max(scores, axis=-1, keepdims=True))
        weights = scores / jnp.sum(scores, axis=-1, keepdims=True)
        attend_ref[h] = weights
        mixture_ref[:, h * HEAD : (h + 1) * HEAD] = mm(weights.astype(BF16), v).astype(BF16)
    send(attend_ref)
    send(mixture_ref)
    x1 = x + mm(mixture_ref[...], w_out[...])
    mid_ref[...] = x1
    send(mid_ref)
    normed, _ = norm_parts(x1)
    up = mm(normed.astype(BF16), w_up[...])
    up_ref[...] = up
    send(up_ref)
    hidden, _ = gelu_parts(up)
    out = x1 + mm(hidden.astype(BF16), w_down[...])
    out_ref[...] = out
    send(out_ref)
    return out


def encode_back(grad, x, w_qkv, w_out, w_up, w_down, heads, res, packed_grad, put, slope=None):
    packed_ref, attend_ref, mixture_ref, mid_ref, up_ref, _ = res
    width = x.shape[1]
    grad_b = grad.astype(BF16)
    hidden = mixture = None
    if slope is None:
        hidden, slope = gelu_parts(up_ref[...])
        hidden, mixture = hidden.astype(BF16), mixture_ref[...]
    up_grad = (mm_nt(grad_b, w_down[...]).astype(BF16).astype(F32) * slope[...]).astype(BF16)
    put(3, hidden, grad_b)
    normed, rstd = norm_parts(mid_ref[...])
    put(2, normed.astype(BF16), up_grad)
    normed_grad = mm_nt(up_grad, w_up[...]).astype(BF16).astype(F32)
    mid_grad = grad + norm_back(normed_grad, normed, rstd)
    mid_b = mid_grad.astype(BF16)
    put(1, mixture, mid_b)
    mix_grad = mm_nt(mid_b, w_out[...]).astype(BF16)
    for h in range(heads):
        q = packed_ref[:, h * HEAD : (h + 1) * HEAD]
        k = packed_ref[:, width + h * HEAD : width + (h + 1) * HEAD]
        v = packed_ref[:, 2 * width + h * HEAD : 2 * width + (h + 1) * HEAD]
        head_grad = mix_grad[:, h * HEAD : (h + 1) * HEAD]
        weights = attend_ref[h]
        weights_grad = mm_nt(head_grad, v).astype(BF16).astype(F32)
        v_grad = mm_tn(weights.astype(BF16), head_grad)
        inner = jnp.sum(weights_grad * weights, axis=-1, keepdims=True)
        scores_grad = (weights * (weights_grad - inner) * 0.125).astype(BF16)
        packed_grad[:, h * HEAD : (h + 1) * HEAD] = mm(scores_grad, k).astype(BF16)
        packed_grad[:, width + h * HEAD : width + (h + 1) * HEAD] = mm_tn(scores_grad, q).astype(BF16)
        packed_grad[:, 2 * width + h * HEAD : 2 * width + (h + 1) * HEAD] = v_grad.astype(BF16)
    normed, rstd = norm_parts(x)
    put(0, normed.astype(BF16), packed_grad[...])
    normed_grad = mm_nt(packed_grad[...], w_qkv[...]).astype(BF16).astype(F32)
    return mid_grad + norm_back(normed_grad, normed, rstd)


def put_rows(flat, base, left, b):
    rows, columns = left.shape[0], b.shape[1]
    chunks = columns // 128
    for c in range(0, chunks, 3):
        part = mm(left, b[:, c * 128 : (c + 3) * 128]).astype(BF16).astype(F32)
        for j in range(3):
            flat[pl.ds(base + c + j, rows, stride=chunks), :] = part[:, j * 128 : (j + 1) * 128]


def same_tile():
    row = lax.broadcasted_iota(jnp.int32, (128, 128), 0)
    column = lax.broadcasted_iota(jnp.int32, (128, 128), 1)
    return lax.rem(row, 32) == lax.rem(column, 32)


class Late:
    def __init__(self, source, buffer, sem):
        self.copy = pltpu.make_async_copy(source, buffer, sem)
        self.buffer, self.here = buffer, False
        self.copy.start()

    def ref(self):
        if not self.here:
            self.copy.wait()
            self.here = True
        return self.buffer

    def __getitem__(self, index):
        return self.ref()[index]


class Early:
    def __init__(self, target, buffer, sem):
        self.copy = pltpu.make_async_copy(buffer, target, sem)
        self.buffer = buffer

    def __getitem__(self, index):
        return self.buffer[index]

    def __setitem__(self, index, value):
        self.buffer[index] = value

    def finish(self):
        self.copy.wait()


def send(ref):
    if isinstance(ref, Early):
        ref.copy.start()


def leave(pairs, sems):
    copies = [pltpu.make_async_copy(a, b, sems.at[i]) for i, (a, b) in enumerate(pairs)]
    for copy in copies:
        copy.start()
    for copy in copies:
        copy.wait()


def broadcast_out(block, out, sems):
    copies = [pltpu.make_async_copy(block, out.at[i], sems.at[i]) for i in range(16)]
    for copy in copies:
        copy.start()
    for copy in copies:
        copy.wait()


def tile_forward(where, ids, slide, *refs):
    ins, outs, bufs, obufs, block, sems, osems, bsems = cut(refs, 6, 8, 6, 7, 1, 1, 1, 1)
    late = [Late(r, b, sems[0].at[i]) for i, (r, b) in enumerate(zip(ins, bufs))]
    res = [Early(r, b, osems[0].at[i]) for i, (r, b) in enumerate(zip(outs[1:], obufs))]
    patches, patch_w, w_qkv, w_out, w_up, w_down = late
    x = mm(patches[...], patch_w[...])
    res[0][...] = x
    send(res[0])
    out = encode(x, same_tile(), w_qkv, w_out, w_up, w_down, HEADS, res[1:])
    normed, _ = norm_parts(out)
    total = (normed[0:32] + normed[32:64]) + (normed[64:96] + normed[96:128])
    total = (total * 0.25).astype(BF16)
    message = block[0]
    for c in range(3):
        message[c * 32 : (c + 1) * 32, :] = total[:, c * LANES : (c + 1) * LANES]
    row = lax.broadcasted_iota(jnp.int32, (16, LANES), 0)
    lane = lax.broadcasted_iota(jnp.int32, (16, LANES), 1)
    mine = (lane >= 32 * lax.rem(where[0], 4)) & (lane < 32 * lax.rem(where[0], 4) + 32)
    four = jnp.concatenate([ids[...].astype(F32)] * 4, axis=1)
    tail = jnp.where((row == 0) & mine, four, 0.0) + jnp.where(row == 1, slide[...].astype(F32), 0.0)
    message[96:112, :] = tail.astype(BF16)
    leave([(message, outs[0])], bsems[0])
    for r in res:
        r.finish()


def cut(refs, *sizes):
    parts, at = [], 0
    for size in sizes:
        parts.append(refs[at : at + size])
        at += size
    assert at == len(refs)
    return parts


def tails_of(tails):
    tails = tails.astype(F32)
    row = lax.broadcasted_iota(jnp.int32, tails.shape, 1)
    ids = jnp.sum(jnp.where(row == 0, tails, 0.0), axis=1)
    slides = jnp.sum(jnp.where(row == 1, tails, 0.0), axis=1)
    to = lax.broadcasted_iota(jnp.int32, (8, 32), 0)
    source = lax.broadcasted_iota(jnp.int32, (8, 32), 1)
    near = (source >= 4 * to) & (source < 4 * to + 4)
    ids = mm(jnp.where(near, 1.0, 0.0).astype(BF16), ids.astype(BF16))
    return ids, slides[:, 0:1]


def slots_of(ids, region):
    member = jnp.where(ids == region.astype(F32), 1.0, 0.0)
    row = lax.broadcasted_iota(jnp.int32, (128, 128), 0)
    column = lax.broadcasted_iota(jnp.int32, (128, 128), 1)
    within = mm(member.astype(BF16), jnp.where(row < column, 1.0, 0.0).astype(BF16))
    sums = jnp.sum(member, axis=1, keepdims=True)
    row8 = lax.broadcasted_iota(jnp.int32, (8, 8), 0)
    column8 = lax.broadcasted_iota(jnp.int32, (8, 8), 1)
    earlier = jnp.where(column8 < row8, 1.0, 0.0).astype(BF16)
    ahead = mm(earlier, jnp.broadcast_to(sums, (8, 128)).astype(BF16))
    count = jnp.sum(sums, axis=0, keepdims=True)
    return member, (within + ahead).astype(jnp.int32), count


def both_slots(ids, device):
    first = device - 4 * lax.rem(device // 4, 2)
    return first, [slots_of(ids, first + 4 * b) for b in range(2)]


def choice(slots, i):
    k = lax.broadcasted_iota(jnp.int32, (SLOTS, 128), 0)
    parts = [jnp.where((slot[i : i + 1] == k) & (member[i : i + 1] > 0.0), 1.0, 0.0) for member, slot, _ in slots]
    return jnp.concatenate(parts, axis=0).astype(BF16)


def usable_of(slots):
    k = lax.broadcasted_iota(jnp.int32, (SLOTS, 1), 0).astype(F32)
    return [k < count for _, _, count in slots]


def prepare(more, *refs):
    ins, outs, bufs, obufs, sems, osems = cut(refs, 4 + more, 5 + more, 4 + more, 5 + more, 1, 1)
    up, mid, x, mixture, *others = [Late(r, b, sems[0].at[i]) for i, (r, b) in enumerate(zip(ins, bufs))]
    early = [Early(r, b, osems[0].at[i]) for i, (r, b) in enumerate(zip(outs, obufs))]
    hidden, slope = gelu_parts(up[...])
    early[0][...] = slope
    early[1][...] = hidden.astype(BF16).T
    early[2][...] = norm_parts(mid[...])[0].astype(BF16).T
    early[3][...] = mixture[...].T
    early[4][...] = norm_parts(x[...])[0].astype(BF16).T
    for e, other in zip(early[5:], others):
        e[...] = other[...].T
    for e in early:
        send(e)
    for e in early:
        e.finish()


def region_forward(where, *refs):
    ins, _, outs, bufs, rows, obufs, block, sems, osems, bsems, rsems = cut(refs, 5, 1, 9, 4, 1, 7, 1, 1, 1, 1, 1)
    rows = rows[0]
    h = lax.rem(where[0] // 4, 2)
    arriving = []
    for i in range(16):
        base = i // 4 * 8 + i % 4
        for side, z in enumerate((h, 1 - h)):
            source = ins[0].at[i, 112 * side : 112 * side + 112, :]
            arriving.append(pltpu.make_async_copy(source, rows.at[base + 4 * z], rsems[0].at[2 * i + side]))
            arriving[-1].start()
    w_qkv, w_out, w_up, w_down = [Late(r, b, sems[0].at[i]) for i, (r, b) in enumerate(zip(ins[1:], bufs))]
    res = [Early(r, b, osems[0].at[i]) for i, (r, b) in enumerate(zip(outs[2:], obufs))]
    for copy in arriving:
        copy.wait()
    tails = pltpu.make_async_copy(rows.at[:, 96:112, :], outs[1], bsems[0].at[32])
    tails.start()
    ids, _ = tails_of(rows[:, 96:112, :])
    _, slots = both_slots(ids, where[0])
    parts = [jnp.zeros((2 * SLOTS, LANES), F32)] * 3
    for b in range(8):
        pick = choice(slots, b)
        for c in range(3):
            block_rows = rows[4 * b : 4 * b + 4, 32 * c : 32 * c + 32, :].reshape(128, LANES)
            parts[c] = parts[c] + mm(pick, block_rows)
    for c in range(3):
        res[0][:, c * LANES : (c + 1) * LANES] = parts[c]
    send(res[0])
    row = lax.broadcasted_iota(jnp.int32, (2 * SLOTS, 2 * SLOTS), 0)
    key = lax.broadcasted_iota(jnp.int32, (2 * SLOTS, 2 * SLOTS), 1)
    at = key.astype(F32)
    allowed = ((row < SLOTS) & (at < slots[0][2])) | ((row >= SLOTS) & (key >= SLOTS) & (at < slots[1][2] + SLOTS))
    out = encode(res[0][...], allowed, w_qkv, w_out, w_up, w_down, HEADS, res[1:])
    normed, _ = norm_parts(out)
    message = block[0]
    message[...] = jnp.zeros((8, LANES), F32)
    for b, usable in enumerate(usable_of(slots)):
        total = jnp.sum(jnp.where(usable, normed[b * SLOTS : (b + 1) * SLOTS], 0.0), axis=0, keepdims=True)
        embed = (total / slots[b][2]).astype(BF16).astype(F32)
        for c in range(3):
            message[3 * b + c : 3 * b + c + 1, :] = embed[:, c * LANES : (c + 1) * LANES]
    broadcast_out(message, outs[0], bsems[0])
    tails.wait()
    for r in res:
        r.finish()


def slide_step(embeds, slide_row, slide_col, label, censor, slide_in, w_qkv, w_out, w_up, w_down, head, losses, grads, res, packed_grad, scaling):
    emb = embeds[...]
    x = mm(emb, slide_in[...])
    out = encode(x, slide_col == slide_row, w_qkv, w_out, w_up, w_down, H_SL, res)
    normed, rstd = norm_parts(out)
    sums, sizes, masks = [], [], []
    for s in range(SL_GRP):
        mask = jnp.where(slide_col == float(s), 1.0, 0.0)
        size = jnp.sum(mask, axis=0, keepdims=True)
        masks.append(mask)
        sizes.append(size)
        sums.append(jnp.sum(mask * normed, axis=0, keepdims=True) / size)
    pooled = jnp.concatenate(sums, axis=0).astype(BF16)
    logits = mm(pooled, head[...])
    soft = jnp.log1p(jnp.exp(-jnp.abs(logits)))
    log_hazard = -(jnp.maximum(-logits, 0.0) + soft)
    log_stay = -(jnp.maximum(logits, 0.0) + soft)
    bin_at = lax.broadcasted_iota(jnp.int32, (SL_GRP, NBINS), 1)
    at = (bin_at == label[...]).astype(F32)
    before = (bin_at < label[...]).astype(F32)
    held = censor[...].astype(F32)
    past = jnp.sum(before * log_stay, axis=1, keepdims=True)
    seen = past + jnp.sum(at * log_hazard, axis=1, keepdims=True)
    lived = past + jnp.sum(at * log_stay, axis=1, keepdims=True)
    losses[...] = -(1.0 - held) * seen - held * lived
    chance = 1.0 / (1.0 + jnp.exp(-logits))
    logit_grad = (scaling * (before * chance + at * (chance - (1.0 - held)))).astype(BF16)
    grads[5][...] = mm_tn(pooled, logit_grad).astype(BF16)
    pooled_grad = mm_nt(logit_grad, head[...]).astype(BF16).astype(F32)
    grad = jnp.zeros_like(normed)
    for s in range(SL_GRP):
        grad = grad + masks[s] * (pooled_grad[s : s + 1] / sizes[s])
    grad = norm_back(grad, normed, rstd)

    def put(i, a, b):
        grads[i + 1][...] = mm_tn(a, b).astype(BF16)

    grad = encode_back(grad, x, w_qkv, w_out, w_up, w_down, H_SL, res, packed_grad, put).astype(BF16)
    grads[0][...] = mm_tn(emb, grad).astype(BF16)
    return mm_nt(grad, slide_in[...]).astype(BF16)


def region_backward(scaling, where, label, censor, *refs):
    ins, outs, bufs, obufs, extra, sems, osems = cut(refs, 18, 12, 18, 12, 10, 1, 1)
    h = lax.rem(where[0] // 4, 2)
    order = list(range(8)) + [17, 11, 16, 15, 10, 9, 14, 13, 8, 12]
    late = dict()
    for i in list(dict.fromkeys(order)):
        late[i] = Late(ins[i], bufs[i], sems[0].at[i])
    early = []
    for i, (r, b) in enumerate(zip(outs, obufs)):
        early.append(Early(r, b, osems[0].at[i]) if i != 1 else b)
    message, tails = late[0], late[1]
    slide_weights = [late[i] for i in range(2, 8)]
    w_qkv, w_out, w_up, w_down = [late[i] for i in range(8, 12)]
    x_ref, res = late[12], [late[13], late[14], None, late[15], None, late[17]]
    losses, spread, pairs, slide_grads = early[0], early[1], early[2:6], early[6:12]
    packed_grad, slide_packed_grad, embeds, placed = extra[:4]
    ids, slide_col = tails_of(tails[...])
    rows32 = lax.broadcasted_iota(jnp.int32, (32, 32), 0)
    columns32 = lax.broadcasted_iota(jnp.int32, (32, 32), 1)
    slide_row = jnp.sum(jnp.where(rows32 == columns32, slide_col, 0.0), axis=0, keepdims=True)
    arrived = message[...]
    at = lax.broadcasted_iota(jnp.int32, arrived.shape, 1)
    for b in range(2):
        for c in range(3):
            part = jnp.sum(jnp.where(at == 3 * b + c, arrived, 0.0), axis=1)
            for y in range(4):
                placed[8 * y + 4 * b : 8 * y + 4 * b + 4, c * LANES : (c + 1) * LANES] = part[4 * y : 4 * y + 4]
    embeds[...] = placed[...].astype(BF16)
    cots = slide_step(
        embeds, slide_row, slide_col, label, censor, *slide_weights, losses, slide_grads, extra[4:10], slide_packed_grad, scaling
    ).astype(F32)
    for g in [losses] + slide_grads:
        send(g)
    first, slots = both_slots(ids, where[0])
    grads = []
    for b, usable in enumerate(usable_of(slots)):
        mine = lax.broadcasted_iota(jnp.int32, (32, 1), 0) == first + 4 * b
        own = jnp.sum(jnp.where(mine, cots, 0.0), axis=0, keepdims=True)
        grads.append(jnp.where(usable, own / slots[b][2], 0.0))
    grad = jnp.concatenate(grads, axis=0)
    normed, rstd = norm_parts(res[5][...])
    grad = norm_back(grad, normed, rstd)

    def put(i, a, b):
        pairs[i][...] = b
        send(pairs[i])

    grad = encode_back(grad, x_ref[...], w_qkv, w_out, w_up, w_down, HEADS, res, packed_grad, put, late[16]).astype(BF16)
    for b in range(8):
        spread[b] = mm_tn(choice(slots, b), grad).astype(BF16)
    leave([(spread.at[2 * y + h], outs[1].at[y]) for y in range(4)], sems[0])
    for e in early:
        if e is not spread:
            e.finish()


def two_halves(flat, runs, core, halves, stage, sems):
    run = 32 * 63
    copies = []
    for side in range(2):
        which = core if side == 0 else 1 - core
        for z in runs:
            start = pl.multiple_of((2 * z + which) * run, 32)
            stage[side, z * run : (z + 1) * run, :] = flat[pl.ds(start, run), :].astype(BF16)
            part = pl.ds(z * run, run)
            copies.append(pltpu.make_async_copy(stage.at[side, part, :], halves[side].at[part, :], sems.at[side, z]))
            copies[-1].start()
    return copies


def region_weights(core, where, *refs):
    ins, halves, bufs, flat, run_buf, stage, sems, osems = cut(refs, 8, 2, 8, 1, 1, 1, 1, 1)
    late = [Late(r, b, sems[0].at[i]) for i, (r, b) in enumerate(zip(ins, bufs))]
    hidden, second, mixture, first, packed_grad, mid_grad, up_grad, grad = late
    put_rows(flat[0], 9216, hidden[...], grad[...])
    put_rows(flat[0], 4608, second[...], up_grad[...])
    put_rows(flat[0], 3456, mixture[...], mid_grad[...])
    put_rows(flat[0], 0, first[...], packed_grad[...])
    h = lax.rem(where[0] // 4, 2)
    copies = []
    for side in range(2):
        which = core[0] if side == 0 else 1 - core[0]
        for z in range(4):
            for y in range(4):
                start = pl.multiple_of((2 * z + which) * 1728 + y * 432 + h * 216, 8)
                run_buf[0][y * 216 : (y + 1) * 216, :] = flat[0][pl.ds(start, 216), :]
            part = pl.ds(z * 864, 864)
            stage[0][side, z * 864 : (z + 1) * 864, :] = run_buf[0][...].astype(BF16)
            copies.append(pltpu.make_async_copy(stage[0].at[side, part, :], halves[side].at[part, :], osems[0].at[side, z]))
            copies[-1].start()
    for copy in copies:
        copy.wait()


def tile_backward(core, ids, *refs):
    ins, _, halves, bufs, packed_grad, flat, stage, sems, osems = cut(refs, 16, 1, 2, 16, 1, 1, 1, 1, 1)
    late = {i: Late(ins[i], bufs[i], sems[0].at[i]) for i in (0, 9, 4, 10, 11, 8, 3, 12, 2, 13, 6, 7, 1, 5, 14, 15)}
    arrived, x_ref = late[0], late[5]
    w_qkv, w_out, w_up, w_down = [late[i] for i in range(1, 5)]
    res = [late[6], late[7], None, late[8], None, late[9]]
    rows32 = lax.broadcasted_iota(jnp.int32, (32, 32), 0)
    columns32 = lax.broadcasted_iota(jnp.int32, (32, 32), 1)
    assign = jnp.sum(jnp.where(rows32 == columns32, ids[...].astype(F32), 0.0), axis=1, keepdims=True)
    cot = jnp.zeros((32, D), F32)
    for i in range(16):
        region = float(i // 4 * 8 + i % 4)
        cot = cot + jnp.where((assign == region) | (assign == region + 4.0), arrived[i].astype(F32), 0.0)
    cot = cot * 0.25
    grad = jnp.concatenate([cot] * PATCHES, axis=0)
    normed, rstd = norm_parts(res[5][...])
    grad = norm_back(grad, normed, rstd)
    bases = (2304, 5760, 6912, 11520)

    leaving = []

    def put(i, a, b):
        put_rows(flat[0], bases[i], late[14 - i][...], b)
        if i == 2:
            leaving.extend(two_halves(flat[0], (2, 3), core[0], halves, stage[0], osems[0]))

    grad = encode_back(grad, x_ref[...], w_qkv, w_out, w_up, w_down, HEADS, res, packed_grad[0], put, late[10])
    put_rows(flat[0], 0, late[15][...], grad.astype(BF16))
    leaving.extend(two_halves(flat[0], (0, 1), core[0], halves, stage[0], osems[0]))
    for copy in leaving:
        copy.wait()


def fold(planes, rows, pad, *refs):
    unread = planes - 1
    ins, _, outs, bufs, total, stage, chunks, sems, osems = cut(refs, 2, unread, 1, 2, 1, 1, 1, 1, 1)
    stage, total = stage[0], total[0]
    run = 16 * planes * rows
    arriving = []
    for z in range(4):
        part = pl.ds(z * run, run)
        for side in range(2):
            arriving.append(pltpu.make_async_copy(ins[side].at[part, :], bufs[side].at[part, :], sems[0].at[side, z]))
            arriving[-1].start()
    for z in range(4):
        arriving[2 * z].wait()
        arriving[2 * z + 1].wait()
        part = pl.ds(z * run, run)
        total[part, :] = bufs[0][part, :].astype(F32) + bufs[1][part, :].astype(F32)
    leaving = []
    stage[4 * planes * rows :, :] = jnp.zeros((pad, LANES), F32)
    for y in range(4):
        for x in range(4):
            for z in range(4):
                for h in range(planes):
                    source = (z * 16 * planes + y * 4 * planes + h * 4 + x) * rows
                    target = (z * planes + h) * rows
                    stage[target : target + rows, :] = total[source : source + rows, :]
            to = y * 4 + x
            chunks[0][to] = stage[...].astype(BF16)
            leaving.append(pltpu.make_async_copy(chunks[0].at[to], outs[0].at[to], osems[0].at[to]))
            leaving[-1].start()
    for copy in leaving:
        copy.wait()


def plane_sum(parts, out, buffer, total, sems):
    copies = []
    for i in range(2):
        part = pl.ds(i * 112, 112)
        copies.append(pltpu.make_async_copy(parts.at[:, part, :], buffer.at[:, part, :], sems.at[i]))
        copies[-1].start()
    for i in range(2):
        copies[i].wait()
        rows = slice(i * 112, (i + 1) * 112)
        value = buffer[0, rows, :].astype(F32)
        for j in range(1, 16):
            value = value + buffer[j, rows, :].astype(F32)
        total[rows, :] = value
    leave([(total, out)], sems)


def merge(where, tile_in, region_in, slide_in, out, tile_buf, region_buf, slide_buf, total, slide_total, stage, chunks, sems, osems):
    tile_late = Late(tile_in, tile_buf, sems.at[0])
    region_late = Late(region_in, region_buf, sems.at[1])
    slide_late = Late(slide_in, slide_buf, sems.at[2])
    slide_total[...] = slide_late[...].astype(F32)

    for start in range(0, 512, 64):
        value = tile_late[0, start : start + 64, :].astype(F32)
        for i in range(1, 16):
            value = value + tile_late[i, start : start + 64, :].astype(F32)
        total[start : start + 64, :] = value
    region_total = region_late.ref()
    h = lax.rem(where[0] // 4, 2)
    leaving = []
    for i in range(8):
        stage[0:63, :] = total[i * 63 : (i + 1) * 63, :]
        stage[63:64, :] = jnp.zeros((1, LANES), F32)
        rows = region_total[i // 2 * 54 : (i // 2 + 1) * 54, :]
        stage[64:118, :] = jnp.where(h == i % 2, rows, 0.0)
        stage[118:128, :] = slide_total[i * 10 : (i + 1) * 10, :]
        chunks[i] = stage[...].astype(BF16)
        leaving.append(pltpu.make_async_copy(chunks.at[i], out.at[i], osems.at[i]))
        leaving[-1].start()
    for copy in leaving:
        copy.wait()


def call(kernel, macs, outs, scratch, inputs, scalars=0, whole=0):
    specs = [pl.BlockSpec(memory_space=pltpu.SMEM)] * scalars
    specs += [pl.BlockSpec(memory_space=pltpu.VMEM)] * whole
    specs += [pl.BlockSpec(memory_space=pl.ANY)] * (len(inputs) - scalars - whole)
    moved = sum(math.prod(a.shape) * a.dtype.itemsize for a in inputs) + sum(math.prod(a) * jnp.dtype(k).itemsize for a, k in outs)
    cost = pl.CostEstimate(flops=2 * macs, bytes_accessed=moved, transcendentals=0)
    return pl.pallas_call(
        kernel,
        out_shape=[jax.ShapeDtypeStruct(shape, kind) for shape, kind in outs],
        in_specs=specs,
        out_specs=[pl.BlockSpec(memory_space=pl.ANY)] * len(outs),
        scratch_shapes=[pltpu.VMEM(*item) if isinstance(item, tuple) else item for item in scratch],
        compiler_params=pltpu.CompilerParams(vmem_limit_bytes=60 * 1024 * 1024),
        cost_estimate=cost,
    )(*inputs)


def like(arrays):
    return [(a.shape, a.dtype) for a in arrays]


def semaphores(*shape):
    return pltpu.SemaphoreType.DMA(shape)


def residuals(tokens, width, hidden, heads):
    return [
        ((tokens, 3 * width), BF16),
        ((heads, tokens, tokens), F32),
        ((tokens, width), BF16),
        ((tokens, width), F32),
        ((tokens, hidden), F32),
        ((tokens, width), F32),
    ]


def index_of(z, core, y, z_hi, x):
    return (z * 2 + core) * 32 + y * 8 + z_hi * 4 + x


PLANES = [[index_of(z, c, y, h, x) for y in range(4) for x in range(4)] for z in range(4) for c in range(2) for h in range(2)]
COLUMNS = [[index_of(z, c, y, h, x) for z in range(4) for h in range(2)] for c in range(2) for y in range(4) for x in range(4)]
OTHER_CORE = [(g, g + 1 - 2 * (g % 2)) for g in range(8)]
OTHER_PLANE = [(d, d + 4 - 8 * (d // 4 % 2)) for d in range(32)]
ALL = ("grp", "dev")


def exchange(array, groups):
    return lax.all_to_all(array, ALL, 0, 0, axis_index_groups=groups)


def folded(mine, other, planes, rows, pad, after=()):
    got = lax.ppermute(other, "grp", OTHER_CORE)
    height = 64 * planes * rows
    chunk = 4 * planes * rows + pad
    (out,) = call(
        functools.partial(fold, planes, rows, pad),
        4 * US,
        [((16, chunk, LANES), BF16)],
        [((height, LANES), BF16)] * 2
        + [((height, LANES), F32), ((chunk, LANES), F32), ((16, chunk, LANES), BF16)]
        + [semaphores(2, 4), semaphores(16)],
        (mine, got) + after,
    )
    return out


def prepared(kept, more):
    x, packed, attend, mixture, mid, up, out = kept
    ins = (up, mid, x, mixture) + more
    outs = [(up.shape, F32)] + [((a.shape[1], a.shape[0]), BF16) for a in ins[:1] + ins[1:2] + ins[3:4] + ins[2:3] + more]
    return call(
        functools.partial(prepare, len(more)),
        3 * US,
        outs,
        like(ins) + outs + [semaphores(len(ins)), semaphores(len(outs))],
        ins,
    )


def body(
    patches,
    tile_region,
    region_slide,
    bin_label,
    censored,
    patch_w,
    tile_qkv,
    tile_out,
    tile_up,
    tile_down,
    region_qkv,
    region_out,
    region_up,
    region_down,
    slide_in,
    slide_qkv,
    slide_out,
    slide_up,
    slide_down,
    slide_head,
):
    member_index = lax.axis_index("dev").astype(jnp.int32)
    where = member_index.reshape(1)
    core = lax.rem(lax.axis_index("grp").astype(jnp.int32), 2).reshape(1)
    scaling = 1.0 / (bin_label.shape[1] * lax.axis_size("grp"))
    tokens = patches.transpose(1, 0, 2).reshape(128, 768)
    tile_res = [((128, D), F32)] + residuals(128, D, FF, HEADS)
    ins = (tokens, patch_w, tile_qkv, tile_out, tile_up, tile_down)
    message, *tile_kept = call(
        tile_forward,
        7 * US,
        [((112, LANES), BF16)] + tile_res,
        like(ins) + tile_res + [((112, LANES), BF16), semaphores(6), semaphores(7), semaphores(1)],
        (where, tile_region, region_slide) + ins,
        scalars=1,
        whole=2,
    )
    both = jnp.concatenate([message, lax.ppermute(message, "dev", OTHER_PLANE)], axis=0)
    rows = exchange(jnp.broadcast_to(both[None], (16, 224, LANES)), PLANES)
    tile_slope, *tile_left = prepared(tile_kept, (tokens,))
    region_res = [((2 * SLOTS, D), F32)] + residuals(2 * SLOTS, D, FF, HEADS)
    ins = (region_qkv, region_out, region_up, region_down)
    message, tails, *region_kept = call(
        region_forward,
        6 * US,
        [((16, 8, LANES), F32), ((32, 16, LANES), BF16)] + region_res,
        like(ins)
        + [((32, 112, LANES), BF16)]
        + region_res
        + [((8, LANES), F32), semaphores(4), semaphores(7), semaphores(33), semaphores(32)],
        (where, rows) + ins + (tile_slope,),
        scalars=1,
    )
    all_regions = exchange(message, PLANES)
    slide_weights = (slide_in, slide_qkv, slide_out, slide_up, slide_down, slide_head)
    widths = (3 * D, D, FF, D)
    region_slope, *region_left = prepared(region_kept, ())
    x, packed, attend, _, mid, _, out = region_kept
    pairs = [((2 * SLOTS, n), BF16) for n in widths]
    losses_out = [((SL_GRP, 1), F32)]
    outs = losses_out + [((4, 128, D), BF16)] + pairs + like(slide_weights)
    buffers = losses_out + [((8, 128, D), BF16)] + pairs + like(slide_weights)
    ins = (all_regions, tails) + slide_weights + (region_qkv, region_out, region_up, region_down)
    ins = ins + (x, packed, attend, mid, region_slope, out)
    losses, spread, *rest = call(
        functools.partial(region_backward, scaling),
        12 * US,
        outs,
        like(ins)
        + buffers
        + [((2 * SLOTS, 3 * D), BF16), ((32, 3 * D_SL), BF16), ((32, D), BF16), ((32, D), F32)]
        + residuals(32, D_SL, D_SL, H_SL)
        + [semaphores(18), semaphores(12)],
        (where, bin_label.reshape(SL_GRP, 1), censored.reshape(SL_GRP, 1)) + ins,
        scalars=1,
        whole=2,
    )
    arrived = exchange(spread.reshape(16, 32, D), PLANES)
    ins = tuple(region_left) + tuple(rest[:4])
    mine, other = call(
        region_weights,
        5 * US,
        [((3456, LANES), BF16)] * 2,
        like(ins)
        + [((13824, LANES), F32), ((864, LANES), F32), ((2, 3456, LANES), BF16), semaphores(8), semaphores(2, 4)],
        (core, where) + ins,
        scalars=2,
    )
    region_chunks = folded(mine, other, 1, 54, 8)
    region_parts = exchange(region_chunks, PLANES)
    (region_sums,) = call(
        plane_sum,
        20 * US,
        [((224, LANES), F32)],
        like((region_parts,)) + [((224, LANES), F32), semaphores(2)],
        (region_parts,),
    )
    slide_flat = jnp.concatenate([g.astype(F32).reshape(-1) for g in rest[4:]]).reshape(4, 2, 4, 2, 4, 1155)
    y, x = member_index // 8, lax.rem(member_index, 4)
    zero = jnp.zeros((), jnp.int32)

    def slide_part(c):
        part = lax.dynamic_slice(slide_flat, (zero, c, y, zero, x, zero), (4, 1, 1, 2, 1, 1155))
        return jnp.pad(part.reshape(8, 1155), ((0, 0), (0, 125))).astype(BF16).reshape(80, LANES)

    slide_got = lax.ppermute(slide_part(1 - core[0]), "grp", OTHER_CORE)
    slide_sums = (slide_part(core[0]).astype(F32) + slide_got.astype(F32)).astype(BF16)
    x, packed, attend, _, mid, _, out = tile_kept
    ins = (arrived, tile_qkv, tile_out, tile_up, tile_down, x, packed, attend, mid, out, tile_slope) + tuple(tile_left)
    mine, other = call(
        tile_backward,
        13 * US,
        [((8064, LANES), BF16)] * 2,
        like(ins)
        + [((128, 3 * D), BF16), ((16128, LANES), F32), ((2, 8064, LANES), BF16), semaphores(16), semaphores(2, 4)],
        (core, tile_region) + ins + (region_chunks,),
        scalars=1,
        whole=1,
    )
    tile_chunks = folded(mine, other, 2, 63, 8, (region_sums,))
    tile_parts = exchange(tile_chunks, PLANES)
    ins = (tile_parts, region_sums, slide_sums)
    (last,) = call(
        merge,
        3 * US,
        [((8, 128, LANES), BF16)],
        like(ins)
        + [((512, LANES), F32), ((80, LANES), F32), ((128, LANES), F32), ((8, 128, LANES), BF16)]
        + [semaphores(3), semaphores(8)],
        (where,) + ins,
        scalars=1,
    )
    total = jnp.sum(exchange(last, COLUMNS).astype(F32), axis=0)
    tile_result = total[0:63].reshape(8064)
    region_result = total[64:118].reshape(6912)
    slide_result = total[118:128].reshape(1280)[:1155] * 0.5
    return (losses.reshape(1, SL_GRP), tile_result, region_result, slide_result)


def solution(mesh):
    placed = (P(ALL, None, None), P("grp", "dev"), P("grp", "dev"), P("grp", None), P("grp", None)) + (P(),) * 15
    return jax.shard_map(
        body,
        mesh=mesh,
        in_specs=placed,
        out_specs=(P("grp", None), P(ALL), P(ALL), P(ALL)),
        check_vma=False,
    )
```

```python
import functools
import math

import jax
import jax.numpy as jnp
from jax import lax
from jax.experimental import pallas as pl
from jax.experimental.pallas import tpu as pltpu
from jax.sharding import PartitionSpec as P

D = 384
HEADS = 6
FF = 1536
PATCHES = 4
SLOTS = 64
D_SL = 192
H_SL = 3
NBINS = 4
SL_GRP = 4
HEAD = 64
F32 = jnp.float32
BF16 = jnp.bfloat16
LANES = 128
US = 550_000_000
GELU_C = math.sqrt(2.0 / math.pi)


def mm(a, b):
    return jnp.dot(a, b, preferred_element_type=F32)


def mm_nt(a, b):
    return lax.dot_general(a, b, (((1,), (1,)), ((), ())), preferred_element_type=F32)


def mm_tn(a, b):
    return lax.dot_general(a, b, (((0,), (0,)), ((), ())), preferred_element_type=F32)


def norm_parts(x):
    average = jnp.mean(x, axis=-1, keepdims=True)
    centred = x - average
    variance = jnp.mean(centred * centred, axis=-1, keepdims=True)
    rstd = lax.rsqrt(variance + 1e-06)
    return centred * rstd, rstd


def norm_back(grad, normed, rstd):
    first = jnp.mean(grad, axis=-1, keepdims=True)
    second = jnp.mean(grad * normed, axis=-1, keepdims=True)
    return rstd * (grad - first - normed * second)


def gelu_parts(x):
    t = jnp.tanh(GELU_C * (x + 0.044715 * (x * x * x)))
    value = 0.5 * x * (1.0 + t)
    slope = 0.5 * (1.0 + t) + 0.5 * x * (1.0 - t * t) * (GELU_C * (1.0 + 3.0 * 0.044715 * (x * x)))
    return value, slope


def encode(x, allowed, w_qkv, w_out, w_up, w_down, heads, res):
    packed_ref, attend_ref, mixture_ref, mid_ref, up_ref, out_ref = res
    width = x.shape[1]
    normed, _ = norm_parts(x)
    packed_ref[...] = mm(normed.astype(BF16), w_qkv[...]).astype(BF16)
    send(packed_ref)
    for h in range(heads):
        q = packed_ref[:, h * HEAD : (h + 1) * HEAD]
        k = packed_ref[:, width + h * HEAD : width + (h + 1) * HEAD]
        v = packed_ref[:, 2 * width + h * HEAD : 2 * width + (h + 1) * HEAD]
        scores = jnp.where(allowed, mm_nt(q, k) * 0.125, -1e30)
        scores = jnp.exp(scores - jnp.max(scores, axis=-1, keepdims=True))
        weights = scores / jnp.sum(scores, axis=-1, keepdims=True)
        attend_ref[h] = weights
        mixture_ref[:, h * HEAD : (h + 1) * HEAD] = mm(weights.astype(BF16), v).astype(BF16)
    send(attend_ref)
    send(mixture_ref)
    x1 = x + mm(mixture_ref[...], w_out[...])
    mid_ref[...] = x1
    send(mid_ref)
    normed, _ = norm_parts(x1)
    up = mm(normed.astype(BF16), w_up[...])
    up_ref[...] = up
    send(up_ref)
    hidden, _ = gelu_parts(up)
    out = x1 + mm(hidden.astype(BF16), w_down[...])
    out_ref[...] = out
    send(out_ref)
    return out


def encode_back(grad, x, w_qkv, w_out, w_up, w_down, heads, res, packed_grad, put):
    packed_ref, attend_ref, mixture_ref, mid_ref, up_ref, _ = res
    width = x.shape[1]
    grad_b = grad.astype(BF16)
    hidden, slope = gelu_parts(up_ref[...])
    up_grad = (mm_nt(grad_b, w_down[...]).astype(BF16).astype(F32) * slope).astype(BF16)
    put(3, hidden.astype(BF16), grad_b)
    normed, rstd = norm_parts(mid_ref[...])
    put(2, normed.astype(BF16), up_grad)
    normed_grad = mm_nt(up_grad, w_up[...]).astype(BF16).astype(F32)
    mid_grad = grad + norm_back(normed_grad, normed, rstd)
    mid_b = mid_grad.astype(BF16)
    put(1, mixture_ref[...], mid_b)
    mix_grad = mm_nt(mid_b, w_out[...]).astype(BF16)
    for h in range(heads):
        q = packed_ref[:, h * HEAD : (h + 1) * HEAD]
        k = packed_ref[:, width + h * HEAD : width + (h + 1) * HEAD]
        v = packed_ref[:, 2 * width + h * HEAD : 2 * width + (h + 1) * HEAD]
        head_grad = mix_grad[:, h * HEAD : (h + 1) * HEAD]
        weights = attend_ref[h]
        weights_grad = mm_nt(head_grad, v).astype(BF16).astype(F32)
        v_grad = mm_tn(weights.astype(BF16), head_grad)
        inner = jnp.sum(weights_grad * weights, axis=-1, keepdims=True)
        scores_grad = (weights * (weights_grad - inner) * 0.125).astype(BF16)
        packed_grad[:, h * HEAD : (h + 1) * HEAD] = mm(scores_grad, k).astype(BF16)
        packed_grad[:, width + h * HEAD : width + (h + 1) * HEAD] = mm_tn(scores_grad, q).astype(BF16)
        packed_grad[:, 2 * width + h * HEAD : 2 * width + (h + 1) * HEAD] = v_grad.astype(BF16)
    normed, rstd = norm_parts(x)
    put(0, normed.astype(BF16), packed_grad[...])
    normed_grad = mm_nt(packed_grad[...], w_qkv[...]).astype(BF16).astype(F32)
    return mid_grad + norm_back(normed_grad, normed, rstd)


def put_rows(flat, base, a, b):
    rows, columns = a.shape[1], b.shape[1]
    chunks = columns // 128
    left = a.T
    for c in range(0, chunks, 3):
        part = mm(left, b[:, c * 128 : (c + 3) * 128]).astype(BF16).astype(F32)
        for j in range(3):
            flat[pl.ds(base + c + j, rows, stride=chunks), :] = part[:, j * 128 : (j + 1) * 128]


def same_tile():
    row = lax.broadcasted_iota(jnp.int32, (128, 128), 0)
    column = lax.broadcasted_iota(jnp.int32, (128, 128), 1)
    return lax.rem(row, 32) == lax.rem(column, 32)


class Late:
    def __init__(self, source, buffer, sem):
        self.copy = pltpu.make_async_copy(source, buffer, sem)
        self.buffer, self.here = buffer, False
        self.copy.start()

    def ref(self):
        if not self.here:
            self.copy.wait()
            self.here = True
        return self.buffer

    def __getitem__(self, index):
        return self.ref()[index]


class Early:
    def __init__(self, target, buffer, sem):
        self.copy = pltpu.make_async_copy(buffer, target, sem)
        self.buffer = buffer

    def __getitem__(self, index):
        return self.buffer[index]

    def __setitem__(self, index, value):
        self.buffer[index] = value

    def finish(self):
        self.copy.wait()


def send(ref):
    if isinstance(ref, Early):
        ref.copy.start()


def leave(pairs, sems):
    copies = [pltpu.make_async_copy(a, b, sems.at[i]) for i, (a, b) in enumerate(pairs)]
    for copy in copies:
        copy.start()
    for copy in copies:
        copy.wait()


def broadcast_out(block, out, sems):
    copies = [pltpu.make_async_copy(block, out.at[i], sems.at[i]) for i in range(16)]
    for copy in copies:
        copy.start()
    for copy in copies:
        copy.wait()


def tile_forward(where, ids, slide, *refs):
    ins, outs, bufs, obufs, block, sems, osems, bsems = cut(refs, 6, 8, 6, 7, 1, 1, 1, 1)
    late = [Late(r, b, sems[0].at[i]) for i, (r, b) in enumerate(zip(ins, bufs))]
    res = [Early(r, b, osems[0].at[i]) for i, (r, b) in enumerate(zip(outs[1:], obufs))]
    patches, patch_w, w_qkv, w_out, w_up, w_down = late
    x = mm(patches[...], patch_w[...])
    res[0][...] = x
    send(res[0])
    out = encode(x, same_tile(), w_qkv, w_out, w_up, w_down, HEADS, res[1:])
    normed, _ = norm_parts(out)
    total = (normed[0:32] + normed[32:64]) + (normed[64:96] + normed[96:128])
    total = (total * 0.25).astype(BF16)
    message = block[0]
    for c in range(3):
        message[c * 32 : (c + 1) * 32, :] = total[:, c * LANES : (c + 1) * LANES]
    row = lax.broadcasted_iota(jnp.int32, (16, LANES), 0)
    lane = lax.broadcasted_iota(jnp.int32, (16, LANES), 1)
    mine = (lane >= 32 * lax.rem(where[0], 4)) & (lane < 32 * lax.rem(where[0], 4) + 32)
    four = jnp.concatenate([ids[...].astype(F32)] * 4, axis=1)
    tail = jnp.where((row == 0) & mine, four, 0.0) + jnp.where(row == 1, slide[...].astype(F32), 0.0)
    message[96:112, :] = tail.astype(BF16)
    leave([(message, outs[0])], bsems[0])
    for r in res:
        r.finish()


def cut(refs, *sizes):
    parts, at = [], 0
    for size in sizes:
        parts.append(refs[at : at + size])
        at += size
    assert at == len(refs)
    return parts


def tails_of(tails):
    tails = tails.astype(F32)
    row = lax.broadcasted_iota(jnp.int32, tails.shape, 1)
    ids = jnp.sum(jnp.where(row == 0, tails, 0.0), axis=1)
    slides = jnp.sum(jnp.where(row == 1, tails, 0.0), axis=1)
    to = lax.broadcasted_iota(jnp.int32, (8, 32), 0)
    source = lax.broadcasted_iota(jnp.int32, (8, 32), 1)
    near = (source >= 4 * to) & (source < 4 * to + 4)
    ids = mm(jnp.where(near, 1.0, 0.0).astype(BF16), ids.astype(BF16))
    return ids, slides[:, 0:1]


def slots_of(ids, region):
    member = jnp.where(ids == region.astype(F32), 1.0, 0.0)
    row = lax.broadcasted_iota(jnp.int32, (128, 128), 0)
    column = lax.broadcasted_iota(jnp.int32, (128, 128), 1)
    within = mm(member.astype(BF16), jnp.where(row < column, 1.0, 0.0).astype(BF16))
    sums = jnp.sum(member, axis=1, keepdims=True)
    row8 = lax.broadcasted_iota(jnp.int32, (8, 8), 0)
    column8 = lax.broadcasted_iota(jnp.int32, (8, 8), 1)
    earlier = jnp.where(column8 < row8, 1.0, 0.0).astype(BF16)
    ahead = mm(earlier, jnp.broadcast_to(sums, (8, 128)).astype(BF16))
    count = jnp.sum(sums, axis=0, keepdims=True)
    return member, (within + ahead).astype(jnp.int32), count


def both_slots(ids, device):
    first = device - 4 * lax.rem(device // 4, 2)
    return first, [slots_of(ids, first + 4 * b) for b in range(2)]


def choice(slots, i):
    k = lax.broadcasted_iota(jnp.int32, (SLOTS, 128), 0)
    parts = [jnp.where((slot[i : i + 1] == k) & (member[i : i + 1] > 0.0), 1.0, 0.0) for member, slot, _ in slots]
    return jnp.concatenate(parts, axis=0).astype(BF16)


def usable_of(slots):
    k = lax.broadcasted_iota(jnp.int32, (SLOTS, 1), 0).astype(F32)
    return [k < count for _, _, count in slots]


def region_forward(where, *refs):
    ins, outs, bufs, rows, obufs, block, sems, osems, bsems, rsems = cut(refs, 5, 9, 4, 1, 7, 1, 1, 1, 1, 1)
    rows = rows[0]
    h = lax.rem(where[0] // 4, 2)
    arriving = []
    for i in range(16):
        base = i // 4 * 8 + i % 4
        for side, z in enumerate((h, 1 - h)):
            source = ins[0].at[i, 112 * side : 112 * side + 112, :]
            arriving.append(pltpu.make_async_copy(source, rows.at[base + 4 * z], rsems[0].at[2 * i + side]))
            arriving[-1].start()
    w_qkv, w_out, w_up, w_down = [Late(r, b, sems[0].at[i]) for i, (r, b) in enumerate(zip(ins[1:], bufs))]
    res = [Early(r, b, osems[0].at[i]) for i, (r, b) in enumerate(zip(outs[2:], obufs))]
    for copy in arriving:
        copy.wait()
    tails = pltpu.make_async_copy(rows.at[:, 96:112, :], outs[1], bsems[0].at[32])
    tails.start()
    ids, _ = tails_of(rows[:, 96:112, :])
    _, slots = both_slots(ids, where[0])
    parts = [jnp.zeros((2 * SLOTS, LANES), F32)] * 3
    for b in range(8):
        pick = choice(slots, b)
        for c in range(3):
            block_rows = rows[4 * b : 4 * b + 4, 32 * c : 32 * c + 32, :].reshape(128, LANES)
            parts[c] = parts[c] + mm(pick, block_rows)
    for c in range(3):
        res[0][:, c * LANES : (c + 1) * LANES] = parts[c]
    send(res[0])
    row = lax.broadcasted_iota(jnp.int32, (2 * SLOTS, 2 * SLOTS), 0)
    key = lax.broadcasted_iota(jnp.int32, (2 * SLOTS, 2 * SLOTS), 1)
    at = key.astype(F32)
    allowed = ((row < SLOTS) & (at < slots[0][2])) | ((row >= SLOTS) & (key >= SLOTS) & (at < slots[1][2] + SLOTS))
    out = encode(res[0][...], allowed, w_qkv, w_out, w_up, w_down, HEADS, res[1:])
    normed, _ = norm_parts(out)
    message = block[0]
    message[...] = jnp.zeros((8, LANES), F32)
    for b, usable in enumerate(usable_of(slots)):
        total = jnp.sum(jnp.where(usable, normed[b * SLOTS : (b + 1) * SLOTS], 0.0), axis=0, keepdims=True)
        embed = (total / slots[b][2]).astype(BF16).astype(F32)
        for c in range(3):
            message[3 * b + c : 3 * b + c + 1, :] = embed[:, c * LANES : (c + 1) * LANES]
    broadcast_out(message, outs[0], bsems[0])
    tails.wait()
    for r in res:
        r.finish()


def slide_step(embeds, slide_row, slide_col, label, censor, slide_in, w_qkv, w_out, w_up, w_down, head, losses, grads, res, packed_grad, scaling):
    emb = embeds[...]
    x = mm_nt(emb, slide_in[...])
    out = encode(x, slide_col == slide_row, w_qkv, w_out, w_up, w_down, H_SL, res)
    normed, rstd = norm_parts(out)
    sums, sizes, masks = [], [], []
    for s in range(SL_GRP):
        mask = jnp.where(slide_col == float(s), 1.0, 0.0)
        size = jnp.sum(mask, axis=0, keepdims=True)
        masks.append(mask)
        sizes.append(size)
        sums.append(jnp.sum(mask * normed, axis=0, keepdims=True) / size)
    pooled = jnp.concatenate(sums, axis=0).astype(BF16)
    logits = mm_nt(pooled, head[...])
    soft = jnp.log1p(jnp.exp(-jnp.abs(logits)))
    log_hazard = -(jnp.maximum(-logits, 0.0) + soft)
    log_stay = -(jnp.maximum(logits, 0.0) + soft)
    bin_at = lax.broadcasted_iota(jnp.int32, (SL_GRP, NBINS), 1).astype(F32)
    same = lax.broadcasted_iota(jnp.int32, (SL_GRP, SL_GRP), 0) == lax.broadcasted_iota(jnp.int32, (SL_GRP, SL_GRP), 1)
    bins = jnp.sum(jnp.where(same, label[...].astype(F32), 0.0), axis=1, keepdims=True)
    held = jnp.sum(jnp.where(same, censor[...].astype(F32), 0.0), axis=1, keepdims=True)
    at = jnp.where(bin_at == bins, 1.0, 0.0)
    before = jnp.where(bin_at < bins, 1.0, 0.0)
    past = jnp.sum(before * log_stay, axis=1, keepdims=True)
    seen = past + jnp.sum(at * log_hazard, axis=1, keepdims=True)
    lived = past + jnp.sum(at * log_stay, axis=1, keepdims=True)
    losses[...] = jnp.sum(jnp.where(same, -(1.0 - held) * seen - held * lived, 0.0), axis=0, keepdims=True)
    chance = 1.0 / (1.0 + jnp.exp(-logits))
    logit_grad = (scaling * (before * chance + at * (chance - (1.0 - held)))).astype(BF16)
    grads[5][...] = mm_tn(pooled, logit_grad).astype(BF16)
    pooled_grad = mm(logit_grad, head[...]).astype(BF16).astype(F32)
    grad = jnp.zeros_like(normed)
    for s in range(SL_GRP):
        grad = grad + masks[s] * (pooled_grad[s : s + 1] / sizes[s])
    grad = norm_back(grad, normed, rstd)

    def put(i, a, b):
        grads[i + 1][...] = mm_tn(a, b).astype(BF16)

    grad = encode_back(grad, x, w_qkv, w_out, w_up, w_down, H_SL, res, packed_grad, put).astype(BF16)
    grads[0][...] = mm_tn(emb, grad).astype(BF16)
    return mm(grad, slide_in[...]).astype(BF16)


def region_backward(scaling, where, label, censor, *refs):
    ins, outs, bufs, obufs, extra, sems, osems = cut(refs, 19, 16, 19, 16, 10, 1, 1)
    h = lax.rem(where[0] // 4, 2)
    order = list(range(8)) + [18, 13, 17, 16, 14, 15, 9, 8, 10, 11, 12]
    late = dict()
    for i in list(dict.fromkeys(order)):
        late[i] = Late(ins[i], bufs[i], sems[0].at[i])
    early = []
    for i, (r, b) in enumerate(zip(outs, obufs)):
        early.append(Early(r, b, osems[0].at[i]) if i != 1 else b)
    message, tails = late[0], late[1]
    slide_weights = [late[i] for i in range(2, 8)]
    w_qkv, w_out, w_up, w_down = [late[i] for i in range(8, 12)]
    x_ref, res = late[12], [late[i] for i in range(13, 19)]
    losses, spread, pairs, slide_grads = early[0], early[1], early[2:10], early[10:16]
    packed_grad, slide_packed_grad, embeds, placed = extra[:4]
    ids, slide_col = tails_of(tails[...])
    rows32 = lax.broadcasted_iota(jnp.int32, (32, 32), 0)
    columns32 = lax.broadcasted_iota(jnp.int32, (32, 32), 1)
    slide_row = jnp.sum(jnp.where(rows32 == columns32, slide_col, 0.0), axis=0, keepdims=True)
    arrived = message[...]
    at = lax.broadcasted_iota(jnp.int32, arrived.shape, 1)
    for b in range(2):
        for c in range(3):
            part = jnp.sum(jnp.where(at == 3 * b + c, arrived, 0.0), axis=1)
            for y in range(4):
                placed[8 * y + 4 * b : 8 * y + 4 * b + 4, c * LANES : (c + 1) * LANES] = part[4 * y : 4 * y + 4]
    embeds[...] = placed[...].astype(BF16)
    cots = slide_step(
        embeds, slide_row, slide_col, label, censor, *slide_weights, losses, slide_grads, extra[4:10], slide_packed_grad, scaling
    ).astype(F32)
    for g in [losses] + slide_grads:
        send(g)
    first, slots = both_slots(ids, where[0])
    grads = []
    for b, usable in enumerate(usable_of(slots)):
        mine = lax.broadcasted_iota(jnp.int32, (32, 1), 0) == first + 4 * b
        own = jnp.sum(jnp.where(mine, cots, 0.0), axis=0, keepdims=True)
        grads.append(jnp.where(usable, own / slots[b][2], 0.0))
    grad = jnp.concatenate(grads, axis=0)
    normed, rstd = norm_parts(res[5][...])
    grad = norm_back(grad, normed, rstd)

    def put(i, a, b):
        for at, value in ((6 - 2 * i, a), (7 - 2 * i, b)):
            pairs[at][...] = value
            send(pairs[at])

    grad = encode_back(grad, x_ref[...], w_qkv, w_out, w_up, w_down, HEADS, res, packed_grad, put).astype(BF16)
    for b in range(8):
        spread[b] = mm_tn(choice(slots, b), grad).astype(BF16)
    leave([(spread.at[2 * y + h], outs[1].at[y]) for y in range(4)], sems[0])
    for e in early:
        if e is not spread:
            e.finish()


def two_halves(flat, runs, core, halves, stage, sems):
    run = 32 * 63
    copies = []
    for side in range(2):
        which = core if side == 0 else 1 - core
        for z in runs:
            start = pl.multiple_of((2 * z + which) * run, 32)
            stage[side, z * run : (z + 1) * run, :] = flat[pl.ds(start, run), :].astype(BF16)
            part = pl.ds(z * run, run)
            copies.append(pltpu.make_async_copy(stage.at[side, part, :], halves[side].at[part, :], sems.at[side, z]))
            copies[-1].start()
    return copies


def region_weights(core, where, *refs):
    ins, halves, bufs, flat, run_buf, stage, sems, osems = cut(refs, 8, 2, 8, 1, 1, 1, 1, 1)
    late = [Late(r, b, sems[0].at[i]) for i, (r, b) in enumerate(zip(ins, bufs))]
    hidden, grad, second, up_grad, mixture, mid_grad, first, packed_grad = late
    put_rows(flat[0], 9216, hidden[...], grad[...])
    put_rows(flat[0], 4608, second[...], up_grad[...])
    put_rows(flat[0], 3456, mixture[...], mid_grad[...])
    put_rows(flat[0], 0, first[...], packed_grad[...])
    h = lax.rem(where[0] // 4, 2)
    copies = []
    for side in range(2):
        which = core[0] if side == 0 else 1 - core[0]
        for z in range(4):
            for y in range(4):
                start = pl.multiple_of((2 * z + which) * 1728 + y * 432 + h * 216, 8)
                run_buf[0][y * 216 : (y + 1) * 216, :] = flat[0][pl.ds(start, 216), :]
            part = pl.ds(z * 864, 864)
            stage[0][side, z * 864 : (z + 1) * 864, :] = run_buf[0][...].astype(BF16)
            copies.append(pltpu.make_async_copy(stage[0].at[side, part, :], halves[side].at[part, :], osems[0].at[side, z]))
            copies[-1].start()
    for copy in copies:
        copy.wait()


def tile_backward(core, ids, *refs):
    ins, _, halves, bufs, packed_grad, flat, stage, sems, osems = cut(refs, 14, 1, 2, 14, 1, 1, 1, 1, 1)
    late = [Late(ins[i], bufs[i], sems[0].at[i]) for i in (0, 13, 6, 12, 11, 5, 10, 4, 9, 8, 3, 7, 1, 2)]
    late = dict(zip((0, 13, 6, 12, 11, 5, 10, 4, 9, 8, 3, 7, 1, 2), late))
    arrived, patches, slide_rows = late[0], late[1], late[2]
    w_qkv, w_out, w_up, w_down = [late[i] for i in range(3, 7)]
    x_ref, res = late[7], [late[i] for i in range(8, 14)]
    rows32 = lax.broadcasted_iota(jnp.int32, (32, 32), 0)
    columns32 = lax.broadcasted_iota(jnp.int32, (32, 32), 1)
    assign = jnp.sum(jnp.where(rows32 == columns32, ids[...].astype(F32), 0.0), axis=1, keepdims=True)
    cot = jnp.zeros((32, D), F32)
    for i in range(16):
        region = float(i // 4 * 8 + i % 4)
        cot = cot + jnp.where((assign == region) | (assign == region + 4.0), arrived[i].astype(F32), 0.0)
    cot = cot * 0.25
    grad = jnp.concatenate([cot] * PATCHES, axis=0)
    normed, rstd = norm_parts(res[5][...])
    grad = norm_back(grad, normed, rstd)
    bases = (2304, 5760, 6912, 11520)

    leaving = []

    def put(i, a, b):
        put_rows(flat[0], bases[i], a, b)
        if i == 2:
            leaving.extend(two_halves(flat[0], (2, 3), core[0], halves, stage[0], osems[0]))

    grad = encode_back(grad, x_ref[...], w_qkv, w_out, w_up, w_down, HEADS, res, packed_grad[0], put)
    for side in range(2):
        which = core[0] if side == 0 else 1 - core[0]
        stage[0][side, 8064:8144, :] = slide_rows.ref()[which]
        part = pl.ds(8064, 80)
        leaving.append(pltpu.make_async_copy(stage[0].at[side, part, :], halves[side].at[part, :], osems[0].at[side, 4]))
        leaving[-1].start()
    put_rows(flat[0], 0, patches[...], grad.astype(BF16))
    leaving.extend(two_halves(flat[0], (0, 1), core[0], halves, stage[0], osems[0]))
    for copy in leaving:
        copy.wait()


def fold(rows, pad, tail, *refs):
    mine, got = refs[:2]
    refs = refs[2 + tail :]
    if tail:
        out, extra = refs[:2]
        refs = refs[2:]
    else:
        out = refs[0]
        refs = refs[1:]
    a, b, total, stage, chunks, sems, osems = refs[:7]
    planes = 2 if tail else 1
    run = 16 * planes * rows
    arriving = []
    for z in range(4 + tail):
        part = pl.ds(z * run, run if z < 4 else 80)
        for side, (source, buffer) in enumerate(((mine, a), (got, b))):
            arriving.append(pltpu.make_async_copy(source.at[part, :], buffer.at[part, :], sems.at[side, z]))
            arriving[-1].start()
    for z in range(4):
        arriving[2 * z].wait()
        arriving[2 * z + 1].wait()
        part = pl.ds(z * run, run)
        total[part, :] = a[part, :].astype(F32) + b[part, :].astype(F32)
    leaving = []
    if tail:
        arriving[8].wait()
        arriving[9].wait()
        part = pl.ds(4 * run, 80)
        refs[7][...] = (a[part, :].astype(F32) + b[part, :].astype(F32)).astype(BF16)
        leaving.append(pltpu.make_async_copy(refs[7], extra, osems.at[16]))
        leaving[-1].start()
    if pad:
        stage[4 * planes * rows :, :] = jnp.zeros((pad, LANES), F32)
    for y in range(4):
        for x in range(4):
            for z in range(4):
                for h in range(planes):
                    source = (z * 16 * planes + y * 4 * planes + h * 4 + x) * rows
                    target = (z * planes + h) * rows
                    stage[target : target + rows, :] = total[source : source + rows, :]
            chunks[y * 4 + x] = stage[...].astype(BF16)
            leaving.append(pltpu.make_async_copy(chunks.at[y * 4 + x], out.at[y * 4 + x], osems.at[y * 4 + x]))
            leaving[-1].start()
    for copy in leaving:
        copy.wait()


def plane_sum(parts, out, buffer, total, sems):
    copies = []
    for i in range(2):
        part = pl.ds(i * 112, 112)
        copies.append(pltpu.make_async_copy(parts.at[:, part, :], buffer.at[:, part, :], sems.at[i]))
        copies[-1].start()
    for i in range(2):
        copies[i].wait()
        rows = slice(i * 112, (i + 1) * 112)
        value = buffer[0, rows, :].astype(F32)
        for j in range(1, 16):
            value = value + buffer[j, rows, :].astype(F32)
        total[rows, :] = value
    leave([(total, out)], sems)


def merge(where, tile_in, region_in, slide_in, out, tile_buf, region_buf, slide_buf, total, slide_total, stage, chunks, sems, osems):
    tile_late = Late(tile_in, tile_buf, sems.at[0])
    region_late = Late(region_in, region_buf, sems.at[1])
    slide_late = Late(slide_in, slide_buf, sems.at[2])
    slide_total[...] = slide_late[...].astype(F32)

    for start in range(0, 512, 64):
        value = tile_late[0, start : start + 64, :].astype(F32)
        for i in range(1, 16):
            value = value + tile_late[i, start : start + 64, :].astype(F32)
        total[start : start + 64, :] = value
    region_total = region_late.ref()
    h = lax.rem(where[0] // 4, 2)
    leaving = []
    for i in range(8):
        stage[0:63, :] = total[i * 63 : (i + 1) * 63, :]
        stage[63:64, :] = jnp.zeros((1, LANES), F32)
        rows = region_total[i // 2 * 54 : (i // 2 + 1) * 54, :]
        stage[64:118, :] = jnp.where(h == i % 2, rows, 0.0)
        stage[118:128, :] = slide_total[i * 10 : (i + 1) * 10, :]
        chunks[i] = stage[...].astype(BF16)
        leaving.append(pltpu.make_async_copy(chunks.at[i], out.at[i], osems.at[i]))
        leaving[-1].start()
    for copy in leaving:
        copy.wait()


def call(kernel, macs, outs, scratch, inputs, scalars=0, whole=0, mebibytes=60):
    specs = [pl.BlockSpec(memory_space=pltpu.SMEM)] * scalars
    specs += [pl.BlockSpec(memory_space=pltpu.VMEM)] * whole
    specs += [pl.BlockSpec(memory_space=pl.ANY)] * (len(inputs) - scalars - whole)
    moved = sum(math.prod(a.shape) * a.dtype.itemsize for a in inputs) + sum(math.prod(a) * jnp.dtype(k).itemsize for a, k in outs)
    cost = pl.CostEstimate(flops=2 * macs, bytes_accessed=moved, transcendentals=0)
    return pl.pallas_call(
        kernel,
        out_shape=[jax.ShapeDtypeStruct(shape, kind) for shape, kind in outs],
        in_specs=specs,
        out_specs=[pl.BlockSpec(memory_space=pl.ANY)] * len(outs),
        scratch_shapes=[pltpu.VMEM(*item) if isinstance(item, tuple) else item for item in scratch],
        compiler_params=pltpu.CompilerParams(vmem_limit_bytes=mebibytes * 1024 * 1024),
        cost_estimate=cost,
    )(*inputs)


def like(arrays):
    return [(a.shape, a.dtype) for a in arrays]


def semaphores(*shape):
    return pltpu.SemaphoreType.DMA(shape)


def residuals(tokens, width, hidden, heads):
    return [
        ((tokens, 3 * width), BF16),
        ((heads, tokens, tokens), F32),
        ((tokens, width), BF16),
        ((tokens, width), F32),
        ((tokens, hidden), F32),
        ((tokens, width), F32),
    ]


def index_of(z, core, y, z_hi, x):
    return (z * 2 + core) * 32 + y * 8 + z_hi * 4 + x


PLANES = [[index_of(z, c, y, h, x) for y in range(4) for x in range(4)] for z in range(4) for c in range(2) for h in range(2)]
COLUMNS = [[index_of(z, c, y, h, x) for z in range(4) for h in range(2)] for c in range(2) for y in range(4) for x in range(4)]
OTHER_CORE = [(g, g + 1 - 2 * (g % 2)) for g in range(8)]
OTHER_PLANE = [(d, d + 4 - 8 * (d // 4 % 2)) for d in range(32)]
ALL = ("grp", "dev")


def exchange(array, groups):
    return lax.all_to_all(array, ALL, 0, 0, axis_index_groups=groups)


def folded(mine, other, rows, pad, tail, after=()):
    got = lax.ppermute(other, "grp", OTHER_CORE)
    planes = 1 + tail
    height = 64 * planes * rows + 80 * tail
    chunk = 4 * planes * rows + pad
    return call(
        functools.partial(fold, rows, pad, tail),
        4 * US,
        [((16, chunk, LANES), BF16)] + [((80, LANES), BF16)] * tail,
        [((height, LANES), BF16)] * 2
        + [((64 * planes * rows, LANES), F32), ((chunk, LANES), F32), ((16, chunk, LANES), BF16)]
        + [semaphores(2, 5), semaphores(17)]
        + [((80, LANES), BF16)] * tail,
        (mine, got) + after,
        mebibytes=24 if tail else 60,
    )


def body(
    patches,
    tile_region,
    region_slide,
    bin_label,
    censored,
    patch_w,
    tile_qkv,
    tile_out,
    tile_up,
    tile_down,
    region_qkv,
    region_out,
    region_up,
    region_down,
    slide_in,
    slide_qkv,
    slide_out,
    slide_up,
    slide_down,
    slide_head,
):
    member_index = lax.axis_index("dev").astype(jnp.int32)
    where = member_index.reshape(1)
    core = lax.rem(lax.axis_index("grp").astype(jnp.int32), 2).reshape(1)
    scaling = 1.0 / (bin_label.shape[1] * lax.axis_size("grp"))
    tokens = patches.transpose(1, 0, 2).reshape(128, 768)
    tile_res = [((128, D), F32)] + residuals(128, D, FF, HEADS)
    ins = (tokens, patch_w, tile_qkv, tile_out, tile_up, tile_down)
    message, *tile_kept = call(
        tile_forward,
        7 * US,
        [((112, LANES), BF16)] + tile_res,
        like(ins) + tile_res + [((112, LANES), BF16), semaphores(6), semaphores(7), semaphores(1)],
        (where, tile_region, region_slide) + ins,
        scalars=1,
        whole=2,
    )
    both = jnp.concatenate([message, lax.ppermute(message, "dev", OTHER_PLANE)], axis=0)
    rows = exchange(jnp.broadcast_to(both[None], (16, 224, LANES)), PLANES)
    region_res = [((2 * SLOTS, D), F32)] + residuals(2 * SLOTS, D, FF, HEADS)
    ins = (region_qkv, region_out, region_up, region_down)
    message, tails, *region_kept = call(
        region_forward,
        6 * US,
        [((16, 8, LANES), F32), ((32, 16, LANES), BF16)] + region_res,
        like(ins)
        + [((32, 112, LANES), BF16)]
        + region_res
        + [((8, LANES), F32), semaphores(4), semaphores(7), semaphores(33), semaphores(32)],
        (where, rows) + ins,
        scalars=1,
    )
    all_regions = exchange(message, PLANES)
    slide_weights = (slide_in, slide_qkv, slide_out, slide_up, slide_down, slide_head)
    widths = (FF, D, D, FF, D, D, D, 3 * D)
    pairs = [((2 * SLOTS, n), BF16) for n in widths]
    losses_out = [((1, SL_GRP), F32)]
    outs = losses_out + [((4, 128, D), BF16)] + pairs + like(slide_weights)
    buffers = losses_out + [((8, 128, D), BF16)] + pairs + like(slide_weights)
    ins = (all_regions, tails, slide_in.T) + slide_weights[1:5] + (slide_head.T,) + (region_qkv, region_out, region_up, region_down) + tuple(region_kept)
    losses, spread, *rest = call(
        functools.partial(region_backward, scaling),
        12 * US,
        outs,
        like(ins)
        + buffers
        + [((2 * SLOTS, 3 * D), BF16), ((32, 3 * D_SL), BF16), ((32, D), BF16), ((32, D), F32)]
        + residuals(32, D_SL, D_SL, H_SL)
        + [semaphores(19), semaphores(16)],
        (where, bin_label, censored) + ins,
        scalars=1,
        whole=2,
    )
    arrived = exchange(spread.reshape(16, 32, D), PLANES)
    ins = tuple(rest[:8])
    mine, other = call(
        region_weights,
        5 * US,
        [((3456, LANES), BF16)] * 2,
        like(ins)
        + [((13824, LANES), F32), ((864, LANES), F32), ((2, 3456, LANES), BF16), semaphores(8), semaphores(2, 4)],
        (core, where) + ins,
        scalars=2,
    )
    (region_chunks,) = folded(mine, other, 54, 8, 0)
    region_parts = exchange(region_chunks, PLANES)
    (region_sums,) = call(
        plane_sum,
        20 * US,
        [((224, LANES), F32)],
        like((region_parts,)) + [((224, LANES), F32), semaphores(2)],
        (region_parts,),
        mebibytes=24,
    )
    slide_flat = jnp.concatenate([g.astype(F32).reshape(-1) for g in rest[8:]]).reshape(4, 2, 4, 2, 4, 1155)
    y, x = member_index // 8, lax.rem(member_index, 4)
    zero = jnp.zeros((), jnp.int32)
    slide_rows = lax.dynamic_slice(slide_flat, (zero, zero, y, zero, x, zero), (4, 2, 1, 2, 1, 1155))
    slide_rows = slide_rows.reshape(4, 2, 2, 1155).transpose(1, 0, 2, 3)
    slide_rows = jnp.pad(slide_rows, ((0, 0), (0, 0), (0, 0), (0, 125))).astype(BF16).reshape(2, 80, LANES)
    ins = (arrived, tokens, slide_rows, tile_qkv, tile_out, tile_up, tile_down) + tuple(tile_kept)
    mine, other = call(
        tile_backward,
        13 * US,
        [((8144, LANES), BF16)] * 2,
        like(ins)
        + [((128, 3 * D), BF16), ((16128, LANES), F32), ((2, 8144, LANES), BF16), semaphores(14), semaphores(2, 5)],
        (core, tile_region) + ins + (region_chunks,),
        scalars=1,
        whole=1,
    )
    tile_chunks, slide_sums = folded(mine, other, 63, 8, 1, (region_sums,))
    tile_parts = exchange(tile_chunks, PLANES)
    ins = (tile_parts, region_sums, slide_sums)
    (last,) = call(
        merge,
        3 * US,
        [((8, 128, LANES), BF16)],
        like(ins)
        + [((512, LANES), F32), ((80, LANES), F32), ((128, LANES), F32), ((8, 128, LANES), BF16)]
        + [semaphores(3), semaphores(8)],
        (where,) + ins,
        scalars=1,
        mebibytes=24,
    )
    total = jnp.sum(exchange(last, COLUMNS).astype(F32), axis=0)
    tile_result = total[0:63].reshape(8064)
    region_result = total[64:118].reshape(6912)
    slide_result = total[118:128].reshape(1280)[:1155] * 0.5
    return (losses, tile_result, region_result, slide_result)


def solution(mesh):
    placed = (P(ALL, None, None), P("grp", "dev"), P("grp", "dev"), P("grp", None), P("grp", None)) + (P(),) * 15
    return jax.shard_map(
        body,
        mesh=mesh,
        in_specs=placed,
        out_specs=(P("grp", None), P(ALL), P(ALL), P(ALL)),
        check_vma=False,
    )
```

```python
import functools
import math

import jax
import jax.numpy as jnp
from jax import lax
from jax.experimental import pallas as pl
from jax.experimental.pallas import tpu as pltpu
from jax.sharding import PartitionSpec as P

D = 384
HEADS = 6
FF = 1536
PATCHES = 4
SLOTS = 64
D_SL = 192
H_SL = 3
NBINS = 4
SL_GRP = 4
HEAD = 64
F32 = jnp.float32
BF16 = jnp.bfloat16
LANES = 128
US = 550_000_000
GELU_C = math.sqrt(2.0 / math.pi)


def mm(a, b):
    return jnp.dot(a, b, preferred_element_type=F32)


def mm_nt(a, b):
    return lax.dot_general(a, b, (((1,), (1,)), ((), ())), preferred_element_type=F32)


def mm_tn(a, b):
    return lax.dot_general(a, b, (((0,), (0,)), ((), ())), preferred_element_type=F32)


def norm_parts(x):
    average = jnp.mean(x, axis=-1, keepdims=True)
    centred = x - average
    variance = jnp.mean(centred * centred, axis=-1, keepdims=True)
    rstd = lax.rsqrt(variance + 1e-06)
    return centred * rstd, rstd


def norm_back(grad, normed, rstd):
    first = jnp.mean(grad, axis=-1, keepdims=True)
    second = jnp.mean(grad * normed, axis=-1, keepdims=True)
    return rstd * (grad - first - normed * second)


def gelu_parts(x):
    t = jnp.tanh(GELU_C * (x + 0.044715 * (x * x * x)))
    value = 0.5 * x * (1.0 + t)
    slope = 0.5 * (1.0 + t) + 0.5 * x * (1.0 - t * t) * (GELU_C * (1.0 + 3.0 * 0.044715 * (x * x)))
    return value, slope


def encode(x, allowed, w_qkv, w_out, w_up, w_down, heads, res):
    packed_ref, attend_ref, mixture_ref, mid_ref, up_ref, out_ref = res
    width = x.shape[1]
    normed, _ = norm_parts(x)
    packed_ref[...] = mm(normed.astype(BF16), w_qkv[...]).astype(BF16)
    send(packed_ref)
    for h in range(heads):
        q = packed_ref[:, h * HEAD : (h + 1) * HEAD]
        k = packed_ref[:, width + h * HEAD : width + (h + 1) * HEAD]
        v = packed_ref[:, 2 * width + h * HEAD : 2 * width + (h + 1) * HEAD]
        scores = jnp.where(allowed, mm_nt(q, k) * 0.125, -1e30)
        scores = jnp.exp(scores - jnp.max(scores, axis=-1, keepdims=True))
        weights = scores / jnp.sum(scores, axis=-1, keepdims=True)
        attend_ref[h] = weights
        mixture_ref[:, h * HEAD : (h + 1) * HEAD] = mm(weights.astype(BF16), v).astype(BF16)
    send(attend_ref)
    send(mixture_ref)
    x1 = x + mm(mixture_ref[...], w_out[...])
    mid_ref[...] = x1
    send(mid_ref)
    normed, _ = norm_parts(x1)
    up = mm(normed.astype(BF16), w_up[...])
    up_ref[...] = up
    send(up_ref)
    hidden, _ = gelu_parts(up)
    out = x1 + mm(hidden.astype(BF16), w_down[...])
    out_ref[...] = out
    send(out_ref)
    return out


def encode_back(grad, x, w_qkv, w_out, w_up, w_down, heads, res, packed_grad, put):
    packed_ref, attend_ref, mixture_ref, mid_ref, up_ref, _ = res
    width = x.shape[1]
    grad_b = grad.astype(BF16)
    hidden, slope = gelu_parts(up_ref[...])
    up_grad = (mm_nt(grad_b, w_down[...]).astype(BF16).astype(F32) * slope).astype(BF16)
    put(3, hidden.astype(BF16), grad_b)
    normed, rstd = norm_parts(mid_ref[...])
    put(2, normed.astype(BF16), up_grad)
    normed_grad = mm_nt(up_grad, w_up[...]).astype(BF16).astype(F32)
    mid_grad = grad + norm_back(normed_grad, normed, rstd)
    mid_b = mid_grad.astype(BF16)
    put(1, mixture_ref[...], mid_b)
    mix_grad = mm_nt(mid_b, w_out[...]).astype(BF16)
    for h in range(heads):
        q = packed_ref[:, h * HEAD : (h + 1) * HEAD]
        k = packed_ref[:, width + h * HEAD : width + (h + 1) * HEAD]
        v = packed_ref[:, 2 * width + h * HEAD : 2 * width + (h + 1) * HEAD]
        head_grad = mix_grad[:, h * HEAD : (h + 1) * HEAD]
        weights = attend_ref[h]
        weights_grad = mm_nt(head_grad, v).astype(BF16).astype(F32)
        v_grad = mm_tn(weights.astype(BF16), head_grad)
        inner = jnp.sum(weights_grad * weights, axis=-1, keepdims=True)
        scores_grad = (weights * (weights_grad - inner) * 0.125).astype(BF16)
        packed_grad[:, h * HEAD : (h + 1) * HEAD] = mm(scores_grad, k).astype(BF16)
        packed_grad[:, width + h * HEAD : width + (h + 1) * HEAD] = mm_tn(scores_grad, q).astype(BF16)
        packed_grad[:, 2 * width + h * HEAD : 2 * width + (h + 1) * HEAD] = v_grad.astype(BF16)
    normed, rstd = norm_parts(x)
    put(0, normed.astype(BF16), packed_grad[...])
    normed_grad = mm_nt(packed_grad[...], w_qkv[...]).astype(BF16).astype(F32)
    return mid_grad + norm_back(normed_grad, normed, rstd)


def put_rows(flat, base, a, b):
    rows, columns = a.shape[1], b.shape[1]
    chunks = columns // 128
    left = a.T
    for c in range(0, chunks, 3):
        part = mm(left, b[:, c * 128 : (c + 3) * 128]).astype(BF16).astype(F32)
        for j in range(3):
            flat[pl.ds(base + c + j, rows, stride=chunks), :] = part[:, j * 128 : (j + 1) * 128]


def same_tile():
    row = lax.broadcasted_iota(jnp.int32, (128, 128), 0)
    column = lax.broadcasted_iota(jnp.int32, (128, 128), 1)
    return lax.rem(row, 32) == lax.rem(column, 32)


class Late:
    def __init__(self, source, buffer, sem):
        self.copy = pltpu.make_async_copy(source, buffer, sem)
        self.buffer, self.here = buffer, False
        self.copy.start()

    def ref(self):
        if not self.here:
            self.copy.wait()
            self.here = True
        return self.buffer

    def __getitem__(self, index):
        return self.ref()[index]


class Early:
    def __init__(self, target, buffer, sem):
        self.copy = pltpu.make_async_copy(buffer, target, sem)
        self.buffer = buffer

    def __getitem__(self, index):
        return self.buffer[index]

    def __setitem__(self, index, value):
        self.buffer[index] = value

    def finish(self):
        self.copy.wait()


def send(ref):
    if isinstance(ref, Early):
        ref.copy.start()


def leave(pairs, sems):
    copies = [pltpu.make_async_copy(a, b, sems.at[i]) for i, (a, b) in enumerate(pairs)]
    for copy in copies:
        copy.start()
    for copy in copies:
        copy.wait()


def broadcast_out(block, out, sems):
    copies = [pltpu.make_async_copy(block, out.at[i], sems.at[i]) for i in range(16)]
    for copy in copies:
        copy.start()
    for copy in copies:
        copy.wait()


def tile_forward(where, ids, slide, *refs):
    ins, outs, bufs, obufs, block, sems, osems, bsems = cut(refs, 6, 8, 6, 7, 1, 1, 1, 1)
    late = [Late(r, b, sems[0].at[i]) for i, (r, b) in enumerate(zip(ins, bufs))]
    res = [Early(r, b, osems[0].at[i]) for i, (r, b) in enumerate(zip(outs[1:], obufs))]
    patches, patch_w, w_qkv, w_out, w_up, w_down = late
    x = mm(patches[...], patch_w[...])
    res[0][...] = x
    send(res[0])
    out = encode(x, same_tile(), w_qkv, w_out, w_up, w_down, HEADS, res[1:])
    normed, _ = norm_parts(out)
    total = (normed[0:32] + normed[32:64]) + (normed[64:96] + normed[96:128])
    total = (total * 0.25).astype(BF16)
    message = block[0]
    for c in range(3):
        message[c * 32 : (c + 1) * 32, :] = total[:, c * LANES : (c + 1) * LANES]
    row = lax.broadcasted_iota(jnp.int32, (16, LANES), 0)
    lane = lax.broadcasted_iota(jnp.int32, (16, LANES), 1)
    mine = (lane >= 32 * lax.rem(where[0], 4)) & (lane < 32 * lax.rem(where[0], 4) + 32)
    four = jnp.concatenate([ids[...].astype(F32)] * 4, axis=1)
    tail = jnp.where((row == 0) & mine, four, 0.0) + jnp.where(row == 1, slide[...].astype(F32), 0.0)
    message[96:112, :] = tail.astype(BF16)
    leave([(message, outs[0])], bsems[0])
    for r in res:
        r.finish()


def cut(refs, *sizes):
    parts, at = [], 0
    for size in sizes:
        parts.append(refs[at : at + size])
        at += size
    assert at == len(refs)
    return parts


def tails_of(tails):
    tails = tails.astype(F32)
    row = lax.broadcasted_iota(jnp.int32, tails.shape, 1)
    ids = jnp.sum(jnp.where(row == 0, tails, 0.0), axis=1)
    slides = jnp.sum(jnp.where(row == 1, tails, 0.0), axis=1)
    to = lax.broadcasted_iota(jnp.int32, (8, 32), 0)
    source = lax.broadcasted_iota(jnp.int32, (8, 32), 1)
    near = (source >= 4 * to) & (source < 4 * to + 4)
    ids = mm(jnp.where(near, 1.0, 0.0).astype(BF16), ids.astype(BF16))
    return ids, slides[:, 0:1]


def slots_of(ids, region):
    member = jnp.where(ids == region.astype(F32), 1.0, 0.0)
    row = lax.broadcasted_iota(jnp.int32, (128, 128), 0)
    column = lax.broadcasted_iota(jnp.int32, (128, 128), 1)
    within = mm(member.astype(BF16), jnp.where(row < column, 1.0, 0.0).astype(BF16))
    sums = jnp.sum(member, axis=1, keepdims=True)
    row8 = lax.broadcasted_iota(jnp.int32, (8, 8), 0)
    column8 = lax.broadcasted_iota(jnp.int32, (8, 8), 1)
    earlier = jnp.where(column8 < row8, 1.0, 0.0).astype(BF16)
    ahead = mm(earlier, jnp.broadcast_to(sums, (8, 128)).astype(BF16))
    count = jnp.sum(sums, axis=0, keepdims=True)
    return member, (within + ahead).astype(jnp.int32), count


def both_slots(ids, device):
    first = device - 4 * lax.rem(device // 4, 2)
    return first, [slots_of(ids, first + 4 * b) for b in range(2)]


def choice(slots, i):
    k = lax.broadcasted_iota(jnp.int32, (SLOTS, 128), 0)
    parts = [jnp.where((slot[i : i + 1] == k) & (member[i : i + 1] > 0.0), 1.0, 0.0) for member, slot, _ in slots]
    return jnp.concatenate(parts, axis=0).astype(BF16)


def usable_of(slots):
    k = lax.broadcasted_iota(jnp.int32, (SLOTS, 1), 0).astype(F32)
    return [k < count for _, _, count in slots]


def region_forward(where, *refs):
    ins, outs, bufs, rows, obufs, block, sems, osems, bsems, rsems = cut(refs, 5, 9, 4, 1, 7, 1, 1, 1, 1, 1)
    rows = rows[0]
    h = lax.rem(where[0] // 4, 2)
    arriving = []
    for i in range(16):
        base = i // 4 * 8 + i % 4
        for side, z in enumerate((h, 1 - h)):
            source = ins[0].at[i, 112 * side : 112 * side + 112, :]
            arriving.append(pltpu.make_async_copy(source, rows.at[base + 4 * z], rsems[0].at[2 * i + side]))
            arriving[-1].start()
    w_qkv, w_out, w_up, w_down = [Late(r, b, sems[0].at[i]) for i, (r, b) in enumerate(zip(ins[1:], bufs))]
    res = [Early(r, b, osems[0].at[i]) for i, (r, b) in enumerate(zip(outs[2:], obufs))]
    for copy in arriving:
        copy.wait()
    tails = pltpu.make_async_copy(rows.at[:, 96:112, :], outs[1], bsems[0].at[32])
    tails.start()
    ids, _ = tails_of(rows[:, 96:112, :])
    _, slots = both_slots(ids, where[0])
    parts = [jnp.zeros((2 * SLOTS, LANES), F32)] * 3
    for b in range(8):
        pick = choice(slots, b)
        for c in range(3):
            block_rows = rows[4 * b : 4 * b + 4, 32 * c : 32 * c + 32, :].reshape(128, LANES)
            parts[c] = parts[c] + mm(pick, block_rows)
    for c in range(3):
        res[0][:, c * LANES : (c + 1) * LANES] = parts[c]
    send(res[0])
    row = lax.broadcasted_iota(jnp.int32, (2 * SLOTS, 2 * SLOTS), 0)
    key = lax.broadcasted_iota(jnp.int32, (2 * SLOTS, 2 * SLOTS), 1)
    at = key.astype(F32)
    allowed = ((row < SLOTS) & (at < slots[0][2])) | ((row >= SLOTS) & (key >= SLOTS) & (at < slots[1][2] + SLOTS))
    out = encode(res[0][...], allowed, w_qkv, w_out, w_up, w_down, HEADS, res[1:])
    normed, _ = norm_parts(out)
    message = block[0]
    message[...] = jnp.zeros((8, LANES), F32)
    for b, usable in enumerate(usable_of(slots)):
        total = jnp.sum(jnp.where(usable, normed[b * SLOTS : (b + 1) * SLOTS], 0.0), axis=0, keepdims=True)
        embed = (total / slots[b][2]).astype(BF16).astype(F32)
        for c in range(3):
            message[3 * b + c : 3 * b + c + 1, :] = embed[:, c * LANES : (c + 1) * LANES]
    broadcast_out(message, outs[0], bsems[0])
    tails.wait()
    for r in res:
        r.finish()


def slide_step(embeds, slide_row, slide_col, label, censor, slide_in, w_qkv, w_out, w_up, w_down, head, losses, grads, res, packed_grad, scaling):
    emb = embeds[...]
    x = mm_nt(emb, slide_in[...])
    out = encode(x, slide_col == slide_row, w_qkv, w_out, w_up, w_down, H_SL, res)
    normed, rstd = norm_parts(out)
    sums, sizes, masks = [], [], []
    for s in range(SL_GRP):
        mask = jnp.where(slide_col == float(s), 1.0, 0.0)
        size = jnp.sum(mask, axis=0, keepdims=True)
        masks.append(mask)
        sizes.append(size)
        sums.append(jnp.sum(mask * normed, axis=0, keepdims=True) / size)
    pooled = jnp.concatenate(sums, axis=0).astype(BF16)
    logits = mm_nt(pooled, head[...])
    soft = jnp.log1p(jnp.exp(-jnp.abs(logits)))
    log_hazard = -(jnp.maximum(-logits, 0.0) + soft)
    log_stay = -(jnp.maximum(logits, 0.0) + soft)
    bin_at = lax.broadcasted_iota(jnp.int32, (SL_GRP, NBINS), 1).astype(F32)
    same = lax.broadcasted_iota(jnp.int32, (SL_GRP, SL_GRP), 0) == lax.broadcasted_iota(jnp.int32, (SL_GRP, SL_GRP), 1)
    bins = jnp.sum(jnp.where(same, label[...].astype(F32), 0.0), axis=1, keepdims=True)
    held = jnp.sum(jnp.where(same, censor[...].astype(F32), 0.0), axis=1, keepdims=True)
    at = jnp.where(bin_at == bins, 1.0, 0.0)
    before = jnp.where(bin_at < bins, 1.0, 0.0)
    past = jnp.sum(before * log_stay, axis=1, keepdims=True)
    seen = past + jnp.sum(at * log_hazard, axis=1, keepdims=True)
    lived = past + jnp.sum(at * log_stay, axis=1, keepdims=True)
    losses[...] = jnp.sum(jnp.where(same, -(1.0 - held) * seen - held * lived, 0.0), axis=0, keepdims=True)
    chance = 1.0 / (1.0 + jnp.exp(-logits))
    logit_grad = (scaling * (before * chance + at * (chance - (1.0 - held)))).astype(BF16)
    grads[5][...] = mm_tn(pooled, logit_grad).astype(BF16)
    pooled_grad = mm(logit_grad, head[...]).astype(BF16).astype(F32)
    grad = jnp.zeros_like(normed)
    for s in range(SL_GRP):
        grad = grad + masks[s] * (pooled_grad[s : s + 1] / sizes[s])
    grad = norm_back(grad, normed, rstd)

    def put(i, a, b):
        grads[i + 1][...] = mm_tn(a, b).astype(BF16)

    grad = encode_back(grad, x, w_qkv, w_out, w_up, w_down, H_SL, res, packed_grad, put).astype(BF16)
    grads[0][...] = mm_tn(emb, grad).astype(BF16)
    return mm(grad, slide_in[...]).astype(BF16)


def region_backward(scaling, where, label, censor, *refs):
    ins, outs, bufs, obufs, extra, sems, osems = cut(refs, 19, 16, 19, 16, 10, 1, 1)
    h = lax.rem(where[0] // 4, 2)
    order = list(range(8)) + [18, 13, 17, 16, 14, 15, 9, 8, 10, 11, 12]
    late = dict()
    for i in list(dict.fromkeys(order)):
        late[i] = Late(ins[i], bufs[i], sems[0].at[i])
    early = []
    for i, (r, b) in enumerate(zip(outs, obufs)):
        early.append(Early(r, b, osems[0].at[i]) if i != 1 else b)
    message, tails = late[0], late[1]
    slide_weights = [late[i] for i in range(2, 8)]
    w_qkv, w_out, w_up, w_down = [late[i] for i in range(8, 12)]
    x_ref, res = late[12], [late[i] for i in range(13, 19)]
    losses, spread, pairs, slide_grads = early[0], early[1], early[2:10], early[10:16]
    packed_grad, slide_packed_grad, embeds, placed = extra[:4]
    ids, slide_col = tails_of(tails[...])
    rows32 = lax.broadcasted_iota(jnp.int32, (32, 32), 0)
    columns32 = lax.broadcasted_iota(jnp.int32, (32, 32), 1)
    slide_row = jnp.sum(jnp.where(rows32 == columns32, slide_col, 0.0), axis=0, keepdims=True)
    arrived = message[...]
    at = lax.broadcasted_iota(jnp.int32, arrived.shape, 1)
    for b in range(2):
        for c in range(3):
            part = jnp.sum(jnp.where(at == 3 * b + c, arrived, 0.0), axis=1)
            for y in range(4):
                placed[8 * y + 4 * b : 8 * y + 4 * b + 4, c * LANES : (c + 1) * LANES] = part[4 * y : 4 * y + 4]
    embeds[...] = placed[...].astype(BF16)
    cots = slide_step(
        embeds, slide_row, slide_col, label, censor, *slide_weights, losses, slide_grads, extra[4:10], slide_packed_grad, scaling
    ).astype(F32)
    for g in [losses] + slide_grads:
        send(g)
    first, slots = both_slots(ids, where[0])
    grads = []
    for b, usable in enumerate(usable_of(slots)):
        mine = lax.broadcasted_iota(jnp.int32, (32, 1), 0) == first + 4 * b
        own = jnp.sum(jnp.where(mine, cots, 0.0), axis=0, keepdims=True)
        grads.append(jnp.where(usable, own / slots[b][2], 0.0))
    grad = jnp.concatenate(grads, axis=0)
    normed, rstd = norm_parts(res[5][...])
    grad = norm_back(grad, normed, rstd)

    def put(i, a, b):
        for at, value in ((6 - 2 * i, a), (7 - 2 * i, b)):
            pairs[at][...] = value
            send(pairs[at])

    grad = encode_back(grad, x_ref[...], w_qkv, w_out, w_up, w_down, HEADS, res, packed_grad, put).astype(BF16)
    for b in range(8):
        spread[b] = mm_tn(choice(slots, b), grad).astype(BF16)
    leave([(spread.at[2 * y + h], outs[1].at[y]) for y in range(4)], sems[0])
    for e in early:
        if e is not spread:
            e.finish()


def two_halves(flat, runs, core, halves, stage, sems):
    run = 32 * 63
    copies = []
    for side in range(2):
        which = core if side == 0 else 1 - core
        for z in runs:
            start = pl.multiple_of((2 * z + which) * run, 32)
            stage[side, z * run : (z + 1) * run, :] = flat[pl.ds(start, run), :].astype(BF16)
            part = pl.ds(z * run, run)
            copies.append(pltpu.make_async_copy(stage.at[side, part, :], halves[side].at[part, :], sems.at[side, z]))
            copies[-1].start()
    return copies


def region_weights(core, where, *refs):
    ins, halves, bufs, flat, run_buf, stage, sems, osems = cut(refs, 8, 2, 8, 1, 1, 1, 1, 1)
    late = [Late(r, b, sems[0].at[i]) for i, (r, b) in enumerate(zip(ins, bufs))]
    hidden, grad, second, up_grad, mixture, mid_grad, first, packed_grad = late
    put_rows(flat[0], 9216, hidden[...], grad[...])
    put_rows(flat[0], 4608, second[...], up_grad[...])
    put_rows(flat[0], 3456, mixture[...], mid_grad[...])
    put_rows(flat[0], 0, first[...], packed_grad[...])
    h = lax.rem(where[0] // 4, 2)
    copies = []
    for side in range(2):
        which = core[0] if side == 0 else 1 - core[0]
        for z in range(4):
            for y in range(4):
                start = pl.multiple_of((2 * z + which) * 1728 + y * 432 + h * 216, 8)
                run_buf[0][y * 216 : (y + 1) * 216, :] = flat[0][pl.ds(start, 216), :]
            part = pl.ds(z * 864, 864)
            stage[0][side, z * 864 : (z + 1) * 864, :] = run_buf[0][...].astype(BF16)
            copies.append(pltpu.make_async_copy(stage[0].at[side, part, :], halves[side].at[part, :], osems[0].at[side, z]))
            copies[-1].start()
    for copy in copies:
        copy.wait()


def tile_backward(core, ids, *refs):
    ins, _, halves, bufs, packed_grad, flat, stage, sems, osems = cut(refs, 14, 1, 2, 14, 1, 1, 1, 1, 1)
    late = [Late(ins[i], bufs[i], sems[0].at[i]) for i in (0, 13, 6, 12, 11, 5, 10, 4, 9, 8, 3, 7, 1, 2)]
    late = dict(zip((0, 13, 6, 12, 11, 5, 10, 4, 9, 8, 3, 7, 1, 2), late))
    arrived, patches, slide_rows = late[0], late[1], late[2]
    w_qkv, w_out, w_up, w_down = [late[i] for i in range(3, 7)]
    x_ref, res = late[7], [late[i] for i in range(8, 14)]
    rows32 = lax.broadcasted_iota(jnp.int32, (32, 32), 0)
    columns32 = lax.broadcasted_iota(jnp.int32, (32, 32), 1)
    assign = jnp.sum(jnp.where(rows32 == columns32, ids[...].astype(F32), 0.0), axis=1, keepdims=True)
    cot = jnp.zeros((32, D), F32)
    for i in range(16):
        region = float(i // 4 * 8 + i % 4)
        cot = cot + jnp.where((assign == region) | (assign == region + 4.0), arrived[i].astype(F32), 0.0)
    cot = cot * 0.25
    grad = jnp.concatenate([cot] * PATCHES, axis=0)
    normed, rstd = norm_parts(res[5][...])
    grad = norm_back(grad, normed, rstd)
    bases = (2304, 5760, 6912, 11520)

    leaving = []

    def put(i, a, b):
        put_rows(flat[0], bases[i], a, b)
        if i == 2:
            leaving.extend(two_halves(flat[0], (2, 3), core[0], halves, stage[0], osems[0]))

    grad = encode_back(grad, x_ref[...], w_qkv, w_out, w_up, w_down, HEADS, res, packed_grad[0], put)
    for side in range(2):
        which = core[0] if side == 0 else 1 - core[0]
        stage[0][side, 8064:8144, :] = slide_rows.ref()[which]
        part = pl.ds(8064, 80)
        leaving.append(pltpu.make_async_copy(stage[0].at[side, part, :], halves[side].at[part, :], osems[0].at[side, 4]))
        leaving[-1].start()
    put_rows(flat[0], 0, patches[...], grad.astype(BF16))
    leaving.extend(two_halves(flat[0], (0, 1), core[0], halves, stage[0], osems[0]))
    for copy in leaving:
        copy.wait()


def fold(rows, pad, tail, mine, got, *refs):
    _, (out,), extra, (total, stage) = cut(refs, tail, 1, tail, 2)
    planes = 1 + tail
    run = 16 * planes * rows
    for z in range(4):
        part = pl.ds(z * run, run)
        total[part, :] = mine[part, :].astype(F32) + got[part, :].astype(F32)
    if tail:
        part = pl.ds(4 * run, 80)
        extra[0][...] = (mine[part, :].astype(F32) + got[part, :].astype(F32)).astype(BF16)
    stage[4 * planes * rows :, :] = jnp.zeros((pad, LANES), F32)
    for y in range(4):
        for x in range(4):
            for z in range(4):
                for h in range(planes):
                    source = (z * 16 * planes + y * 4 * planes + h * 4 + x) * rows
                    target = (z * planes + h) * rows
                    stage[target : target + rows, :] = total[source : source + rows, :]
            out[y * 4 + x] = stage[...].astype(BF16)


def plane_sum(parts, out, buffer, total, sems):
    copies = []
    for i in range(2):
        part = pl.ds(i * 112, 112)
        copies.append(pltpu.make_async_copy(parts.at[:, part, :], buffer.at[:, part, :], sems.at[i]))
        copies[-1].start()
    for i in range(2):
        copies[i].wait()
        rows = slice(i * 112, (i + 1) * 112)
        value = buffer[0, rows, :].astype(F32)
        for j in range(1, 16):
            value = value + buffer[j, rows, :].astype(F32)
        total[rows, :] = value
    leave([(total, out)], sems)


def merge(where, tile_in, region_in, slide_in, out, tile_buf, region_buf, slide_buf, total, slide_total, stage, chunks, sems, osems):
    tile_late = Late(tile_in, tile_buf, sems.at[0])
    region_late = Late(region_in, region_buf, sems.at[1])
    slide_late = Late(slide_in, slide_buf, sems.at[2])
    slide_total[...] = slide_late[...].astype(F32)

    for start in range(0, 512, 64):
        value = tile_late[0, start : start + 64, :].astype(F32)
        for i in range(1, 16):
            value = value + tile_late[i, start : start + 64, :].astype(F32)
        total[start : start + 64, :] = value
    region_total = region_late.ref()
    h = lax.rem(where[0] // 4, 2)
    leaving = []
    for i in range(8):
        stage[0:63, :] = total[i * 63 : (i + 1) * 63, :]
        stage[63:64, :] = jnp.zeros((1, LANES), F32)
        rows = region_total[i // 2 * 54 : (i // 2 + 1) * 54, :]
        stage[64:118, :] = jnp.where(h == i % 2, rows, 0.0)
        stage[118:128, :] = slide_total[i * 10 : (i + 1) * 10, :]
        chunks[i] = stage[...].astype(BF16)
        leaving.append(pltpu.make_async_copy(chunks.at[i], out.at[i], osems.at[i]))
        leaving[-1].start()
    for copy in leaving:
        copy.wait()


def call(kernel, macs, outs, scratch, inputs, scalars=0, whole=0, mebibytes=60):
    specs = [pl.BlockSpec(memory_space=pltpu.SMEM)] * scalars
    specs += [pl.BlockSpec(memory_space=pltpu.VMEM)] * whole
    specs += [pl.BlockSpec(memory_space=pl.ANY)] * (len(inputs) - scalars - whole)
    moved = sum(math.prod(a.shape) * a.dtype.itemsize for a in inputs) + sum(math.prod(a) * jnp.dtype(k).itemsize for a, k in outs)
    cost = pl.CostEstimate(flops=2 * macs, bytes_accessed=moved, transcendentals=0)
    return pl.pallas_call(
        kernel,
        out_shape=[jax.ShapeDtypeStruct(shape, kind) for shape, kind in outs],
        in_specs=specs,
        out_specs=[pl.BlockSpec(memory_space=pl.ANY)] * len(outs),
        scratch_shapes=[pltpu.VMEM(*item) if isinstance(item, tuple) else item for item in scratch],
        compiler_params=pltpu.CompilerParams(vmem_limit_bytes=mebibytes * 1024 * 1024),
        cost_estimate=cost,
    )(*inputs)


def like(arrays):
    return [(a.shape, a.dtype) for a in arrays]


def semaphores(*shape):
    return pltpu.SemaphoreType.DMA(shape)


def residuals(tokens, width, hidden, heads):
    return [
        ((tokens, 3 * width), BF16),
        ((heads, tokens, tokens), F32),
        ((tokens, width), BF16),
        ((tokens, width), F32),
        ((tokens, hidden), F32),
        ((tokens, width), F32),
    ]


def index_of(z, core, y, z_hi, x):
    return (z * 2 + core) * 32 + y * 8 + z_hi * 4 + x


PLANES = [[index_of(z, c, y, h, x) for y in range(4) for x in range(4)] for z in range(4) for c in range(2) for h in range(2)]
COLUMNS = [[index_of(z, c, y, h, x) for z in range(4) for h in range(2)] for c in range(2) for y in range(4) for x in range(4)]
OTHER_CORE = [(g, g + 1 - 2 * (g % 2)) for g in range(8)]
OTHER_PLANE = [(d, d + 4 - 8 * (d // 4 % 2)) for d in range(32)]
ALL = ("grp", "dev")


def exchange(array, groups):
    return lax.all_to_all(array, ALL, 0, 0, axis_index_groups=groups)


def folded(mine, other, rows, pad, tail, after=()):
    got = lax.ppermute(other, "grp", OTHER_CORE)
    planes = 1 + tail
    chunk = 4 * planes * rows + pad
    outs = [(16, chunk, LANES)] + [(80, LANES)] * tail
    return pl.pallas_call(
        functools.partial(fold, rows, pad, tail),
        out_shape=[jax.ShapeDtypeStruct(shape, BF16) for shape in outs],
        in_specs=[pl.BlockSpec(memory_space=pltpu.VMEM)] * 2 + [pl.BlockSpec(memory_space=pl.ANY)] * tail,
        out_specs=[pl.BlockSpec(memory_space=pltpu.VMEM)] * len(outs),
        scratch_shapes=[pltpu.VMEM((64 * planes * rows, LANES), F32), pltpu.VMEM((chunk, LANES), F32)],
        compiler_params=pltpu.CompilerParams(vmem_limit_bytes=24 * 1024 * 1024),
        cost_estimate=pl.CostEstimate(flops=8 * US, bytes_accessed=1 << 20, transcendentals=0),
    )(mine, got, *after)


def body(
    patches,
    tile_region,
    region_slide,
    bin_label,
    censored,
    patch_w,
    tile_qkv,
    tile_out,
    tile_up,
    tile_down,
    region_qkv,
    region_out,
    region_up,
    region_down,
    slide_in,
    slide_qkv,
    slide_out,
    slide_up,
    slide_down,
    slide_head,
):
    member_index = lax.axis_index("dev").astype(jnp.int32)
    where = member_index.reshape(1)
    core = lax.rem(lax.axis_index("grp").astype(jnp.int32), 2).reshape(1)
    scaling = 1.0 / (bin_label.shape[1] * lax.axis_size("grp"))
    tokens = patches.transpose(1, 0, 2).reshape(128, 768)
    tile_res = [((128, D), F32)] + residuals(128, D, FF, HEADS)
    ins = (tokens, patch_w, tile_qkv, tile_out, tile_up, tile_down)
    message, *tile_kept = call(
        tile_forward,
        7 * US,
        [((112, LANES), BF16)] + tile_res,
        like(ins) + tile_res + [((112, LANES), BF16), semaphores(6), semaphores(7), semaphores(1)],
        (where, tile_region, region_slide) + ins,
        scalars=1,
        whole=2,
    )
    both = jnp.concatenate([message, lax.ppermute(message, "dev", OTHER_PLANE)], axis=0)
    rows = exchange(jnp.broadcast_to(both[None], (16, 224, LANES)), PLANES)
    region_res = [((2 * SLOTS, D), F32)] + residuals(2 * SLOTS, D, FF, HEADS)
    ins = (region_qkv, region_out, region_up, region_down)
    message, tails, *region_kept = call(
        region_forward,
        6 * US,
        [((16, 8, LANES), F32), ((32, 16, LANES), BF16)] + region_res,
        like(ins)
        + [((32, 112, LANES), BF16)]
        + region_res
        + [((8, LANES), F32), semaphores(4), semaphores(7), semaphores(33), semaphores(32)],
        (where, rows) + ins,
        scalars=1,
    )
    all_regions = exchange(message, PLANES)
    slide_weights = (slide_in, slide_qkv, slide_out, slide_up, slide_down, slide_head)
    widths = (FF, D, D, FF, D, D, D, 3 * D)
    pairs = [((2 * SLOTS, n), BF16) for n in widths]
    losses_out = [((1, SL_GRP), F32)]
    outs = losses_out + [((4, 128, D), BF16)] + pairs + like(slide_weights)
    buffers = losses_out + [((8, 128, D), BF16)] + pairs + like(slide_weights)
    ins = (all_regions, tails, slide_in.T) + slide_weights[1:5] + (slide_head.T,) + (region_qkv, region_out, region_up, region_down) + tuple(region_kept)
    losses, spread, *rest = call(
        functools.partial(region_backward, scaling),
        12 * US,
        outs,
        like(ins)
        + buffers
        + [((2 * SLOTS, 3 * D), BF16), ((32, 3 * D_SL), BF16), ((32, D), BF16), ((32, D), F32)]
        + residuals(32, D_SL, D_SL, H_SL)
        + [semaphores(19), semaphores(16)],
        (where, bin_label, censored) + ins,
        scalars=1,
        whole=2,
    )
    arrived = exchange(spread.reshape(16, 32, D), PLANES)
    ins = tuple(rest[:8])
    mine, other = call(
        region_weights,
        5 * US,
        [((3456, LANES), BF16)] * 2,
        like(ins)
        + [((13824, LANES), F32), ((864, LANES), F32), ((2, 3456, LANES), BF16), semaphores(8), semaphores(2, 4)],
        (core, where) + ins,
        scalars=2,
    )
    (region_chunks,) = folded(mine, other, 54, 8, 0)
    region_parts = exchange(region_chunks, PLANES)
    (region_sums,) = call(
        plane_sum,
        20 * US,
        [((224, LANES), F32)],
        like((region_parts,)) + [((224, LANES), F32), semaphores(2)],
        (region_parts,),
        mebibytes=24,
    )
    slide_flat = jnp.concatenate([g.astype(F32).reshape(-1) for g in rest[8:]]).reshape(4, 2, 4, 2, 4, 1155)
    y, x = member_index // 8, lax.rem(member_index, 4)
    zero = jnp.zeros((), jnp.int32)
    slide_rows = lax.dynamic_slice(slide_flat, (zero, zero, y, zero, x, zero), (4, 2, 1, 2, 1, 1155))
    slide_rows = slide_rows.reshape(4, 2, 2, 1155).transpose(1, 0, 2, 3)
    slide_rows = jnp.pad(slide_rows, ((0, 0), (0, 0), (0, 0), (0, 125))).astype(BF16).reshape(2, 80, LANES)
    ins = (arrived, tokens, slide_rows, tile_qkv, tile_out, tile_up, tile_down) + tuple(tile_kept)
    mine, other = call(
        tile_backward,
        13 * US,
        [((8144, LANES), BF16)] * 2,
        like(ins)
        + [((128, 3 * D), BF16), ((16128, LANES), F32), ((2, 8144, LANES), BF16), semaphores(14), semaphores(2, 5)],
        (core, tile_region) + ins + (region_chunks,),
        scalars=1,
        whole=1,
    )
    tile_chunks, slide_sums = folded(mine, other, 63, 8, 1, (region_sums,))
    tile_parts = exchange(tile_chunks, PLANES)
    ins = (tile_parts, region_sums, slide_sums)
    (last,) = call(
        merge,
        3 * US,
        [((8, 128, LANES), BF16)],
        like(ins)
        + [((512, LANES), F32), ((80, LANES), F32), ((128, LANES), F32), ((8, 128, LANES), BF16)]
        + [semaphores(3), semaphores(8)],
        (where,) + ins,
        scalars=1,
        mebibytes=24,
    )
    total = jnp.sum(exchange(last, COLUMNS).astype(F32), axis=0)
    tile_result = total[0:63].reshape(8064)
    region_result = total[64:118].reshape(6912)
    slide_result = total[118:128].reshape(1280)[:1155] * 0.5
    return (losses, tile_result, region_result, slide_result)


def solution(mesh):
    placed = (P(ALL, None, None), P("grp", "dev"), P("grp", "dev"), P("grp", None), P("grp", None)) + (P(),) * 15
    return jax.shard_map(
        body,
        mesh=mesh,
        in_specs=placed,
        out_specs=(P("grp", None), P(ALL), P(ALL), P(ALL)),
        check_vma=False,
    )
```

```python
import functools
import math

import jax
import jax.numpy as jnp
from jax import lax
from jax.experimental import pallas as pl
from jax.experimental.pallas import tpu as pltpu
from jax.sharding import PartitionSpec as P

D = 384
HEADS = 6
FF = 1536
PATCHES = 4
SLOTS = 64
D_SL = 192
H_SL = 3
NBINS = 4
SL_GRP = 4
HEAD = 64
F32 = jnp.float32
BF16 = jnp.bfloat16
LANES = 128
US = 550_000_000
GELU_C = math.sqrt(2.0 / math.pi)


def mm(a, b):
    return jnp.dot(a, b, preferred_element_type=F32)


def mm_nt(a, b):
    return lax.dot_general(a, b, (((1,), (1,)), ((), ())), preferred_element_type=F32)


def mm_tn(a, b):
    return lax.dot_general(a, b, (((0,), (0,)), ((), ())), preferred_element_type=F32)


def norm_parts(x):
    average = jnp.mean(x, axis=-1, keepdims=True)
    centred = x - average
    variance = jnp.mean(centred * centred, axis=-1, keepdims=True)
    rstd = lax.rsqrt(variance + 1e-06)
    return centred * rstd, rstd


def norm_back(grad, normed, rstd):
    first = jnp.mean(grad, axis=-1, keepdims=True)
    second = jnp.mean(grad * normed, axis=-1, keepdims=True)
    return rstd * (grad - first - normed * second)


def gelu_parts(x):
    t = jnp.tanh(GELU_C * (x + 0.044715 * (x * x * x)))
    value = 0.5 * x * (1.0 + t)
    slope = 0.5 * (1.0 + t) + 0.5 * x * (1.0 - t * t) * (GELU_C * (1.0 + 3.0 * 0.044715 * (x * x)))
    return value, slope


def encode(x, allowed, w_qkv, w_out, w_up, w_down, heads, res):
    packed_ref, attend_ref, mixture_ref, mid_ref, up_ref, out_ref = res
    width = x.shape[1]
    normed, _ = norm_parts(x)
    packed_ref[...] = mm(normed.astype(BF16), w_qkv[...]).astype(BF16)
    send(packed_ref)
    for h in range(heads):
        q = packed_ref[:, h * HEAD : (h + 1) * HEAD]
        k = packed_ref[:, width + h * HEAD : width + (h + 1) * HEAD]
        v = packed_ref[:, 2 * width + h * HEAD : 2 * width + (h + 1) * HEAD]
        scores = jnp.where(allowed, mm_nt(q, k) * 0.125, -1e30)
        scores = jnp.exp(scores - jnp.max(scores, axis=-1, keepdims=True))
        weights = scores / jnp.sum(scores, axis=-1, keepdims=True)
        attend_ref[h] = weights
        mixture_ref[:, h * HEAD : (h + 1) * HEAD] = mm(weights.astype(BF16), v).astype(BF16)
    send(attend_ref)
    send(mixture_ref)
    x1 = x + mm(mixture_ref[...], w_out[...])
    mid_ref[...] = x1
    send(mid_ref)
    normed, _ = norm_parts(x1)
    up = mm(normed.astype(BF16), w_up[...])
    up_ref[...] = up
    send(up_ref)
    hidden, _ = gelu_parts(up)
    out = x1 + mm(hidden.astype(BF16), w_down[...])
    out_ref[...] = out
    send(out_ref)
    return out


def encode_back(grad, x, w_qkv, w_out, w_up, w_down, heads, res, packed_grad, put):
    packed_ref, attend_ref, mixture_ref, mid_ref, up_ref, _ = res
    width = x.shape[1]
    grad_b = grad.astype(BF16)
    hidden, slope = gelu_parts(up_ref[...])
    up_grad = (mm_nt(grad_b, w_down[...]).astype(BF16).astype(F32) * slope).astype(BF16)
    put(3, hidden.astype(BF16), grad_b)
    normed, rstd = norm_parts(mid_ref[...])
    put(2, normed.astype(BF16), up_grad)
    normed_grad = mm_nt(up_grad, w_up[...]).astype(BF16).astype(F32)
    mid_grad = grad + norm_back(normed_grad, normed, rstd)
    mid_b = mid_grad.astype(BF16)
    put(1, mixture_ref[...], mid_b)
    mix_grad = mm_nt(mid_b, w_out[...]).astype(BF16)
    for h in range(heads):
        q = packed_ref[:, h * HEAD : (h + 1) * HEAD]
        k = packed_ref[:, width + h * HEAD : width + (h + 1) * HEAD]
        v = packed_ref[:, 2 * width + h * HEAD : 2 * width + (h + 1) * HEAD]
        head_grad = mix_grad[:, h * HEAD : (h + 1) * HEAD]
        weights = attend_ref[h]
        weights_grad = mm_nt(head_grad, v).astype(BF16).astype(F32)
        v_grad = mm_tn(weights.astype(BF16), head_grad)
        inner = jnp.sum(weights_grad * weights, axis=-1, keepdims=True)
        scores_grad = (weights * (weights_grad - inner) * 0.125).astype(BF16)
        packed_grad[:, h * HEAD : (h + 1) * HEAD] = mm(scores_grad, k).astype(BF16)
        packed_grad[:, width + h * HEAD : width + (h + 1) * HEAD] = mm_tn(scores_grad, q).astype(BF16)
        packed_grad[:, 2 * width + h * HEAD : 2 * width + (h + 1) * HEAD] = v_grad.astype(BF16)
    normed, rstd = norm_parts(x)
    put(0, normed.astype(BF16), packed_grad[...])
    normed_grad = mm_nt(packed_grad[...], w_qkv[...]).astype(BF16).astype(F32)
    return mid_grad + norm_back(normed_grad, normed, rstd)


def put_rows(flat, base, a, b):
    rows, columns = a.shape[1], b.shape[1]
    chunks = columns // 128
    left = a.T
    for c in range(0, chunks, 3):
        part = mm(left, b[:, c * 128 : (c + 3) * 128]).astype(BF16).astype(F32)
        for j in range(3):
            flat[pl.ds(base + c + j, rows, stride=chunks), :] = part[:, j * 128 : (j + 1) * 128]


def same_tile():
    row = lax.broadcasted_iota(jnp.int32, (128, 128), 0)
    column = lax.broadcasted_iota(jnp.int32, (128, 128), 1)
    return lax.rem(row, 32) == lax.rem(column, 32)


class Late:
    def __init__(self, source, buffer, sem):
        self.copy = pltpu.make_async_copy(source, buffer, sem)
        self.buffer, self.here = buffer, False
        self.copy.start()

    def ref(self):
        if not self.here:
            self.copy.wait()
            self.here = True
        return self.buffer

    def __getitem__(self, index):
        return self.ref()[index]


class Early:
    def __init__(self, target, buffer, sem):
        self.copy = pltpu.make_async_copy(buffer, target, sem)
        self.buffer = buffer

    def __getitem__(self, index):
        return self.buffer[index]

    def __setitem__(self, index, value):
        self.buffer[index] = value

    def finish(self):
        self.copy.wait()


def send(ref):
    if isinstance(ref, Early):
        ref.copy.start()


def leave(pairs, sems):
    copies = [pltpu.make_async_copy(a, b, sems.at[i]) for i, (a, b) in enumerate(pairs)]
    for copy in copies:
        copy.start()
    for copy in copies:
        copy.wait()


def broadcast_out(block, out, sems):
    copies = [pltpu.make_async_copy(block, out.at[i], sems.at[i]) for i in range(16)]
    for copy in copies:
        copy.start()
    for copy in copies:
        copy.wait()


def tile_forward(where, ids, slide, *refs):
    ins, outs, bufs, obufs, block, sems, osems, bsems = cut(refs, 6, 8, 6, 7, 1, 1, 1, 1)
    late = [Late(r, b, sems[0].at[i]) for i, (r, b) in enumerate(zip(ins, bufs))]
    res = [Early(r, b, osems[0].at[i]) for i, (r, b) in enumerate(zip(outs[1:], obufs))]
    patches, patch_w, w_qkv, w_out, w_up, w_down = late
    x = mm(patches[...], patch_w[...])
    res[0][...] = x
    send(res[0])
    out = encode(x, same_tile(), w_qkv, w_out, w_up, w_down, HEADS, res[1:])
    normed, _ = norm_parts(out)
    total = (normed[0:32] + normed[32:64]) + (normed[64:96] + normed[96:128])
    total = (total * 0.25).astype(BF16)
    message = block[0]
    for c in range(3):
        message[c * 32 : (c + 1) * 32, :] = total[:, c * LANES : (c + 1) * LANES]
    row = lax.broadcasted_iota(jnp.int32, (16, LANES), 0)
    lane = lax.broadcasted_iota(jnp.int32, (16, LANES), 1)
    mine = (lane >= 32 * lax.rem(where[0], 4)) & (lane < 32 * lax.rem(where[0], 4) + 32)
    four = jnp.concatenate([ids[...].astype(F32)] * 4, axis=1)
    tail = jnp.where((row == 0) & mine, four, 0.0) + jnp.where(row == 1, slide[...].astype(F32), 0.0)
    message[96:112, :] = tail.astype(BF16)
    leave([(message, outs[0])], bsems[0])
    for r in res:
        r.finish()


def cut(refs, *sizes):
    parts, at = [], 0
    for size in sizes:
        parts.append(refs[at : at + size])
        at += size
    assert at == len(refs)
    return parts


def tails_of(tails):
    tails = tails.astype(F32)
    row = lax.broadcasted_iota(jnp.int32, tails.shape, 1)
    ids = jnp.sum(jnp.where(row == 0, tails, 0.0), axis=1)
    slides = jnp.sum(jnp.where(row == 1, tails, 0.0), axis=1)
    to = lax.broadcasted_iota(jnp.int32, (8, 32), 0)
    source = lax.broadcasted_iota(jnp.int32, (8, 32), 1)
    near = (source >= 4 * to) & (source < 4 * to + 4)
    ids = mm(jnp.where(near, 1.0, 0.0).astype(BF16), ids.astype(BF16))
    return ids, slides[:, 0:1]


def slots_of(ids, region):
    member = jnp.where(ids == region.astype(F32), 1.0, 0.0)
    row = lax.broadcasted_iota(jnp.int32, (128, 128), 0)
    column = lax.broadcasted_iota(jnp.int32, (128, 128), 1)
    within = mm(member.astype(BF16), jnp.where(row < column, 1.0, 0.0).astype(BF16))
    sums = jnp.sum(member, axis=1, keepdims=True)
    row8 = lax.broadcasted_iota(jnp.int32, (8, 8), 0)
    column8 = lax.broadcasted_iota(jnp.int32, (8, 8), 1)
    earlier = jnp.where(column8 < row8, 1.0, 0.0).astype(BF16)
    ahead = mm(earlier, jnp.broadcast_to(sums, (8, 128)).astype(BF16))
    count = jnp.sum(sums, axis=0, keepdims=True)
    return member, (within + ahead).astype(jnp.int32), count


def both_slots(ids, device):
    first = device - 4 * lax.rem(device // 4, 2)
    return first, [slots_of(ids, first + 4 * b) for b in range(2)]


def choice(slots, i):
    k = lax.broadcasted_iota(jnp.int32, (SLOTS, 128), 0)
    parts = [jnp.where((slot[i : i + 1] == k) & (member[i : i + 1] > 0.0), 1.0, 0.0) for member, slot, _ in slots]
    return jnp.concatenate(parts, axis=0).astype(BF16)


def usable_of(slots):
    k = lax.broadcasted_iota(jnp.int32, (SLOTS, 1), 0).astype(F32)
    return [k < count for _, _, count in slots]


def region_forward(where, *refs):
    ins, outs, bufs, rows, obufs, block, sems, osems, bsems, rsems = cut(refs, 5, 9, 4, 1, 7, 1, 1, 1, 1, 1)
    rows = rows[0]
    h = lax.rem(where[0] // 4, 2)
    arriving = []
    for i in range(16):
        base = i // 4 * 8 + i % 4
        for side, z in enumerate((h, 1 - h)):
            source = ins[0].at[i, 112 * side : 112 * side + 112, :]
            arriving.append(pltpu.make_async_copy(source, rows.at[base + 4 * z], rsems[0].at[2 * i + side]))
            arriving[-1].start()
    w_qkv, w_out, w_up, w_down = [Late(r, b, sems[0].at[i]) for i, (r, b) in enumerate(zip(ins[1:], bufs))]
    res = [Early(r, b, osems[0].at[i]) for i, (r, b) in enumerate(zip(outs[2:], obufs))]
    for copy in arriving:
        copy.wait()
    tails = pltpu.make_async_copy(rows.at[:, 96:112, :], outs[1], bsems[0].at[32])
    tails.start()
    ids, _ = tails_of(rows[:, 96:112, :])
    _, slots = both_slots(ids, where[0])
    parts = [jnp.zeros((2 * SLOTS, LANES), F32)] * 3
    for b in range(8):
        pick = choice(slots, b)
        for c in range(3):
            block_rows = rows[4 * b : 4 * b + 4, 32 * c : 32 * c + 32, :].reshape(128, LANES)
            parts[c] = parts[c] + mm(pick, block_rows)
    for c in range(3):
        res[0][:, c * LANES : (c + 1) * LANES] = parts[c]
    send(res[0])
    row = lax.broadcasted_iota(jnp.int32, (2 * SLOTS, 2 * SLOTS), 0)
    key = lax.broadcasted_iota(jnp.int32, (2 * SLOTS, 2 * SLOTS), 1)
    at = key.astype(F32)
    allowed = ((row < SLOTS) & (at < slots[0][2])) | ((row >= SLOTS) & (key >= SLOTS) & (at < slots[1][2] + SLOTS))
    out = encode(res[0][...], allowed, w_qkv, w_out, w_up, w_down, HEADS, res[1:])
    normed, _ = norm_parts(out)
    message = block[0]
    message[...] = jnp.zeros((8, LANES), F32)
    for b, usable in enumerate(usable_of(slots)):
        total = jnp.sum(jnp.where(usable, normed[b * SLOTS : (b + 1) * SLOTS], 0.0), axis=0, keepdims=True)
        embed = (total / slots[b][2]).astype(BF16).astype(F32)
        for c in range(3):
            message[3 * b + c : 3 * b + c + 1, :] = embed[:, c * LANES : (c + 1) * LANES]
    broadcast_out(message, outs[0], bsems[0])
    tails.wait()
    for r in res:
        r.finish()


def slide_step(embeds, slide_row, slide_col, label, censor, slide_in, w_qkv, w_out, w_up, w_down, head, losses, grads, res, packed_grad, scaling):
    emb = embeds[...]
    x = mm_nt(emb, slide_in[...])
    out = encode(x, slide_col == slide_row, w_qkv, w_out, w_up, w_down, H_SL, res)
    normed, rstd = norm_parts(out)
    sums, sizes, masks = [], [], []
    for s in range(SL_GRP):
        mask = jnp.where(slide_col == float(s), 1.0, 0.0)
        size = jnp.sum(mask, axis=0, keepdims=True)
        masks.append(mask)
        sizes.append(size)
        sums.append(jnp.sum(mask * normed, axis=0, keepdims=True) / size)
    pooled = jnp.concatenate(sums, axis=0).astype(BF16)
    logits = mm_nt(pooled, head[...])
    soft = jnp.log1p(jnp.exp(-jnp.abs(logits)))
    log_hazard = -(jnp.maximum(-logits, 0.0) + soft)
    log_stay = -(jnp.maximum(logits, 0.0) + soft)
    bin_at = lax.broadcasted_iota(jnp.int32, (SL_GRP, NBINS), 1).astype(F32)
    same = lax.broadcasted_iota(jnp.int32, (SL_GRP, SL_GRP), 0) == lax.broadcasted_iota(jnp.int32, (SL_GRP, SL_GRP), 1)
    bins = jnp.sum(jnp.where(same, label[...].astype(F32), 0.0), axis=1, keepdims=True)
    held = jnp.sum(jnp.where(same, censor[...].astype(F32), 0.0), axis=1, keepdims=True)
    at = jnp.where(bin_at == bins, 1.0, 0.0)
    before = jnp.where(bin_at < bins, 1.0, 0.0)
    past = jnp.sum(before * log_stay, axis=1, keepdims=True)
    seen = past + jnp.sum(at * log_hazard, axis=1, keepdims=True)
    lived = past + jnp.sum(at * log_stay, axis=1, keepdims=True)
    losses[...] = jnp.sum(jnp.where(same, -(1.0 - held) * seen - held * lived, 0.0), axis=0, keepdims=True)
    chance = 1.0 / (1.0 + jnp.exp(-logits))
    logit_grad = (scaling * (before * chance + at * (chance - (1.0 - held)))).astype(BF16)
    grads[5][...] = mm_tn(pooled, logit_grad).astype(BF16)
    pooled_grad = mm(logit_grad, head[...]).astype(BF16).astype(F32)
    grad = jnp.zeros_like(normed)
    for s in range(SL_GRP):
        grad = grad + masks[s] * (pooled_grad[s : s + 1] / sizes[s])
    grad = norm_back(grad, normed, rstd)

    def put(i, a, b):
        grads[i + 1][...] = mm_tn(a, b).astype(BF16)

    grad = encode_back(grad, x, w_qkv, w_out, w_up, w_down, H_SL, res, packed_grad, put).astype(BF16)
    grads[0][...] = mm_tn(emb, grad).astype(BF16)
    return mm(grad, slide_in[...]).astype(BF16)


def region_backward(scaling, where, label, censor, *refs):
    ins, outs, bufs, obufs, extra, sems, osems = cut(refs, 19, 16, 19, 16, 10, 1, 1)
    h = lax.rem(where[0] // 4, 2)
    order = list(range(8)) + [18, 13, 17, 16, 14, 15, 9, 8, 10, 11, 12]
    late = dict()
    for i in list(dict.fromkeys(order)):
        late[i] = Late(ins[i], bufs[i], sems[0].at[i])
    early = []
    for i, r in enumerate(outs):
        early.append(Early(r, obufs[i], osems[0].at[i]) if i != 1 else obufs[1])
    message, tails = late[0], late[1]
    slide_weights = [late[i] for i in range(2, 8)]
    w_qkv, w_out, w_up, w_down = [late[i] for i in range(8, 12)]
    x_ref, res = late[12], [late[i] for i in range(13, 19)]
    losses, spread, pairs, slide_grads = early[0], early[1], early[2:10], early[10:16]
    packed_grad, slide_packed_grad, embeds, placed = extra[:4]
    ids, slide_col = tails_of(tails[...])
    rows32 = lax.broadcasted_iota(jnp.int32, (32, 32), 0)
    columns32 = lax.broadcasted_iota(jnp.int32, (32, 32), 1)
    slide_row = jnp.sum(jnp.where(rows32 == columns32, slide_col, 0.0), axis=0, keepdims=True)
    arrived = message[...]
    at = lax.broadcasted_iota(jnp.int32, arrived.shape, 1)
    for b in range(2):
        for c in range(3):
            part = jnp.sum(jnp.where(at == 3 * b + c, arrived, 0.0), axis=1)
            for y in range(4):
                placed[8 * y + 4 * b : 8 * y + 4 * b + 4, c * LANES : (c + 1) * LANES] = part[4 * y : 4 * y + 4]
    embeds[...] = placed[...].astype(BF16)
    cots = slide_step(
        embeds, slide_row, slide_col, label, censor, *slide_weights, losses, slide_grads, extra[4:10], slide_packed_grad, scaling
    ).astype(F32)
    for g in [losses] + slide_grads:
        send(g)
    first, slots = both_slots(ids, where[0])
    grads = []
    for b, usable in enumerate(usable_of(slots)):
        mine = lax.broadcasted_iota(jnp.int32, (32, 1), 0) == first + 4 * b
        own = jnp.sum(jnp.where(mine, cots, 0.0), axis=0, keepdims=True)
        grads.append(jnp.where(usable, own / slots[b][2], 0.0))
    grad = jnp.concatenate(grads, axis=0)
    normed, rstd = norm_parts(res[5][...])
    grad = norm_back(grad, normed, rstd)

    def put(i, a, b):
        for at, value in ((6 - 2 * i, a), (7 - 2 * i, b)):
            pairs[at][...] = value
            send(pairs[at])

    grad = encode_back(grad, x_ref[...], w_qkv, w_out, w_up, w_down, HEADS, res, packed_grad, put).astype(BF16)
    for b in range(8):
        spread[b] = mm_tn(choice(slots, b), grad).astype(BF16)
    leave([(spread.at[2 * y + h], outs[1].at[y]) for y in range(4)], sems[0])
    for e in early:
        if isinstance(e, Early):
            e.finish()


def two_halves(flat, runs, core, halves):
    run = 32 * 63
    for side in range(2):
        which = core if side == 0 else 1 - core
        for z in runs:
            start = pl.multiple_of((2 * z + which) * run, 32)
            halves[side][z * run : (z + 1) * run, :] = flat[pl.ds(start, run), :].astype(BF16)


def region_weights(core, where, *refs):
    ins, halves, bufs, (flat, run_buf), (sems,) = cut(refs, 8, 2, 8, 2, 1)
    late = [Late(r, b, sems.at[i]) for i, (r, b) in enumerate(zip(ins, bufs))]
    hidden, grad, second, up_grad, mixture, mid_grad, first, packed_grad = late
    put_rows(flat, 9216, hidden[...], grad[...])
    put_rows(flat, 4608, second[...], up_grad[...])
    put_rows(flat, 3456, mixture[...], mid_grad[...])
    put_rows(flat, 0, first[...], packed_grad[...])
    h = lax.rem(where[0] // 4, 2)
    for side in range(2):
        which = core[0] if side == 0 else 1 - core[0]
        for z in range(4):
            for y in range(4):
                start = pl.multiple_of((2 * z + which) * 1728 + y * 432 + h * 216, 8)
                run_buf[y * 216 : (y + 1) * 216, :] = flat[pl.ds(start, 216), :]
            halves[side][z * 864 : (z + 1) * 864, :] = run_buf[...].astype(BF16)


def tile_backward(core, ids, *refs):
    ins, _, halves, packed_grad, flat = cut(refs, 14, 1, 2, 1, 1)
    late = ins
    arrived, patches, slide_rows = late[0], late[1], late[2]
    w_qkv, w_out, w_up, w_down = [late[i] for i in range(3, 7)]
    x_ref, res = late[7], [late[i] for i in range(8, 14)]
    rows32 = lax.broadcasted_iota(jnp.int32, (32, 32), 0)
    columns32 = lax.broadcasted_iota(jnp.int32, (32, 32), 1)
    assign = jnp.sum(jnp.where(rows32 == columns32, ids[...].astype(F32), 0.0), axis=1, keepdims=True)
    cot = jnp.zeros((32, D), F32)
    for i in range(16):
        region = float(i // 4 * 8 + i % 4)
        cot = cot + jnp.where((assign == region) | (assign == region + 4.0), arrived[i].astype(F32), 0.0)
    cot = cot * 0.25
    grad = jnp.concatenate([cot] * PATCHES, axis=0)
    normed, rstd = norm_parts(res[5][...])
    grad = norm_back(grad, normed, rstd)
    bases = (2304, 5760, 6912, 11520)


    def put(i, a, b):
        put_rows(flat[0], bases[i], a, b)
        if i == 2:
            two_halves(flat[0], (2, 3), core[0], halves)

    grad = encode_back(grad, x_ref[...], w_qkv, w_out, w_up, w_down, HEADS, res, packed_grad[0], put)
    for side in range(2):
        which = core[0] if side == 0 else 1 - core[0]
        halves[side][8064:8144, :] = slide_rows[which]
    put_rows(flat[0], 0, patches[...], grad.astype(BF16))
    two_halves(flat[0], (0, 1), core[0], halves)


def fold(rows, pad, tail, mine, got, *refs):
    _, (out,), extra, (total, stage) = cut(refs, tail, 1, tail, 2)
    planes = 1 + tail
    run = 16 * planes * rows
    for z in range(4):
        part = pl.ds(z * run, run)
        total[part, :] = mine[part, :].astype(F32) + got[part, :].astype(F32)
    if tail:
        part = pl.ds(4 * run, 80)
        extra[0][...] = (mine[part, :].astype(F32) + got[part, :].astype(F32)).astype(BF16)
    stage[4 * planes * rows :, :] = jnp.zeros((pad, LANES), F32)
    for y in range(4):
        for x in range(4):
            for z in range(4):
                for h in range(planes):
                    source = (z * 16 * planes + y * 4 * planes + h * 4 + x) * rows
                    target = (z * planes + h) * rows
                    stage[target : target + rows, :] = total[source : source + rows, :]
            out[y * 4 + x] = stage[...].astype(BF16)


def plane_sum(parts, out, buffer, total, sems):
    copies = []
    for i in range(2):
        part = pl.ds(i * 112, 112)
        copies.append(pltpu.make_async_copy(parts.at[:, part, :], buffer.at[:, part, :], sems.at[i]))
        copies[-1].start()
    for i in range(2):
        copies[i].wait()
        rows = slice(i * 112, (i + 1) * 112)
        value = buffer[0, rows, :].astype(F32)
        for j in range(1, 16):
            value = value + buffer[j, rows, :].astype(F32)
        total[rows, :] = value
    leave([(total, out)], sems)


def merge(where, tile_in, region_in, slide_in, out, tile_buf, region_buf, slide_buf, total, slide_total, stage, chunks, sems, osems):
    tile_late = Late(tile_in, tile_buf, sems.at[0])
    region_late = Late(region_in, region_buf, sems.at[1])
    slide_late = Late(slide_in, slide_buf, sems.at[2])
    slide_total[...] = slide_late[...].astype(F32)

    for start in range(0, 512, 64):
        value = tile_late[0, start : start + 64, :].astype(F32)
        for i in range(1, 16):
            value = value + tile_late[i, start : start + 64, :].astype(F32)
        total[start : start + 64, :] = value
    region_total = region_late.ref()
    h = lax.rem(where[0] // 4, 2)
    leaving = []
    for i in range(8):
        stage[0:63, :] = total[i * 63 : (i + 1) * 63, :]
        stage[63:64, :] = jnp.zeros((1, LANES), F32)
        rows = region_total[i // 2 * 54 : (i // 2 + 1) * 54, :]
        stage[64:118, :] = jnp.where(h == i % 2, rows, 0.0)
        stage[118:128, :] = slide_total[i * 10 : (i + 1) * 10, :]
        chunks[i] = stage[...].astype(BF16)
        leaving.append(pltpu.make_async_copy(chunks.at[i], out.at[i], osems.at[i]))
        leaving[-1].start()
    for copy in leaving:
        copy.wait()


def call(kernel, macs, outs, scratch, inputs, scalars=0, whole=0, mebibytes=60, direct=()):
    specs = [pl.BlockSpec(memory_space=pltpu.SMEM)] * scalars
    specs += [pl.BlockSpec(memory_space=pltpu.VMEM)] * whole
    specs += [pl.BlockSpec(memory_space=pl.ANY)] * (len(inputs) - scalars - whole)
    moved = sum(math.prod(a.shape) * a.dtype.itemsize for a in inputs) + sum(math.prod(a) * jnp.dtype(k).itemsize for a, k in outs)
    cost = pl.CostEstimate(flops=2 * macs, bytes_accessed=moved, transcendentals=0)
    return pl.pallas_call(
        kernel,
        out_shape=[jax.ShapeDtypeStruct(shape, kind) for shape, kind in outs],
        in_specs=specs,
        out_specs=[pl.BlockSpec(memory_space=pltpu.VMEM if i in direct else pl.ANY) for i in range(len(outs))],
        scratch_shapes=[pltpu.VMEM(*item) if isinstance(item, tuple) else item for item in scratch],
        compiler_params=pltpu.CompilerParams(vmem_limit_bytes=mebibytes * 1024 * 1024),
        cost_estimate=cost,
    )(*inputs)


def like(arrays):
    return [(a.shape, a.dtype) for a in arrays]


def semaphores(*shape):
    return pltpu.SemaphoreType.DMA(shape)


def residuals(tokens, width, hidden, heads):
    return [
        ((tokens, 3 * width), BF16),
        ((heads, tokens, tokens), F32),
        ((tokens, width), BF16),
        ((tokens, width), F32),
        ((tokens, hidden), F32),
        ((tokens, width), F32),
    ]


def index_of(z, core, y, z_hi, x):
    return (z * 2 + core) * 32 + y * 8 + z_hi * 4 + x


PLANES = [[index_of(z, c, y, h, x) for y in range(4) for x in range(4)] for z in range(4) for c in range(2) for h in range(2)]
COLUMNS = [[index_of(z, c, y, h, x) for z in range(4) for h in range(2)] for c in range(2) for y in range(4) for x in range(4)]
OTHER_CORE = [(g, g + 1 - 2 * (g % 2)) for g in range(8)]
OTHER_PLANE = [(d, d + 4 - 8 * (d // 4 % 2)) for d in range(32)]
ALL = ("grp", "dev")


def exchange(array, groups):
    return lax.all_to_all(array, ALL, 0, 0, axis_index_groups=groups)


def folded(mine, other, rows, pad, tail, after=()):
    got = lax.ppermute(other, "grp", OTHER_CORE)
    planes = 1 + tail
    chunk = 4 * planes * rows + pad
    outs = [(16, chunk, LANES)] + [(80, LANES)] * tail
    return pl.pallas_call(
        functools.partial(fold, rows, pad, tail),
        out_shape=[jax.ShapeDtypeStruct(shape, BF16) for shape in outs],
        in_specs=[pl.BlockSpec(memory_space=pltpu.VMEM)] * 2 + [pl.BlockSpec(memory_space=pl.ANY)] * tail,
        out_specs=[pl.BlockSpec(memory_space=pltpu.VMEM)] * len(outs),
        scratch_shapes=[pltpu.VMEM((64 * planes * rows, LANES), F32), pltpu.VMEM((chunk, LANES), F32)],
        compiler_params=pltpu.CompilerParams(vmem_limit_bytes=24 * 1024 * 1024),
        cost_estimate=pl.CostEstimate(flops=8 * US, bytes_accessed=1 << 20, transcendentals=0),
    )(mine, got, *after)


def body(
    patches,
    tile_region,
    region_slide,
    bin_label,
    censored,
    patch_w,
    tile_qkv,
    tile_out,
    tile_up,
    tile_down,
    region_qkv,
    region_out,
    region_up,
    region_down,
    slide_in,
    slide_qkv,
    slide_out,
    slide_up,
    slide_down,
    slide_head,
):
    member_index = lax.axis_index("dev").astype(jnp.int32)
    where = member_index.reshape(1)
    core = lax.rem(lax.axis_index("grp").astype(jnp.int32), 2).reshape(1)
    scaling = 1.0 / (bin_label.shape[1] * lax.axis_size("grp"))
    tokens = patches.transpose(1, 0, 2).reshape(128, 768)
    tile_res = [((128, D), F32)] + residuals(128, D, FF, HEADS)
    ins = (tokens, patch_w, tile_qkv, tile_out, tile_up, tile_down)
    message, *tile_kept = call(
        tile_forward,
        7 * US,
        [((112, LANES), BF16)] + tile_res,
        like(ins) + tile_res + [((112, LANES), BF16), semaphores(6), semaphores(7), semaphores(1)],
        (where, tile_region, region_slide) + ins,
        scalars=1,
        whole=2,
    )
    both = jnp.concatenate([message, lax.ppermute(message, "dev", OTHER_PLANE)], axis=0)
    rows = exchange(jnp.broadcast_to(both[None], (16, 224, LANES)), PLANES)
    region_res = [((2 * SLOTS, D), F32)] + residuals(2 * SLOTS, D, FF, HEADS)
    ins = (region_qkv, region_out, region_up, region_down)
    message, tails, *region_kept = call(
        region_forward,
        6 * US,
        [((16, 8, LANES), F32), ((32, 16, LANES), BF16)] + region_res,
        like(ins)
        + [((32, 112, LANES), BF16)]
        + region_res
        + [((8, LANES), F32), semaphores(4), semaphores(7), semaphores(33), semaphores(32)],
        (where, rows) + ins,
        scalars=1,
    )
    all_regions = exchange(message, PLANES)
    slide_weights = (slide_in, slide_qkv, slide_out, slide_up, slide_down, slide_head)
    widths = (FF, D, D, FF, D, D, D, 3 * D)
    pairs = [((2 * SLOTS, n), BF16) for n in widths]
    losses_out = [((1, SL_GRP), F32)]
    outs = losses_out + [((4, 128, D), BF16)] + pairs + like(slide_weights)
    buffers = losses_out + [((8, 128, D), BF16)] + pairs + like(slide_weights)
    ins = (all_regions, tails, slide_in.T) + slide_weights[1:5] + (slide_head.T,) + (region_qkv, region_out, region_up, region_down) + tuple(region_kept)
    losses, spread, *rest = call(
        functools.partial(region_backward, scaling),
        12 * US,
        outs,
        like(ins)
        + buffers
        + [((2 * SLOTS, 3 * D), BF16), ((32, 3 * D_SL), BF16), ((32, D), BF16), ((32, D), F32)]
        + residuals(32, D_SL, D_SL, H_SL)
        + [semaphores(19), semaphores(16)],
        (where, bin_label, censored) + ins,
        scalars=1,
        whole=2,
    )
    arrived = exchange(spread.reshape(16, 32, D), PLANES)
    ins = tuple(rest[:8])
    mine, other = call(
        region_weights,
        5 * US,
        [((3456, LANES), BF16)] * 2,
        like(ins) + [((13824, LANES), F32), ((864, LANES), F32), semaphores(8)],
        (core, where) + ins,
        scalars=2,
        mebibytes=56,
        direct=(0, 1),
    )
    (region_chunks,) = folded(mine, other, 54, 8, 0)
    region_parts = exchange(region_chunks, PLANES)
    (region_sums,) = call(
        plane_sum,
        20 * US,
        [((224, LANES), F32)],
        like((region_parts,)) + [((224, LANES), F32), semaphores(2)],
        (region_parts,),
        mebibytes=24,
    )
    slide_flat = jnp.concatenate([g.astype(F32).reshape(-1) for g in rest[8:]]).reshape(4, 2, 4, 2, 4, 1155)
    y, x = member_index // 8, lax.rem(member_index, 4)
    zero = jnp.zeros((), jnp.int32)
    slide_rows = lax.dynamic_slice(slide_flat, (zero, zero, y, zero, x, zero), (4, 2, 1, 2, 1, 1155))
    slide_rows = slide_rows.reshape(4, 2, 2, 1155).transpose(1, 0, 2, 3)
    slide_rows = jnp.pad(slide_rows, ((0, 0), (0, 0), (0, 0), (0, 125))).astype(BF16).reshape(2, 80, LANES)
    ins = (arrived, tokens, slide_rows, tile_qkv, tile_out, tile_up, tile_down) + tuple(tile_kept)
    mine, other = call(
        tile_backward,
        13 * US,
        [((8144, LANES), BF16)] * 2,
        [((128, 3 * D), BF16), ((16128, LANES), F32)],
        (core, tile_region) + ins + (region_chunks,),
        scalars=1,
        whole=15,
        mebibytes=30,
        direct=(0, 1),
    )
    tile_chunks, slide_sums = folded(mine, other, 63, 8, 1, (region_sums,))
    tile_parts = exchange(tile_chunks, PLANES)
    ins = (tile_parts, region_sums, slide_sums)
    (last,) = call(
        merge,
        3 * US,
        [((8, 128, LANES), BF16)],
        like(ins)
        + [((512, LANES), F32), ((80, LANES), F32), ((128, LANES), F32), ((8, 128, LANES), BF16)]
        + [semaphores(3), semaphores(8)],
        (where,) + ins,
        scalars=1,
        mebibytes=24,
    )
    total = jnp.sum(exchange(last, COLUMNS).astype(F32), axis=0)
    tile_result = total[0:63].reshape(8064)
    region_result = total[64:118].reshape(6912)
    slide_result = total[118:128].reshape(1280)[:1155] * 0.5
    return (losses, tile_result, region_result, slide_result)


def solution(mesh):
    placed = (P(ALL, None, None), P("grp", "dev"), P("grp", "dev"), P("grp", None), P("grp", None)) + (P(),) * 15
    return jax.shard_map(
        body,
        mesh=mesh,
        in_specs=placed,
        out_specs=(P("grp", None), P(ALL), P(ALL), P(ALL)),
        check_vma=False,
    )
```

```python
import functools
import math

import jax
import jax.numpy as jnp
from jax import lax
from jax.experimental import pallas as pl
from jax.experimental.pallas import tpu as pltpu
from jax.sharding import PartitionSpec as P

D = 384
HEADS = 6
FF = 1536
PATCHES = 4
SLOTS = 64
D_SL = 192
H_SL = 3
NBINS = 4
SL_GRP = 4
HEAD = 64
F32 = jnp.float32
BF16 = jnp.bfloat16
LANES = 128
US = 550_000_000
GELU_C = math.sqrt(2.0 / math.pi)


def mm(a, b):
    return jnp.dot(a, b, preferred_element_type=F32)


def mm_nt(a, b):
    return lax.dot_general(a, b, (((1,), (1,)), ((), ())), preferred_element_type=F32)


def mm_tn(a, b):
    return lax.dot_general(a, b, (((0,), (0,)), ((), ())), preferred_element_type=F32)


def norm_parts(x):
    average = jnp.mean(x, axis=-1, keepdims=True)
    centred = x - average
    variance = jnp.mean(centred * centred, axis=-1, keepdims=True)
    rstd = lax.rsqrt(variance + 1e-06)
    return centred * rstd, rstd


def norm_back(grad, normed, rstd):
    first = jnp.mean(grad, axis=-1, keepdims=True)
    second = jnp.mean(grad * normed, axis=-1, keepdims=True)
    return rstd * (grad - first - normed * second)


def gelu_parts(x):
    t = jnp.tanh(GELU_C * (x + 0.044715 * (x * x * x)))
    value = 0.5 * x * (1.0 + t)
    slope = 0.5 * (1.0 + t) + 0.5 * x * (1.0 - t * t) * (GELU_C * (1.0 + 3.0 * 0.044715 * (x * x)))
    return value, slope


def encode(x, allowed, w_qkv, w_out, w_up, w_down, heads, res):
    packed_ref, attend_ref, mixture_ref, mid_ref, up_ref, out_ref = res
    width = x.shape[1]
    normed, _ = norm_parts(x)
    packed_ref[...] = mm(normed.astype(BF16), w_qkv[...]).astype(BF16)
    send(packed_ref)
    for h in range(heads):
        q = packed_ref[:, h * HEAD : (h + 1) * HEAD]
        k = packed_ref[:, width + h * HEAD : width + (h + 1) * HEAD]
        v = packed_ref[:, 2 * width + h * HEAD : 2 * width + (h + 1) * HEAD]
        scores = jnp.where(allowed, mm_nt(q, k) * 0.125, -1e30)
        scores = jnp.exp(scores - jnp.max(scores, axis=-1, keepdims=True))
        weights = scores / jnp.sum(scores, axis=-1, keepdims=True)
        attend_ref[h] = weights
        mixture_ref[:, h * HEAD : (h + 1) * HEAD] = mm(weights.astype(BF16), v).astype(BF16)
    send(attend_ref)
    send(mixture_ref)
    x1 = x + mm(mixture_ref[...], w_out[...])
    mid_ref[...] = x1
    send(mid_ref)
    normed, _ = norm_parts(x1)
    up = mm(normed.astype(BF16), w_up[...])
    up_ref[...] = up
    send(up_ref)
    hidden, _ = gelu_parts(up)
    out = x1 + mm(hidden.astype(BF16), w_down[...])
    out_ref[...] = out
    send(out_ref)
    return out


def encode_back(grad, x, w_qkv, w_out, w_up, w_down, heads, res, packed_grad, put):
    packed_ref, attend_ref, mixture_ref, mid_ref, up_ref, _ = res
    width = x.shape[1]
    grad_b = grad.astype(BF16)
    hidden, slope = gelu_parts(up_ref[...])
    up_grad = (mm_nt(grad_b, w_down[...]).astype(BF16).astype(F32) * slope).astype(BF16)
    put(3, hidden.astype(BF16), grad_b)
    normed, rstd = norm_parts(mid_ref[...])
    put(2, normed.astype(BF16), up_grad)
    normed_grad = mm_nt(up_grad, w_up[...]).astype(BF16).astype(F32)
    mid_grad = grad + norm_back(normed_grad, normed, rstd)
    mid_b = mid_grad.astype(BF16)
    put(1, mixture_ref[...], mid_b)
    mix_grad = mm_nt(mid_b, w_out[...]).astype(BF16)
    for h in range(heads):
        q = packed_ref[:, h * HEAD : (h + 1) * HEAD]
        k = packed_ref[:, width + h * HEAD : width + (h + 1) * HEAD]
        v = packed_ref[:, 2 * width + h * HEAD : 2 * width + (h + 1) * HEAD]
        head_grad = mix_grad[:, h * HEAD : (h + 1) * HEAD]
        weights = attend_ref[h]
        weights_grad = mm_nt(head_grad, v).astype(BF16).astype(F32)
        v_grad = mm_tn(weights.astype(BF16), head_grad)
        inner = jnp.sum(weights_grad * weights, axis=-1, keepdims=True)
        scores_grad = (weights * (weights_grad - inner) * 0.125).astype(BF16)
        packed_grad[:, h * HEAD : (h + 1) * HEAD] = mm(scores_grad, k).astype(BF16)
        packed_grad[:, width + h * HEAD : width + (h + 1) * HEAD] = mm_tn(scores_grad, q).astype(BF16)
        packed_grad[:, 2 * width + h * HEAD : 2 * width + (h + 1) * HEAD] = v_grad.astype(BF16)
    normed, rstd = norm_parts(x)
    put(0, normed.astype(BF16), packed_grad[...])
    normed_grad = mm_nt(packed_grad[...], w_qkv[...]).astype(BF16).astype(F32)
    return mid_grad + norm_back(normed_grad, normed, rstd)


def put_rows(flat, base, a, b):
    rows, columns = a.shape[1], b.shape[1]
    chunks = columns // 128
    left = a.T
    for c in range(0, chunks, 3):
        part = mm(left, b[:, c * 128 : (c + 3) * 128]).astype(BF16).astype(F32)
        for j in range(3):
            flat[pl.ds(base + c + j, rows, stride=chunks), :] = part[:, j * 128 : (j + 1) * 128]


def same_tile():
    row = lax.broadcasted_iota(jnp.int32, (128, 128), 0)
    column = lax.broadcasted_iota(jnp.int32, (128, 128), 1)
    return lax.rem(row, 32) == lax.rem(column, 32)


class Late:
    def __init__(self, source, buffer, sem):
        self.copy = pltpu.make_async_copy(source, buffer, sem)
        self.buffer, self.here = buffer, False
        self.copy.start()

    def ref(self):
        if not self.here:
            self.copy.wait()
            self.here = True
        return self.buffer

    def __getitem__(self, index):
        return self.ref()[index]


class Early:
    def __init__(self, target, buffer, sem):
        self.copy = pltpu.make_async_copy(buffer, target, sem)
        self.buffer = buffer

    def __getitem__(self, index):
        return self.buffer[index]

    def __setitem__(self, index, value):
        self.buffer[index] = value

    def finish(self):
        self.copy.wait()


def send(ref):
    if isinstance(ref, Early):
        ref.copy.start()


def leave(pairs, sems):
    copies = [pltpu.make_async_copy(a, b, sems.at[i]) for i, (a, b) in enumerate(pairs)]
    for copy in copies:
        copy.start()
    for copy in copies:
        copy.wait()


def broadcast_out(block, out, sems):
    copies = [pltpu.make_async_copy(block, out.at[i], sems.at[i]) for i in range(16)]
    for copy in copies:
        copy.start()
    for copy in copies:
        copy.wait()


def tile_forward(where, ids, slide, *refs):
    ins, outs, bufs, obufs, block, sems, osems, bsems = cut(refs, 6, 8, 6, 7, 1, 1, 1, 1)
    late = [Late(r, b, sems[0].at[i]) for i, (r, b) in enumerate(zip(ins, bufs))]
    res = [Early(r, b, osems[0].at[i]) for i, (r, b) in enumerate(zip(outs[1:], obufs))]
    patches, patch_w, w_qkv, w_out, w_up, w_down = late
    x = mm(patches[...], patch_w[...])
    res[0][...] = x
    send(res[0])
    out = encode(x, same_tile(), w_qkv, w_out, w_up, w_down, HEADS, res[1:])
    normed, _ = norm_parts(out)
    total = (normed[0:32] + normed[32:64]) + (normed[64:96] + normed[96:128])
    total = (total * 0.25).astype(BF16)
    message = block[0]
    for c in range(3):
        message[c * 32 : (c + 1) * 32, :] = total[:, c * LANES : (c + 1) * LANES]
    row = lax.broadcasted_iota(jnp.int32, (16, LANES), 0)
    lane = lax.broadcasted_iota(jnp.int32, (16, LANES), 1)
    mine = (lane >= 32 * lax.rem(where[0], 4)) & (lane < 32 * lax.rem(where[0], 4) + 32)
    four = jnp.concatenate([ids[...].astype(F32)] * 4, axis=1)
    tail = jnp.where((row == 0) & mine, four, 0.0) + jnp.where(row == 1, slide[...].astype(F32), 0.0)
    message[96:112, :] = tail.astype(BF16)
    leave([(message, outs[0])], bsems[0])
    for r in res:
        r.finish()


def cut(refs, *sizes):
    parts, at = [], 0
    for size in sizes:
        parts.append(refs[at : at + size])
        at += size
    assert at == len(refs)
    return parts


def tails_of(tails):
    tails = tails.astype(F32)
    row = lax.broadcasted_iota(jnp.int32, tails.shape, 1)
    ids = jnp.sum(jnp.where(row == 0, tails, 0.0), axis=1)
    slides = jnp.sum(jnp.where(row == 1, tails, 0.0), axis=1)
    to = lax.broadcasted_iota(jnp.int32, (8, 32), 0)
    source = lax.broadcasted_iota(jnp.int32, (8, 32), 1)
    near = (source >= 4 * to) & (source < 4 * to + 4)
    ids = mm(jnp.where(near, 1.0, 0.0).astype(BF16), ids.astype(BF16))
    return ids, slides[:, 0:1]


def slots_of(ids, region):
    member = jnp.where(ids == region.astype(F32), 1.0, 0.0)
    row = lax.broadcasted_iota(jnp.int32, (128, 128), 0)
    column = lax.broadcasted_iota(jnp.int32, (128, 128), 1)
    within = mm(member.astype(BF16), jnp.where(row < column, 1.0, 0.0).astype(BF16))
    sums = jnp.sum(member, axis=1, keepdims=True)
    row8 = lax.broadcasted_iota(jnp.int32, (8, 8), 0)
    column8 = lax.broadcasted_iota(jnp.int32, (8, 8), 1)
    earlier = jnp.where(column8 < row8, 1.0, 0.0).astype(BF16)
    ahead = mm(earlier, jnp.broadcast_to(sums, (8, 128)).astype(BF16))
    count = jnp.sum(sums, axis=0, keepdims=True)
    return member, (within + ahead).astype(jnp.int32), count


def both_slots(ids, device):
    first = device - 4 * lax.rem(device // 4, 2)
    return first, [slots_of(ids, first + 4 * b) for b in range(2)]


def choice(slots, i):
    k = lax.broadcasted_iota(jnp.int32, (SLOTS, 128), 0)
    parts = [jnp.where((slot[i : i + 1] == k) & (member[i : i + 1] > 0.0), 1.0, 0.0) for member, slot, _ in slots]
    return jnp.concatenate(parts, axis=0).astype(BF16)


def usable_of(slots):
    k = lax.broadcasted_iota(jnp.int32, (SLOTS, 1), 0).astype(F32)
    return [k < count for _, _, count in slots]


def region_forward(where, *refs):
    ins, outs, bufs, rows, obufs, block, sems, osems, bsems, rsems = cut(refs, 5, 9, 4, 1, 7, 1, 1, 1, 1, 1)
    rows = rows[0]
    h = lax.rem(where[0] // 4, 2)
    arriving = []
    for i in range(16):
        base = i // 4 * 8 + i % 4
        for side, z in enumerate((h, 1 - h)):
            source = ins[0].at[i, 112 * side : 112 * side + 112, :]
            arriving.append(pltpu.make_async_copy(source, rows.at[base + 4 * z], rsems[0].at[2 * i + side]))
            arriving[-1].start()
    w_qkv, w_out, w_up, w_down = [Late(r, b, sems[0].at[i]) for i, (r, b) in enumerate(zip(ins[1:], bufs))]
    res = [Early(r, b, osems[0].at[i]) for i, (r, b) in enumerate(zip(outs[2:], obufs))]
    for copy in arriving:
        copy.wait()
    tails = pltpu.make_async_copy(rows.at[:, 96:112, :], outs[1], bsems[0].at[32])
    tails.start()
    ids, _ = tails_of(rows[:, 96:112, :])
    _, slots = both_slots(ids, where[0])
    parts = [jnp.zeros((2 * SLOTS, LANES), F32)] * 3
    for b in range(8):
        pick = choice(slots, b)
        for c in range(3):
            block_rows = rows[4 * b : 4 * b + 4, 32 * c : 32 * c + 32, :].reshape(128, LANES)
            parts[c] = parts[c] + mm(pick, block_rows)
    for c in range(3):
        res[0][:, c * LANES : (c + 1) * LANES] = parts[c]
    send(res[0])
    row = lax.broadcasted_iota(jnp.int32, (2 * SLOTS, 2 * SLOTS), 0)
    key = lax.broadcasted_iota(jnp.int32, (2 * SLOTS, 2 * SLOTS), 1)
    at = key.astype(F32)
    allowed = ((row < SLOTS) & (at < slots[0][2])) | ((row >= SLOTS) & (key >= SLOTS) & (at < slots[1][2] + SLOTS))
    out = encode(res[0][...], allowed, w_qkv, w_out, w_up, w_down, HEADS, res[1:])
    normed, _ = norm_parts(out)
    message = block[0]
    message[...] = jnp.zeros((8, LANES), F32)
    for b, usable in enumerate(usable_of(slots)):
        total = jnp.sum(jnp.where(usable, normed[b * SLOTS : (b + 1) * SLOTS], 0.0), axis=0, keepdims=True)
        embed = (total / slots[b][2]).astype(BF16).astype(F32)
        for c in range(3):
            message[3 * b + c : 3 * b + c + 1, :] = embed[:, c * LANES : (c + 1) * LANES]
    broadcast_out(message, outs[0], bsems[0])
    tails.wait()
    for r in res:
        r.finish()


def slide_step(embeds, slide_row, slide_col, label, censor, slide_in, w_qkv, w_out, w_up, w_down, head, losses, grads, res, packed_grad, scaling):
    emb = embeds[...]
    x = mm_nt(emb, slide_in[...])
    out = encode(x, slide_col == slide_row, w_qkv, w_out, w_up, w_down, H_SL, res)
    normed, rstd = norm_parts(out)
    sums, sizes, masks = [], [], []
    for s in range(SL_GRP):
        mask = jnp.where(slide_col == float(s), 1.0, 0.0)
        size = jnp.sum(mask, axis=0, keepdims=True)
        masks.append(mask)
        sizes.append(size)
        sums.append(jnp.sum(mask * normed, axis=0, keepdims=True) / size)
    pooled = jnp.concatenate(sums, axis=0).astype(BF16)
    logits = mm_nt(pooled, head[...])
    soft = jnp.log1p(jnp.exp(-jnp.abs(logits)))
    log_hazard = -(jnp.maximum(-logits, 0.0) + soft)
    log_stay = -(jnp.maximum(logits, 0.0) + soft)
    bin_at = lax.broadcasted_iota(jnp.int32, (SL_GRP, NBINS), 1).astype(F32)
    same = lax.broadcasted_iota(jnp.int32, (SL_GRP, SL_GRP), 0) == lax.broadcasted_iota(jnp.int32, (SL_GRP, SL_GRP), 1)
    bins = jnp.sum(jnp.where(same, label[...].astype(F32), 0.0), axis=1, keepdims=True)
    held = jnp.sum(jnp.where(same, censor[...].astype(F32), 0.0), axis=1, keepdims=True)
    at = jnp.where(bin_at == bins, 1.0, 0.0)
    before = jnp.where(bin_at < bins, 1.0, 0.0)
    past = jnp.sum(before * log_stay, axis=1, keepdims=True)
    seen = past + jnp.sum(at * log_hazard, axis=1, keepdims=True)
    lived = past + jnp.sum(at * log_stay, axis=1, keepdims=True)
    losses[...] = jnp.sum(jnp.where(same, -(1.0 - held) * seen - held * lived, 0.0), axis=0, keepdims=True)
    chance = 1.0 / (1.0 + jnp.exp(-logits))
    logit_grad = (scaling * (before * chance + at * (chance - (1.0 - held)))).astype(BF16)
    grads[5][...] = mm_tn(pooled, logit_grad).astype(BF16)
    pooled_grad = mm(logit_grad, head[...]).astype(BF16).astype(F32)
    grad = jnp.zeros_like(normed)
    for s in range(SL_GRP):
        grad = grad + masks[s] * (pooled_grad[s : s + 1] / sizes[s])
    grad = norm_back(grad, normed, rstd)

    def put(i, a, b):
        grads[i + 1][...] = mm_tn(a, b).astype(BF16)

    grad = encode_back(grad, x, w_qkv, w_out, w_up, w_down, H_SL, res, packed_grad, put).astype(BF16)
    grads[0][...] = mm_tn(emb, grad).astype(BF16)
    return mm(grad, slide_in[...]).astype(BF16)


def region_backward(scaling, where, label, censor, *refs):
    ins, outs, bufs, obufs, extra, sems, osems = cut(refs, 19, 16, 19, 16, 10, 1, 1)
    h = lax.rem(where[0] // 4, 2)
    order = list(range(8)) + [18, 13, 17, 16, 14, 15, 9, 8, 10, 11, 12]
    late = dict()
    for i in list(dict.fromkeys(order)):
        late[i] = Late(ins[i], bufs[i], sems[0].at[i])
    early = []
    for i, r in enumerate(outs):
        early.append(Early(r, obufs[i], osems[0].at[i]) if i != 1 else obufs[1])
    message, tails = late[0], late[1]
    slide_weights = [late[i] for i in range(2, 8)]
    w_qkv, w_out, w_up, w_down = [late[i] for i in range(8, 12)]
    x_ref, res = late[12], [late[i] for i in range(13, 19)]
    losses, spread, pairs, slide_grads = early[0], early[1], early[2:10], early[10:16]
    packed_grad, slide_packed_grad, embeds, placed = extra[:4]
    ids, slide_col = tails_of(tails[...])
    rows32 = lax.broadcasted_iota(jnp.int32, (32, 32), 0)
    columns32 = lax.broadcasted_iota(jnp.int32, (32, 32), 1)
    slide_row = jnp.sum(jnp.where(rows32 == columns32, slide_col, 0.0), axis=0, keepdims=True)
    arrived = message[...]
    at = lax.broadcasted_iota(jnp.int32, arrived.shape, 1)
    for b in range(2):
        for c in range(3):
            part = jnp.sum(jnp.where(at == 3 * b + c, arrived, 0.0), axis=1)
            for y in range(4):
                placed[8 * y + 4 * b : 8 * y + 4 * b + 4, c * LANES : (c + 1) * LANES] = part[4 * y : 4 * y + 4]
    embeds[...] = placed[...].astype(BF16)
    cots = slide_step(
        embeds, slide_row, slide_col, label, censor, *slide_weights, losses, slide_grads, extra[4:10], slide_packed_grad, scaling
    ).astype(F32)
    for g in [losses] + slide_grads:
        send(g)
    first, slots = both_slots(ids, where[0])
    grads = []
    for b, usable in enumerate(usable_of(slots)):
        mine = lax.broadcasted_iota(jnp.int32, (32, 1), 0) == first + 4 * b
        own = jnp.sum(jnp.where(mine, cots, 0.0), axis=0, keepdims=True)
        grads.append(jnp.where(usable, own / slots[b][2], 0.0))
    grad = jnp.concatenate(grads, axis=0)
    normed, rstd = norm_parts(res[5][...])
    grad = norm_back(grad, normed, rstd)

    def put(i, a, b):
        for at, value in ((6 - 2 * i, a), (7 - 2 * i, b)):
            pairs[at][...] = value
            send(pairs[at])

    grad = encode_back(grad, x_ref[...], w_qkv, w_out, w_up, w_down, HEADS, res, packed_grad, put).astype(BF16)
    for b in range(8):
        spread[b] = mm_tn(choice(slots, b), grad).astype(BF16)
    leave([(spread.at[2 * y + h], outs[1].at[y]) for y in range(4)], sems[0])
    for e in early:
        if isinstance(e, Early):
            e.finish()


def two_halves(flat, runs, core, halves):
    run = 32 * 63
    for side in range(2):
        which = core if side == 0 else 1 - core
        for z in runs:
            start = pl.multiple_of((2 * z + which) * run, 32)
            halves[side][z * run : (z + 1) * run, :] = flat[pl.ds(start, run), :].astype(BF16)


def region_weights(core, where, *refs):
    ins, halves, bufs, (flat, run_buf), (sems,) = cut(refs, 8, 2, 8, 2, 1)
    late = [Late(r, b, sems.at[i]) for i, (r, b) in enumerate(zip(ins, bufs))]
    hidden, grad, second, up_grad, mixture, mid_grad, first, packed_grad = late
    put_rows(flat, 9216, hidden[...], grad[...])
    put_rows(flat, 4608, second[...], up_grad[...])
    put_rows(flat, 3456, mixture[...], mid_grad[...])
    put_rows(flat, 0, first[...], packed_grad[...])
    h = lax.rem(where[0] // 4, 2)
    for side in range(2):
        which = core[0] if side == 0 else 1 - core[0]
        for z in range(4):
            for y in range(4):
                start = pl.multiple_of((2 * z + which) * 1728 + y * 432 + h * 216, 8)
                run_buf[y * 216 : (y + 1) * 216, :] = flat[pl.ds(start, 216), :]
            halves[side][z * 864 : (z + 1) * 864, :] = run_buf[...].astype(BF16)


def tile_backward(core, ids, *refs):
    near, far, _, halves, bufs, packed_grad, flat, sems = cut(refs, 7, 7, 1, 2, 7, 1, 1, 1)
    arriving = {i: Late(far[i], bufs[i], sems[0].at[i]) for i in (6, 1, 5, 4, 3, 2, 0)}
    late = list(near[:3]) + [arriving[0], near[3], near[4], arriving[1], arriving[2], arriving[3], near[5], near[6]]
    late += [arriving[4], arriving[5], arriving[6]]
    arrived, patches, slide_rows = late[0], late[1], late[2]
    w_qkv, w_out, w_up, w_down = [late[i] for i in range(3, 7)]
    x_ref, res = late[7], [late[i] for i in range(8, 14)]
    rows32 = lax.broadcasted_iota(jnp.int32, (32, 32), 0)
    columns32 = lax.broadcasted_iota(jnp.int32, (32, 32), 1)
    assign = jnp.sum(jnp.where(rows32 == columns32, ids[...].astype(F32), 0.0), axis=1, keepdims=True)
    cot = jnp.zeros((32, D), F32)
    for i in range(16):
        region = float(i // 4 * 8 + i % 4)
        cot = cot + jnp.where((assign == region) | (assign == region + 4.0), arrived[i].astype(F32), 0.0)
    cot = cot * 0.25
    grad = jnp.concatenate([cot] * PATCHES, axis=0)
    normed, rstd = norm_parts(res[5][...])
    grad = norm_back(grad, normed, rstd)
    bases = (2304, 5760, 6912, 11520)


    def put(i, a, b):
        put_rows(flat[0], bases[i], a, b)
        if i == 2:
            two_halves(flat[0], (2, 3), core[0], halves)

    grad = encode_back(grad, x_ref[...], w_qkv, w_out, w_up, w_down, HEADS, res, packed_grad[0], put)
    for side in range(2):
        which = core[0] if side == 0 else 1 - core[0]
        halves[side][8064:8144, :] = slide_rows[which]
    put_rows(flat[0], 0, patches[...], grad.astype(BF16))
    two_halves(flat[0], (0, 1), core[0], halves)


def fold(rows, pad, tail, mine, got, *refs):
    _, (out,), extra, (total, stage) = cut(refs, tail, 1, tail, 2)
    planes = 1 + tail
    run = 16 * planes * rows
    for z in range(4):
        part = pl.ds(z * run, run)
        total[part, :] = mine[part, :].astype(F32) + got[part, :].astype(F32)
    if tail:
        part = pl.ds(4 * run, 80)
        extra[0][...] = (mine[part, :].astype(F32) + got[part, :].astype(F32)).astype(BF16)
    stage[4 * planes * rows :, :] = jnp.zeros((pad, LANES), F32)
    for y in range(4):
        for x in range(4):
            for z in range(4):
                for h in range(planes):
                    source = (z * 16 * planes + y * 4 * planes + h * 4 + x) * rows
                    target = (z * planes + h) * rows
                    stage[target : target + rows, :] = total[source : source + rows, :]
            out[y * 4 + x] = stage[...].astype(BF16)


def plane_sum(parts, out, buffer, total, sems):
    copies = []
    for i in range(2):
        part = pl.ds(i * 112, 112)
        copies.append(pltpu.make_async_copy(parts.at[:, part, :], buffer.at[:, part, :], sems.at[i]))
        copies[-1].start()
    for i in range(2):
        copies[i].wait()
        rows = slice(i * 112, (i + 1) * 112)
        value = buffer[0, rows, :].astype(F32)
        for j in range(1, 16):
            value = value + buffer[j, rows, :].astype(F32)
        total[rows, :] = value
    leave([(total, out)], sems)


def merge(where, tile_in, region_in, slide_in, out, tile_buf, region_buf, slide_buf, total, slide_total, stage, chunks, sems, osems):
    tile_late = Late(tile_in, tile_buf, sems.at[0])
    region_late = Late(region_in, region_buf, sems.at[1])
    slide_late = Late(slide_in, slide_buf, sems.at[2])
    slide_total[...] = slide_late[...].astype(F32)

    for start in range(0, 512, 64):
        value = tile_late[0, start : start + 64, :].astype(F32)
        for i in range(1, 16):
            value = value + tile_late[i, start : start + 64, :].astype(F32)
        total[start : start + 64, :] = value
    region_total = region_late.ref()
    h = lax.rem(where[0] // 4, 2)
    leaving = []
    for i in range(8):
        stage[0:63, :] = total[i * 63 : (i + 1) * 63, :]
        stage[63:64, :] = jnp.zeros((1, LANES), F32)
        rows = region_total[i // 2 * 54 : (i // 2 + 1) * 54, :]
        stage[64:118, :] = jnp.where(h == i % 2, rows, 0.0)
        stage[118:128, :] = slide_total[i * 10 : (i + 1) * 10, :]
        chunks[i] = stage[...].astype(BF16)
        leaving.append(pltpu.make_async_copy(chunks.at[i], out.at[i], osems.at[i]))
        leaving[-1].start()
    for copy in leaving:
        copy.wait()


def call(kernel, macs, outs, scratch, inputs, scalars=0, whole=0, mebibytes=60, direct=()):
    specs = [pl.BlockSpec(memory_space=pltpu.SMEM)] * scalars
    specs += [pl.BlockSpec(memory_space=pltpu.VMEM)] * whole
    specs += [pl.BlockSpec(memory_space=pl.ANY)] * (len(inputs) - scalars - whole)
    moved = sum(math.prod(a.shape) * a.dtype.itemsize for a in inputs) + sum(math.prod(a) * jnp.dtype(k).itemsize for a, k in outs)
    cost = pl.CostEstimate(flops=2 * macs, bytes_accessed=moved, transcendentals=0)
    return pl.pallas_call(
        kernel,
        out_shape=[jax.ShapeDtypeStruct(shape, kind) for shape, kind in outs],
        in_specs=specs,
        out_specs=[pl.BlockSpec(memory_space=pltpu.VMEM if i in direct else pl.ANY) for i in range(len(outs))],
        scratch_shapes=[pltpu.VMEM(*item) if isinstance(item, tuple) else item for item in scratch],
        compiler_params=pltpu.CompilerParams(vmem_limit_bytes=mebibytes * 1024 * 1024),
        cost_estimate=cost,
    )(*inputs)


def like(arrays):
    return [(a.shape, a.dtype) for a in arrays]


def semaphores(*shape):
    return pltpu.SemaphoreType.DMA(shape)


def residuals(tokens, width, hidden, heads):
    return [
        ((tokens, 3 * width), BF16),
        ((heads, tokens, tokens), F32),
        ((tokens, width), BF16),
        ((tokens, width), F32),
        ((tokens, hidden), F32),
        ((tokens, width), F32),
    ]


def index_of(z, core, y, z_hi, x):
    return (z * 2 + core) * 32 + y * 8 + z_hi * 4 + x


PLANES = [[index_of(z, c, y, h, x) for y in range(4) for x in range(4)] for z in range(4) for c in range(2) for h in range(2)]
COLUMNS = [[index_of(z, c, y, h, x) for z in range(4) for h in range(2)] for c in range(2) for y in range(4) for x in range(4)]
OTHER_CORE = [(g, g + 1 - 2 * (g % 2)) for g in range(8)]
OTHER_PLANE = [(d, d + 4 - 8 * (d // 4 % 2)) for d in range(32)]
ALL = ("grp", "dev")


def exchange(array, groups):
    return lax.all_to_all(array, ALL, 0, 0, axis_index_groups=groups)


def folded(mine, other, rows, pad, tail, after=()):
    got = lax.ppermute(other, "grp", OTHER_CORE)
    planes = 1 + tail
    chunk = 4 * planes * rows + pad
    outs = [(16, chunk, LANES)] + [(80, LANES)] * tail
    return pl.pallas_call(
        functools.partial(fold, rows, pad, tail),
        out_shape=[jax.ShapeDtypeStruct(shape, BF16) for shape in outs],
        in_specs=[pl.BlockSpec(memory_space=pltpu.VMEM)] * 2 + [pl.BlockSpec(memory_space=pl.ANY)] * tail,
        out_specs=[pl.BlockSpec(memory_space=pltpu.VMEM)] * len(outs),
        scratch_shapes=[pltpu.VMEM((64 * planes * rows, LANES), F32), pltpu.VMEM((chunk, LANES), F32)],
        compiler_params=pltpu.CompilerParams(vmem_limit_bytes=24 * 1024 * 1024),
        cost_estimate=pl.CostEstimate(flops=8 * US, bytes_accessed=1 << 20, transcendentals=0),
    )(mine, got, *after)


def body(
    patches,
    tile_region,
    region_slide,
    bin_label,
    censored,
    patch_w,
    tile_qkv,
    tile_out,
    tile_up,
    tile_down,
    region_qkv,
    region_out,
    region_up,
    region_down,
    slide_in,
    slide_qkv,
    slide_out,
    slide_up,
    slide_down,
    slide_head,
):
    member_index = lax.axis_index("dev").astype(jnp.int32)
    where = member_index.reshape(1)
    core = lax.rem(lax.axis_index("grp").astype(jnp.int32), 2).reshape(1)
    scaling = 1.0 / (bin_label.shape[1] * lax.axis_size("grp"))
    tokens = patches.transpose(1, 0, 2).reshape(128, 768)
    tile_res = [((128, D), F32)] + residuals(128, D, FF, HEADS)
    ins = (tokens, patch_w, tile_qkv, tile_out, tile_up, tile_down)
    message, *tile_kept = call(
        tile_forward,
        7 * US,
        [((112, LANES), BF16)] + tile_res,
        like(ins) + tile_res + [((112, LANES), BF16), semaphores(6), semaphores(7), semaphores(1)],
        (where, tile_region, region_slide) + ins,
        scalars=1,
        whole=2,
    )
    both = jnp.concatenate([message, lax.ppermute(message, "dev", OTHER_PLANE)], axis=0)
    rows = exchange(jnp.broadcast_to(both[None], (16, 224, LANES)), PLANES)
    region_res = [((2 * SLOTS, D), F32)] + residuals(2 * SLOTS, D, FF, HEADS)
    ins = (region_qkv, region_out, region_up, region_down)
    message, tails, *region_kept = call(
        region_forward,
        6 * US,
        [((16, 8, LANES), F32), ((32, 16, LANES), BF16)] + region_res,
        like(ins)
        + [((32, 112, LANES), BF16)]
        + region_res
        + [((8, LANES), F32), semaphores(4), semaphores(7), semaphores(33), semaphores(32)],
        (where, rows) + ins,
        scalars=1,
    )
    all_regions = exchange(message, PLANES)
    slide_weights = (slide_in, slide_qkv, slide_out, slide_up, slide_down, slide_head)
    widths = (FF, D, D, FF, D, D, D, 3 * D)
    pairs = [((2 * SLOTS, n), BF16) for n in widths]
    losses_out = [((1, SL_GRP), F32)]
    outs = losses_out + [((4, 128, D), BF16)] + pairs + like(slide_weights)
    buffers = losses_out + [((8, 128, D), BF16)] + pairs + like(slide_weights)
    ins = (all_regions, tails, slide_in.T) + slide_weights[1:5] + (slide_head.T,) + (region_qkv, region_out, region_up, region_down) + tuple(region_kept)
    losses, spread, *rest = call(
        functools.partial(region_backward, scaling),
        12 * US,
        outs,
        like(ins)
        + buffers
        + [((2 * SLOTS, 3 * D), BF16), ((32, 3 * D_SL), BF16), ((32, D), BF16), ((32, D), F32)]
        + residuals(32, D_SL, D_SL, H_SL)
        + [semaphores(19), semaphores(16)],
        (where, bin_label, censored) + ins,
        scalars=1,
        whole=2,
    )
    arrived = exchange(spread.reshape(16, 32, D), PLANES)
    ins = tuple(rest[:8])
    mine, other = call(
        region_weights,
        5 * US,
        [((3456, LANES), BF16)] * 2,
        like(ins) + [((13824, LANES), F32), ((864, LANES), F32), semaphores(8)],
        (core, where) + ins,
        scalars=2,
        mebibytes=56,
        direct=(0, 1),
    )
    (region_chunks,) = folded(mine, other, 54, 8, 0)
    region_parts = exchange(region_chunks, PLANES)
    (region_sums,) = call(
        plane_sum,
        20 * US,
        [((224, LANES), F32)],
        like((region_parts,)) + [((224, LANES), F32), semaphores(2)],
        (region_parts,),
        mebibytes=24,
    )
    slide_flat = jnp.concatenate([g.astype(F32).reshape(-1) for g in rest[8:]]).reshape(4, 2, 4, 2, 4, 1155)
    y, x = member_index // 8, lax.rem(member_index, 4)
    zero = jnp.zeros((), jnp.int32)
    slide_rows = lax.dynamic_slice(slide_flat, (zero, zero, y, zero, x, zero), (4, 2, 1, 2, 1, 1155))
    slide_rows = slide_rows.reshape(4, 2, 2, 1155).transpose(1, 0, 2, 3)
    slide_rows = jnp.pad(slide_rows, ((0, 0), (0, 0), (0, 0), (0, 125))).astype(BF16).reshape(2, 80, LANES)
    x, packed, attend, mixture, mid, up, out = tile_kept
    near = (arrived, tokens, slide_rows, tile_out, tile_up, attend, mixture)
    far = (tile_qkv, tile_down, x, packed, mid, up, out)
    mine, other = call(
        tile_backward,
        13 * US,
        [((8144, LANES), BF16)] * 2,
        like(far) + [((128, 3 * D), BF16), ((16128, LANES), F32), semaphores(7)],
        (core, tile_region) + near + far + (region_chunks,),
        scalars=1,
        whole=8,
        mebibytes=30,
        direct=(0, 1),
    )
    tile_chunks, slide_sums = folded(mine, other, 63, 8, 1, (region_sums,))
    tile_parts = exchange(tile_chunks, PLANES)
    ins = (tile_parts, region_sums, slide_sums)
    (last,) = call(
        merge,
        3 * US,
        [((8, 128, LANES), BF16)],
        like(ins)
        + [((512, LANES), F32), ((80, LANES), F32), ((128, LANES), F32), ((8, 128, LANES), BF16)]
        + [semaphores(3), semaphores(8)],
        (where,) + ins,
        scalars=1,
        mebibytes=24,
    )
    total = jnp.sum(exchange(last, COLUMNS).astype(F32), axis=0)
    tile_result = total[0:63].reshape(8064)
    region_result = total[64:118].reshape(6912)
    slide_result = total[118:128].reshape(1280)[:1155] * 0.5
    return (losses, tile_result, region_result, slide_result)


def solution(mesh):
    placed = (P(ALL, None, None), P("grp", "dev"), P("grp", "dev"), P("grp", None), P("grp", None)) + (P(),) * 15
    return jax.shard_map(
        body,
        mesh=mesh,
        in_specs=placed,
        out_specs=(P("grp", None), P(ALL), P(ALL), P(ALL)),
        check_vma=False,
    )
```
